32 devices in a mesh: dp: 8 (over z, y), tensor: 4 (over x, core).
Axes of the slice: x: 2, y: 2, z: 4, core: 2. Of those that a mesh axis runs over, the one named last changes fastest.
Arguments:
- frames_in: bfloat16 [8192, 1024], P(('dp', 'tensor')), may hold values from -6 to 6
- code_emb: bfloat16 [8192, 3, 1024], P(('dp', 'tensor')), may hold values from -6 to 6
- cotangent: bfloat16 [8192, 3, 1024], P(('dp', 'tensor')), may hold values from -6 to 6
- lengths: int32 [8], P('dp'), may hold values from 204 to 1024, as said below
- owner_list: int32 [8], replicated, may hold values from 0 to 7, each once
- master: float32 [2, 1024, 12288], P(None, 'dp', 'tensor'), may hold values from -2 to 2
- first_moment: float32 [2, 1024, 12288], P(None, 'dp', 'tensor'), may hold values from -300 to 300
- second_moment: float32 [2, 1024, 12288], P(None, 'dp', 'tensor'), may hold values from 100 to 100000
- ema: float32 [2, 1024, 12288], P(None, 'dp', 'tensor'), may hold values from -0.2 to 0.2
- left_basis: float32 [2, 1024, 512], P(None, 'dp', 'tensor'), may hold values from -1 to 1
- right_basis: float32 [2, 192, 128, 512], P(None, 'dp', None, 'tensor'), may hold values from -1 to 1
- gains: float32 [4, 1024], replicated, may hold values from 0.5 to 1.5
- gain_first: float32 [4, 1024], replicated, may hold values from -300 to 300
- gain_second: float32 [4, 1024], replicated, may hold values from 100 to 100000
Outputs:
- local_out: bfloat16 [8192, 3, 1024], P(('dp', 'tensor'))
- input_grad: float32 [8192, 1024], P(('dp', 'tensor'))
- weight_grads: float32 [2, 1024, 12288], P(None, 'dp', 'tensor')
- gain_grads: float32 [4, 1024], replicated
- new_master: float32 [2, 1024, 12288], P(None, 'dp', 'tensor')
- new_first: float32 [2, 1024, 12288], P(None, 'dp', 'tensor')
- new_second: float32 [2, 1024, 12288], P(None, 'dp', 'tensor')
- new_ema: float32 [2, 1024, 12288], P(None, 'dp', 'tensor')
- new_gains: float32 [4, 1024], replicated
- new_gain_first: float32 [4, 1024], replicated
- new_gain_second: float32 [4, 1024], replicated
The draws below stay inside these ranges and needn't reach their ends.
Inputs may be any that keep to these rules, and one draw needn't show every extreme that they name: lengths[i] counts the valid frames of item i, at least 204; in every draw some item has exactly 1024. owner_list is a permutation of 0 to 7.
All inputs are finite; a program needn't handle non-finite values.
Results may differ from the reference program's by a relative error of at most 0.035.
Values may be sent and summed in bfloat16 or wider, within the bound.
A program may use at most 320 MiB of HBM per device.

```python
import math
import jax
import jax.numpy as jnp
from jax import lax

D = 1024
HEADS = 16
HD = 64
FF = 4096
CB = 3
LMAX = 1024
ITEMS = 1
BLK = 128
HEAD_COLS = 256
FF_DEV = 1024
COLS_DEV = 3072
COLS = 12288
NB = 24
R = 128
FRAMES = 8192
ITEMS_ALL = 8
N_DP = 8
N_TENSOR = 4


def draw_lengths(key, part):
    shortest = LMAX // 5
    spread_len = LMAX - shortest
    item_count = ITEMS * N_DP
    first_key, second_key, pick_key = jax.random.split(key, 3)
    first_draw = jax.random.randint(first_key, (item_count,), 0, spread_len + 1)
    second_draw = jax.random.randint(second_key, (item_count,), 0, spread_len + 1)
    lengths_out = shortest + first_draw * second_draw // max(spread_len, 1)
    longest_at = jax.random.randint(pick_key, (), 0, item_count)
    lengths_out = jnp.where(jnp.arange(item_count) == longest_at, LMAX, lengths_out)
    return lengths_out.astype(jnp.int32)


def draw_master(key, part):
    shape_all = (2, D, COLS)
    base_values = jnp.clip(jax.random.normal(key, shape_all, jnp.float32), -4.0, 4.0)
    within = lax.broadcasted_iota(jnp.int32, shape_all, 2) % COLS_DEV
    column_scale = jnp.where(within < 3 * HEAD_COLS, D ** (-0.5), jnp.where(within < 4 * HEAD_COLS, 4.0 * D ** (-0.5), jnp.where(within < 4 * HEAD_COLS + FF_DEV, D ** (-0.5), FF ** (-0.5))))
    return (base_values * column_scale).astype(jnp.float32)


def hadamard_sign(row_at, col_at, width):
    common_bits = jnp.bitwise_and(row_at, col_at)
    parity = jnp.zeros_like(common_bits)
    for shift_at in range(max(width.bit_length() - 1, 1)):
        parity = jnp.bitwise_xor(parity, jnp.bitwise_and(jnp.right_shift(common_bits, shift_at), 1))
    return 1.0 - 2.0 * parity.astype(jnp.float32)


def rotation_tiles(key, outer, width, blocks_rows, blocks_cols):
    sign_key, angle_key = jax.random.split(key)
    row_signs = jnp.where(jax.random.bernoulli(sign_key, 0.5, (outer, blocks_rows, width, blocks_cols, 1)), 1.0, -1.0)
    angles = jax.random.uniform(angle_key, (outer, blocks_rows, 1, blocks_cols, width // 2, 1), jnp.float32, -math.pi, math.pi)
    angles = jnp.broadcast_to(angles, (outer, blocks_rows, 1, blocks_cols, width // 2, 2)).reshape(outer, blocks_rows, 1, blocks_cols, width)
    row_at = lax.broadcasted_iota(jnp.int32, (width, 1, width), 0)
    col_at = lax.broadcasted_iota(jnp.int32, (width, 1, width), 2)
    partner = jnp.bitwise_xor(col_at, 1)
    own_sign = hadamard_sign(row_at, col_at, width)
    pair_sign = hadamard_sign(row_at, partner, width)
    even_cols = col_at % 2 == 0
    cosine = jnp.cos(angles)
    sine_part = jnp.sin(angles)
    tile_values = (cosine * own_sign + jnp.where(even_cols, sine_part, -sine_part) * pair_sign) * width ** (-0.5) * row_signs
    return tile_values.reshape(outer, blocks_rows * width, blocks_cols * width).astype(jnp.float32)


def draw_left_basis(key, part):
    return rotation_tiles(key, 2, R, N_DP, N_TENSOR)


def draw_right_basis(key, part):
    tiles_all = rotation_tiles(key, 2 * N_DP * NB, BLK, 1, N_TENSOR)
    return tiles_all.reshape(2, N_DP * NB, BLK, N_TENSOR * BLK)


def block_scale(own_key, extent, pieces, smallest, high):
    def one(axis_at, blocks):
        draws = jax.random.uniform(jax.random.fold_in(jax.random.fold_in(own_key, 6), axis_at), (blocks,), jnp.float32, smallest / len(pieces), high / len(pieces))
        return jnp.repeat(jnp.exp(draws), extent[axis_at] // blocks).reshape((-1,) + (1,) * (len(extent) - axis_at - 1))

    level = one(*pieces[0])
    for cut in pieces[1:]:
        level = level * one(*cut)
    return level


def bell_draw(stream_key, dims, scale, bound, cuts=(), kind=jnp.bfloat16):
    values = scale * jax.random.normal(stream_key, dims, jnp.float32)
    if cuts:
        values = values * block_scale(stream_key, dims, cuts, -0.22, 0.18)
    return jnp.clip(values, -bound, bound).astype(kind)


def setup_inputs(seed: int = 0) -> dict:
    key_of = jax.random.split(jax.random.key(seed), 15)
    return {
        "frames_in": bell_draw(key_of[0], (FRAMES, D), 1.0, 6.0, ((0, 32),)),
        "code_emb": bell_draw(key_of[1], (FRAMES, CB, D), 1.0, 6.0, ((0, 32),)),
        "cotangent": bell_draw(key_of[2], (FRAMES, CB, D), 1.0, 6.0, ((0, 32),)),
        "lengths": draw_lengths(jax.random.fold_in(key_of[14], 71), 0),
        "owner_list": jax.random.permutation(key_of[4], N_DP).astype(jnp.int32),
        "master": draw_master(jax.random.fold_in(key_of[14], 71), 0),
        "first_moment": bell_draw(key_of[6], (2, D, COLS), 50.0, 300.0, ((1, 8), (2, 4)), jnp.float32),
        "second_moment": jnp.clip(jnp.exp(math.log(100000.0) - 6.9077553 * jax.random.uniform(key_of[7], (2, D, COLS), jnp.float32) ** block_scale(key_of[7], (2, D, COLS), ((1, 8), (2, 4)), -0.2, 0.2)), 100.0, 100000.0),
        "ema": bell_draw(key_of[8], (2, D, COLS), 0.03, 0.2, ((1, 8), (2, 4)), jnp.float32),
        "left_basis": draw_left_basis(jax.random.fold_in(key_of[14], 71), 0),
        "right_basis": draw_right_basis(jax.random.fold_in(key_of[14], 71), 0),
        "gains": jnp.clip(1.0 + 0.1 * jax.random.normal(key_of[11], (4, D), jnp.float32), 0.5, 1.5),
        "gain_first": bell_draw(key_of[12], (4, D), 50.0, 300.0, (), jnp.float32),
        "gain_second": jnp.clip(jnp.exp(jax.random.uniform(key_of[13], (4, D), jnp.float32, math.log(100.0), math.log(100000.0))), 100.0, 100000.0),
    }


@jax.custom_vjp
def low(v):
    return lax.optimization_barrier(v.astype(jnp.bfloat16)).astype(jnp.float32)

@jax.custom_vjp
def low_back(v):
    return v

def low_keep(v):
    return (low(v), None)

def low_pass(kept, grad):
    return (grad,)

def back_keep(v):
    return (v, None)

def back_low(kept, grad):
    return (low(grad),)
low.defvjp(low_keep, low_pass)
low_back.defvjp(back_keep, back_low)
norm_eps = 1e-06
beta_first = 0.5
beta_second = 0.5
adam_eps = 1e-08
step_rate = 0.05
gain_rate = 0.4
ema_decay = 0.9
masked_fill = -1e+30
highest = lax.Precision.HIGHEST

def matmul(left, right):
    return jnp.dot(left, right, precision=highest, preferred_element_type=jnp.float32)

def rms_norm(rows_in, gain):
    return rows_in * lax.rsqrt(lax.optimization_barrier(jnp.mean(rows_in * rows_in, axis=-1, keepdims=True)) + norm_eps) * gain

def split_reference(layer):
    grouped = layer.reshape(D, N_TENSOR, COLS_DEV)

    def columns(begin, width):
        return grouped[:, :, begin:begin + width].reshape(D, N_TENSOR * width)
    return (columns(0, HEAD_COLS), columns(HEAD_COLS, HEAD_COLS), columns(2 * HEAD_COLS, HEAD_COLS), columns(3 * HEAD_COLS, HEAD_COLS), columns(4 * HEAD_COLS, FF_DEV), columns(4 * HEAD_COLS + FF_DEV, FF_DEV))

def block(rows_in, matrices, gain_a, gain_b, attend):
    w_query, w_key, w_value, w_out, w_up, w_down = matrices
    normed_a = low(rms_norm(rows_in, gain_a))
    queries = low(low_back(matmul(normed_a, w_query)))
    key_rows = low(low_back(matmul(normed_a, w_key)))
    value_rows = low(low_back(matmul(normed_a, w_value)))
    mixed = low(low_back(attend(queries, key_rows, value_rows)))
    middle = rows_in + low_back(matmul(mixed, w_out.T))
    normed_b = low(rms_norm(middle, gain_b))
    upper = low_back(matmul(normed_b, w_up))
    active = low(jax.nn.gelu(upper, approximate=False))
    return middle + low_back(matmul(active, w_down.T))

def global_attention(queries, key_rows, value_rows, length):
    span = queries.shape[0]
    query_heads = queries.reshape(span, HEADS, HD)
    key_heads = key_rows.reshape(span, HEADS, HD)
    value_heads = value_rows.reshape(span, HEADS, HD)
    scores = low_back(jnp.einsum('qhd,khd->hqk', query_heads, key_heads, precision=highest) * HD ** (-0.5))
    rows_at = lax.broadcasted_iota(jnp.int32, (span, span), 0)
    cols_at = lax.broadcasted_iota(jnp.int32, (span, span), 1)
    allowed = (cols_at <= rows_at) & (cols_at < length)
    scores = jnp.where(allowed[None], scores, masked_fill)
    probability = low(jax.nn.softmax(scores, axis=-1))
    return jnp.einsum('hqk,khd->qhd', probability, value_heads, precision=highest).reshape(span, D)

def local_attention(queries, key_rows, value_rows):
    frame_count = queries.shape[0] // CB
    query_heads = queries.reshape(frame_count, CB, HEADS, HD)
    key_heads = key_rows.reshape(frame_count, CB, HEADS, HD)
    value_heads = value_rows.reshape(frame_count, CB, HEADS, HD)
    scores = low_back(jnp.einsum('fqhd,fkhd->fhqk', query_heads, key_heads, precision=highest) * HD ** (-0.5))
    rows_at = lax.broadcasted_iota(jnp.int32, (CB, CB), 0)
    cols_at = lax.broadcasted_iota(jnp.int32, (CB, CB), 1)
    scores = jnp.where(cols_at <= rows_at, scores, masked_fill)
    probability = low(jax.nn.softmax(scores, axis=-1))
    return jnp.einsum('fhqk,fkhd->fqhd', probability, value_heads, precision=highest).reshape(queries.shape[0], D)

def reference(frames_in, code_emb, cotangent, lengths, owner_list, master, first_moment, second_moment, ema, left_basis, right_basis, gains, gain_first, gain_second):
    true_weights = master.reshape(2, N_DP, R, COLS)[:, owner_list].reshape(2, D, COLS)
    rows_all = frames_in.astype(jnp.float32).reshape(ITEMS_ALL, LMAX, D)
    codes_all = code_emb.astype(jnp.float32).reshape(ITEMS_ALL, LMAX, CB, D)
    cot_all = cotangent.astype(jnp.float32).reshape(ITEMS_ALL, LMAX, CB, D)

    def per_item(totals, packed):
        item_rows, item_codes, item_cot, length = packed

        def attend_global(queries, key_rows, value_rows):
            return global_attention(queries, key_rows, value_rows, length)

        def forward(rows_in, weight_values, norm_gains):
            rounded = low(weight_values)
            first_out = block(rows_in, split_reference(rounded[0]), norm_gains[0], norm_gains[1], attend_global)
            local_rows = (first_out[:, None, :] + item_codes).reshape(LMAX * CB, D)
            return block(local_rows, split_reference(rounded[1]), norm_gains[2], norm_gains[3], local_attention)
        result, pullback = jax.vjp(forward, item_rows, true_weights, gains)
        valid = (jnp.arange(LMAX, dtype=jnp.int32) < length).astype(jnp.float32)
        seed_grad = (item_cot * valid[:, None, None]).reshape(LMAX * CB, D)
        grad_rows, grad_weights, grad_gains = pullback(seed_grad)
        return ((totals[0] + grad_weights, totals[1] + grad_gains), (result, grad_rows))
    start_totals = (jnp.zeros((2, D, COLS), jnp.float32), jnp.zeros((4, D), jnp.float32))
    (weight_total, gain_grads), (results, grad_rows) = lax.scan(per_item, start_totals, (rows_all, codes_all, cot_all, lengths))
    local_out = results.reshape(FRAMES, CB, D).astype(jnp.bfloat16)
    input_grad = grad_rows.reshape(FRAMES, D)
    slots = jnp.arange(N_DP, dtype=jnp.int32)
    inverse = lax.optimization_barrier(jnp.sum(jnp.where(owner_list[None, :] == slots[:, None], slots[None, :], 0), axis=1)).astype(jnp.int32)
    weight_grads = weight_total.reshape(2, N_DP, R, COLS)[:, inverse].reshape(2, D, COLS)
    tile_shape = (2, N_DP, R, N_TENSOR, NB, BLK)
    left_tiles = left_basis.reshape(2, N_DP, R, N_TENSOR, R)
    right_tiles = right_basis.reshape(2, N_DP, NB, BLK, N_TENSOR, BLK)
    turned_left = jnp.einsum('liatb,liatkc->libtkc', left_tiles, weight_grads.reshape(tile_shape), precision=highest)
    rotated = jnp.einsum('libtkc,likcte->libtke', turned_left, right_tiles, precision=highest).reshape(2, D, COLS)
    new_first = beta_first * first_moment + (1.0 - beta_first) * rotated
    new_second = beta_second * second_moment + (1.0 - beta_second) * rotated * rotated
    turned = new_first / (jnp.sqrt(new_second) + adam_eps)
    back_right = jnp.einsum('libtke,likcte->libtkc', turned.reshape(tile_shape), right_tiles, precision=highest)
    back_full = jnp.einsum('liatb,libtkc->liatkc', left_tiles, back_right, precision=highest).reshape(2, D, COLS)
    new_master = master - step_rate * back_full
    new_ema = ema_decay * ema + (1.0 - ema_decay) * new_master
    new_gain_first = beta_first * gain_first + (1.0 - beta_first) * gain_grads
    new_gain_second = beta_second * gain_second + (1.0 - beta_second) * gain_grads * gain_grads
    new_gains = gains - gain_rate * new_gain_first / (jnp.sqrt(new_gain_second) + adam_eps)
    return (local_out, input_grad, weight_grads, gain_grads, new_master, new_first, new_second, new_ema, new_gains, new_gain_first, new_gain_second)
```

```python
import math

import jax
import jax.numpy as jnp
from jax import lax
from jax.experimental import pallas as pl
from jax.experimental.pallas import tpu as pltpu
from jax.sharding import PartitionSpec as P

D = 1024
HD = 64
FF = 4096
CB = 3
LMAX = 1024


norm_eps = 1e-06
beta_first = 0.5
beta_second = 0.5
adam_eps = 1e-08
step_rate = 0.05
gain_rate = 0.4
ema_decay = 0.9
masked_fill = -1e30
highest = lax.Precision.HIGHEST


def dot_rows(left, right):
    return jnp.dot(left, right, preferred_element_type=jnp.float32)


def dot_transposed(left, right):
    return lax.dot_general(
        left, right, (((1,), (1,)), ((), ())), preferred_element_type=jnp.float32
    )


def dot_over_rows(left, right):
    return lax.dot_general(
        left, right, (((0,), (0,)), ((), ())), preferred_element_type=jnp.float32
    )


def keep_rows(values):
    return values


def row_term(operand, weight):
    return dot_transposed(operand, weight)


def rms_forward(rows_in, gain):
    return (
        rows_in * lax.rsqrt(jnp.mean(rows_in * rows_in, axis=-1, keepdims=True) + norm_eps) * gain
    )


def rms_backward(rows_in, gain, grad_out):
    width = rows_in.shape[-1]
    scale_rows = lax.rsqrt(jnp.mean(rows_in * rows_in, axis=-1, keepdims=True) + norm_eps)
    scaled_grad = grad_out * gain
    inner_total = jnp.sum(scaled_grad * rows_in, axis=-1, keepdims=True)
    grad_in = (
        scale_rows * scaled_grad
        - rows_in * (scale_rows * scale_rows * scale_rows) * inner_total / width
    )
    gain_grad = jnp.sum(grad_out * rows_in * scale_rows, axis=0)
    return (grad_in, gain_grad)


def gelu_slope(upper):
    normal_cdf = 0.5 * (1.0 + lax.erf(upper * (1.0 / math.sqrt(2.0))))
    density = jnp.exp(-0.5 * upper * upper) * (1.0 / math.sqrt(2.0 * math.pi))
    return normal_cdf + upper * density


def split_layer(layer_cols, groups, head_cols, ff_cols):
    width = layer_cols.shape[0]
    grouped = layer_cols.reshape(width, groups, -1)

    def columns(begin, extent):
        return grouped[:, :, begin : begin + extent].reshape(width, groups * extent)

    w_qkv = jnp.concatenate(
        [columns(0, head_cols), columns(head_cols, head_cols), columns(2 * head_cols, head_cols)],
        axis=1,
    )
    return (
        w_qkv,
        columns(3 * head_cols, head_cols),
        columns(4 * head_cols, ff_cols),
        columns(4 * head_cols + ff_cols, ff_cols),
    )


def join_layer(grad_parts, groups):
    grad_qkv, grad_out, grad_up, grad_down = grad_parts
    width = grad_qkv.shape[0]
    head_width = grad_qkv.shape[1] // 3
    pieces = [
        grad_qkv[:, 0:head_width],
        grad_qkv[:, head_width : 2 * head_width],
        grad_qkv[:, 2 * head_width :],
        grad_out,
        grad_up,
        grad_down,
    ]
    return jnp.concatenate([piece.reshape(width, groups, -1) for piece in pieces], axis=2).reshape(
        width, -1
    )


def global_scores(queries, key_rows, length):
    span = queries.shape[0]
    heads = queries.shape[1] // HD
    scores = jnp.einsum(
        "qhd,khd->hqk",
        queries.reshape(span, heads, HD),
        key_rows.reshape(span, heads, HD),
        preferred_element_type=jnp.float32,
    ) * HD ** (-0.5)
    rows_at = lax.broadcasted_iota(jnp.int32, (span, span), 0)
    cols_at = lax.broadcasted_iota(jnp.int32, (span, span), 1)
    allowed = (cols_at <= rows_at) & (cols_at < length)
    return jnp.where(allowed[None], scores, masked_fill)


def global_attend(queries, key_rows, value_rows, lengths):
    items = lengths.shape[0]
    span = queries.shape[0] // items
    heads = queries.shape[1] // HD

    def one_item(packed):
        item_query, item_key, item_value, length = packed
        scores = global_scores(item_query, item_key, length)
        row_max = jnp.max(scores, axis=-1, keepdims=True)
        expanded = jnp.exp(scores - row_max)
        row_total = jnp.sum(expanded, axis=-1, keepdims=True)
        probability = (expanded / row_total).astype(jnp.bfloat16)
        mixed = jnp.einsum(
            "hqk,khd->qhd",
            probability,
            item_value.reshape(span, heads, HD),
            preferred_element_type=jnp.float32,
        )
        return (
            mixed.reshape(span, -1).astype(jnp.bfloat16),
            (row_max + jnp.log(row_total))[..., 0],
        )

    mixed, log_total = lax.map(
        one_item,
        (
            queries.reshape(items, span, -1),
            key_rows.reshape(items, span, -1),
            value_rows.reshape(items, span, -1),
            lengths,
        ),
    )
    return (mixed.reshape(items * span, -1), log_total)


def global_attend_back(queries, key_rows, value_rows, lengths, log_total, grad_mixed):
    items = lengths.shape[0]
    span = queries.shape[0] // items
    heads = queries.shape[1] // HD
    scale_score = HD ** (-0.5)

    def one_item(packed):
        item_query, item_key, item_value, length, item_lse, item_grad = packed
        scores = global_scores(item_query, item_key, length)
        probability = jnp.exp(scores - item_lse[..., None])
        grad_heads = item_grad.reshape(span, heads, HD)
        query_heads = item_query.reshape(span, heads, HD)
        key_heads = item_key.reshape(span, heads, HD)
        value_heads = item_value.reshape(span, heads, HD)
        grad_value = jnp.einsum(
            "hqk,qhd->khd",
            probability.astype(jnp.bfloat16),
            grad_heads,
            preferred_element_type=jnp.float32,
        )
        grad_prob = jnp.einsum(
            "qhd,khd->hqk", grad_heads, value_heads, preferred_element_type=jnp.float32
        )
        center = jnp.sum(probability * grad_prob, axis=-1, keepdims=True)
        grad_scores = (probability * (grad_prob - center)).astype(jnp.bfloat16)
        grad_query = (
            jnp.einsum("hqk,khd->qhd", grad_scores, key_heads, preferred_element_type=jnp.float32)
            * scale_score
        )
        grad_key = (
            jnp.einsum("hqk,qhd->khd", grad_scores, query_heads, preferred_element_type=jnp.float32)
            * scale_score
        )
        return jnp.concatenate(
            [
                grad_query.reshape(span, -1),
                grad_key.reshape(span, -1),
                grad_value.reshape(span, -1),
            ],
            axis=1,
        ).astype(jnp.bfloat16)

    grads = lax.map(
        one_item,
        (
            queries.reshape(items, span, -1),
            key_rows.reshape(items, span, -1),
            value_rows.reshape(items, span, -1),
            lengths,
            log_total,
            grad_mixed.reshape(items, span, -1),
        ),
    )
    return grads.reshape(items * span, -1)


def local_probability(queries, key_rows):
    frame_count = queries.shape[0] // CB
    heads = queries.shape[1] // HD
    scores = jnp.einsum(
        "fqhd,fkhd->fhqk",
        queries.reshape(frame_count, CB, heads, HD),
        key_rows.reshape(frame_count, CB, heads, HD),
        preferred_element_type=jnp.float32,
    ) * HD ** (-0.5)
    rows_at = lax.broadcasted_iota(jnp.int32, (CB, CB), 0)
    cols_at = lax.broadcasted_iota(jnp.int32, (CB, CB), 1)
    scores = jnp.where(cols_at <= rows_at, scores, masked_fill)
    row_max = jnp.max(scores, axis=-1, keepdims=True)
    expanded = jnp.exp(scores - row_max)
    return expanded / jnp.sum(expanded, axis=-1, keepdims=True)


def local_attend(queries, key_rows, value_rows):
    frame_count = queries.shape[0] // CB
    heads = queries.shape[1] // HD
    probability = local_probability(queries, key_rows).astype(jnp.bfloat16)
    mixed = jnp.einsum(
        "fhqk,fkhd->fqhd",
        probability,
        value_rows.reshape(frame_count, CB, heads, HD),
        preferred_element_type=jnp.float32,
    )
    return (mixed.reshape(queries.shape[0], -1).astype(jnp.bfloat16), jnp.zeros((), jnp.float32))


def local_attend_back(queries, key_rows, value_rows, saved, grad_mixed):
    frame_count = queries.shape[0] // CB
    heads = queries.shape[1] // HD
    scale_score = HD ** (-0.5)
    probability = local_probability(queries, key_rows)
    grad_heads = grad_mixed.reshape(frame_count, CB, heads, HD)
    query_heads = queries.reshape(frame_count, CB, heads, HD)
    key_heads = key_rows.reshape(frame_count, CB, heads, HD)
    value_heads = value_rows.reshape(frame_count, CB, heads, HD)
    grad_value = jnp.einsum(
        "fhqk,fqhd->fkhd",
        probability.astype(jnp.bfloat16),
        grad_heads,
        preferred_element_type=jnp.float32,
    )
    grad_prob = jnp.einsum(
        "fqhd,fkhd->fhqk", grad_heads, value_heads, preferred_element_type=jnp.float32
    )
    center = jnp.sum(probability * grad_prob, axis=-1, keepdims=True)
    grad_scores = (probability * (grad_prob - center)).astype(jnp.bfloat16)
    grad_query = (
        jnp.einsum("fhqk,fkhd->fqhd", grad_scores, key_heads, preferred_element_type=jnp.float32)
        * scale_score
    )
    grad_key = (
        jnp.einsum("fhqk,fqhd->fkhd", grad_scores, query_heads, preferred_element_type=jnp.float32)
        * scale_score
    )
    total_rows = queries.shape[0]
    return jnp.concatenate(
        [
            grad_query.reshape(total_rows, -1),
            grad_key.reshape(total_rows, -1),
            grad_value.reshape(total_rows, -1),
        ],
        axis=1,
    ).astype(jnp.bfloat16)


def block_forward(rows_in, matrices, gain_a, gain_b, path, attend):
    gather_rows, sum_rows = (path[0], path[1])
    w_qkv, w_out, w_up, w_down = matrices
    normed_a = gather_rows(rms_forward(rows_in, gain_a).astype(jnp.bfloat16))
    projected = dot_rows(normed_a, w_qkv).astype(jnp.bfloat16)
    head_width = projected.shape[1] // 3
    mixed, saved = attend(
        projected[:, :head_width],
        projected[:, head_width : 2 * head_width],
        projected[:, 2 * head_width :],
    )
    middle = rows_in + sum_rows(mixed, w_out)
    normed_b = gather_rows(rms_forward(middle, gain_b).astype(jnp.bfloat16))
    upper = dot_rows(normed_b, w_up)
    active = jax.nn.gelu(upper, approximate=False).astype(jnp.bfloat16)
    result = middle + sum_rows(active, w_down)
    return (result, (rows_in, normed_a, projected, mixed, saved, middle, normed_b, upper, active))


def block_backward(grad_result, kept, matrices, gain_a, gain_b, path, attend_back):
    gather_grads, sum_back = (path[2], path[3])
    rows_in, normed_a, projected, mixed, saved, middle, normed_b, upper, active = kept
    w_qkv, w_out, w_up, w_down = matrices
    grad_branch = gather_grads(grad_result.astype(jnp.bfloat16))
    grad_down = dot_over_rows(grad_branch, active)
    grad_active = dot_rows(grad_branch, w_down)
    grad_upper = (grad_active * gelu_slope(upper)).astype(jnp.bfloat16)
    grad_up = dot_over_rows(normed_b, grad_upper)
    grad_normed_b = sum_back(grad_upper, w_up)
    grad_middle_part, gain_b_grad = rms_backward(middle, gain_b, grad_normed_b)
    grad_middle = grad_result + grad_middle_part
    grad_attn = gather_grads(grad_middle.astype(jnp.bfloat16))
    grad_out = dot_over_rows(grad_attn, mixed)
    grad_mixed = dot_rows(grad_attn, w_out).astype(jnp.bfloat16)
    head_width = projected.shape[1] // 3
    grad_qkv = attend_back(
        projected[:, :head_width],
        projected[:, head_width : 2 * head_width],
        projected[:, 2 * head_width :],
        saved,
        grad_mixed,
    )
    grad_weight_qkv = dot_over_rows(normed_a, grad_qkv)
    grad_normed_a = sum_back(grad_qkv, w_qkv)
    grad_rows_part, gain_a_grad = rms_backward(rows_in, gain_a, grad_normed_a)
    return (
        grad_middle + grad_rows_part,
        (grad_weight_qkv, grad_out, grad_up, grad_down),
        gain_a_grad,
        gain_b_grad,
    )


def shards_any(
    frames_in,
    code_emb,
    cotangent,
    lengths,
    owner_list,
    master,
    first_moment,
    second_moment,
    ema,
    left_basis,
    right_basis,
    gains,
    gain_first,
    gain_second,
):
    tensor_count = lax.axis_size("tensor")
    group_count = lax.axis_size("dp")
    head_cols = D // tensor_count
    ff_cols = FF // tensor_count
    share = frames_in.shape[0]
    owned_rows = master.shape[1]
    gathered = lax.all_gather(master.astype(jnp.bfloat16), "dp", axis=1, tiled=True)
    layers = jnp.take(gathered.reshape(2, group_count, owned_rows, -1), owner_list, axis=1).reshape(
        2, group_count * owned_rows, -1
    )

    def gather_rows(values):
        return lax.all_gather(values, "tensor", axis=0, tiled=True)

    def gather_grads(values):
        return lax.all_gather(values, "tensor", axis=0, tiled=True)

    def sum_rows(operand, weight):
        return lax.psum_scatter(
            row_term(operand, weight).astype(jnp.bfloat16),
            "tensor",
            scatter_dimension=0,
            tiled=True,
        ).astype(jnp.float32)

    def sum_back(operand, weight):
        return lax.psum_scatter(
            row_term(operand, weight).astype(jnp.bfloat16),
            "tensor",
            scatter_dimension=0,
            tiled=True,
        ).astype(jnp.float32)

    heads_path = (gather_rows, sum_rows, gather_grads, sum_back)
    rows_path = (keep_rows, dot_transposed, keep_rows, dot_transposed)

    def attend_global(queries, key_rows, value_rows):
        return global_attend(queries, key_rows, value_rows, lengths)

    def attend_global_back(queries, key_rows, value_rows, saved, grad_mixed):
        return global_attend_back(queries, key_rows, value_rows, lengths, saved, grad_mixed)

    global_matrices = split_layer(layers[0], 1, head_cols, ff_cols)
    global_out, global_kept = block_forward(
        frames_in.astype(jnp.float32),
        global_matrices,
        gains[0],
        gains[1],
        heads_path,
        attend_global,
    )
    local_in = (global_out[:, None, :] + code_emb.astype(jnp.float32)).reshape(share * CB, -1)
    local_layer = lax.all_gather(layers[1], "tensor", axis=1, tiled=True)
    local_matrices = split_layer(local_layer, tensor_count, head_cols, ff_cols)
    local_result, local_kept = block_forward(
        local_in, local_matrices, gains[2], gains[3], rows_path, local_attend
    )
    local_out = local_result.reshape(share, CB, -1).astype(jnp.bfloat16)
    frame_at = lax.axis_index("tensor") * share + jnp.arange(share, dtype=jnp.int32)
    item_at = frame_at // LMAX
    item_slots = jnp.arange(lengths.shape[0], dtype=jnp.int32)
    item_length = jnp.sum(
        jnp.where(item_at[:, None] == item_slots[None, :], lengths[None, :], 0), axis=1
    )
    valid = (frame_at % LMAX < item_length).astype(jnp.float32)
    grad_local = (cotangent.astype(jnp.float32) * valid[:, None, None]).reshape(share * CB, -1)
    grad_local_in, local_weight_grads, gain_c_grad, gain_d_grad = block_backward(
        grad_local, local_kept, local_matrices, gains[2], gains[3], rows_path, local_attend_back
    )
    grad_global_out = jnp.sum(grad_local_in.reshape(share, CB, -1), axis=1)
    input_grad, global_weight_grads, gain_a_grad, gain_b_grad = block_backward(
        grad_global_out,
        global_kept,
        global_matrices,
        gains[0],
        gains[1],
        heads_path,
        attend_global_back,
    )
    local_grads = join_layer(local_weight_grads, tensor_count)
    local_grads = lax.psum_scatter(
        local_grads.astype(jnp.bfloat16), "tensor", scatter_dimension=1, tiled=True
    ).astype(jnp.float32)
    layer_grads = jnp.stack([join_layer(global_weight_grads, 1), local_grads])
    slots = jnp.arange(group_count, dtype=jnp.int32)
    inverse = jnp.sum(jnp.where(owner_list[None, :] == slots[:, None], slots[None, :], 0), axis=1)
    ordered = jnp.take(
        layer_grads.reshape(2, group_count, owned_rows, -1), inverse, axis=1
    ).reshape(2, group_count * owned_rows, -1)
    weight_grads = lax.psum_scatter(
        ordered.astype(jnp.bfloat16), "dp", scatter_dimension=1, tiled=True
    ).astype(jnp.float32)
    gain_grads = lax.psum(
        jnp.stack([gain_a_grad, gain_b_grad, gain_c_grad, gain_d_grad]), ("dp", "tensor")
    )
    tile_count = right_basis.shape[1]
    turned_left = jnp.einsum("lab,lac->lbc", left_basis, weight_grads, precision=highest)
    rotated = jnp.einsum(
        "lbkc,lkce->lbke",
        turned_left.reshape(2, owned_rows, tile_count, -1),
        right_basis,
        precision=highest,
    ).reshape(weight_grads.shape)
    new_first = beta_first * first_moment + (1.0 - beta_first) * rotated
    new_second = beta_second * second_moment + (1.0 - beta_second) * rotated * rotated
    turned = new_first / (jnp.sqrt(new_second) + adam_eps)
    back_right = jnp.einsum(
        "lbke,lkce->lbkc",
        turned.reshape(2, owned_rows, tile_count, -1),
        right_basis,
        precision=highest,
    )
    back_full = jnp.einsum(
        "lab,lbc->lac", left_basis, back_right.reshape(weight_grads.shape), precision=highest
    )
    new_master = master - step_rate * back_full
    new_ema = ema_decay * ema + (1.0 - ema_decay) * new_master
    new_gain_first = beta_first * gain_first + (1.0 - beta_first) * gain_grads
    new_gain_second = beta_second * gain_second + (1.0 - beta_second) * gain_grads * gain_grads
    new_gains = gains - gain_rate * new_gain_first / (jnp.sqrt(new_gain_second) + adam_eps)
    return (
        local_out,
        input_grad,
        weight_grads,
        gain_grads,
        new_master,
        new_first,
        new_second,
        new_ema,
        new_gains,
        new_gain_first,
        new_gain_second,
    )


MIB = 1024 * 1024
VMEM_WHOLE = pl.BlockSpec(memory_space=pltpu.VMEM)
IN_SMEM = pl.BlockSpec(memory_space=pltpu.SMEM)
IN_HBM = pl.BlockSpec(memory_space=pl.ANY)


def shaped(shape, kind):
    return jax.ShapeDtypeStruct(shape, kind)


def cost(flops, moved, exps=0):
    return pl.CostEstimate(flops=int(flops), bytes_accessed=int(moved), transcendentals=int(exps))


def settings(limit=48):
    return pltpu.CompilerParams(vmem_limit_bytes=limit * MIB)

class Line:
    def __init__(self):
        self.token = None

    def run(self, body, args, in_specs, out_specs, out_shape, aliases=None, **rest):
        lead = 0 if self.token is None else 1
        inputs, outputs = lead + len(args), len(out_shape)

        def inner(*refs):
            body(*refs[lead:inputs], *refs[inputs : inputs + outputs], *refs[inputs + outputs + 1 :])

        found = pl.pallas_call(
            inner,
            in_specs=[IN_HBM] * lead + list(in_specs),
            out_specs=list(out_specs) + [IN_HBM],
            out_shape=list(out_shape) + [shaped((8, 128), jnp.float32)],
            input_output_aliases={lead + at: to for at, to in (aliases or {}).items()},
            cost_estimate=cost(1000, 1000),
            **rest,
        )(*([self.token] * lead), *args)
        self.token = found[-1]
        return list(found[:-1])


def lanes_of(source_ref, at, width):
    return pl.ds(pl.multiple_of(source_ref[at] * width, width), width)


def norm_rows(rows, gain):
    scale = lax.rsqrt(jnp.mean(rows * rows, axis=-1, keepdims=True) + norm_eps)
    return rows * scale * gain


def norm_rows_back(rows, gain, grad):
    scale = lax.rsqrt(jnp.mean(rows * rows, axis=-1, keepdims=True) + norm_eps)
    scaled = grad * gain
    inner = jnp.sum(scaled * rows, axis=-1, keepdims=True)
    grad_in = scale * scaled - rows * (scale * scale * scale) * inner / rows.shape[-1]
    return grad_in, jnp.sum(grad * rows * scale, axis=0, keepdims=True)


def gelu_both(upper):
    size = jnp.abs(upper)
    base = 1.0 + (0.3275911 / math.sqrt(2.0)) * size
    guess = pl.reciprocal(base, approx=True)
    ratio = guess * (2.0 - base * guess)
    bell = jnp.exp(-0.5 * upper * upper)
    series = ratio * (
        0.5 * 0.254829592
        + ratio
        * (
            -0.5 * 0.284496736
            + ratio * (0.5 * 1.421413741 + ratio * (-0.5 * 1.453152027 + ratio * (0.5 * 1.061405429)))
        )
    )
    tail = series * bell
    cdf = jnp.where(upper >= 0.0, 1.0 - tail, tail)
    density = bell * (1.0 / math.sqrt(2.0 * math.pi))
    return (upper * cdf).astype(jnp.bfloat16), (cdf + upper * density).astype(jnp.bfloat16)


def both(rows, near, far):
    depth = near.shape[0]
    return dot_rows(rows[:, :depth], near) + dot_rows(rows[:, depth:], far)


def prep_body(source_ref, frames_ref, gains_ref, rows_ref, gains_out_ref, normed_ref):
    owned = frames_ref.shape[1] // source_ref.shape[0]
    for at in range(source_ref.shape[0]):
        here = slice(at * owned, (at + 1) * owned)
        rows_ref[:, here] = frames_ref[:, lanes_of(source_ref, at, owned)]
        gains_out_ref[:, here] = gains_ref[:, lanes_of(source_ref, at, owned)]
    normed_ref[...] = norm_rows(rows_ref[...].astype(jnp.float32), gains_out_ref[0:1, :]).astype(
        jnp.bfloat16
    )


def prep(line, source, frames, gains):
    return line.run(
        prep_body,
        (source, frames, gains,),
        in_specs=[IN_SMEM, VMEM_WHOLE, VMEM_WHOLE],
        out_specs=[VMEM_WHOLE] * 3,
        out_shape=[
            shaped(frames.shape, jnp.bfloat16),
            shaped(gains.shape, jnp.float32),
            shaped(frames.shape, jnp.bfloat16),
        ],
        compiler_params=settings(16),
        name="prep_rows",
    )


def merge_body(which, base_ref, one_ref, two_ref, three_ref, gains_ref, middle_ref, normed_ref=None):
    total = base_ref[...].astype(jnp.float32)
    for ref in (one_ref, two_ref, three_ref):
        total = total + ref[...].astype(jnp.float32)
    middle_ref[...] = total
    if normed_ref is not None:
        normed_ref[...] = norm_rows(total, gains_ref[which : which + 1, :]).astype(jnp.bfloat16)


def merge(line, base, terms, gains, which, normed=True):
    outs = [shaped(base.shape, jnp.float32)]
    if normed:
        outs.append(shaped(base.shape, jnp.bfloat16))
    return line.run(
        lambda *refs: merge_body(which, *refs),
        (base, *terms, gains,),
        in_specs=[VMEM_WHOLE] * 5,
        out_specs=[VMEM_WHOLE] * len(outs),
        out_shape=outs,
        compiler_params=settings(16),
        name="merge_rows",
    )


def merge_back_body(
    which, rows_ref, one_ref, two_ref, three_ref, grad_ref, gains_ref, total_ref, small_ref, gain_ref
):
    grad = one_ref[...].astype(jnp.float32)
    for ref in (two_ref, three_ref):
        grad = grad + ref[...].astype(jnp.float32)
    part, gain_grad = norm_rows_back(
        rows_ref[...].astype(jnp.float32), gains_ref[which : which + 1, :], grad
    )
    total = grad_ref[...] + part
    total_ref[...] = total
    small_ref[...] = total.astype(jnp.bfloat16)
    gain_ref[...] = gain_grad


def merge_back(line, rows, terms, grad, gains, which):
    return line.run(
        lambda *refs: merge_back_body(which, *refs),
        (rows, *terms, grad, gains,),
        in_specs=[VMEM_WHOLE] * 6,
        out_specs=[VMEM_WHOLE] * 3,
        out_shape=[
            shaped(rows.shape, jnp.float32),
            shaped(rows.shape, jnp.bfloat16),
            shaped((1, rows.shape[1]), jnp.float32),
        ],
        compiler_params=settings(16),
        name="merge_rows_back",
    )


def finish_body(
    source_ref, rows_ref, one_ref, two_ref, three_ref, grad_ref, gains_ref, gb_ref, gc_ref, gd_ref,
    out_ref, gain_ref,
):
    grad = one_ref[...].astype(jnp.float32)
    for ref in (two_ref, three_ref):
        grad = grad + ref[...].astype(jnp.float32)
    part, gain_grad = norm_rows_back(rows_ref[...].astype(jnp.float32), gains_ref[0:1, :], grad)
    total = grad_ref[...] + part
    owned = out_ref.shape[1] // source_ref.shape[0]
    for at in range(source_ref.shape[0]):
        here = slice(at * owned, (at + 1) * owned)
        there = lanes_of(source_ref, at, owned)
        out_ref[:, there] = total[:, here]
        gain_ref[0:1, there] = gain_grad[:, here]
        gain_ref[1:2, there] = gb_ref[:, here]
        gain_ref[2:3, there] = gc_ref[:, here]
        gain_ref[3:4, there] = gd_ref[:, here]


def finish(line, source, rows, terms, grad, gains, others):
    return line.run(
        finish_body,
        (source, rows, *terms, grad, gains, *others,),
        in_specs=[IN_SMEM] + [VMEM_WHOLE] * 9,
        out_specs=[VMEM_WHOLE] * 2,
        out_shape=[shaped(rows.shape, jnp.float32), shaped((4, rows.shape[1]), jnp.float32)],
        compiler_params=settings(16),
        name="input_grad",
    )


def global_heads_body(
    info_ref, x0, x1, x2, x3, near_ref, far_ref, qkv_ref, mixed_ref, lse_ref, p0, p1, p2, p3, acc, lse_wide
):
    share = x0.shape[0]
    span = 4 * share
    width = mixed_ref.shape[1]
    mine, length = info_ref[0], info_ref[1]
    scale = HD ** (-0.5)
    for rel, x_ref in enumerate((x0, x1, x2, x3)):
        at = pl.ds(pl.multiple_of((mine ^ rel) * share, share), share)
        full = both(x_ref[...], near_ref[:, : 3 * width], far_ref[:, : 3 * width])
        qkv_ref[at, :] = full.astype(jnp.bfloat16)
    acc[...] = jnp.zeros_like(acc)
    lse_wide[...] = jnp.zeros_like(lse_wide)
    head_of = lax.broadcasted_iota(jnp.int32, (1, width), 1) // HD
    lane = lax.broadcasted_iota(jnp.int32, (1, 128), 1)

    @pl.loop(0, width // HD)
    def per_head(head):
        own = head_of == head
        for block in range(4):
            rows = slice(block * share, (block + 1) * share)
            reach = (block + 1) * share
            query = jnp.where(own, qkv_ref[rows, :width] * scale, 0.0).astype(jnp.bfloat16)
            scores = dot_transposed(query, qkv_ref[:reach, width : 2 * width])
            row_at = block * share + lax.broadcasted_iota(jnp.int32, scores.shape, 0)
            col_at = lax.broadcasted_iota(jnp.int32, scores.shape, 1)
            scores = jnp.where((col_at <= row_at) & (col_at < length), scores, masked_fill)
            top = jnp.max(scores, axis=-1, keepdims=True)
            expanded = jnp.exp(scores - top)
            total = jnp.sum(expanded, axis=-1, keepdims=True)
            prob = (expanded * (1.0 / total)).astype(jnp.bfloat16)
            value = jnp.where(own, qkv_ref[:reach, 2 * width :], 0.0).astype(jnp.bfloat16)
            acc[rows, :] += dot_rows(prob, value)
            lse_wide[rows, :] = jnp.where(lane == head, top + jnp.log(total), lse_wide[rows, :])

    mixed_ref[...] = acc[...].astype(jnp.bfloat16)
    lse_ref[...] = jnp.transpose(lse_wide[...])[: lse_ref.shape[0], :]
    half = near_ref.shape[0]
    for rel, p_ref in enumerate((p0, p1, p2, p3)):
        at = pl.ds(pl.multiple_of((mine ^ rel) * share, share), share)
        rows = mixed_ref[at, :]
        p_ref[:, :half] = dot_transposed(rows, near_ref[:, 3 * width :]).astype(jnp.bfloat16)
        p_ref[:, half:] = dot_transposed(rows, far_ref[:, 3 * width :]).astype(jnp.bfloat16)


def global_heads(line, info, rows, halves):
    share, width = rows[0].shape[0], halves[0].shape[1] // 4
    span = 4 * share
    return line.run(
        global_heads_body,
        (info, *rows, *halves,),
        in_specs=[IN_SMEM] + [VMEM_WHOLE] * 6,
        out_specs=[VMEM_WHOLE] * 7,
        out_shape=[
            shaped((span, 3 * width), jnp.bfloat16),
            shaped((span, width), jnp.bfloat16),
            shaped((8, span), jnp.float32),
        ]
        + [shaped((share, D), jnp.bfloat16)] * 4,
        scratch_shapes=[pltpu.VMEM((span, width), jnp.float32), pltpu.VMEM((span, 128), jnp.float32)],
        compiler_params=settings(40),
        name="global_heads",
    )


def global_heads_back_body(
    info_ref, g0, g1, g2, g3, near_ref, far_ref, qkv_ref, mixed_ref, lse_ref, dqkv_ref, p0, p1, p2, p3,
    dmix, dq_t, dk_acc, dv_acc, center, k_t,
):
    share = g0.shape[0]
    width = mixed_ref.shape[1]
    heads = width // HD
    mine, length = info_ref[0], info_ref[1]
    scale = HD ** (-0.5)
    for rel, g_ref in enumerate((g0, g1, g2, g3)):
        at = pl.ds(pl.multiple_of((mine ^ rel) * share, share), share)
        full = both(g_ref[...], near_ref[:, 3 * width :], far_ref[:, 3 * width :])
        dmix[at, :] = full.astype(jnp.bfloat16)
    head_of = lax.broadcasted_iota(jnp.int32, (1, width), 1) // HD
    pick = (
        lax.broadcasted_iota(jnp.int32, (8, width), 1) // HD
        == lax.broadcasted_iota(jnp.int32, (8, width), 0)
    ).astype(jnp.bfloat16)
    product = dmix[...].astype(jnp.float32) * mixed_ref[...].astype(jnp.float32)
    high = product.astype(jnp.bfloat16)
    low = (product - high.astype(jnp.float32)).astype(jnp.bfloat16)
    center[...] = dot_transposed(pick, high) + dot_transposed(pick, low)
    k_t[...] = jnp.transpose(qkv_ref[:, width : 2 * width])
    dq_t[...] = jnp.zeros_like(dq_t)
    dk_acc[...] = jnp.zeros_like(dk_acc)
    dv_acc[...] = jnp.zeros_like(dv_acc)
    for head in range(heads):
        own = head_of == head
        for block in range(4):
            rows = slice(block * share, (block + 1) * share)
            reach = (block + 1) * share
            query = jnp.where(own, qkv_ref[rows, :width] * scale, 0.0).astype(jnp.bfloat16)
            grad = jnp.where(own, dmix[rows, :], 0.0).astype(jnp.bfloat16)
            scores = dot_transposed(qkv_ref[:reach, width : 2 * width], query)
            key_at = lax.broadcasted_iota(jnp.int32, scores.shape, 0)
            row_at = block * share + lax.broadcasted_iota(jnp.int32, scores.shape, 1)
            prob = jnp.where(
                (key_at <= row_at) & (key_at < length),
                jnp.exp(scores - lse_ref[head : head + 1, rows]),
                0.0,
            )
            dprob = dot_transposed(qkv_ref[:reach, 2 * width :], grad)
            dscore = (prob * (dprob - center[head : head + 1, rows])).astype(jnp.bfloat16)
            dv_acc[:reach, :] += dot_rows(prob.astype(jnp.bfloat16), grad)
            dk_acc[:reach, :] += dot_rows(dscore, query)
            lanes = slice(head * HD, (head + 1) * HD)
            dq_t[lanes, rows] += dot_rows(k_t[lanes, :reach], dscore)
    dqkv_ref[:, :width] = (jnp.transpose(dq_t[...]) * scale).astype(jnp.bfloat16)
    dqkv_ref[:, width : 2 * width] = dk_acc[...].astype(jnp.bfloat16)
    dqkv_ref[:, 2 * width :] = dv_acc[...].astype(jnp.bfloat16)
    half = near_ref.shape[0]
    for rel, p_ref in enumerate((p0, p1, p2, p3)):
        at = pl.ds(pl.multiple_of((mine ^ rel) * share, share), share)
        rows = dqkv_ref[at, :]
        p_ref[:, :half] = dot_transposed(rows, near_ref[:, : 3 * width]).astype(jnp.bfloat16)
        p_ref[:, half:] = dot_transposed(rows, far_ref[:, : 3 * width]).astype(jnp.bfloat16)


def global_heads_back(line, info, grads, halves, qkv, mixed, lse):
    share, width = grads[0].shape[0], mixed.shape[1]
    span = 4 * share
    return line.run(
        global_heads_back_body,
        (info, *grads, *halves, qkv, mixed, lse,),
        in_specs=[IN_SMEM] + [VMEM_WHOLE] * 9,
        out_specs=[VMEM_WHOLE] * 5,
        out_shape=[shaped((span, 3 * width), jnp.bfloat16)]
        + [shaped((share, D), jnp.bfloat16)] * 4,
        scratch_shapes=[
            pltpu.VMEM((span, width), jnp.bfloat16),
            pltpu.VMEM((width, span), jnp.float32),
            pltpu.VMEM((span, width), jnp.float32),
            pltpu.VMEM((span, width), jnp.float32),
            pltpu.VMEM((8, span), jnp.float32),
            pltpu.VMEM((width, span), jnp.bfloat16),
        ],
        compiler_params=settings(40),
        name="global_heads_back",
    )


def global_grads_heads_body(
    info_ref, a0, a1, a2, a3, g0, g1, g2, g3, dqkv_ref, mixed_ref, near_ref, far_ref, a_t, g_t
):
    share = a0.shape[0]
    width = mixed_ref.shape[1]
    mine = info_ref[0]
    for rel in range(4):
        at = pl.ds(pl.multiple_of((mine ^ rel) * share, share), share)
        a_t[:, at] = jnp.transpose((a0, a1, a2, a3)[rel][...])
        g_t[:, at] = jnp.transpose((g0, g1, g2, g3)[rel][...])

    for at in range(D // 256):
        rows = slice(at * 256, (at + 1) * 256)
        out_ref, begin = (near_ref, 0) if at * 256 < D // 2 else (far_ref, D // 2)
        there = slice(at * 256 - begin, at * 256 - begin + 256)
        out_ref[there, : 3 * width] = dot_rows(a_t[rows, :], dqkv_ref[...]).astype(jnp.bfloat16)
        out_ref[there, 3 * width :] = dot_rows(g_t[rows, :], mixed_ref[...]).astype(jnp.bfloat16)


def global_grads_heads(line, info, normed, grads, dqkv, mixed):
    span, width = mixed.shape
    return line.run(
        global_grads_heads_body,
        (info, *normed, *grads, dqkv, mixed,),
        in_specs=[IN_SMEM] + [VMEM_WHOLE] * 10,
        out_specs=[VMEM_WHOLE] * 2,
        out_shape=[shaped((D // 2, 4 * width), jnp.bfloat16)] * 2,
        scratch_shapes=[pltpu.VMEM((D, span), jnp.bfloat16)] * 2,
        compiler_params=settings(40),
        name="global_heads_grads",
    )


def global_ff_body(x0, x1, x2, x3, up0, up1, down0, down1, active_ref, slope_ref, p0, p1, p2, p3, acc):
    step = pl.program_id(0)
    share = x0.shape[0]
    half = up0.shape[0]

    @pl.when(step == 0)
    def _():
        acc[...] = jnp.zeros_like(acc)

    for rel, x_ref in enumerate((x0, x1, x2, x3)):
        rows = slice(rel * share, (rel + 1) * share)
        active, slope = gelu_both(both(x_ref[...], up0[...], up1[...]))
        active_ref[rows, :] = active
        slope_ref[rows, :] = slope
        for at, down in enumerate((down0, down1)):
            lanes = slice(at * half, (at + 1) * half)
            acc[rows, lanes] += dot_transposed(active, down[...])

    @pl.when(step == pl.num_programs(0) - 1)
    def _():
        for rel, p_ref in enumerate((p0, p1, p2, p3)):
            p_ref[...] = acc[rel * share : (rel + 1) * share, :].astype(jnp.bfloat16)


def held(shape):
    return pl.BlockSpec(shape, lambda step: (0,) * len(shape), pipeline_mode=pl.Buffered(1))


def by_cols(shape):
    return pl.BlockSpec(shape, lambda step: (0, step))


def global_ff(line, rows, up, down, tile=256):
    share = rows[0].shape[0]
    span, hidden, half = 4 * share, up[0].shape[1], up[0].shape[0]
    return line.run(
        global_ff_body,
        (*rows, *up, *down,),
        grid=(hidden // tile,),
        in_specs=[held((share, D))] * 4 + [by_cols((half, tile))] * 4,
        out_specs=[by_cols((span, tile))] * 2 + [held((share, D))] * 4,
        out_shape=[shaped((span, hidden), jnp.bfloat16)] * 2
        + [shaped((share, D), jnp.bfloat16)] * 4,
        scratch_shapes=[pltpu.VMEM((span, D), jnp.float32)],
        compiler_params=settings(40),
        name="global_ff",
    )


def global_ff_back_body(g0, g1, g2, g3, slope_ref, up0, up1, down0, down1, dup_ref, p0, p1, p2, p3, acc):
    step = pl.program_id(0)
    share = g0.shape[0]
    half = up0.shape[0]

    @pl.when(step == 0)
    def _():
        acc[...] = jnp.zeros_like(acc)

    for rel, g_ref in enumerate((g0, g1, g2, g3)):
        rows = slice(rel * share, (rel + 1) * share)
        grad = both(g_ref[...], down0[...], down1[...])
        dup = (grad * slope_ref[rows, :].astype(jnp.float32)).astype(jnp.bfloat16)
        dup_ref[rows, :] = dup
        for at, up in enumerate((up0, up1)):
            lanes = slice(at * half, (at + 1) * half)
            acc[rows, lanes] += dot_transposed(dup, up[...])

    @pl.when(step == pl.num_programs(0) - 1)
    def _():
        for rel, p_ref in enumerate((p0, p1, p2, p3)):
            p_ref[...] = acc[rel * share : (rel + 1) * share, :].astype(jnp.bfloat16)


def global_ff_back(line, grads, slope, up, down, tile=256):
    share = grads[0].shape[0]
    span, hidden, half = 4 * share, up[0].shape[1], up[0].shape[0]
    return line.run(
        global_ff_back_body,
        (*grads, slope, *up, *down,),
        grid=(hidden // tile,),
        in_specs=[held((share, D))] * 4 + [by_cols((span, tile))] + [by_cols((half, tile))] * 4,
        out_specs=[by_cols((span, tile))] + [held((share, D))] * 4,
        out_shape=[shaped((span, hidden), jnp.bfloat16)] + [shaped((share, D), jnp.bfloat16)] * 4,
        scratch_shapes=[pltpu.VMEM((span, D), jnp.float32)],
        compiler_params=settings(40),
        name="global_ff_back",
    )


def outer_body(r0, r1, r2, r3, right_ref, near_ref, far_ref, left_t):
    share = r0.shape[0]

    @pl.when(pl.program_id(0) == 0)
    def _():
        for rel, ref in enumerate((r0, r1, r2, r3)):
            left_t[:, rel * share : (rel + 1) * share] = jnp.transpose(ref[...])

    for at in range(D // 256):
        rows = slice(at * 256, (at + 1) * 256)
        out_ref, begin = (near_ref, 0) if at * 256 < D // 2 else (far_ref, D // 2)
        out_ref[at * 256 - begin : at * 256 - begin + 256, :] = dot_rows(
            left_t[rows, :], right_ref[...]
        ).astype(jnp.bfloat16)


def global_outer(line, rows, right, tile=256):
    share = rows[0].shape[0]
    span, hidden = right.shape
    return line.run(
        outer_body,
        (*rows, right,),
        grid=(hidden // tile,),
        in_specs=[held((share, D))] * 4 + [by_cols((span, tile))],
        out_specs=[by_cols((D // 2, tile))] * 2,
        out_shape=[shaped((D // 2, hidden), jnp.bfloat16)] * 2,
        scratch_shapes=[pltpu.VMEM((D, span), jnp.bfloat16)],
        compiler_params=settings(32),
        name="global_ff_grads",
    )


def head_sums(width):
    row_at = lax.broadcasted_iota(jnp.int32, (width, width), 0) // HD
    col_at = lax.broadcasted_iota(jnp.int32, (width, width), 1) // HD
    return (row_at == col_at).astype(jnp.bfloat16)


def over_heads(product, ones):
    high = product.astype(jnp.bfloat16)
    low = (product - high.astype(jnp.float32)).astype(jnp.bfloat16)
    return dot_rows(high, ones) + dot_rows(low, ones)


def frame_probs(queries, keys, ones):
    found = []
    for at in range(CB):
        scores = [over_heads(queries[at] * keys[c2], ones) * HD ** (-0.5) for c2 in range(at + 1)]
        top = scores[0]
        for one in scores[1:]:
            top = jnp.maximum(top, one)
        expanded = [jnp.exp(one - top) for one in scores]
        total = expanded[0]
        for one in expanded[1:]:
            total = total + one
        inverse = 1.0 / total
        found.append([one * inverse for one in expanded])
    return found


def rounded_f32(values):
    return values.astype(jnp.bfloat16).astype(jnp.float32)


def start_weights(parts, buffer, sems):
    for at, pair in enumerate(parts):
        for half, ref in enumerate(pair):
            pltpu.make_async_copy(ref, buffer.at[at, half], sems.at[at, half]).start()


def wait_weights(parts, buffer, sems, at):
    for half in range(2):
        pltpu.make_async_copy(parts[0][half], buffer.at[at, half], sems.at[at, half]).wait()


def local_heads_body(
    source_ref, out_ref_in, code_ref, gains_ref, *refs
):
    count = 4
    parts = [refs[2 * at : 2 * at + 2] for at in range(count)]
    qkv_ref, mixed_ref, middle_ref, normed_b_ref, a_t_ref, normed_a, local_in, buffer, sems = refs[2 * count :]
    step = pl.program_id(0)
    frames = out_ref_in.shape[0]
    width = mixed_ref.shape[2]
    half = D // 2

    @pl.when(step == 0)
    def _():
        start_weights(parts, buffer, sems)
        owned = D // source_ref.shape[0]
        for c in range(CB):
            rows = slice(c * frames, (c + 1) * frames)
            for at in range(source_ref.shape[0]):
                here = slice(at * owned, (at + 1) * owned)
                local_in[rows, here] = out_ref_in[:, here] + code_ref[
                    c, :, lanes_of(source_ref, at, owned)
                ].astype(jnp.float32)
            normed = norm_rows(local_in[rows, :], gains_ref[2:3, :]).astype(jnp.bfloat16)
            normed_a[rows, :] = normed
            a_t_ref[:, rows] = jnp.transpose(normed)
        middle_ref[...] = local_in[...]

    wait_weights(parts, buffer, sems, step)
    ones = head_sums(width)
    queries, keys, values = ([], [], [])
    for c in range(CB):
        rows = slice(c * frames, (c + 1) * frames)
        qkv = (
            dot_rows(normed_a[rows, :half], buffer[step, 0, :, : 3 * width])
            + dot_rows(normed_a[rows, half:], buffer[step, 1, :, : 3 * width])
        ).astype(jnp.bfloat16)
        qkv_ref[0, rows, :] = qkv
        queries.append(qkv[:, :width].astype(jnp.float32))
        keys.append(qkv[:, width : 2 * width].astype(jnp.float32))
        values.append(qkv[:, 2 * width :].astype(jnp.float32))
    prob = frame_probs(queries, keys, ones)
    for c in range(CB):
        rows = slice(c * frames, (c + 1) * frames)
        mix = rounded_f32(prob[c][0]) * values[0]
        for c2 in range(1, c + 1):
            mix = mix + rounded_f32(prob[c][c2]) * values[c2]
        mix = mix.astype(jnp.bfloat16)
        mixed_ref[0, rows, :] = mix
        for at in range(2):
            lanes = slice(at * half, (at + 1) * half)
            middle_ref[rows, lanes] += dot_transposed(mix, buffer[step, at, :, 3 * width :])

    @pl.when(step == count - 1)
    def _():
        for c in range(CB):
            rows = slice(c * frames, (c + 1) * frames)
            normed_b_ref[rows, :] = norm_rows(middle_ref[rows, :], gains_ref[3:4, :]).astype(
                jnp.bfloat16
            )


def local_heads(line, source, global_out, codes, gains, parts):
    frames = global_out.shape[0]
    rows = CB * frames
    width = parts[0][0].shape[1] // 4
    half = D // 2
    flat = [ref for pair in parts for ref in pair]
    return line.run(
        local_heads_body,
        (source, global_out, codes, gains, *flat,),
        grid=(4,),
        in_specs=[IN_SMEM, held((frames, D)), held((CB, frames, D)), held((4, D))] + [IN_HBM] * 8,
        out_specs=[
            pl.BlockSpec((1, rows, 3 * width), lambda step: (step, 0, 0)),
            pl.BlockSpec((1, rows, width), lambda step: (step, 0, 0)),
            held((rows, D)),
            held((rows, D)),
            held((D, rows)),
        ],
        out_shape=[
            shaped((4, rows, 3 * width), jnp.bfloat16),
            shaped((4, rows, width), jnp.bfloat16),
            shaped((rows, D), jnp.float32),
            shaped((rows, D), jnp.bfloat16),
            shaped((D, rows), jnp.bfloat16),
        ],
        scratch_shapes=[
            pltpu.VMEM((rows, D), jnp.bfloat16),
            pltpu.VMEM((rows, D), jnp.float32),
            pltpu.VMEM((4, 2, half, 4 * width), jnp.bfloat16),
            pltpu.SemaphoreType.DMA((4, 2)),
        ],
        compiler_params=settings(52),
        name="local_heads",
    )


def local_ff_body(source_ref, normed_ref, middle_ref, *refs):
    count = 4
    ups = [refs[2 * at : 2 * at + 2] for at in range(count)]
    downs = [refs[2 * count + 2 * at : 2 * count + 2 * at + 2] for at in range(count)]
    active_ref, slope_ref, out_ref, b_t_ref, acc, up_buf, down_buf, up_sems, down_sems = refs[4 * count :]
    step = pl.program_id(0)
    rows_all = normed_ref.shape[0]
    frames = rows_all // CB
    half = D // 2
    tile = active_ref.shape[2]
    per = up_buf.shape[3] // tile
    group = step // per
    cols_at = pl.ds(pl.multiple_of((step % per) * tile, tile), tile)

    @pl.when(step == 0)
    def _():
        for at in range(count):
            start_weights_at(ups, up_buf, up_sems, at)
            start_weights_at(downs, down_buf, down_sems, at)
        b_t_ref[...] = jnp.transpose(normed_ref[...])
        acc[...] = middle_ref[...]

    @pl.when(step % per == 0)
    def _():
        wait_weights(ups, up_buf, up_sems, group)
        wait_weights(downs, down_buf, down_sems, group)

    for c in range(CB):
        rows = slice(c * frames, (c + 1) * frames)
        upper = dot_rows(normed_ref[rows, :half], up_buf[group, 0, :, cols_at]) + dot_rows(
            normed_ref[rows, half:], up_buf[group, 1, :, cols_at]
        )
        active, slope = gelu_both(upper)
        active_ref[0, rows, :] = active
        slope_ref[0, rows, :] = slope
        for at in range(2):
            lanes = slice(at * half, (at + 1) * half)
            acc[rows, lanes] += dot_transposed(active, down_buf[group, at, :, cols_at])

    @pl.when(step == pl.num_programs(0) - 1)
    def _():
        owned = D // source_ref.shape[0]
        for c in range(CB):
            rows = slice(c * frames, (c + 1) * frames)
            for at in range(source_ref.shape[0]):
                here = slice(at * owned, (at + 1) * owned)
                out_ref[c, :, lanes_of(source_ref, at, owned)] = acc[rows, here].astype(jnp.bfloat16)


def start_weights_at(parts, buffer, sems, at):
    for half in range(2):
        pltpu.make_async_copy(parts[at][half], buffer.at[at, half], sems.at[at, half]).start()


def local_ff(line, source, normed, middle, ups, downs, tile=512):
    rows = normed.shape[0]
    hidden = ups[0][0].shape[1]
    half = D // 2
    per = hidden // tile
    flat = [ref for pair in ups for ref in pair] + [ref for pair in downs for ref in pair]
    hidden_block = pl.BlockSpec((1, rows, tile), lambda step: (step // per, 0, step % per))
    return line.run(
        local_ff_body,
        (source, normed, middle, *flat,),
        grid=(4 * per,),
        in_specs=[IN_SMEM, held((rows, D)), held((rows, D))] + [IN_HBM] * 16,
        out_specs=[hidden_block, hidden_block, held((CB, rows // CB, D)), held((D, rows))],
        out_shape=[
            shaped((4, rows, hidden), jnp.bfloat16),
            shaped((4, rows, hidden), jnp.bfloat16),
            shaped((CB, rows // CB, D), jnp.bfloat16),
            shaped((D, rows), jnp.bfloat16),
        ],
        scratch_shapes=[
            pltpu.VMEM((rows, D), jnp.float32),
            pltpu.VMEM((4, 2, half, hidden), jnp.bfloat16),
            pltpu.VMEM((4, 2, half, hidden), jnp.bfloat16),
            pltpu.SemaphoreType.DMA((4, 2)),
            pltpu.SemaphoreType.DMA((4, 2)),
        ],
        compiler_params=settings(56),
        name="local_ff",
    )


def seed_body(source_ref, count_ref, cot_ref, grad_ref, grad_t_ref):
    frames = cot_ref.shape[1]
    owned = D // source_ref.shape[0]
    keep = lax.broadcasted_iota(jnp.int32, (frames, 1), 0) < count_ref[0]
    for c in range(CB):
        rows = slice(c * frames, (c + 1) * frames)
        for at in range(source_ref.shape[0]):
            here = slice(at * owned, (at + 1) * owned)
            values = cot_ref[c, :, lanes_of(source_ref, at, owned)].astype(jnp.float32)
            grad_ref[rows, here] = jnp.where(keep, values, 0.0).astype(jnp.bfloat16)
        grad_t_ref[:, rows] = jnp.transpose(grad_ref[rows, :])


def seed(line, source, count, cot):
    frames = cot.shape[1]
    rows = CB * frames
    return line.run(
        seed_body,
        (source, count, cot,),
        in_specs=[IN_SMEM, IN_SMEM, VMEM_WHOLE],
        out_specs=[VMEM_WHOLE] * 2,
        out_shape=[shaped((rows, D), jnp.bfloat16), shaped((D, rows), jnp.bfloat16)],
        compiler_params=settings(24),
        name="seed_grads",
    )


def local_ff_back_body(last, summed, first, grad_ref, grad_t_ref, b_t_ref, active_ref, slope_ref, up0, up1, down0, down1, *refs):
    if summed:
        met_ref, refs = refs[0], refs[1:]
    so_far_ref, refs = (None, refs) if first else (refs[0], refs[1:])
    if last:
        middle_ref, gains_ref, refs = refs[0], refs[1], refs[2:]
    if summed:
        down_near, down_far, g_up, refs = refs[0], refs[1], refs[2], refs[3:]
    else:
        both_ref, refs = refs[0], refs[1:]
    outs, (acc, dup) = refs[:-2], refs[-2:]
    step = pl.program_id(0)
    frames = grad_ref.shape[0] // CB
    half = D // 2

    @pl.when(step == 0)
    def _():
        if so_far_ref is not None:
            acc[...] = so_far_ref[...]
        else:
            acc[...] = jnp.zeros_like(acc)

    for c in range(CB):
        rows = slice(c * frames, (c + 1) * frames)
        grad = dot_rows(grad_ref[rows, :half], down0[...]) + dot_rows(grad_ref[rows, half:], down1[...])
        one = (grad * slope_ref[0, rows, :].astype(jnp.float32)).astype(jnp.bfloat16)
        dup[rows, :] = one
        for at, up in enumerate((up0, up1)):
            lanes = slice(at * half, (at + 1) * half)
            acc[rows, lanes] += dot_transposed(one, up[...])
    for at in range(D // 256):
        rows = slice(at * 256, (at + 1) * 256)
        down = dot_rows(grad_t_ref[rows, :], active_ref[0])
        up = dot_rows(b_t_ref[rows, :], dup[...])
        if summed:
            down = (down + met_ref[0, rows, :].astype(jnp.float32)).astype(jnp.bfloat16)
            if at * 256 < half:
                down_near[rows, :] = down
            else:
                down_far[at * 256 - half : at * 256 - half + 256, :] = down
            g_up[rows, :] = (up + met_ref[1, rows, :].astype(jnp.float32)).astype(jnp.bfloat16)
        else:
            both_ref[0, rows, :] = down.astype(jnp.bfloat16)
            both_ref[1, rows, :] = up.astype(jnp.bfloat16)

    @pl.when(step == pl.num_programs(0) - 1)
    def _():
        if last:
            grad_mid_ref, small_ref, small_t_ref, gain_ref = outs
            total_gain = jnp.zeros((1, D), jnp.float32)
            for c in range(CB):
                rows = slice(c * frames, (c + 1) * frames)
                part, gain_grad = norm_rows_back(middle_ref[rows, :], gains_ref[3:4, :], acc[rows, :])
                total = grad_ref[rows, :].astype(jnp.float32) + part
                grad_mid_ref[rows, :] = total
                small = total.astype(jnp.bfloat16)
                small_ref[rows, :] = small
                small_t_ref[:, rows] = jnp.transpose(small)
                total_gain = total_gain + gain_grad
            gain_ref[...] = total_gain
        else:
            outs[0][...] = acc[...]


def local_ff_back(line, rel, grad, grad_t, b_t, active, slope, up, down, met=None, so_far=None, tail=None, tile=512):
    rows = grad.shape[0]
    hidden = active.shape[2]
    half = D // 2
    last, summed = tail is not None, met is not None
    hidden_block = pl.BlockSpec((1, rows, tile), lambda step: (rel, 0, step))
    pair_block = pl.BlockSpec((2, D, tile), lambda step: (0, 0, step))
    extra_args, extra = ([], [])
    if summed:
        extra_args.append(met)
        extra.append(pair_block)
    if so_far is not None:
        extra_args.append(so_far)
        extra.append(held((rows, D)))
    first = so_far is None
    if last:
        extra_args += list(tail)
        extra += [held((rows, D)), held((4, D))]
        outs = [
            shaped((rows, D), jnp.float32),
            shaped((rows, D), jnp.bfloat16),
            shaped((D, rows), jnp.bfloat16),
            shaped((1, D), jnp.float32),
        ]
    else:
        outs = [shaped((rows, D), jnp.float32)]
    if summed:
        grad_specs = [by_cols((half, tile)), by_cols((half, tile)), by_cols((D, tile))]
        grad_shapes = [shaped((half, hidden), jnp.bfloat16)] * 2 + [shaped((D, hidden), jnp.bfloat16)]
    else:
        grad_specs = [pair_block]
        grad_shapes = [shaped((2, D, hidden), jnp.bfloat16)]

    def body(*refs):
        local_ff_back_body(last, summed, first, *refs)

    found = line.run(
        body,
        (grad, grad_t, b_t, active, slope, *up, *down, *extra_args),
        grid=(hidden // tile,),
        in_specs=[held((rows, D)), held((D, rows)), held((D, rows)), hidden_block, hidden_block]
        + [by_cols((half, tile))] * 4
        + extra,
        out_specs=grad_specs + [held(one.shape) for one in outs],
        out_shape=grad_shapes + outs,
        scratch_shapes=[pltpu.VMEM((rows, D), jnp.float32), pltpu.VMEM((rows, tile), jnp.bfloat16)],
        compiler_params=settings(52),
        name="local_ff_back",
    )
    return found[: len(grad_shapes)], found[len(grad_shapes) :]


def local_heads_back_body(last, summed, first, grad_ref, grad_t_ref, a_t_ref, qkv_ref, mixed_ref, near_ref, far_ref, *refs):
    if summed:
        met_ref, refs = refs[0], refs[1:]
    if not first:
        so_far_ref, refs = refs[0], refs[1:]
    if last:
        grad_mid_ref, out_in_ref, code_ref, source_ref, gains_ref = refs[:5]
        refs = refs[5:]
    out_ref, refs = refs[0], refs[1:]
    outs, (acc, dqkv) = refs[:-2], refs[-2:]
    frames = grad_ref.shape[0] // CB
    width = mixed_ref.shape[2]
    half = D // 2
    scale = HD ** (-0.5)
    ones = head_sums(width)
    queries, keys, values, dmix = ([], [], [], [])
    for c in range(CB):
        rows = slice(c * frames, (c + 1) * frames)
        qkv = qkv_ref[0, rows, :].astype(jnp.float32)
        queries.append(qkv[:, :width])
        keys.append(qkv[:, width : 2 * width])
        values.append(qkv[:, 2 * width :])
        one = dot_rows(grad_ref[rows, :half], near_ref[:, 3 * width :]) + dot_rows(
            grad_ref[rows, half:], far_ref[:, 3 * width :]
        )
        dmix.append(rounded_f32(one))
    prob = frame_probs(queries, keys, ones)
    dq, dk, dv = ([None] * CB, [None] * CB, [None] * CB)

    def more(total, term):
        return term if total is None else total + term

    for c in range(CB):
        dprob = [over_heads(dmix[c] * values[c2], ones) for c2 in range(c + 1)]
        center = prob[c][0] * dprob[0]
        for c2 in range(1, c + 1):
            center = center + prob[c][c2] * dprob[c2]
        for c2 in range(c + 1):
            dv[c2] = more(dv[c2], rounded_f32(prob[c][c2]) * dmix[c])
            dscore = rounded_f32(prob[c][c2] * (dprob[c2] - center))
            dq[c] = more(dq[c], dscore * keys[c2])
            dk[c2] = more(dk[c2], dscore * queries[c])
    for c in range(CB):
        rows = slice(c * frames, (c + 1) * frames)
        dqkv[rows, :width] = (dq[c] * scale).astype(jnp.bfloat16)
        dqkv[rows, width : 2 * width] = (dk[c] * scale).astype(jnp.bfloat16)
        dqkv[rows, 2 * width :] = dv[c].astype(jnp.bfloat16)
        for at, ref in enumerate((near_ref, far_ref)):
            lanes = slice(at * half, (at + 1) * half)
            term = dot_transposed(dqkv[rows, :], ref[:, : 3 * width])
            acc[rows, lanes] = term if first else so_far_ref[rows, lanes] + term
    for at in range(D // 256):
        rows = slice(at * 256, (at + 1) * 256)
        three = dot_rows(a_t_ref[rows, :], dqkv[...])
        one = dot_rows(grad_t_ref[rows, :], mixed_ref[0])
        if summed:
            three = three + met_ref[rows, : 3 * width].astype(jnp.float32)
            one = one + met_ref[rows, 3 * width :].astype(jnp.float32)
        out_ref[rows, : 3 * width] = three.astype(jnp.bfloat16)
        out_ref[rows, 3 * width :] = one.astype(jnp.bfloat16)
    if last:
        total_ref, small_ref, gain_ref = outs
        owned = D // source_ref.shape[0]
        total_gain = jnp.zeros((1, D), jnp.float32)
        total = jnp.zeros((frames, D), jnp.float32)
        for c in range(CB):
            rows = slice(c * frames, (c + 1) * frames)
            local_in = jnp.concatenate(
                [
                    out_in_ref[:, at * owned : (at + 1) * owned]
                    + code_ref[c, :, lanes_of(source_ref, at, owned)].astype(jnp.float32)
                    for at in range(source_ref.shape[0])
                ],
                axis=1,
            )
            part, gain_grad = norm_rows_back(local_in, gains_ref[2:3, :], acc[rows, :])
            total = total + (grad_mid_ref[rows, :] + part)
            total_gain = total_gain + gain_grad
        total_ref[...] = total
        small_ref[...] = total.astype(jnp.bfloat16)
        gain_ref[...] = total_gain
    else:
        outs[0][...] = acc[...]


def local_heads_back(line, rel, grad, grad_t, a_t, qkv, mixed, halves, met=None, so_far=None, tail=None):
    rows = grad.shape[0]
    frames = rows // CB
    width = mixed.shape[2]
    last, summed, first = tail is not None, met is not None, so_far is None
    extra_args, extra = ([], [])
    if summed:
        extra_args.append(met)
        extra.append(held((D, 4 * width)))
    if not first:
        extra_args.append(so_far)
        extra.append(held((rows, D)))
    if last:
        extra_args += list(tail)
        extra += [held((rows, D)), held((frames, D)), held((CB, frames, D)), IN_SMEM, held((4, D))]
        outs = [
            shaped((frames, D), jnp.float32),
            shaped((frames, D), jnp.bfloat16),
            shaped((1, D), jnp.float32),
        ]
    else:
        outs = [shaped((rows, D), jnp.float32)]

    def body(*refs):
        local_heads_back_body(last, summed, first, *refs)

    found = line.run(
        body,
        (grad, grad_t, a_t, qkv, mixed, *halves, *extra_args),
        grid=(1,),
        in_specs=[
            held((rows, D)),
            held((D, rows)),
            held((D, rows)),
            pl.BlockSpec((1, rows, 3 * width), lambda step: (rel, 0, 0)),
            pl.BlockSpec((1, rows, width), lambda step: (rel, 0, 0)),
        ]
        + [held((D // 2, 4 * width))] * 2
        + extra,
        out_specs=[held((D, 4 * width))] + [held(one.shape) for one in outs],
        out_shape=[shaped((D, 4 * width), jnp.bfloat16)] + outs,
        scratch_shapes=[
            pltpu.VMEM((rows, D), jnp.float32),
            pltpu.VMEM((rows, 3 * width), jnp.bfloat16),
        ],
        compiler_params=settings(52),
        name="local_heads_back",
    )
    return found[0], found[1:]


def cast_body(master_ref, out_ref):
    out_ref[...] = master_ref[0].astype(jnp.bfloat16)


def cast(line, master, layer, third):
    owned, columns = master.shape[1], master.shape[2] // 3
    return line.run(
        cast_body,
        (master,),
        grid=(1,),
        in_specs=[pl.BlockSpec((1, owned, columns), lambda step: (layer, 0, third))],
        out_specs=[held((owned, columns))],
        out_shape=[shaped((owned, columns), jnp.bfloat16)],
        compiler_params=settings(16),
        name="cast_shard",
    )[0]


def stack_body(p0, p1, p2, p3, out_ref):
    rows = p0.shape[0]
    for at, ref in enumerate((p0, p1, p2, p3)):
        out_ref[at * rows : (at + 1) * rows, :] = ref[...]


def stack_rows(line, parts):
    rows, columns = parts[0].shape
    return line.run(
        stack_body,
        tuple(parts),
        in_specs=[VMEM_WHOLE] * 4,
        out_specs=[VMEM_WHOLE],
        out_shape=[shaped((4 * rows, columns), jnp.bfloat16)],
        compiler_params=settings(16),
        name="stack_shards",
    )[0]


def add_body(*refs):
    total = refs[0][...].astype(jnp.float32)
    for ref in refs[1:-1]:
        total = total + ref[...].astype(jnp.float32)
    refs[-1][...] = total.astype(jnp.bfloat16)


def add_rows(line, terms, part=0, parts=1):
    rows = min(term.shape[0] for term in terms) if parts == 1 else terms[0].shape[0] // parts
    columns = terms[0].shape[1]

    def spec(term):
        return pl.BlockSpec(
            (rows, columns), (lambda step: (part, 0)) if term.shape[0] > rows else (lambda step: (0, 0))
        )

    return line.run(
        add_body,
        tuple(terms),
        grid=(1,),
        in_specs=[spec(term) for term in terms],
        out_specs=[pl.BlockSpec((rows, columns), lambda step: (0, 0))],
        out_shape=[shaped((rows, columns), jnp.bfloat16)],
        compiler_params=settings(24),
        name="add_terms",
    )[0]


def pieces_body(*refs):
    terms, outs = refs[:-4], refs[-4:]
    rows = outs[0].shape[0]
    for at, out_ref in enumerate(outs):
        here = slice(at * rows, (at + 1) * rows)
        total = terms[0][here, :].astype(jnp.float32)
        for ref in terms[1:]:
            total = total + ref[here, :].astype(jnp.float32)
        out_ref[...] = total.astype(jnp.bfloat16)


def sum_pieces(line, terms):
    half, columns = D // 2, terms[0].shape[1]
    near = pl.BlockSpec((half, columns), lambda step: (0, 0))
    return line.run(
        pieces_body,
        tuple(terms),
        grid=(1,),
        in_specs=[near] * len(terms),
        out_specs=[held((half // 4, columns))] * 4,
        out_shape=[shaped((half // 4, columns), jnp.bfloat16)] * 4,
        compiler_params=settings(24),
        name="sum_pieces",
    )


def pass_body(*refs):
    pass


def in_turn(line, *values):
    return line.run(
        pass_body,
        tuple(values),
        in_specs=[IN_HBM] * len(values),
        out_specs=[IN_HBM] * len(values),
        out_shape=[shaped(one.shape, one.dtype) for one in values],
        aliases={at: at for at in range(len(values))},
        name="in_turn",
    )


def split_dot(left, right):
    left_high = left.astype(jnp.bfloat16)
    left_low = (left - left_high.astype(jnp.float32)).astype(jnp.bfloat16)
    right_high = right.astype(jnp.bfloat16)
    right_low = (right - right_high.astype(jnp.float32)).astype(jnp.bfloat16)
    return (
        dot_rows(left_high, right_high) + dot_rows(left_high, right_low) + dot_rows(left_low, right_high)
    )


def adam_body(chained, p0, p1, p2, p3, left_ref, right_ref, master_ref, first_ref, second_ref, ema_ref, *refs):
    grads_ref, new_master_ref, new_first_ref, new_second_ref, new_ema_ref = refs[5:] if chained else refs
    left = left_ref[0]
    left_t = jnp.transpose(left)
    grads = p0[...].astype(jnp.float32)
    for ref in (p1, p2, p3):
        grads = grads + ref[...].astype(jnp.float32)
    grads_ref[0] = grads
    turned_left = split_dot(left_t, grads)
    back = []
    for at in range(right_ref.shape[1]):
        tile = slice(at * 128, (at + 1) * 128)
        right = right_ref[0, at]
        rotated = split_dot(turned_left[:, tile], right)
        new_first = beta_first * first_ref[0, :, tile] + (1.0 - beta_first) * rotated
        new_second = beta_second * second_ref[0, :, tile] + (1.0 - beta_second) * rotated * rotated
        new_first_ref[0, :, tile] = new_first
        new_second_ref[0, :, tile] = new_second
        turned = new_first / (jnp.sqrt(new_second) + adam_eps)
        back.append(split_dot(turned, jnp.transpose(right)))
    back_full = split_dot(left, jnp.concatenate(back, axis=1))
    new_master = master_ref[0] - step_rate * back_full
    new_master_ref[0] = new_master
    new_ema_ref[0] = ema_decay * ema_ref[0] + (1.0 - ema_decay) * new_master


def adam(line, layer, third, pieces, left, right, master, first, second, ema, before, tile=256):
    owned, columns = pieces[0].shape
    steps = columns // tile
    first_step = third * steps

    def state(step):
        return (layer, 0, first_step + step)

    state_spec = pl.BlockSpec((1, owned, tile), state)
    chained = before is not None
    return line.run(
        lambda *refs: adam_body(chained, *refs),
        (*pieces, left, right, master, first, second, ema, *(before or ()),),
        grid=(steps,),
        in_specs=[by_cols((owned, tile))] * 4
        + [
            pl.BlockSpec((1,) + left.shape[1:], lambda step: (layer, 0, 0)),
            pl.BlockSpec(
                (1, tile // 128) + right.shape[2:], lambda step: (layer, first_step + step, 0, 0)
            ),
        ]
        + [state_spec] * 4
        + ([IN_HBM] * 5 if chained else []),
        out_specs=[state_spec] * 5,
        out_shape=[shaped(master.shape, jnp.float32)] * 5,
        aliases={10 + at: at for at in range(5)} if chained else {},
        compiler_params=settings(32),
        name="adam_update",
    )


def hop_x(values):
    return lax.ppermute(values, "tensor", [(at, at ^ 2) for at in range(4)])


def hop_core(values):
    return lax.ppermute(values, "tensor", [(at, at ^ 1) for at in range(4)])


def hop_y(values):
    return lax.ppermute(values, "dp", [(at, at ^ 1) for at in range(8)])


def hop_z(values, step):
    return lax.ppermute(values, "dp", [(at, at ^ (2 * step)) for at in range(8)])


def rows_gather(rows):
    over_x = hop_x(rows)
    return [rows, hop_core(rows), over_x, hop_core(over_x)]


def depth_hops(piece):
    return [hop_z(piece, step) for step in (1, 2, 3)]


def total_everywhere(values):
    for hop in (hop_core, hop_x, hop_y):
        values = values + hop(values)
    for step in (1, 2):
        values = values + hop_z(values, step)
    return values


def shards_grid(
    frames_in,
    code_emb,
    cotangent,
    lengths,
    owner_list,
    master,
    first_moment,
    second_moment,
    ema,
    left_basis,
    right_basis,
    gains,
    gain_first,
    gain_second,
):
    share = frames_in.shape[0]
    owned = master.shape[1]
    groups = D // owned
    heads_w = D // lax.axis_size("tensor")
    ff_w = FF // lax.axis_size("tensor")
    my_dp = lax.axis_index("dp")
    my_group = lax.axis_index("tensor").astype(jnp.int32)

    rel = jnp.array([2 * z + y for y in range(2) for z in range(4)], jnp.int32)
    slots = jnp.arange(groups, dtype=jnp.int32)
    source = jnp.sum(
        jnp.where(owner_list[None, :] == (my_dp ^ rel)[:, None], slots[None, :], 0), axis=1
    ).astype(jnp.int32)
    info = jnp.stack([my_group, lengths[0]])
    count = (lengths - my_group * share).astype(jnp.int32)

    line = Line()
    codes = jnp.transpose(code_emb, (1, 0, 2))

    def share_shard(layer, third):
        shard = cast(line, master, layer, third)
        return [shard] + depth_hops(shard)

    g_heads = share_shard(0, 0)
    rows_in, gains_here, normed = prep(line, source, frames_in, gains)
    normed_a = rows_gather(normed)
    l_heads = share_shard(1, 0)
    near = stack_rows(line, g_heads)
    g_heads = (near, hop_y(near))
    g_up = share_shard(0, 1)
    lh_near = stack_rows(line, l_heads)
    lh_far, lh_near_c, lh_near_x = hop_y(lh_near), hop_core(lh_near), hop_x(lh_near)
    l_up = share_shard(1, 1)
    qkv, mixed, lse, *parts = global_heads(line, info, normed_a, g_heads)
    near_term, far_term = hop_core(parts[1]), hop_core(parts[3])
    near = stack_rows(line, g_up)
    g_up = (near, hop_y(near))
    to_x = hop_x(add_rows(line, [parts[2], far_term]))
    g_down = share_shard(0, 2)
    (lh_far,) = in_turn(line, lh_far)
    lh_far_c, lh_far_x = hop_core(lh_far), hop_x(lh_far)
    lu_near = stack_rows(line, l_up)
    lu_far, lu_near_c, lu_near_x = hop_y(lu_near), hop_core(lu_near), hop_x(lu_near)
    middle, normed = merge(line, rows_in, (parts[0], near_term, to_x), gains_here, 1)
    normed_b = rows_gather(normed)
    l_down = share_shard(1, 2)
    (lh_near_x,) = in_turn(line, lh_near_x)
    lh_near_xc = hop_core(lh_near_x)
    grad, grad_t = seed(line, source, count, jnp.transpose(cotangent, (1, 0, 2)))
    near = stack_rows(line, g_down)
    g_down = (near, hop_y(near))
    (lu_far,) = in_turn(line, lu_far)
    lu_far_c, lu_far_x = hop_core(lu_far), hop_x(lu_far)
    ld_near = stack_rows(line, l_down)
    ld_far, ld_near_c, ld_near_x = hop_y(ld_near), hop_core(ld_near), hop_x(ld_near)
    active, slope, *parts = global_ff(line, normed_b, g_up, g_down)
    near_term, far_term = hop_core(parts[1]), hop_core(parts[3])
    (lh_far_x,) = in_turn(line, lh_far_x)
    lh_far_xc = hop_core(lh_far_x)
    to_x = hop_x(add_rows(line, [parts[2], far_term]))
    (lu_near_x,) = in_turn(line, lu_near_x)
    lu_near_xc = hop_core(lu_near_x)
    (global_out,) = merge(line, middle, (parts[0], near_term, to_x), gains_here, 1, normed=False)
    (ld_near_x,) = in_turn(line, ld_near_x)
    ld_near_xc, ld_far_x = hop_core(ld_near_x), hop_y(ld_near_x)
    (ld_far,) = in_turn(line, ld_far)
    ld_far_c = hop_core(ld_far)

    l_heads = [(lh_near, lh_far), (lh_near_c, lh_far_c), (lh_near_x, lh_far_x), (lh_near_xc, lh_far_xc)]
    l_qkv, l_mixed, l_middle, l_normed_b, l_a_t = local_heads(
        line, source, global_out, codes, gains_here, l_heads
    )
    lu_far_x, ld_far_x = in_turn(line, lu_far_x, ld_far_x)
    lu_far_xc, ld_far_xc = hop_core(lu_far_x), hop_core(ld_far_x)
    l_up = [(lu_near, lu_far), (lu_near_c, lu_far_c), (lu_near_x, lu_far_x), (lu_near_xc, lu_far_xc)]
    l_down = [(ld_near, ld_far), (ld_near_c, ld_far_c), (ld_near_x, ld_far_x), (ld_near_xc, ld_far_xc)]
    l_active, l_slope, local_out, l_b_t = local_ff(line, source, l_normed_b, l_middle, l_up, l_down)
    local_out = jnp.transpose(local_out, (1, 0, 2))

    def ff_back(rel, **more):
        return local_ff_back(
            line, rel, grad, grad_t, l_b_t, l_active, l_slope, l_up[rel], l_down[rel], **more
        )

    (pair,), (so_far,) = ff_back(3)
    met_far = hop_core(pair)
    (pair,), (so_far,) = ff_back(1, so_far=so_far)
    met_near = hop_core(pair)
    (d2_near, d2_far, up2), (so_far,) = ff_back(2, met=met_far, so_far=so_far)
    d2_far, up2 = hop_y(d2_far), hop_x(up2)
    (d0_near, d0_far, up0), (l_grad_mid, l_small, l_small_t, gain_d) = ff_back(
        0, met=met_near, so_far=so_far, tail=(l_middle, gains_here)
    )
    d0_far = hop_y(d0_far)

    def heads_back(rel, **more):
        return local_heads_back(
            line, rel, l_small, l_small_t, l_a_t, l_qkv, l_mixed, l_heads[rel], **more
        )

    far_heads, (so_far,) = heads_back(3)
    met_far = hop_core(far_heads)
    near_heads, (so_far,) = heads_back(1, so_far=so_far)
    met_near = hop_core(near_heads)
    heads2, (so_far,) = heads_back(2, met=met_far, so_far=so_far)
    heads2 = hop_x(heads2)
    heads0, (grad_global, small, gain_c) = heads_back(
        0, met=met_near, so_far=so_far, tail=(l_grad_mid, global_out, codes, source, gains_here)
    )

    grad_rows = rows_gather(small)
    up_far = hop_y(add_rows(line, [up0, up2], 1, 2))
    d2 = hop_x(add_rows(line, [d2_near, d2_far]))
    grad_upper, *parts = global_ff_back(line, grad_rows, slope, g_up, g_down)
    near_term, far_term = hop_core(parts[1]), hop_core(parts[3])
    gd_near, gd_far = global_outer(line, grad_rows, active)
    gd_far = hop_y(gd_far)
    to_x = hop_x(add_rows(line, [parts[2], far_term]))
    gu_near, gu_far = global_outer(line, normed_b, grad_upper)
    gu_far = hop_y(gu_far)
    grad_middle, small, gain_b = merge_back(
        line, middle, (parts[0], near_term, to_x), grad_global, gains_here, 1
    )
    grad_attn = rows_gather(small)
    lu = sum_pieces(line, [up0, up2, up_far])
    lu = [lu[0]] + [hop_z(lu[at], at) for at in (1, 2, 3)]
    heads_far = hop_y(add_rows(line, [heads0, heads2], 1, 2))
    grad_qkv, *parts = global_heads_back(line, info, grad_attn, g_heads, qkv, mixed, lse)
    near_term, far_term = hop_core(parts[1]), hop_core(parts[3])
    gh_near, gh_far = global_grads_heads(line, info, normed_a, grad_attn, grad_qkv, mixed)
    gh_far = hop_y(gh_far)
    to_x = hop_x(add_rows(line, [parts[2], far_term]))
    ld = sum_pieces(line, [d0_near, d0_far, d2])
    ld = [ld[0]] + [hop_z(ld[at], at) for at in (1, 2, 3)]
    gd = sum_pieces(line, [gd_near, gd_far])
    gd = [gd[0]] + [hop_z(gd[at], at) for at in (1, 2, 3)]
    input_grad, gain_grads = finish(
        line, source, rows_in, (parts[0], near_term, to_x), grad_middle, gains_here, (gain_b, gain_c, gain_d)
    )
    gain_grads = total_everywhere(gain_grads)
    gu = sum_pieces(line, [gu_near, gu_far])
    gu = [gu[0]] + [hop_z(gu[at], at) for at in (1, 2, 3)]
    lh = sum_pieces(line, [heads0, heads2, heads_far])
    lh = [lh[0]] + [hop_z(lh[at], at) for at in (1, 2, 3)]

    def update(layer, third, pieces, before):
        return adam(
            line, layer, third, pieces, left_basis, right_basis, master, first_moment, second_moment, ema, before
        )

    found = update(1, 1, lu, None)
    gh = sum_pieces(line, [gh_near, gh_far])
    gh = [gh[0]] + [hop_z(gh[at], at) for at in (1, 2, 3)]
    found = update(1, 2, ld, found)
    found = update(0, 2, gd, found)
    found = update(0, 1, gu, found)
    found = update(1, 0, lh, found)
    found = update(0, 0, gh, found)
    weight_grads, new_master, new_first, new_second, new_ema = found
    new_gain_first = beta_first * gain_first + (1.0 - beta_first) * gain_grads
    new_gain_second = beta_second * gain_second + (1.0 - beta_second) * gain_grads * gain_grads
    new_gains = gains - gain_rate * new_gain_first / (jnp.sqrt(new_gain_second) + adam_eps)
    return (
        local_out,
        input_grad,
        weight_grads,
        gain_grads,
        new_master,
        new_first,
        new_second,
        new_ema,
        new_gains,
        new_gain_first,
        new_gain_second,
    )


def solution(mesh):
    fits = mesh.shape["dp"] == 8 and mesh.shape["tensor"] == 4
    return jax.shard_map(
        shards_grid if fits else shards_any,
        mesh=mesh,
        in_specs=(
            P(("dp", "tensor"), None),
            P(("dp", "tensor"), None, None),
            P(("dp", "tensor"), None, None),
            P("dp"),
            P(),
            P(None, "dp", "tensor"),
            P(None, "dp", "tensor"),
            P(None, "dp", "tensor"),
            P(None, "dp", "tensor"),
            P(None, "dp", "tensor"),
            P(None, "dp", None, "tensor"),
            P(),
            P(),
            P(),
        ),
        out_specs=(
            P(("dp", "tensor"), None, None),
            P(("dp", "tensor"), None),
            P(None, "dp", "tensor"),
            P(),
            P(None, "dp", "tensor"),
            P(None, "dp", "tensor"),
            P(None, "dp", "tensor"),
            P(None, "dp", "tensor"),
            P(),
            P(),
            P(),
        ),
        check_vma=False,
    )
```

```python
import math

import jax
import jax.numpy as jnp
from jax import lax
from jax.experimental import pallas as pl
from jax.experimental.pallas import tpu as pltpu
from jax.sharding import PartitionSpec as P

D = 1024
HD = 64
FF = 4096
CB = 3
LMAX = 1024


norm_eps = 1e-06
beta_first = 0.5
beta_second = 0.5
adam_eps = 1e-08
step_rate = 0.05
gain_rate = 0.4
ema_decay = 0.9
masked_fill = -1e30
highest = lax.Precision.HIGHEST


def dot_rows(left, right):
    return jnp.dot(left, right, preferred_element_type=jnp.float32)


def dot_transposed(left, right):
    return lax.dot_general(
        left, right, (((1,), (1,)), ((), ())), preferred_element_type=jnp.float32
    )


def dot_over_rows(left, right):
    return lax.dot_general(
        left, right, (((0,), (0,)), ((), ())), preferred_element_type=jnp.float32
    )


def keep_rows(values):
    return values


def row_term(operand, weight):
    return dot_transposed(operand, weight)


def rms_forward(rows_in, gain):
    return (
        rows_in * lax.rsqrt(jnp.mean(rows_in * rows_in, axis=-1, keepdims=True) + norm_eps) * gain
    )


def rms_backward(rows_in, gain, grad_out):
    width = rows_in.shape[-1]
    scale_rows = lax.rsqrt(jnp.mean(rows_in * rows_in, axis=-1, keepdims=True) + norm_eps)
    scaled_grad = grad_out * gain
    inner_total = jnp.sum(scaled_grad * rows_in, axis=-1, keepdims=True)
    grad_in = (
        scale_rows * scaled_grad
        - rows_in * (scale_rows * scale_rows * scale_rows) * inner_total / width
    )
    gain_grad = jnp.sum(grad_out * rows_in * scale_rows, axis=0)
    return (grad_in, gain_grad)


def gelu_slope(upper):
    normal_cdf = 0.5 * (1.0 + lax.erf(upper * (1.0 / math.sqrt(2.0))))
    density = jnp.exp(-0.5 * upper * upper) * (1.0 / math.sqrt(2.0 * math.pi))
    return normal_cdf + upper * density


def split_layer(layer_cols, groups, head_cols, ff_cols):
    width = layer_cols.shape[0]
    grouped = layer_cols.reshape(width, groups, -1)

    def columns(begin, extent):
        return grouped[:, :, begin : begin + extent].reshape(width, groups * extent)

    w_qkv = jnp.concatenate(
        [columns(0, head_cols), columns(head_cols, head_cols), columns(2 * head_cols, head_cols)],
        axis=1,
    )
    return (
        w_qkv,
        columns(3 * head_cols, head_cols),
        columns(4 * head_cols, ff_cols),
        columns(4 * head_cols + ff_cols, ff_cols),
    )


def join_layer(grad_parts, groups):
    grad_qkv, grad_out, grad_up, grad_down = grad_parts
    width = grad_qkv.shape[0]
    head_width = grad_qkv.shape[1] // 3
    pieces = [
        grad_qkv[:, 0:head_width],
        grad_qkv[:, head_width : 2 * head_width],
        grad_qkv[:, 2 * head_width :],
        grad_out,
        grad_up,
        grad_down,
    ]
    return jnp.concatenate([piece.reshape(width, groups, -1) for piece in pieces], axis=2).reshape(
        width, -1
    )


def global_scores(queries, key_rows, length):
    span = queries.shape[0]
    heads = queries.shape[1] // HD
    scores = jnp.einsum(
        "qhd,khd->hqk",
        queries.reshape(span, heads, HD),
        key_rows.reshape(span, heads, HD),
        preferred_element_type=jnp.float32,
    ) * HD ** (-0.5)
    rows_at = lax.broadcasted_iota(jnp.int32, (span, span), 0)
    cols_at = lax.broadcasted_iota(jnp.int32, (span, span), 1)
    allowed = (cols_at <= rows_at) & (cols_at < length)
    return jnp.where(allowed[None], scores, masked_fill)


def global_attend(queries, key_rows, value_rows, lengths):
    items = lengths.shape[0]
    span = queries.shape[0] // items
    heads = queries.shape[1] // HD

    def one_item(packed):
        item_query, item_key, item_value, length = packed
        scores = global_scores(item_query, item_key, length)
        row_max = jnp.max(scores, axis=-1, keepdims=True)
        expanded = jnp.exp(scores - row_max)
        row_total = jnp.sum(expanded, axis=-1, keepdims=True)
        probability = (expanded / row_total).astype(jnp.bfloat16)
        mixed = jnp.einsum(
            "hqk,khd->qhd",
            probability,
            item_value.reshape(span, heads, HD),
            preferred_element_type=jnp.float32,
        )
        return (
            mixed.reshape(span, -1).astype(jnp.bfloat16),
            (row_max + jnp.log(row_total))[..., 0],
        )

    mixed, log_total = lax.map(
        one_item,
        (
            queries.reshape(items, span, -1),
            key_rows.reshape(items, span, -1),
            value_rows.reshape(items, span, -1),
            lengths,
        ),
    )
    return (mixed.reshape(items * span, -1), log_total)


def global_attend_back(queries, key_rows, value_rows, lengths, log_total, grad_mixed):
    items = lengths.shape[0]
    span = queries.shape[0] // items
    heads = queries.shape[1] // HD
    scale_score = HD ** (-0.5)

    def one_item(packed):
        item_query, item_key, item_value, length, item_lse, item_grad = packed
        scores = global_scores(item_query, item_key, length)
        probability = jnp.exp(scores - item_lse[..., None])
        grad_heads = item_grad.reshape(span, heads, HD)
        query_heads = item_query.reshape(span, heads, HD)
        key_heads = item_key.reshape(span, heads, HD)
        value_heads = item_value.reshape(span, heads, HD)
        grad_value = jnp.einsum(
            "hqk,qhd->khd",
            probability.astype(jnp.bfloat16),
            grad_heads,
            preferred_element_type=jnp.float32,
        )
        grad_prob = jnp.einsum(
            "qhd,khd->hqk", grad_heads, value_heads, preferred_element_type=jnp.float32
        )
        center = jnp.sum(probability * grad_prob, axis=-1, keepdims=True)
        grad_scores = (probability * (grad_prob - center)).astype(jnp.bfloat16)
        grad_query = (
            jnp.einsum("hqk,khd->qhd", grad_scores, key_heads, preferred_element_type=jnp.float32)
            * scale_score
        )
        grad_key = (
            jnp.einsum("hqk,qhd->khd", grad_scores, query_heads, preferred_element_type=jnp.float32)
            * scale_score
        )
        return jnp.concatenate(
            [
                grad_query.reshape(span, -1),
                grad_key.reshape(span, -1),
                grad_value.reshape(span, -1),
            ],
            axis=1,
        ).astype(jnp.bfloat16)

    grads = lax.map(
        one_item,
        (
            queries.reshape(items, span, -1),
            key_rows.reshape(items, span, -1),
            value_rows.reshape(items, span, -1),
            lengths,
            log_total,
            grad_mixed.reshape(items, span, -1),
        ),
    )
    return grads.reshape(items * span, -1)


def local_probability(queries, key_rows):
    frame_count = queries.shape[0] // CB
    heads = queries.shape[1] // HD
    scores = jnp.einsum(
        "fqhd,fkhd->fhqk",
        queries.reshape(frame_count, CB, heads, HD),
        key_rows.reshape(frame_count, CB, heads, HD),
        preferred_element_type=jnp.float32,
    ) * HD ** (-0.5)
    rows_at = lax.broadcasted_iota(jnp.int32, (CB, CB), 0)
    cols_at = lax.broadcasted_iota(jnp.int32, (CB, CB), 1)
    scores = jnp.where(cols_at <= rows_at, scores, masked_fill)
    row_max = jnp.max(scores, axis=-1, keepdims=True)
    expanded = jnp.exp(scores - row_max)
    return expanded / jnp.sum(expanded, axis=-1, keepdims=True)


def local_attend(queries, key_rows, value_rows):
    frame_count = queries.shape[0] // CB
    heads = queries.shape[1] // HD
    probability = local_probability(queries, key_rows).astype(jnp.bfloat16)
    mixed = jnp.einsum(
        "fhqk,fkhd->fqhd",
        probability,
        value_rows.reshape(frame_count, CB, heads, HD),
        preferred_element_type=jnp.float32,
    )
    return (mixed.reshape(queries.shape[0], -1).astype(jnp.bfloat16), jnp.zeros((), jnp.float32))


def local_attend_back(queries, key_rows, value_rows, saved, grad_mixed):
    frame_count = queries.shape[0] // CB
    heads = queries.shape[1] // HD
    scale_score = HD ** (-0.5)
    probability = local_probability(queries, key_rows)
    grad_heads = grad_mixed.reshape(frame_count, CB, heads, HD)
    query_heads = queries.reshape(frame_count, CB, heads, HD)
    key_heads = key_rows.reshape(frame_count, CB, heads, HD)
    value_heads = value_rows.reshape(frame_count, CB, heads, HD)
    grad_value = jnp.einsum(
        "fhqk,fqhd->fkhd",
        probability.astype(jnp.bfloat16),
        grad_heads,
        preferred_element_type=jnp.float32,
    )
    grad_prob = jnp.einsum(
        "fqhd,fkhd->fhqk", grad_heads, value_heads, preferred_element_type=jnp.float32
    )
    center = jnp.sum(probability * grad_prob, axis=-1, keepdims=True)
    grad_scores = (probability * (grad_prob - center)).astype(jnp.bfloat16)
    grad_query = (
        jnp.einsum("fhqk,fkhd->fqhd", grad_scores, key_heads, preferred_element_type=jnp.float32)
        * scale_score
    )
    grad_key = (
        jnp.einsum("fhqk,fqhd->fkhd", grad_scores, query_heads, preferred_element_type=jnp.float32)
        * scale_score
    )
    total_rows = queries.shape[0]
    return jnp.concatenate(
        [
            grad_query.reshape(total_rows, -1),
            grad_key.reshape(total_rows, -1),
            grad_value.reshape(total_rows, -1),
        ],
        axis=1,
    ).astype(jnp.bfloat16)


def block_forward(rows_in, matrices, gain_a, gain_b, path, attend):
    gather_rows, sum_rows = (path[0], path[1])
    w_qkv, w_out, w_up, w_down = matrices
    normed_a = gather_rows(rms_forward(rows_in, gain_a).astype(jnp.bfloat16))
    projected = dot_rows(normed_a, w_qkv).astype(jnp.bfloat16)
    head_width = projected.shape[1] // 3
    mixed, saved = attend(
        projected[:, :head_width],
        projected[:, head_width : 2 * head_width],
        projected[:, 2 * head_width :],
    )
    middle = rows_in + sum_rows(mixed, w_out)
    normed_b = gather_rows(rms_forward(middle, gain_b).astype(jnp.bfloat16))
    upper = dot_rows(normed_b, w_up)
    active = jax.nn.gelu(upper, approximate=False).astype(jnp.bfloat16)
    result = middle + sum_rows(active, w_down)
    return (result, (rows_in, normed_a, projected, mixed, saved, middle, normed_b, upper, active))


def block_backward(grad_result, kept, matrices, gain_a, gain_b, path, attend_back):
    gather_grads, sum_back = (path[2], path[3])
    rows_in, normed_a, projected, mixed, saved, middle, normed_b, upper, active = kept
    w_qkv, w_out, w_up, w_down = matrices
    grad_branch = gather_grads(grad_result.astype(jnp.bfloat16))
    grad_down = dot_over_rows(grad_branch, active)
    grad_active = dot_rows(grad_branch, w_down)
    grad_upper = (grad_active * gelu_slope(upper)).astype(jnp.bfloat16)
    grad_up = dot_over_rows(normed_b, grad_upper)
    grad_normed_b = sum_back(grad_upper, w_up)
    grad_middle_part, gain_b_grad = rms_backward(middle, gain_b, grad_normed_b)
    grad_middle = grad_result + grad_middle_part
    grad_attn = gather_grads(grad_middle.astype(jnp.bfloat16))
    grad_out = dot_over_rows(grad_attn, mixed)
    grad_mixed = dot_rows(grad_attn, w_out).astype(jnp.bfloat16)
    head_width = projected.shape[1] // 3
    grad_qkv = attend_back(
        projected[:, :head_width],
        projected[:, head_width : 2 * head_width],
        projected[:, 2 * head_width :],
        saved,
        grad_mixed,
    )
    grad_weight_qkv = dot_over_rows(normed_a, grad_qkv)
    grad_normed_a = sum_back(grad_qkv, w_qkv)
    grad_rows_part, gain_a_grad = rms_backward(rows_in, gain_a, grad_normed_a)
    return (
        grad_middle + grad_rows_part,
        (grad_weight_qkv, grad_out, grad_up, grad_down),
        gain_a_grad,
        gain_b_grad,
    )


def shards_any(
    frames_in,
    code_emb,
    cotangent,
    lengths,
    owner_list,
    master,
    first_moment,
    second_moment,
    ema,
    left_basis,
    right_basis,
    gains,
    gain_first,
    gain_second,
):
    tensor_count = lax.axis_size("tensor")
    group_count = lax.axis_size("dp")
    head_cols = D // tensor_count
    ff_cols = FF // tensor_count
    share = frames_in.shape[0]
    owned_rows = master.shape[1]
    gathered = lax.all_gather(master.astype(jnp.bfloat16), "dp", axis=1, tiled=True)
    layers = jnp.take(gathered.reshape(2, group_count, owned_rows, -1), owner_list, axis=1).reshape(
        2, group_count * owned_rows, -1
    )

    def gather_rows(values):
        return lax.all_gather(values, "tensor", axis=0, tiled=True)

    def gather_grads(values):
        return lax.all_gather(values, "tensor", axis=0, tiled=True)

    def sum_rows(operand, weight):
        return lax.psum_scatter(
            row_term(operand, weight).astype(jnp.bfloat16),
            "tensor",
            scatter_dimension=0,
            tiled=True,
        ).astype(jnp.float32)

    def sum_back(operand, weight):
        return lax.psum_scatter(
            row_term(operand, weight).astype(jnp.bfloat16),
            "tensor",
            scatter_dimension=0,
            tiled=True,
        ).astype(jnp.float32)

    heads_path = (gather_rows, sum_rows, gather_grads, sum_back)
    rows_path = (keep_rows, dot_transposed, keep_rows, dot_transposed)

    def attend_global(queries, key_rows, value_rows):
        return global_attend(queries, key_rows, value_rows, lengths)

    def attend_global_back(queries, key_rows, value_rows, saved, grad_mixed):
        return global_attend_back(queries, key_rows, value_rows, lengths, saved, grad_mixed)

    global_matrices = split_layer(layers[0], 1, head_cols, ff_cols)
    global_out, global_kept = block_forward(
        frames_in.astype(jnp.float32),
        global_matrices,
        gains[0],
        gains[1],
        heads_path,
        attend_global,
    )
    local_in = (global_out[:, None, :] + code_emb.astype(jnp.float32)).reshape(share * CB, -1)
    local_layer = lax.all_gather(layers[1], "tensor", axis=1, tiled=True)
    local_matrices = split_layer(local_layer, tensor_count, head_cols, ff_cols)
    local_result, local_kept = block_forward(
        local_in, local_matrices, gains[2], gains[3], rows_path, local_attend
    )
    local_out = local_result.reshape(share, CB, -1).astype(jnp.bfloat16)
    frame_at = lax.axis_index("tensor") * share + jnp.arange(share, dtype=jnp.int32)
    item_at = frame_at // LMAX
    item_slots = jnp.arange(lengths.shape[0], dtype=jnp.int32)
    item_length = jnp.sum(
        jnp.where(item_at[:, None] == item_slots[None, :], lengths[None, :], 0), axis=1
    )
    valid = (frame_at % LMAX < item_length).astype(jnp.float32)
    grad_local = (cotangent.astype(jnp.float32) * valid[:, None, None]).reshape(share * CB, -1)
    grad_local_in, local_weight_grads, gain_c_grad, gain_d_grad = block_backward(
        grad_local, local_kept, local_matrices, gains[2], gains[3], rows_path, local_attend_back
    )
    grad_global_out = jnp.sum(grad_local_in.reshape(share, CB, -1), axis=1)
    input_grad, global_weight_grads, gain_a_grad, gain_b_grad = block_backward(
        grad_global_out,
        global_kept,
        global_matrices,
        gains[0],
        gains[1],
        heads_path,
        attend_global_back,
    )
    local_grads = join_layer(local_weight_grads, tensor_count)
    local_grads = lax.psum_scatter(
        local_grads.astype(jnp.bfloat16), "tensor", scatter_dimension=1, tiled=True
    ).astype(jnp.float32)
    layer_grads = jnp.stack([join_layer(global_weight_grads, 1), local_grads])
    slots = jnp.arange(group_count, dtype=jnp.int32)
    inverse = jnp.sum(jnp.where(owner_list[None, :] == slots[:, None], slots[None, :], 0), axis=1)
    ordered = jnp.take(
        layer_grads.reshape(2, group_count, owned_rows, -1), inverse, axis=1
    ).reshape(2, group_count * owned_rows, -1)
    weight_grads = lax.psum_scatter(
        ordered.astype(jnp.bfloat16), "dp", scatter_dimension=1, tiled=True
    ).astype(jnp.float32)
    gain_grads = lax.psum(
        jnp.stack([gain_a_grad, gain_b_grad, gain_c_grad, gain_d_grad]), ("dp", "tensor")
    )
    tile_count = right_basis.shape[1]
    turned_left = jnp.einsum("lab,lac->lbc", left_basis, weight_grads, precision=highest)
    rotated = jnp.einsum(
        "lbkc,lkce->lbke",
        turned_left.reshape(2, owned_rows, tile_count, -1),
        right_basis,
        precision=highest,
    ).reshape(weight_grads.shape)
    new_first = beta_first * first_moment + (1.0 - beta_first) * rotated
    new_second = beta_second * second_moment + (1.0 - beta_second) * rotated * rotated
    turned = new_first / (jnp.sqrt(new_second) + adam_eps)
    back_right = jnp.einsum(
        "lbke,lkce->lbkc",
        turned.reshape(2, owned_rows, tile_count, -1),
        right_basis,
        precision=highest,
    )
    back_full = jnp.einsum(
        "lab,lbc->lac", left_basis, back_right.reshape(weight_grads.shape), precision=highest
    )
    new_master = master - step_rate * back_full
    new_ema = ema_decay * ema + (1.0 - ema_decay) * new_master
    new_gain_first = beta_first * gain_first + (1.0 - beta_first) * gain_grads
    new_gain_second = beta_second * gain_second + (1.0 - beta_second) * gain_grads * gain_grads
    new_gains = gains - gain_rate * new_gain_first / (jnp.sqrt(new_gain_second) + adam_eps)
    return (
        local_out,
        input_grad,
        weight_grads,
        gain_grads,
        new_master,
        new_first,
        new_second,
        new_ema,
        new_gains,
        new_gain_first,
        new_gain_second,
    )


MIB = 1024 * 1024
VMEM_WHOLE = pl.BlockSpec(memory_space=pltpu.VMEM)
IN_SMEM = pl.BlockSpec(memory_space=pltpu.SMEM)
IN_HBM = pl.BlockSpec(memory_space=pl.ANY)


def shaped(shape, kind):
    return jax.ShapeDtypeStruct(shape, kind)


def cost(flops, moved, exps=0):
    return pl.CostEstimate(flops=int(flops), bytes_accessed=int(moved), transcendentals=int(exps))


weight_of = {
    "global_heads": 13,
    "global_ff": 12,
    "local_heads": 18,
    "local_ff": 34,
    "local_ff_back": 14,
    "local_heads_back": 11,
    "global_ff_back": 9,
    "global_ff_grads": 5,
    "global_heads_back": 12,
    "global_heads_grads": 5,
    "adam_update": 5,
}


def group_at(rel):
    mine = lax.axis_index("tensor")
    return 2 * ((mine // 2 + rel // 2) % 2) + (mine % 2 + rel % 2) % 2


def partner_of(hop):
    dp, tensor = lax.axis_index("dp"), lax.axis_index("tensor")
    if hop == "core":
        return {"tensor": tensor + 1 - 2 * (tensor % 2)}
    if hop == "x":
        return {"tensor": (tensor + 2) % 4}
    if hop == "y":
        return {"dp": dp + 1 - 2 * (dp % 2)}
    if hop == "z1":
        return {"dp": dp + 2 - 4 * ((dp // 2) % 2)}
    return {"dp": (dp + 4) % 8}


def greet(hops):
    barrier = pltpu.get_barrier_semaphore()
    for hop in hops:
        pl.semaphore_signal(
            barrier, inc=1, device_id=partner_of(hop), device_id_type=pl.DeviceIdType.MESH
        )
    pl.semaphore_wait(barrier, len(hops))


def to_partner(hop, source, target, send, recv):
    return pltpu.make_async_remote_copy(
        src_ref=source,
        dst_ref=target,
        send_sem=send,
        recv_sem=recv,
        device_id=partner_of(hop),
        device_id_type=pl.DeviceIdType.MESH,
    )


def part(array, begin, rows):
    return (array, begin, rows)


class Line:
    def __init__(self):
        self.token = None
        self.moves = ()
        self.arrived = []
        self.calls = 0

    def carry(self, *moves):
        self.moves = moves

    def run(self, body, args, in_specs, out_specs, out_shape, aliases=None, scratch_shapes=(), limit=32, hops=(), **rest):
        moves, self.moves = self.moves, ()
        sources, copies, landed = [], [], []
        for hop, *pieces in moves:
            offset = 0
            for piece in pieces:
                array, begin, rows = piece if isinstance(piece, tuple) else (piece, 0, piece.shape[0])
                which = next((at for at, one in enumerate(sources) if one is array), len(sources))
                if which == len(sources):
                    sources.append(array)
                copies.append((hop, which, begin, rows, len(landed), offset))
                offset += rows
            landed.append(shaped((offset,) + array.shape[1:], array.dtype))
        reach = list(hops) + [hop for hop in dict.fromkeys(move[0] for move in moves) if hop not in hops]
        lead = 0 if self.token is None else 1
        inputs = lead + len(args)
        first_out = inputs + len(sources)
        outputs = len(out_shape)
        first_scratch = first_out + outputs + len(landed) + 1
        steps = rest.get("grid", (1,))[0]

        def inner(*refs):
            scratch = refs[first_scratch:]
            pending = []
            if copies:
                *scratch, send, recv = scratch
                for at, (hop, which, begin, rows, where, offset) in enumerate(copies):
                    pending.append(
                        to_partner(
                            hop,
                            refs[inputs + which].at[pl.ds(begin, rows)],
                            refs[first_out + outputs + where].at[pl.ds(offset, rows)],
                            send.at[at],
                            recv.at[at],
                        )
                    )

            def begin_all():
                greet(reach)
                for one in pending:
                    one.start()

            def end_all():
                for one in pending:
                    one.wait()

            at_ends = (lambda step, act: pl.when(pl.program_id(0) == step)(act)) if steps > 1 else (
                lambda step, act: act()
            )
            if reach:
                at_ends(0, begin_all)
            body(*refs[lead:inputs], *refs[first_out : first_out + outputs], *scratch)
            if pending:
                at_ends(steps - 1, end_all)

        extra = {}
        if reach:
            extra = {"collective_id": self.calls, "has_side_effects": True}
            self.calls += 1
        found = pl.pallas_call(
            inner,
            in_specs=[IN_HBM] * lead + list(in_specs) + [IN_HBM] * len(sources),
            out_specs=list(out_specs) + [IN_HBM] * (len(landed) + 1),
            out_shape=list(out_shape) + landed + [shaped((8, 128), jnp.float32)],
            scratch_shapes=list(scratch_shapes)
            + ([pltpu.SemaphoreType.DMA((len(copies),))] * 2 if copies else []),
            input_output_aliases={lead + at: to for at, to in (aliases or {}).items()},
            cost_estimate=cost(weight_of.get(rest["name"], 1.0) * 0.2e9, 1000),
            compiler_params=pltpu.CompilerParams(vmem_limit_bytes=limit * MIB, **extra),
            **rest,
        )(*([self.token] * lead), *args, *sources)
        self.token = found[-1]
        self.arrived = list(found[outputs:-1])
        return list(found[:outputs])


def lanes_of(source_ref, at, width):
    return pl.ds(pl.multiple_of(source_ref[at] * width, width), width)


def norm_rows(rows, gain):
    scale = lax.rsqrt(jnp.mean(rows * rows, axis=-1, keepdims=True) + norm_eps)
    return rows * scale * gain


def norm_rows_back(rows, gain, grad):
    scale = lax.rsqrt(jnp.mean(rows * rows, axis=-1, keepdims=True) + norm_eps)
    scaled = grad * gain
    inner = jnp.sum(scaled * rows, axis=-1, keepdims=True)
    grad_in = scale * scaled - rows * (scale * scale * scale) * inner / rows.shape[-1]
    return grad_in, jnp.sum(grad * rows * scale, axis=0, keepdims=True)


def gelu_both(upper):
    size = jnp.abs(upper)
    base = 1.0 + (0.3275911 / math.sqrt(2.0)) * size
    guess = pl.reciprocal(base, approx=True)
    ratio = guess * (2.0 - base * guess)
    bell = jnp.exp(-0.5 * upper * upper)
    series = ratio * (
        0.5 * 0.254829592
        + ratio
        * (
            -0.5 * 0.284496736
            + ratio * (0.5 * 1.421413741 + ratio * (-0.5 * 1.453152027 + ratio * (0.5 * 1.061405429)))
        )
    )
    tail = series * bell
    cdf = jnp.where(upper >= 0.0, 1.0 - tail, tail)
    density = bell * (1.0 / math.sqrt(2.0 * math.pi))
    return (upper * cdf).astype(jnp.bfloat16), (cdf + upper * density).astype(jnp.bfloat16)


def both(rows, near, far):
    depth = near.shape[0]
    return dot_rows(rows[:, :depth], near) + dot_rows(rows[:, depth:], far)


def prep_body(source_ref, frames_ref, gains_ref, rows_ref, gains_out_ref, normed_ref):
    owned = frames_ref.shape[1] // source_ref.shape[0]
    for at in range(source_ref.shape[0]):
        here = slice(at * owned, (at + 1) * owned)
        rows_ref[:, here] = frames_ref[:, lanes_of(source_ref, at, owned)]
        gains_out_ref[:, here] = gains_ref[:, lanes_of(source_ref, at, owned)]
    normed_ref[...] = norm_rows(rows_ref[...].astype(jnp.float32), gains_out_ref[0:1, :]).astype(
        jnp.bfloat16
    )


def prep(line, source, frames, gains):
    return line.run(
        prep_body,
        (source, frames, gains,),
        in_specs=[IN_SMEM, VMEM_WHOLE, VMEM_WHOLE],
        out_specs=[VMEM_WHOLE] * 3,
        out_shape=[
            shaped(frames.shape, jnp.bfloat16),
            shaped(gains.shape, jnp.float32),
            shaped(frames.shape, jnp.bfloat16),
        ],
        limit=(16),
        name="prep_rows",
    )


def merge_body(which, base_ref, one_ref, two_ref, three_ref, gains_ref, middle_ref, normed_ref=None):
    total = base_ref[...].astype(jnp.float32)
    for ref in (one_ref, two_ref, three_ref):
        total = total + ref[...].astype(jnp.float32)
    middle_ref[...] = total
    if normed_ref is not None:
        normed_ref[...] = norm_rows(total, gains_ref[which : which + 1, :]).astype(jnp.bfloat16)


def merge(line, base, terms, gains, which, normed=True):
    outs = [shaped(base.shape, jnp.float32)]
    if normed:
        outs.append(shaped(base.shape, jnp.bfloat16))
    return line.run(
        lambda *refs: merge_body(which, *refs),
        (base, *terms, gains,),
        in_specs=[VMEM_WHOLE] * 5,
        out_specs=[VMEM_WHOLE] * len(outs),
        out_shape=outs,
        limit=(16),
        name="merge_rows",
    )


def merge_back_body(
    which, rows_ref, one_ref, two_ref, three_ref, grad_ref, gains_ref, total_ref, small_ref, gain_ref
):
    grad = one_ref[...].astype(jnp.float32)
    for ref in (two_ref, three_ref):
        grad = grad + ref[...].astype(jnp.float32)
    part, gain_grad = norm_rows_back(
        rows_ref[...].astype(jnp.float32), gains_ref[which : which + 1, :], grad
    )
    total = grad_ref[...] + part
    total_ref[...] = total
    small_ref[...] = total.astype(jnp.bfloat16)
    gain_ref[...] = gain_grad


def merge_back(line, rows, terms, grad, gains, which):
    return line.run(
        lambda *refs: merge_back_body(which, *refs),
        (rows, *terms, grad, gains,),
        in_specs=[VMEM_WHOLE] * 6,
        out_specs=[VMEM_WHOLE] * 3,
        out_shape=[
            shaped(rows.shape, jnp.float32),
            shaped(rows.shape, jnp.bfloat16),
            shaped((1, rows.shape[1]), jnp.float32),
        ],
        limit=(16),
        name="merge_rows_back",
    )


def finish_body(
    source_ref, rows_ref, one_ref, two_ref, three_ref, grad_ref, gains_ref, gb_ref, gc_ref, gd_ref,
    out_ref, gain_ref,
):
    grad = one_ref[...].astype(jnp.float32)
    for ref in (two_ref, three_ref):
        grad = grad + ref[...].astype(jnp.float32)
    part, gain_grad = norm_rows_back(rows_ref[...].astype(jnp.float32), gains_ref[0:1, :], grad)
    total = grad_ref[...] + part
    owned = out_ref.shape[1] // source_ref.shape[0]
    for at in range(source_ref.shape[0]):
        here = slice(at * owned, (at + 1) * owned)
        there = lanes_of(source_ref, at, owned)
        out_ref[:, there] = total[:, here]
        gain_ref[0:1, there] = gain_grad[:, here]
        gain_ref[1:2, there] = gb_ref[:, here]
        gain_ref[2:3, there] = gc_ref[:, here]
        gain_ref[3:4, there] = gd_ref[:, here]


def finish(line, source, rows, terms, grad, gains, others):
    return line.run(
        finish_body,
        (source, rows, *terms, grad, gains, *others,),
        in_specs=[IN_SMEM] + [VMEM_WHOLE] * 9,
        out_specs=[VMEM_WHOLE] * 2,
        out_shape=[shaped(rows.shape, jnp.float32), shaped((4, rows.shape[1]), jnp.float32)],
        limit=(16),
        name="input_grad",
    )


def global_heads_body(
    info_ref, x0, x1, x2, x3, near_ref, far_ref, qkv_ref, mixed_ref, lse_ref, p0, p1, p2, p3, acc, lse_wide
):
    share = x0.shape[0]
    span = 4 * share
    width = mixed_ref.shape[1]
    length = info_ref[1]
    scale = HD ** (-0.5)
    for rel, x_ref in enumerate((x0, x1, x2, x3)):
        at = pl.ds(pl.multiple_of(group_at(rel) * share, share), share)
        full = both(x_ref[...], near_ref[:, : 3 * width], far_ref[:, : 3 * width])
        qkv_ref[at, :] = full.astype(jnp.bfloat16)
    acc[...] = jnp.zeros_like(acc)
    lse_wide[...] = jnp.zeros_like(lse_wide)
    head_of = lax.broadcasted_iota(jnp.int32, (1, width), 1) // HD
    lane = lax.broadcasted_iota(jnp.int32, (1, 128), 1)

    @pl.loop(0, width // HD)
    def per_head(head):
        own = head_of == head
        for block in range(4):
            rows = slice(block * share, (block + 1) * share)
            reach = (block + 1) * share
            query = jnp.where(own, qkv_ref[rows, :width] * scale, 0.0).astype(jnp.bfloat16)
            scores = dot_transposed(query, qkv_ref[:reach, width : 2 * width])
            row_at = block * share + lax.broadcasted_iota(jnp.int32, scores.shape, 0)
            col_at = lax.broadcasted_iota(jnp.int32, scores.shape, 1)
            scores = jnp.where((col_at <= row_at) & (col_at < length), scores, masked_fill)
            top = jnp.max(scores, axis=-1, keepdims=True)
            expanded = jnp.exp(scores - top)
            total = jnp.sum(expanded, axis=-1, keepdims=True)
            prob = (expanded * (1.0 / total)).astype(jnp.bfloat16)
            value = jnp.where(own, qkv_ref[:reach, 2 * width :], 0.0).astype(jnp.bfloat16)
            acc[rows, :] += dot_rows(prob, value)
            lse_wide[rows, :] = jnp.where(lane == head, top + jnp.log(total), lse_wide[rows, :])

    mixed_ref[...] = acc[...].astype(jnp.bfloat16)
    lse_ref[...] = jnp.transpose(lse_wide[...])[: lse_ref.shape[0], :]
    half = near_ref.shape[0]
    for rel, p_ref in enumerate((p0, p1, p2, p3)):
        at = pl.ds(pl.multiple_of(group_at(rel) * share, share), share)
        rows = mixed_ref[at, :]
        p_ref[:, :half] = dot_transposed(rows, near_ref[:, 3 * width :]).astype(jnp.bfloat16)
        p_ref[:, half:] = dot_transposed(rows, far_ref[:, 3 * width :]).astype(jnp.bfloat16)


def global_heads(line, info, rows, halves):
    share, width = rows[0].shape[0], halves[0].shape[1] // 4
    span = 4 * share
    return line.run(
        global_heads_body,
        (info, *rows, *halves,),
        in_specs=[IN_SMEM] + [VMEM_WHOLE] * 6,
        out_specs=[VMEM_WHOLE] * 7,
        out_shape=[
            shaped((span, 3 * width), jnp.bfloat16),
            shaped((span, width), jnp.bfloat16),
            shaped((8, span), jnp.float32),
        ]
        + [shaped((share, D), jnp.bfloat16)] * 4,
        scratch_shapes=[pltpu.VMEM((span, width), jnp.float32), pltpu.VMEM((span, 128), jnp.float32)],
        limit=(40),
        name="global_heads",
    )


def global_heads_back_body(
    info_ref, g0, g1, g2, g3, near_ref, far_ref, qkv_ref, mixed_ref, lse_ref, dqkv_ref, p0, p1, p2, p3,
    dmix, dq_t, dk_acc, dv_acc, center, k_t,
):
    share = g0.shape[0]
    width = mixed_ref.shape[1]
    heads = width // HD
    length = info_ref[1]
    scale = HD ** (-0.5)
    for rel, g_ref in enumerate((g0, g1, g2, g3)):
        at = pl.ds(pl.multiple_of(group_at(rel) * share, share), share)
        full = both(g_ref[...], near_ref[:, 3 * width :], far_ref[:, 3 * width :])
        dmix[at, :] = full.astype(jnp.bfloat16)
    head_of = lax.broadcasted_iota(jnp.int32, (1, width), 1) // HD
    pick = (
        lax.broadcasted_iota(jnp.int32, (8, width), 1) // HD
        == lax.broadcasted_iota(jnp.int32, (8, width), 0)
    ).astype(jnp.bfloat16)
    product = dmix[...].astype(jnp.float32) * mixed_ref[...].astype(jnp.float32)
    high = product.astype(jnp.bfloat16)
    low = (product - high.astype(jnp.float32)).astype(jnp.bfloat16)
    center[...] = dot_transposed(pick, high) + dot_transposed(pick, low)
    k_t[...] = jnp.transpose(qkv_ref[:, width : 2 * width])
    dq_t[...] = jnp.zeros_like(dq_t)
    dk_acc[...] = jnp.zeros_like(dk_acc)
    dv_acc[...] = jnp.zeros_like(dv_acc)
    for head in range(heads):
        own = head_of == head
        for block in range(4):
            rows = slice(block * share, (block + 1) * share)
            reach = (block + 1) * share
            query = jnp.where(own, qkv_ref[rows, :width] * scale, 0.0).astype(jnp.bfloat16)
            grad = jnp.where(own, dmix[rows, :], 0.0).astype(jnp.bfloat16)
            scores = dot_transposed(qkv_ref[:reach, width : 2 * width], query)
            key_at = lax.broadcasted_iota(jnp.int32, scores.shape, 0)
            row_at = block * share + lax.broadcasted_iota(jnp.int32, scores.shape, 1)
            prob = jnp.where(
                (key_at <= row_at) & (key_at < length),
                jnp.exp(scores - lse_ref[head : head + 1, rows]),
                0.0,
            )
            dprob = dot_transposed(qkv_ref[:reach, 2 * width :], grad)
            dscore = (prob * (dprob - center[head : head + 1, rows])).astype(jnp.bfloat16)
            dv_acc[:reach, :] += dot_rows(prob.astype(jnp.bfloat16), grad)
            dk_acc[:reach, :] += dot_rows(dscore, query)
            lanes = slice(head * HD, (head + 1) * HD)
            dq_t[lanes, rows] += dot_rows(k_t[lanes, :reach], dscore)
    dqkv_ref[:, :width] = (jnp.transpose(dq_t[...]) * scale).astype(jnp.bfloat16)
    dqkv_ref[:, width : 2 * width] = dk_acc[...].astype(jnp.bfloat16)
    dqkv_ref[:, 2 * width :] = dv_acc[...].astype(jnp.bfloat16)
    half = near_ref.shape[0]
    for rel, p_ref in enumerate((p0, p1, p2, p3)):
        at = pl.ds(pl.multiple_of(group_at(rel) * share, share), share)
        rows = dqkv_ref[at, :]
        p_ref[:, :half] = dot_transposed(rows, near_ref[:, : 3 * width]).astype(jnp.bfloat16)
        p_ref[:, half:] = dot_transposed(rows, far_ref[:, : 3 * width]).astype(jnp.bfloat16)


def global_heads_back(line, info, grads, halves, qkv, mixed, lse):
    share, width = grads[0].shape[0], mixed.shape[1]
    span = 4 * share
    return line.run(
        global_heads_back_body,
        (info, *grads, *halves, qkv, mixed, lse,),
        in_specs=[IN_SMEM] + [VMEM_WHOLE] * 9,
        out_specs=[VMEM_WHOLE] * 5,
        out_shape=[shaped((span, 3 * width), jnp.bfloat16)]
        + [shaped((share, D), jnp.bfloat16)] * 4,
        scratch_shapes=[
            pltpu.VMEM((span, width), jnp.bfloat16),
            pltpu.VMEM((width, span), jnp.float32),
            pltpu.VMEM((span, width), jnp.float32),
            pltpu.VMEM((span, width), jnp.float32),
            pltpu.VMEM((8, span), jnp.float32),
            pltpu.VMEM((width, span), jnp.bfloat16),
        ],
        limit=(40),
        name="global_heads_back",
    )


def global_grads_heads_body(
    info_ref, a0, a1, a2, a3, g0, g1, g2, g3, dqkv_ref, mixed_ref, near_ref, far_ref, a_t, g_t
):
    share = a0.shape[0]
    width = mixed_ref.shape[1]
    for rel in range(4):
        at = pl.ds(pl.multiple_of(group_at(rel) * share, share), share)
        a_t[:, at] = jnp.transpose((a0, a1, a2, a3)[rel][...])
        g_t[:, at] = jnp.transpose((g0, g1, g2, g3)[rel][...])

    for at in range(D // 256):
        rows = slice(at * 256, (at + 1) * 256)
        out_ref, begin = (near_ref, 0) if at * 256 < D // 2 else (far_ref, D // 2)
        there = slice(at * 256 - begin, at * 256 - begin + 256)
        out_ref[there, : 3 * width] = dot_rows(a_t[rows, :], dqkv_ref[...]).astype(jnp.bfloat16)
        out_ref[there, 3 * width :] = dot_rows(g_t[rows, :], mixed_ref[...]).astype(jnp.bfloat16)


def global_grads_heads(line, info, normed, grads, dqkv, mixed):
    span, width = mixed.shape
    return line.run(
        global_grads_heads_body,
        (info, *normed, *grads, dqkv, mixed,),
        in_specs=[IN_SMEM] + [VMEM_WHOLE] * 10,
        out_specs=[VMEM_WHOLE] * 2,
        out_shape=[shaped((D // 2, 4 * width), jnp.bfloat16)] * 2,
        scratch_shapes=[pltpu.VMEM((D, span), jnp.bfloat16)] * 2,
        limit=(40),
        name="global_heads_grads",
    )


def global_ff_body(x0, x1, x2, x3, up0, up1, down0, down1, active_ref, slope_ref, p0, p1, p2, p3, acc):
    step = pl.program_id(0)
    share = x0.shape[0]
    half = up0.shape[0]

    @pl.when(step == 0)
    def _():
        acc[...] = jnp.zeros_like(acc)

    for rel, x_ref in enumerate((x0, x1, x2, x3)):
        rows = slice(rel * share, (rel + 1) * share)
        active, slope = gelu_both(both(x_ref[...], up0[...], up1[...]))
        active_ref[rows, :] = active
        slope_ref[rows, :] = slope
        for at, down in enumerate((down0, down1)):
            lanes = slice(at * half, (at + 1) * half)
            acc[rows, lanes] += dot_transposed(active, down[...])

    @pl.when(step == pl.num_programs(0) - 1)
    def _():
        for rel, p_ref in enumerate((p0, p1, p2, p3)):
            p_ref[...] = acc[rel * share : (rel + 1) * share, :].astype(jnp.bfloat16)


def held(shape):
    return pl.BlockSpec(shape, lambda step: (0,) * len(shape), pipeline_mode=pl.Buffered(1))


def by_cols(shape):
    return pl.BlockSpec(shape, lambda step: (0, step))


def global_ff(line, rows, up, down, tile=256):
    share = rows[0].shape[0]
    span, hidden, half = 4 * share, up[0].shape[1], up[0].shape[0]
    return line.run(
        global_ff_body,
        (*rows, *up, *down,),
        grid=(hidden // tile,),
        in_specs=[held((share, D))] * 4 + [by_cols((half, tile))] * 4,
        out_specs=[by_cols((span, tile))] * 2 + [held((share, D))] * 4,
        out_shape=[shaped((span, hidden), jnp.bfloat16)] * 2
        + [shaped((share, D), jnp.bfloat16)] * 4,
        scratch_shapes=[pltpu.VMEM((span, D), jnp.float32)],
        limit=(40),
        name="global_ff",
    )


def global_ff_back_body(g0, g1, g2, g3, slope_ref, up0, up1, down0, down1, dup_ref, p0, p1, p2, p3, acc):
    step = pl.program_id(0)
    share = g0.shape[0]
    half = up0.shape[0]

    @pl.when(step == 0)
    def _():
        acc[...] = jnp.zeros_like(acc)

    for rel, g_ref in enumerate((g0, g1, g2, g3)):
        rows = slice(rel * share, (rel + 1) * share)
        grad = both(g_ref[...], down0[...], down1[...])
        dup = (grad * slope_ref[rows, :].astype(jnp.float32)).astype(jnp.bfloat16)
        dup_ref[rows, :] = dup
        for at, up in enumerate((up0, up1)):
            lanes = slice(at * half, (at + 1) * half)
            acc[rows, lanes] += dot_transposed(dup, up[...])

    @pl.when(step == pl.num_programs(0) - 1)
    def _():
        for rel, p_ref in enumerate((p0, p1, p2, p3)):
            p_ref[...] = acc[rel * share : (rel + 1) * share, :].astype(jnp.bfloat16)


def global_ff_back(line, grads, slope, up, down, tile=256):
    share = grads[0].shape[0]
    span, hidden, half = 4 * share, up[0].shape[1], up[0].shape[0]
    return line.run(
        global_ff_back_body,
        (*grads, slope, *up, *down,),
        grid=(hidden // tile,),
        in_specs=[held((share, D))] * 4 + [by_cols((span, tile))] + [by_cols((half, tile))] * 4,
        out_specs=[by_cols((span, tile))] + [held((share, D))] * 4,
        out_shape=[shaped((span, hidden), jnp.bfloat16)] + [shaped((share, D), jnp.bfloat16)] * 4,
        scratch_shapes=[pltpu.VMEM((span, D), jnp.float32)],
        limit=(40),
        name="global_ff_back",
    )


def outer_body(r0, r1, r2, r3, right_ref, near_ref, far_ref, left_t):
    share = r0.shape[0]

    @pl.when(pl.program_id(0) == 0)
    def _():
        for rel, ref in enumerate((r0, r1, r2, r3)):
            left_t[:, rel * share : (rel + 1) * share] = jnp.transpose(ref[...])

    for at in range(D // 256):
        rows = slice(at * 256, (at + 1) * 256)
        out_ref, begin = (near_ref, 0) if at * 256 < D // 2 else (far_ref, D // 2)
        out_ref[at * 256 - begin : at * 256 - begin + 256, :] = dot_rows(
            left_t[rows, :], right_ref[...]
        ).astype(jnp.bfloat16)


def global_outer(line, rows, right, tile=256):
    share = rows[0].shape[0]
    span, hidden = right.shape
    return line.run(
        outer_body,
        (*rows, right,),
        grid=(hidden // tile,),
        in_specs=[held((share, D))] * 4 + [by_cols((span, tile))],
        out_specs=[by_cols((D // 2, tile))] * 2,
        out_shape=[shaped((D // 2, hidden), jnp.bfloat16)] * 2,
        scratch_shapes=[pltpu.VMEM((D, span), jnp.bfloat16)],
        limit=(32),
        name="global_ff_grads",
    )


def head_sums(width):
    row_at = lax.broadcasted_iota(jnp.int32, (width, width), 0) // HD
    col_at = lax.broadcasted_iota(jnp.int32, (width, width), 1) // HD
    return (row_at == col_at).astype(jnp.bfloat16)


def over_heads(product, ones):
    high = product.astype(jnp.bfloat16)
    low = (product - high.astype(jnp.float32)).astype(jnp.bfloat16)
    return dot_rows(high, ones) + dot_rows(low, ones)


def frame_probs(queries, keys, ones):
    found = []
    for at in range(CB):
        scores = [over_heads(queries[at] * keys[c2], ones) * HD ** (-0.5) for c2 in range(at + 1)]
        top = scores[0]
        for one in scores[1:]:
            top = jnp.maximum(top, one)
        expanded = [jnp.exp(one - top) for one in scores]
        total = expanded[0]
        for one in expanded[1:]:
            total = total + one
        inverse = 1.0 / total
        found.append([one * inverse for one in expanded])
    return found


def rounded_f32(values):
    return values.astype(jnp.bfloat16).astype(jnp.float32)


def start_weights(parts, buffer, sems):
    for at, pair in enumerate(parts):
        for half, ref in enumerate(pair):
            pltpu.make_async_copy(ref, buffer.at[at, half], sems.at[at, half]).start()


def wait_weights(parts, buffer, sems, at):
    for half in range(2):
        pltpu.make_async_copy(parts[0][half], buffer.at[at, half], sems.at[at, half]).wait()


def local_heads_body(
    out_ref_in, code_ref, gains_ref, *refs
):
    count = 4
    parts = [refs[2 * at : 2 * at + 2] for at in range(count)]
    qkv_ref, mixed_ref, middle_ref, normed_b_ref, a_t_ref, normed_a, local_in, buffer, sems = refs[2 * count :]
    step = pl.program_id(0)
    frames = out_ref_in.shape[0]
    width = mixed_ref.shape[2]
    half = D // 2

    @pl.when(step == 0)
    def _():
        start_weights(parts, buffer, sems)
        for c in range(CB):
            rows = slice(c * frames, (c + 1) * frames)
            local_in[rows, :] = out_ref_in[...] + code_ref[rows, :].astype(jnp.float32)
            normed = norm_rows(local_in[rows, :], gains_ref[2:3, :]).astype(jnp.bfloat16)
            normed_a[rows, :] = normed
            a_t_ref[:, rows] = jnp.transpose(normed)
        middle_ref[...] = local_in[...]

    wait_weights(parts, buffer, sems, step)
    ones = head_sums(width)
    queries, keys, values = ([], [], [])
    for c in range(CB):
        rows = slice(c * frames, (c + 1) * frames)
        qkv = (
            dot_rows(normed_a[rows, :half], buffer[step, 0, :, : 3 * width])
            + dot_rows(normed_a[rows, half:], buffer[step, 1, :, : 3 * width])
        ).astype(jnp.bfloat16)
        qkv_ref[0, rows, :] = qkv
        queries.append(qkv[:, :width].astype(jnp.float32))
        keys.append(qkv[:, width : 2 * width].astype(jnp.float32))
        values.append(qkv[:, 2 * width :].astype(jnp.float32))
    prob = frame_probs(queries, keys, ones)
    for c in range(CB):
        rows = slice(c * frames, (c + 1) * frames)
        mix = rounded_f32(prob[c][0]) * values[0]
        for c2 in range(1, c + 1):
            mix = mix + rounded_f32(prob[c][c2]) * values[c2]
        mix = mix.astype(jnp.bfloat16)
        mixed_ref[0, rows, :] = mix
        for at in range(2):
            lanes = slice(at * half, (at + 1) * half)
            middle_ref[rows, lanes] += dot_transposed(mix, buffer[step, at, :, 3 * width :])

    @pl.when(step == count - 1)
    def _():
        for c in range(CB):
            rows = slice(c * frames, (c + 1) * frames)
            normed_b_ref[rows, :] = norm_rows(middle_ref[rows, :], gains_ref[3:4, :]).astype(
                jnp.bfloat16
            )


def local_heads(line, global_out, codes, gains, parts):
    frames = global_out.shape[0]
    rows = CB * frames
    width = parts[0][0].shape[1] // 4
    half = D // 2
    flat = [ref for pair in parts for ref in pair]
    return line.run(
        local_heads_body,
        (global_out, codes, gains, *flat),
        grid=(4,),
        in_specs=[held((frames, D)), held((rows, D)), held((4, D))] + [IN_HBM] * 8,
        out_specs=[
            pl.BlockSpec((1, rows, 3 * width), lambda step: (step, 0, 0)),
            pl.BlockSpec((1, rows, width), lambda step: (step, 0, 0)),
            held((rows, D)),
            held((rows, D)),
            held((D, rows)),
        ],
        out_shape=[
            shaped((4, rows, 3 * width), jnp.bfloat16),
            shaped((4, rows, width), jnp.bfloat16),
            shaped((rows, D), jnp.float32),
            shaped((rows, D), jnp.bfloat16),
            shaped((D, rows), jnp.bfloat16),
        ],
        scratch_shapes=[
            pltpu.VMEM((rows, D), jnp.bfloat16),
            pltpu.VMEM((rows, D), jnp.float32),
            pltpu.VMEM((4, 2, half, 4 * width), jnp.bfloat16),
            pltpu.SemaphoreType.DMA((4, 2)),
        ],
        limit=(52),
        name="local_heads",
    )


def local_ff_body(source_ref, normed_ref, middle_ref, *refs):
    count = 4
    ups = [refs[2 * at : 2 * at + 2] for at in range(count)]
    downs = [refs[2 * count + 2 * at : 2 * count + 2 * at + 2] for at in range(count)]
    active_ref, slope_ref, out_ref, b_t_ref, acc, up_buf, down_buf, up_sems, down_sems = refs[4 * count :]
    step = pl.program_id(0)
    rows_all = normed_ref.shape[0]
    frames = rows_all // CB
    half = D // 2
    tile = active_ref.shape[2]
    per = up_buf.shape[3] // tile
    group = step // per
    cols_at = pl.ds(pl.multiple_of((step % per) * tile, tile), tile)

    @pl.when(step == 0)
    def _():
        for at in range(count):
            start_weights_at(ups, up_buf, up_sems, at)
            start_weights_at(downs, down_buf, down_sems, at)
        b_t_ref[...] = jnp.transpose(normed_ref[...])
        acc[...] = middle_ref[...]

    @pl.when(step % per == 0)
    def _():
        wait_weights(ups, up_buf, up_sems, group)
        wait_weights(downs, down_buf, down_sems, group)

    for c in range(CB):
        rows = slice(c * frames, (c + 1) * frames)
        upper = dot_rows(normed_ref[rows, :half], up_buf[group, 0, :, cols_at]) + dot_rows(
            normed_ref[rows, half:], up_buf[group, 1, :, cols_at]
        )
        active, slope = gelu_both(upper)
        active_ref[0, rows, :] = active
        slope_ref[0, rows, :] = slope
        for at in range(2):
            lanes = slice(at * half, (at + 1) * half)
            acc[rows, lanes] += dot_transposed(active, down_buf[group, at, :, cols_at])

    @pl.when(step == pl.num_programs(0) - 1)
    def _():
        owned = D // source_ref.shape[0]
        for c in range(CB):
            rows = slice(c * frames, (c + 1) * frames)
            for at in range(source_ref.shape[0]):
                here = slice(at * owned, (at + 1) * owned)
                out_ref[c, :, lanes_of(source_ref, at, owned)] = acc[rows, here].astype(jnp.bfloat16)


def start_weights_at(parts, buffer, sems, at):
    for half in range(2):
        pltpu.make_async_copy(parts[at][half], buffer.at[at, half], sems.at[at, half]).start()


def local_ff(line, source, normed, middle, ups, downs, tile=512):
    rows = normed.shape[0]
    hidden = ups[0][0].shape[1]
    half = D // 2
    per = hidden // tile
    flat = [ref for pair in ups for ref in pair] + [ref for pair in downs for ref in pair]
    hidden_block = pl.BlockSpec((1, rows, tile), lambda step: (step // per, 0, step % per))
    return line.run(
        local_ff_body,
        (source, normed, middle, *flat,),
        grid=(4 * per,),
        in_specs=[IN_SMEM, held((rows, D)), held((rows, D))] + [IN_HBM] * 16,
        out_specs=[hidden_block, hidden_block, held((CB, rows // CB, D)), held((D, rows))],
        out_shape=[
            shaped((4, rows, hidden), jnp.bfloat16),
            shaped((4, rows, hidden), jnp.bfloat16),
            shaped((CB, rows // CB, D), jnp.bfloat16),
            shaped((D, rows), jnp.bfloat16),
        ],
        scratch_shapes=[
            pltpu.VMEM((rows, D), jnp.float32),
            pltpu.VMEM((4, 2, half, hidden), jnp.bfloat16),
            pltpu.VMEM((4, 2, half, hidden), jnp.bfloat16),
            pltpu.SemaphoreType.DMA((4, 2)),
            pltpu.SemaphoreType.DMA((4, 2)),
        ],
        limit=(56),
        name="local_ff",
    )


def seed_body(source_ref, count_ref, cot_ref, code_ref, grad_ref, grad_t_ref, codes_ref):
    frames = cot_ref.shape[1]
    owned = D // source_ref.shape[0]
    keep = lax.broadcasted_iota(jnp.int32, (frames, 1), 0) < count_ref[0]
    for c in range(CB):
        rows = slice(c * frames, (c + 1) * frames)
        for at in range(source_ref.shape[0]):
            here = slice(at * owned, (at + 1) * owned)
            values = cot_ref[c, :, lanes_of(source_ref, at, owned)].astype(jnp.float32)
            grad_ref[rows, here] = jnp.where(keep, values, 0.0).astype(jnp.bfloat16)
            codes_ref[rows, here] = code_ref[c, :, lanes_of(source_ref, at, owned)]
        grad_t_ref[:, rows] = jnp.transpose(grad_ref[rows, :])


def seed(line, source, count, cot, codes):
    frames = cot.shape[1]
    rows = CB * frames
    return line.run(
        seed_body,
        (source, count, cot, codes),
        in_specs=[IN_SMEM, IN_SMEM, VMEM_WHOLE, VMEM_WHOLE],
        out_specs=[VMEM_WHOLE] * 3,
        out_shape=[
            shaped((rows, D), jnp.bfloat16),
            shaped((D, rows), jnp.bfloat16),
            shaped((rows, D), jnp.bfloat16),
        ],
        limit=(24),
        name="seed_grads",
    )


def local_ff_back_body(last, summed, first, grad_ref, grad_t_ref, b_t_ref, active_ref, slope_ref, up0, up1, down0, down1, *refs):
    if summed:
        met_ref, refs = refs[0], refs[1:]
    so_far_ref, refs = (None, refs) if first else (refs[0], refs[1:])
    if last:
        middle_ref, gains_ref, refs = refs[0], refs[1], refs[2:]
    if summed:
        (down_near, down_far, up_near, up_far), refs = refs[:4], refs[4:]
    else:
        both_ref, refs = refs[0], refs[1:]
    outs, (acc, dup) = refs[:-2], refs[-2:]
    step = pl.program_id(0)
    frames = grad_ref.shape[0] // CB
    half = D // 2

    @pl.when(step == 0)
    def _():
        if so_far_ref is not None:
            acc[...] = so_far_ref[...]
        else:
            acc[...] = jnp.zeros_like(acc)

    for c in range(CB):
        rows = slice(c * frames, (c + 1) * frames)
        grad = dot_rows(grad_ref[rows, :half], down0[...]) + dot_rows(grad_ref[rows, half:], down1[...])
        one = (grad * slope_ref[0, rows, :].astype(jnp.float32)).astype(jnp.bfloat16)
        dup[rows, :] = one
        for at, up in enumerate((up0, up1)):
            lanes = slice(at * half, (at + 1) * half)
            acc[rows, lanes] += dot_transposed(one, up[...])
    for at in range(D // 256):
        rows = slice(at * 256, (at + 1) * 256)
        down = dot_rows(grad_t_ref[rows, :], active_ref[0])
        up = dot_rows(b_t_ref[rows, :], dup[...])
        if summed:
            down = (down + met_ref[0, rows, :].astype(jnp.float32)).astype(jnp.bfloat16)
            up = (up + met_ref[1, rows, :].astype(jnp.float32)).astype(jnp.bfloat16)
            begin = 0 if at * 256 < half else half
            there = slice(at * 256 - begin, at * 256 - begin + 256)
            (down_far if begin else down_near)[there, :] = down
            (up_far if begin else up_near)[there, :] = up
        else:
            both_ref[0, rows, :] = down.astype(jnp.bfloat16)
            both_ref[1, rows, :] = up.astype(jnp.bfloat16)

    @pl.when(step == pl.num_programs(0) - 1)
    def _():
        if last:
            grad_mid_ref, small_ref, small_t_ref, gain_ref = outs
            total_gain = jnp.zeros((1, D), jnp.float32)
            for c in range(CB):
                rows = slice(c * frames, (c + 1) * frames)
                part, gain_grad = norm_rows_back(middle_ref[rows, :], gains_ref[3:4, :], acc[rows, :])
                total = grad_ref[rows, :].astype(jnp.float32) + part
                grad_mid_ref[rows, :] = total
                small = total.astype(jnp.bfloat16)
                small_ref[rows, :] = small
                small_t_ref[:, rows] = jnp.transpose(small)
                total_gain = total_gain + gain_grad
            gain_ref[...] = total_gain
        else:
            outs[0][...] = acc[...]


def local_ff_back(line, rel, grad, grad_t, b_t, active, slope, up, down, met=None, so_far=None, tail=None, tile=512):
    rows = grad.shape[0]
    hidden = active.shape[2]
    half = D // 2
    last, summed = tail is not None, met is not None
    hidden_block = pl.BlockSpec((1, rows, tile), lambda step: (rel, 0, step))
    pair_block = pl.BlockSpec((2, D, tile), lambda step: (0, 0, step))
    extra_args, extra = ([], [])
    if summed:
        extra_args.append(met)
        extra.append(pair_block)
    if so_far is not None:
        extra_args.append(so_far)
        extra.append(held((rows, D)))
    first = so_far is None
    if last:
        extra_args += list(tail)
        extra += [held((rows, D)), held((4, D))]
        outs = [
            shaped((rows, D), jnp.float32),
            shaped((rows, D), jnp.bfloat16),
            shaped((D, rows), jnp.bfloat16),
            shaped((1, D), jnp.float32),
        ]
    else:
        outs = [shaped((rows, D), jnp.float32)]
    if summed:
        grad_specs = [by_cols((half, tile))] * 4
        grad_shapes = [shaped((half, hidden), jnp.bfloat16)] * 4
    else:
        grad_specs = [pair_block]
        grad_shapes = [shaped((2, D, hidden), jnp.bfloat16)]

    def body(*refs):
        local_ff_back_body(last, summed, first, *refs)

    found = line.run(
        body,
        (grad, grad_t, b_t, active, slope, *up, *down, *extra_args),
        grid=(hidden // tile,),
        in_specs=[held((rows, D)), held((D, rows)), held((D, rows)), hidden_block, hidden_block]
        + [by_cols((half, tile))] * 4
        + extra,
        out_specs=grad_specs + [held(one.shape) for one in outs],
        out_shape=grad_shapes + outs,
        scratch_shapes=[pltpu.VMEM((rows, D), jnp.float32), pltpu.VMEM((rows, tile), jnp.bfloat16)],
        limit=(52),
        name="local_ff_back",
    )
    return found[: len(grad_shapes)], found[len(grad_shapes) :]


def local_heads_back_body(last, summed, first, grad_ref, grad_t_ref, a_t_ref, qkv_ref, mixed_ref, near_ref, far_ref, *refs):
    if summed:
        met_ref, refs = refs[0], refs[1:]
    if not first:
        so_far_ref, refs = refs[0], refs[1:]
    if last:
        grad_mid_ref, out_in_ref, code_ref, gains_ref = refs[:4]
        refs = refs[4:]
    if summed:
        (near_out, far_out), refs = refs[:2], refs[2:]
    else:
        out_ref, refs = refs[0], refs[1:]
    outs, (acc, dqkv) = refs[:-2], refs[-2:]
    frames = grad_ref.shape[0] // CB
    width = mixed_ref.shape[2]
    half = D // 2
    scale = HD ** (-0.5)
    ones = head_sums(width)
    queries, keys, values, dmix = ([], [], [], [])
    for c in range(CB):
        rows = slice(c * frames, (c + 1) * frames)
        qkv = qkv_ref[0, rows, :].astype(jnp.float32)
        queries.append(qkv[:, :width])
        keys.append(qkv[:, width : 2 * width])
        values.append(qkv[:, 2 * width :])
        one = dot_rows(grad_ref[rows, :half], near_ref[:, 3 * width :]) + dot_rows(
            grad_ref[rows, half:], far_ref[:, 3 * width :]
        )
        dmix.append(rounded_f32(one))
    prob = frame_probs(queries, keys, ones)
    dq, dk, dv = ([None] * CB, [None] * CB, [None] * CB)

    def more(total, term):
        return term if total is None else total + term

    for c in range(CB):
        dprob = [over_heads(dmix[c] * values[c2], ones) for c2 in range(c + 1)]
        center = prob[c][0] * dprob[0]
        for c2 in range(1, c + 1):
            center = center + prob[c][c2] * dprob[c2]
        for c2 in range(c + 1):
            dv[c2] = more(dv[c2], rounded_f32(prob[c][c2]) * dmix[c])
            dscore = rounded_f32(prob[c][c2] * (dprob[c2] - center))
            dq[c] = more(dq[c], dscore * keys[c2])
            dk[c2] = more(dk[c2], dscore * queries[c])
    for c in range(CB):
        rows = slice(c * frames, (c + 1) * frames)
        dqkv[rows, :width] = (dq[c] * scale).astype(jnp.bfloat16)
        dqkv[rows, width : 2 * width] = (dk[c] * scale).astype(jnp.bfloat16)
        dqkv[rows, 2 * width :] = dv[c].astype(jnp.bfloat16)
        for at, ref in enumerate((near_ref, far_ref)):
            lanes = slice(at * half, (at + 1) * half)
            term = dot_transposed(dqkv[rows, :], ref[:, : 3 * width])
            acc[rows, lanes] = term if first else so_far_ref[rows, lanes] + term
    for at in range(D // 256):
        rows = slice(at * 256, (at + 1) * 256)
        three = dot_rows(a_t_ref[rows, :], dqkv[...])
        one = dot_rows(grad_t_ref[rows, :], mixed_ref[0])
        there = rows
        if summed:
            three = three + met_ref[rows, : 3 * width].astype(jnp.float32)
            one = one + met_ref[rows, 3 * width :].astype(jnp.float32)
            begin = 0 if at * 256 < half else half
            out_ref = far_out if begin else near_out
            there = slice(at * 256 - begin, at * 256 - begin + 256)
        out_ref[there, : 3 * width] = three.astype(jnp.bfloat16)
        out_ref[there, 3 * width :] = one.astype(jnp.bfloat16)
    if last:
        total_ref, small_ref, gain_ref = outs
        total_gain = jnp.zeros((1, D), jnp.float32)
        total = jnp.zeros((frames, D), jnp.float32)
        for c in range(CB):
            rows = slice(c * frames, (c + 1) * frames)
            local_in = out_in_ref[...] + code_ref[rows, :].astype(jnp.float32)
            part, gain_grad = norm_rows_back(local_in, gains_ref[2:3, :], acc[rows, :])
            total = total + (grad_mid_ref[rows, :] + part)
            total_gain = total_gain + gain_grad
        total_ref[...] = total
        small_ref[...] = total.astype(jnp.bfloat16)
        gain_ref[...] = total_gain
    else:
        outs[0][...] = acc[...]


def local_heads_back(line, rel, grad, grad_t, a_t, qkv, mixed, halves, met=None, so_far=None, tail=None):
    rows = grad.shape[0]
    frames = rows // CB
    width = mixed.shape[2]
    last, summed, first = tail is not None, met is not None, so_far is None
    extra_args, extra = ([], [])
    if summed:
        extra_args.append(met)
        extra.append(held((D, 4 * width)))
    if not first:
        extra_args.append(so_far)
        extra.append(held((rows, D)))
    if last:
        extra_args += list(tail)
        extra += [held((rows, D)), held((frames, D)), held((rows, D)), held((4, D))]
        outs = [
            shaped((frames, D), jnp.float32),
            shaped((frames, D), jnp.bfloat16),
            shaped((1, D), jnp.float32),
        ]
    else:
        outs = [shaped((rows, D), jnp.float32)]

    if summed:
        grad_shapes = [shaped((D // 2, 4 * width), jnp.bfloat16)] * 2
    else:
        grad_shapes = [shaped((D, 4 * width), jnp.bfloat16)]

    def body(*refs):
        local_heads_back_body(last, summed, first, *refs)

    found = line.run(
        body,
        (grad, grad_t, a_t, qkv, mixed, *halves, *extra_args),
        grid=(1,),
        in_specs=[
            held((rows, D)),
            held((D, rows)),
            held((D, rows)),
            pl.BlockSpec((1, rows, 3 * width), lambda step: (rel, 0, 0)),
            pl.BlockSpec((1, rows, width), lambda step: (rel, 0, 0)),
        ]
        + [held((D // 2, 4 * width))] * 2
        + extra,
        out_specs=[held(one.shape) for one in grad_shapes + outs],
        out_shape=grad_shapes + outs,
        scratch_shapes=[
            pltpu.VMEM((rows, D), jnp.float32),
            pltpu.VMEM((rows, 3 * width), jnp.bfloat16),
        ],
        limit=(52),
        name="local_heads_back",
    )
    return found[: len(grad_shapes)], found[len(grad_shapes) :]


def cast_body(*refs):
    count = len(refs) // 2
    for master_ref, out_ref in zip(refs[:count], refs[count:]):
        out_ref[...] = master_ref[0].astype(jnp.bfloat16)


def cast(line, master, which):
    owned, columns = master.shape[1], master.shape[2] // 3

    def spec(layer, third):
        return pl.BlockSpec((1, owned, columns), lambda step: (layer, 0, third))

    return line.run(
        cast_body,
        (master,) * len(which),
        grid=(1,),
        in_specs=[spec(*one) for one in which],
        out_specs=[held((owned, columns))] * len(which),
        out_shape=[shaped((owned, columns), jnp.bfloat16)] * len(which),
        limit=(24),
        name="cast_shard",
    )


def stack_body(one_ref, two_ref, out_ref):
    rows = one_ref.shape[0]
    out_ref[:rows, :] = one_ref[...]
    out_ref[rows:, :] = two_ref[...]


def stack_rows(line, parts):
    rows, columns = parts[0].shape
    return line.run(
        stack_body,
        tuple(parts),
        in_specs=[VMEM_WHOLE] * 2,
        out_specs=[VMEM_WHOLE],
        out_shape=[shaped((2 * rows, columns), jnp.bfloat16)],
        limit=(16),
        name="stack_shards",
    )[0]


def add_body(*refs):
    total = refs[0][...].astype(jnp.float32)
    for ref in refs[1:-1]:
        total = total + ref[...].astype(jnp.float32)
    refs[-1][...] = total.astype(jnp.bfloat16)


def add_rows(line, terms, part=0, parts=1):
    rows = min(term.shape[0] for term in terms) if parts == 1 else terms[0].shape[0] // parts
    columns = terms[0].shape[1]

    def spec(term):
        return pl.BlockSpec(
            (rows, columns), (lambda step: (part, 0)) if term.shape[0] > rows else (lambda step: (0, 0))
        )

    return line.run(
        add_body,
        tuple(terms),
        grid=(1,),
        in_specs=[spec(term) for term in terms],
        out_specs=[pl.BlockSpec((rows, columns), lambda step: (0, 0))],
        out_shape=[shaped((rows, columns), jnp.bfloat16)],
        limit=(24),
        name="add_terms",
    )[0]


def sum_pieces(line, terms, split=()):
    rows, columns = terms[0].shape[0] // 2, terms[0].shape[1]
    whole = len(terms)
    flat = list(terms) + [one for pair in split for one in pair]

    def body(*refs):
        for at, out_ref in enumerate(refs[-2:]):
            here = slice(at * rows, (at + 1) * rows)
            total = refs[0][here, :].astype(jnp.float32)
            for ref in refs[1:whole]:
                total = total + ref[here, :].astype(jnp.float32)
            for ref in refs[whole + at : -2 : 2]:
                total = total + ref[...].astype(jnp.float32)
            out_ref[...] = total.astype(jnp.bfloat16)

    return line.run(
        body,
        tuple(flat),
        in_specs=[VMEM_WHOLE] * len(flat),
        out_specs=[VMEM_WHOLE] * 2,
        out_shape=[shaped((rows, columns), jnp.bfloat16)] * 2,
        limit=24,
        name="sum_pieces",
    )


def pass_body(*refs):
    pass


def in_turn(line, *values):
    return line.run(
        pass_body,
        tuple(values),
        in_specs=[IN_HBM] * len(values),
        out_specs=[IN_HBM] * len(values),
        out_shape=[shaped(one.shape, one.dtype) for one in values],
        aliases={at: at for at in range(len(values))},
        name="in_turn",
    )


def split_dot(left, right):
    left_high = left.astype(jnp.bfloat16)
    left_low = (left - left_high.astype(jnp.float32)).astype(jnp.bfloat16)
    right_high = right.astype(jnp.bfloat16)
    right_low = (right - right_high.astype(jnp.float32)).astype(jnp.bfloat16)
    return (
        dot_rows(left_high, right_high) + dot_rows(left_high, right_low) + dot_rows(left_low, right_high)
    )


def adam_body(chained, one_ref, two_ref, left_ref, right_ref, master_ref, first_ref, second_ref, ema_ref, *refs):
    grads_ref, new_master_ref, new_first_ref, new_second_ref, new_ema_ref = refs[5:] if chained else refs
    left = left_ref[0]
    left_t = jnp.transpose(left)
    grads = one_ref[...].astype(jnp.float32) + two_ref[...].astype(jnp.float32)
    grads_ref[0] = grads
    turned_left = split_dot(left_t, grads)
    back = []
    for at in range(right_ref.shape[1]):
        tile = slice(at * 128, (at + 1) * 128)
        right = right_ref[0, at]
        rotated = split_dot(turned_left[:, tile], right)
        new_first = beta_first * first_ref[0, :, tile] + (1.0 - beta_first) * rotated
        new_second = beta_second * second_ref[0, :, tile] + (1.0 - beta_second) * rotated * rotated
        new_first_ref[0, :, tile] = new_first
        new_second_ref[0, :, tile] = new_second
        turned = new_first / (jnp.sqrt(new_second) + adam_eps)
        back.append(split_dot(turned, jnp.transpose(right)))
    back_full = split_dot(left, jnp.concatenate(back, axis=1))
    new_master = master_ref[0] - step_rate * back_full
    new_master_ref[0] = new_master
    new_ema_ref[0] = ema_decay * ema_ref[0] + (1.0 - ema_decay) * new_master


def adam(line, layer, third, pieces, left, right, master, first, second, ema, before, tile=256):
    owned, columns = pieces[0].shape
    steps = columns // tile
    first_step = third * steps

    def state(step):
        return (layer, 0, first_step + step)

    state_spec = pl.BlockSpec((1, owned, tile), state)
    chained = before is not None
    return line.run(
        lambda *refs: adam_body(chained, *refs),
        (*pieces, left, right, master, first, second, ema, *(before or ()),),
        grid=(steps,),
        in_specs=[by_cols((owned, tile))] * 2
        + [
            pl.BlockSpec((1,) + left.shape[1:], lambda step: (layer, 0, 0)),
            pl.BlockSpec(
                (1, tile // 128) + right.shape[2:], lambda step: (layer, first_step + step, 0, 0)
            ),
        ]
        + [state_spec] * 4
        + ([IN_HBM] * 5 if chained else []),
        out_specs=[state_spec] * 5,
        out_shape=[shaped(master.shape, jnp.float32)] * 5,
        aliases={8 + at: at for at in range(5)} if chained else {},
        limit=(32),
        name="adam_update",
    )


def hop_x(values):
    return lax.ppermute(values, "tensor", [(at, at ^ 2) for at in range(4)])


def hop_core(values):
    return lax.ppermute(values, "tensor", [(at, at ^ 1) for at in range(4)])


def hop_y(values):
    return lax.ppermute(values, "dp", [(at, at ^ 1) for at in range(8)])


def hop_z(values, step):
    return lax.ppermute(values, "dp", [(at, at ^ (2 * step)) for at in range(8)])


def total_everywhere(values):
    for hop in (hop_core, hop_x, hop_y):
        values = values + hop(values)
    for step in (1, 2):
        values = values + hop_z(values, step)
    return values


def shards_grid(
    frames_in,
    code_emb,
    cotangent,
    lengths,
    owner_list,
    master,
    first_moment,
    second_moment,
    ema,
    left_basis,
    right_basis,
    gains,
    gain_first,
    gain_second,
):
    share = frames_in.shape[0]
    owned = master.shape[1]
    groups = D // owned
    heads_w = D // lax.axis_size("tensor")
    ff_w = FF // lax.axis_size("tensor")
    my_dp = lax.axis_index("dp")
    my_group = lax.axis_index("tensor").astype(jnp.int32)

    rel = jnp.array([2 * z + y for y in range(2) for z in (0, 2, 1, 3)], jnp.int32)
    owner_at = my_dp ^ rel
    slots = jnp.arange(groups, dtype=jnp.int32)
    source = jnp.sum(
        jnp.where(owner_list[None, :] == owner_at[:, None], slots[None, :], 0), axis=1
    ).astype(jnp.int32)
    info = jnp.stack([my_group, lengths[0]])
    count = (lengths - my_group * share).astype(jnp.int32)

    line = Line()
    codes = jnp.transpose(code_emb, (1, 0, 2))

    (ga,) = cast(line, master, [(0, 0)])
    ga_z = hop_z(ga, 2)
    rows_in, gains_here, normed = prep(line, source, frames_in, gains)
    normed_x = hop_x(normed)
    la, gu, lu, gd, ld = cast(line, master, [(1, 0), (0, 1), (1, 1), (0, 2), (1, 2)])
    ga = stack_rows(line, [ga, ga_z])
    ga_z, la_z = hop_z(ga, 1), hop_z(la, 2)
    (normed_x,) = in_turn(line, normed_x)
    normed_a = [normed, hop_core(normed), normed_x, hop_core(normed_x)]
    ga = stack_rows(line, [ga, ga_z])
    la = stack_rows(line, [la, la_z])
    ga_far, la_z, gu_z = hop_y(ga), hop_z(la, 1), hop_z(gu, 2)
    la = stack_rows(line, [la, la_z])
    gu = stack_rows(line, [gu, gu_z])
    la_far, la_x, gu_z, lu_z = hop_y(la), hop_x(la), hop_z(gu, 1), hop_z(lu, 2)
    g_heads = (ga, ga_far)
    qkv, mixed, lse, *parts = global_heads(line, info, normed_a, g_heads)
    near_term, far_term = hop_core(parts[1]), hop_core(parts[3])
    gu = stack_rows(line, [gu, gu_z])
    lu = stack_rows(line, [lu, lu_z])
    gu_far, lu_z, gd_z = hop_y(gu), hop_z(lu, 1), hop_z(gd, 2)
    to_x = hop_x(add_rows(line, [parts[2], far_term]))
    la_far, la_x = in_turn(line, la_far, la_x)
    lu = stack_rows(line, [lu, lu_z])
    gd = stack_rows(line, [gd, gd_z])
    lu_far, gd_z, ld_z = hop_y(lu), hop_z(gd, 1), hop_z(ld, 2)
    middle, normed = merge(line, rows_in, (parts[0], near_term, to_x), gains_here, 1)
    normed_x = hop_x(normed)
    gd = stack_rows(line, [gd, gd_z])
    ld = stack_rows(line, [ld, ld_z])
    gd_far, ld_z = hop_y(gd), hop_z(ld, 1)
    (normed_x, la_far, lu) = in_turn(line, normed_x, la_far, lu)
    normed_b = [normed, hop_core(normed), normed_x, hop_core(normed_x)]
    la_far_x, lu_x = hop_x(la_far), hop_x(lu)
    grad, grad_t, codes_here = seed(line, source, count, jnp.transpose(cotangent, (1, 0, 2)), codes)
    ld = stack_rows(line, [ld, ld_z])
    ld_far, la_c, la_far_c = hop_y(ld), hop_core(la), hop_core(la_far)
    g_up, g_down = (gu, gu_far), (gd, gd_far)
    active, slope, *parts = global_ff(line, normed_b, g_up, g_down)
    near_term, far_term = hop_core(parts[1]), hop_core(parts[3])
    (lu_x, la_far_x, ld) = in_turn(line, lu_x, la_far_x, ld)
    lu_far_x = hop_y(lu_x)
    to_x = hop_x(add_rows(line, [parts[2], far_term]))
    ld_x = hop_x(ld)
    la_xc, la_far_xc = hop_core(la_x), hop_core(la_far_x)
    (global_out,) = merge(line, middle, (parts[0], near_term, to_x), gains_here, 1, normed=False)
    (ld_far, lu_far) = in_turn(line, ld_far, lu_far)

    l_heads = [(la, la_far), (la_c, la_far_c), (la_x, la_far_x), (la_xc, la_far_xc)]
    l_qkv, l_mixed, l_middle, l_normed_b, l_a_t = local_heads(
        line, global_out, codes_here, gains_here, l_heads
    )
    lu_c, lu_far_c, ld_c, ld_far_c = hop_core(lu), hop_core(lu_far), hop_core(ld), hop_core(ld_far)
    (ld_x, lu_far_x) = in_turn(line, ld_x, lu_far_x)
    ld_far_x = hop_y(ld_x)
    lu_xc, lu_far_xc, ld_xc = hop_core(lu_x), hop_core(lu_far_x), hop_core(ld_x)
    (ld_far_x,) = in_turn(line, ld_far_x)
    ld_far_xc = hop_core(ld_far_x)
    l_up = [(lu, lu_far), (lu_c, lu_far_c), (lu_x, lu_far_x), (lu_xc, lu_far_xc)]
    l_down = [(ld, ld_far), (ld_c, ld_far_c), (ld_x, ld_far_x), (ld_xc, ld_far_xc)]
    l_active, l_slope, local_out, l_b_t = local_ff(line, source, l_normed_b, l_middle, l_up, l_down)
    local_out = jnp.transpose(local_out, (1, 0, 2))

    def ff_back(rel, **more):
        return local_ff_back(
            line, rel, grad, grad_t, l_b_t, l_active, l_slope, l_up[rel], l_down[rel], **more
        )

    (pair,), (so_far,) = ff_back(3)
    line.carry(("core", pair))
    (pair,), (so_far,) = ff_back(1, so_far=so_far)
    (met_far,) = line.arrived
    line.carry(("core", pair))
    (d2_near, d2_far, u2_near, u2_far), (so_far,) = ff_back(2, met=met_far, so_far=so_far)
    (met_near,) = line.arrived
    line.carry(("x", u2_far), ("y", d2_far))
    (d0_near, d0_far, u0_near, u0_far), (l_grad_mid, l_small, l_small_t, gain_d) = ff_back(
        0, met=met_near, so_far=so_far, tail=(l_middle, gains_here)
    )
    u2_far, d2_far = line.arrived

    def heads_back(rel, **more):
        return local_heads_back(
            line, rel, l_small, l_small_t, l_a_t, l_qkv, l_mixed, l_heads[rel], **more
        )

    half = D // 4
    line.carry(("x", part(u2_near, 0, half)), ("y", part(d0_far, 0, half)))
    (far_heads,), (so_far,) = heads_back(3)
    u2_near_a, d0_far_a = line.arrived
    u_far = add_rows(line, [u0_far, u2_far])
    d2 = add_rows(line, [d2_near, d2_far])
    line.carry(("x", part(u2_near, half, half)), ("y", part(d0_far, half, half)), ("core", far_heads))
    (near_heads,), (so_far,) = heads_back(1, so_far=so_far)
    u2_near_b, d0_far_b, met_far = line.arrived
    line.carry(("x", part(d2, 0, half)), ("y", part(u_far, 0, half)), ("core", near_heads))
    (h2_near, h2_far), (so_far,) = heads_back(2, met=met_far, so_far=so_far)
    d2_a, u_far_a, met_near = line.arrived
    line.carry(("x", part(d2, half, half)), ("y", part(u_far, half, half)))
    (h0_near, h0_far), (grad_global, small, gain_c) = heads_back(
        0, met=met_near, so_far=so_far, tail=(l_grad_mid, global_out, codes_here, gains_here)
    )
    d2_b, u_far_b = line.arrived
    h2_far = hop_y(h2_far)
    small_x = hop_x(small)
    h0_far = hop_y(h0_far)

    def update(layer, third, pieces, before):
        return adam(
            line, layer, third, pieces, left_basis, right_basis, master, first_moment, second_moment, ema, before
        )

    def depth_first(terms, split=()):
        keep, send = sum_pieces(line, terms, split)
        return keep, hop_z(send, 1)

    def depth_second(keep, met):
        keep, send = sum_pieces(line, [keep, met])
        return keep, hop_z(send, 2)

    lu = depth_first([u0_near], [[u2_near_a, u2_near_b], [u_far_a, u_far_b]])
    (small_x,) = in_turn(line, small_x)
    grad_rows = [small, hop_core(small), small_x, hop_core(small_x)]
    ld = depth_first([d0_near], [[d0_far_a, d0_far_b], [d2_a, d2_b]])
    lu = depth_second(*lu)
    grad_upper, *parts = global_ff_back(line, grad_rows, slope, g_up, g_down)
    near_term, far_term = hop_core(parts[1]), hop_core(parts[3])
    gd_near, gd_far = global_outer(line, grad_rows, active)
    gd_far = hop_y(gd_far)
    to_x = hop_x(add_rows(line, [parts[2], far_term]))
    ld = depth_second(*ld)
    gu_near, gu_far = global_outer(line, normed_b, grad_upper)
    gu_far = hop_y(gu_far)
    found = update(1, 1, lu, None)
    grad_middle, small, gain_b = merge_back(
        line, middle, (parts[0], near_term, to_x), grad_global, gains_here, 1
    )
    small_x = hop_x(small)
    h2 = hop_x(add_rows(line, [h2_near, h2_far]))
    found = update(1, 2, ld, found)
    (small_x,) = in_turn(line, small_x)
    grad_attn = [small, hop_core(small), small_x, hop_core(small_x)]
    grad_qkv, *parts = global_heads_back(line, info, grad_attn, g_heads, qkv, mixed, lse)
    near_term, far_term = hop_core(parts[1]), hop_core(parts[3])
    gh_near, gh_far = global_grads_heads(line, info, normed_a, grad_attn, grad_qkv, mixed)
    gh_far = hop_y(gh_far)
    to_x = hop_x(add_rows(line, [parts[2], far_term]))
    gd = depth_first([gd_near, gd_far])
    lh = depth_first([h0_near, h0_far, h2])
    input_grad, gain_grads = finish(
        line, source, rows_in, (parts[0], near_term, to_x), grad_middle, gains_here, (gain_b, gain_c, gain_d)
    )
    gain_grads = total_everywhere(gain_grads)
    gd = depth_second(*gd)
    lh = depth_second(*lh)
    gu = depth_first([gu_near, gu_far])
    found = update(0, 2, gd, found)
    found = update(1, 0, lh, found)
    gu = depth_second(*gu)
    gh = depth_first([gh_near, gh_far])
    found = update(0, 1, gu, found)
    gh = depth_second(*gh)
    found = update(0, 0, gh, found)
    weight_grads, new_master, new_first, new_second, new_ema = found
    new_gain_first = beta_first * gain_first + (1.0 - beta_first) * gain_grads
    new_gain_second = beta_second * gain_second + (1.0 - beta_second) * gain_grads * gain_grads
    new_gains = gains - gain_rate * new_gain_first / (jnp.sqrt(new_gain_second) + adam_eps)
    return (
        local_out,
        input_grad,
        weight_grads,
        gain_grads,
        new_master,
        new_first,
        new_second,
        new_ema,
        new_gains,
        new_gain_first,
        new_gain_second,
    )


def solution(mesh):
    fits = mesh.shape["dp"] == 8 and mesh.shape["tensor"] == 4
    return jax.shard_map(
        shards_grid if fits else shards_any,
        mesh=mesh,
        in_specs=(
            P(("dp", "tensor"), None),
            P(("dp", "tensor"), None, None),
            P(("dp", "tensor"), None, None),
            P("dp"),
            P(),
            P(None, "dp", "tensor"),
            P(None, "dp", "tensor"),
            P(None, "dp", "tensor"),
            P(None, "dp", "tensor"),
            P(None, "dp", "tensor"),
            P(None, "dp", None, "tensor"),
            P(),
            P(),
            P(),
        ),
        out_specs=(
            P(("dp", "tensor"), None, None),
            P(("dp", "tensor"), None),
            P(None, "dp", "tensor"),
            P(),
            P(None, "dp", "tensor"),
            P(None, "dp", "tensor"),
            P(None, "dp", "tensor"),
            P(None, "dp", "tensor"),
            P(),
            P(),
            P(),
        ),
        check_vma=False,
    )
```

```python
import math

import jax
import jax.numpy as jnp
from jax import lax
from jax.experimental import pallas as pl
from jax.experimental.pallas import tpu as pltpu
from jax.sharding import PartitionSpec as P

D = 1024
HD = 64
FF = 4096
CB = 3
LMAX = 1024


norm_eps = 1e-06
beta_first = 0.5
beta_second = 0.5
adam_eps = 1e-08
step_rate = 0.05
gain_rate = 0.4
ema_decay = 0.9
masked_fill = -1e30
highest = lax.Precision.HIGHEST


def dot_rows(left, right):
    return jnp.dot(left, right, preferred_element_type=jnp.float32)


def dot_transposed(left, right):
    return lax.dot_general(
        left, right, (((1,), (1,)), ((), ())), preferred_element_type=jnp.float32
    )


def dot_over_rows(left, right):
    return lax.dot_general(
        left, right, (((0,), (0,)), ((), ())), preferred_element_type=jnp.float32
    )


def keep_rows(values):
    return values


def row_term(operand, weight):
    return dot_transposed(operand, weight)


def rms_forward(rows_in, gain):
    return (
        rows_in * lax.rsqrt(jnp.mean(rows_in * rows_in, axis=-1, keepdims=True) + norm_eps) * gain
    )


def rms_backward(rows_in, gain, grad_out):
    width = rows_in.shape[-1]
    scale_rows = lax.rsqrt(jnp.mean(rows_in * rows_in, axis=-1, keepdims=True) + norm_eps)
    scaled_grad = grad_out * gain
    inner_total = jnp.sum(scaled_grad * rows_in, axis=-1, keepdims=True)
    grad_in = (
        scale_rows * scaled_grad
        - rows_in * (scale_rows * scale_rows * scale_rows) * inner_total / width
    )
    gain_grad = jnp.sum(grad_out * rows_in * scale_rows, axis=0)
    return (grad_in, gain_grad)


def gelu_slope(upper):
    normal_cdf = 0.5 * (1.0 + lax.erf(upper * (1.0 / math.sqrt(2.0))))
    density = jnp.exp(-0.5 * upper * upper) * (1.0 / math.sqrt(2.0 * math.pi))
    return normal_cdf + upper * density


def split_layer(layer_cols, groups, head_cols, ff_cols):
    width = layer_cols.shape[0]
    grouped = layer_cols.reshape(width, groups, -1)

    def columns(begin, extent):
        return grouped[:, :, begin : begin + extent].reshape(width, groups * extent)

    w_qkv = jnp.concatenate(
        [columns(0, head_cols), columns(head_cols, head_cols), columns(2 * head_cols, head_cols)],
        axis=1,
    )
    return (
        w_qkv,
        columns(3 * head_cols, head_cols),
        columns(4 * head_cols, ff_cols),
        columns(4 * head_cols + ff_cols, ff_cols),
    )


def join_layer(grad_parts, groups):
    grad_qkv, grad_out, grad_up, grad_down = grad_parts
    width = grad_qkv.shape[0]
    head_width = grad_qkv.shape[1] // 3
    pieces = [
        grad_qkv[:, 0:head_width],
        grad_qkv[:, head_width : 2 * head_width],
        grad_qkv[:, 2 * head_width :],
        grad_out,
        grad_up,
        grad_down,
    ]
    return jnp.concatenate([piece.reshape(width, groups, -1) for piece in pieces], axis=2).reshape(
        width, -1
    )


def global_scores(queries, key_rows, length):
    span = queries.shape[0]
    heads = queries.shape[1] // HD
    scores = jnp.einsum(
        "qhd,khd->hqk",
        queries.reshape(span, heads, HD),
        key_rows.reshape(span, heads, HD),
        preferred_element_type=jnp.float32,
    ) * HD ** (-0.5)
    rows_at = lax.broadcasted_iota(jnp.int32, (span, span), 0)
    cols_at = lax.broadcasted_iota(jnp.int32, (span, span), 1)
    allowed = (cols_at <= rows_at) & (cols_at < length)
    return jnp.where(allowed[None], scores, masked_fill)


def global_attend(queries, key_rows, value_rows, lengths):
    items = lengths.shape[0]
    span = queries.shape[0] // items
    heads = queries.shape[1] // HD

    def one_item(packed):
        item_query, item_key, item_value, length = packed
        scores = global_scores(item_query, item_key, length)
        row_max = jnp.max(scores, axis=-1, keepdims=True)
        expanded = jnp.exp(scores - row_max)
        row_total = jnp.sum(expanded, axis=-1, keepdims=True)
        probability = (expanded / row_total).astype(jnp.bfloat16)
        mixed = jnp.einsum(
            "hqk,khd->qhd",
            probability,
            item_value.reshape(span, heads, HD),
            preferred_element_type=jnp.float32,
        )
        return (
            mixed.reshape(span, -1).astype(jnp.bfloat16),
            (row_max + jnp.log(row_total))[..., 0],
        )

    mixed, log_total = lax.map(
        one_item,
        (
            queries.reshape(items, span, -1),
            key_rows.reshape(items, span, -1),
            value_rows.reshape(items, span, -1),
            lengths,
        ),
    )
    return (mixed.reshape(items * span, -1), log_total)


def global_attend_back(queries, key_rows, value_rows, lengths, log_total, grad_mixed):
    items = lengths.shape[0]
    span = queries.shape[0] // items
    heads = queries.shape[1] // HD
    scale_score = HD ** (-0.5)

    def one_item(packed):
        item_query, item_key, item_value, length, item_lse, item_grad = packed
        scores = global_scores(item_query, item_key, length)
        probability = jnp.exp(scores - item_lse[..., None])
        grad_heads = item_grad.reshape(span, heads, HD)
        query_heads = item_query.reshape(span, heads, HD)
        key_heads = item_key.reshape(span, heads, HD)
        value_heads = item_value.reshape(span, heads, HD)
        grad_value = jnp.einsum(
            "hqk,qhd->khd",
            probability.astype(jnp.bfloat16),
            grad_heads,
            preferred_element_type=jnp.float32,
        )
        grad_prob = jnp.einsum(
            "qhd,khd->hqk", grad_heads, value_heads, preferred_element_type=jnp.float32
        )
        center = jnp.sum(probability * grad_prob, axis=-1, keepdims=True)
        grad_scores = (probability * (grad_prob - center)).astype(jnp.bfloat16)
        grad_query = (
            jnp.einsum("hqk,khd->qhd", grad_scores, key_heads, preferred_element_type=jnp.float32)
            * scale_score
        )
        grad_key = (
            jnp.einsum("hqk,qhd->khd", grad_scores, query_heads, preferred_element_type=jnp.float32)
            * scale_score
        )
        return jnp.concatenate(
            [
                grad_query.reshape(span, -1),
                grad_key.reshape(span, -1),
                grad_value.reshape(span, -1),
            ],
            axis=1,
        ).astype(jnp.bfloat16)

    grads = lax.map(
        one_item,
        (
            queries.reshape(items, span, -1),
            key_rows.reshape(items, span, -1),
            value_rows.reshape(items, span, -1),
            lengths,
            log_total,
            grad_mixed.reshape(items, span, -1),
        ),
    )
    return grads.reshape(items * span, -1)


def local_probability(queries, key_rows):
    frame_count = queries.shape[0] // CB
    heads = queries.shape[1] // HD
    scores = jnp.einsum(
        "fqhd,fkhd->fhqk",
        queries.reshape(frame_count, CB, heads, HD),
        key_rows.reshape(frame_count, CB, heads, HD),
        preferred_element_type=jnp.float32,
    ) * HD ** (-0.5)
    rows_at = lax.broadcasted_iota(jnp.int32, (CB, CB), 0)
    cols_at = lax.broadcasted_iota(jnp.int32, (CB, CB), 1)
    scores = jnp.where(cols_at <= rows_at, scores, masked_fill)
    row_max = jnp.max(scores, axis=-1, keepdims=True)
    expanded = jnp.exp(scores - row_max)
    return expanded / jnp.sum(expanded, axis=-1, keepdims=True)


def local_attend(queries, key_rows, value_rows):
    frame_count = queries.shape[0] // CB
    heads = queries.shape[1] // HD
    probability = local_probability(queries, key_rows).astype(jnp.bfloat16)
    mixed = jnp.einsum(
        "fhqk,fkhd->fqhd",
        probability,
        value_rows.reshape(frame_count, CB, heads, HD),
        preferred_element_type=jnp.float32,
    )
    return (mixed.reshape(queries.shape[0], -1).astype(jnp.bfloat16), jnp.zeros((), jnp.float32))


def local_attend_back(queries, key_rows, value_rows, saved, grad_mixed):
    frame_count = queries.shape[0] // CB
    heads = queries.shape[1] // HD
    scale_score = HD ** (-0.5)
    probability = local_probability(queries, key_rows)
    grad_heads = grad_mixed.reshape(frame_count, CB, heads, HD)
    query_heads = queries.reshape(frame_count, CB, heads, HD)
    key_heads = key_rows.reshape(frame_count, CB, heads, HD)
    value_heads = value_rows.reshape(frame_count, CB, heads, HD)
    grad_value = jnp.einsum(
        "fhqk,fqhd->fkhd",
        probability.astype(jnp.bfloat16),
        grad_heads,
        preferred_element_type=jnp.float32,
    )
    grad_prob = jnp.einsum(
        "fqhd,fkhd->fhqk", grad_heads, value_heads, preferred_element_type=jnp.float32
    )
    center = jnp.sum(probability * grad_prob, axis=-1, keepdims=True)
    grad_scores = (probability * (grad_prob - center)).astype(jnp.bfloat16)
    grad_query = (
        jnp.einsum("fhqk,fkhd->fqhd", grad_scores, key_heads, preferred_element_type=jnp.float32)
        * scale_score
    )
    grad_key = (
        jnp.einsum("fhqk,fqhd->fkhd", grad_scores, query_heads, preferred_element_type=jnp.float32)
        * scale_score
    )
    total_rows = queries.shape[0]
    return jnp.concatenate(
        [
            grad_query.reshape(total_rows, -1),
            grad_key.reshape(total_rows, -1),
            grad_value.reshape(total_rows, -1),
        ],
        axis=1,
    ).astype(jnp.bfloat16)


def block_forward(rows_in, matrices, gain_a, gain_b, path, attend):
    gather_rows, sum_rows = (path[0], path[1])
    w_qkv, w_out, w_up, w_down = matrices
    normed_a = gather_rows(rms_forward(rows_in, gain_a).astype(jnp.bfloat16))
    projected = dot_rows(normed_a, w_qkv).astype(jnp.bfloat16)
    head_width = projected.shape[1] // 3
    mixed, saved = attend(
        projected[:, :head_width],
        projected[:, head_width : 2 * head_width],
        projected[:, 2 * head_width :],
    )
    middle = rows_in + sum_rows(mixed, w_out)
    normed_b = gather_rows(rms_forward(middle, gain_b).astype(jnp.bfloat16))
    upper = dot_rows(normed_b, w_up)
    active = jax.nn.gelu(upper, approximate=False).astype(jnp.bfloat16)
    result = middle + sum_rows(active, w_down)
    return (result, (rows_in, normed_a, projected, mixed, saved, middle, normed_b, upper, active))


def block_backward(grad_result, kept, matrices, gain_a, gain_b, path, attend_back):
    gather_grads, sum_back = (path[2], path[3])
    rows_in, normed_a, projected, mixed, saved, middle, normed_b, upper, active = kept
    w_qkv, w_out, w_up, w_down = matrices
    grad_branch = gather_grads(grad_result.astype(jnp.bfloat16))
    grad_down = dot_over_rows(grad_branch, active)
    grad_active = dot_rows(grad_branch, w_down)
    grad_upper = (grad_active * gelu_slope(upper)).astype(jnp.bfloat16)
    grad_up = dot_over_rows(normed_b, grad_upper)
    grad_normed_b = sum_back(grad_upper, w_up)
    grad_middle_part, gain_b_grad = rms_backward(middle, gain_b, grad_normed_b)
    grad_middle = grad_result + grad_middle_part
    grad_attn = gather_grads(grad_middle.astype(jnp.bfloat16))
    grad_out = dot_over_rows(grad_attn, mixed)
    grad_mixed = dot_rows(grad_attn, w_out).astype(jnp.bfloat16)
    head_width = projected.shape[1] // 3
    grad_qkv = attend_back(
        projected[:, :head_width],
        projected[:, head_width : 2 * head_width],
        projected[:, 2 * head_width :],
        saved,
        grad_mixed,
    )
    grad_weight_qkv = dot_over_rows(normed_a, grad_qkv)
    grad_normed_a = sum_back(grad_qkv, w_qkv)
    grad_rows_part, gain_a_grad = rms_backward(rows_in, gain_a, grad_normed_a)
    return (
        grad_middle + grad_rows_part,
        (grad_weight_qkv, grad_out, grad_up, grad_down),
        gain_a_grad,
        gain_b_grad,
    )


def shards_any(
    frames_in,
    code_emb,
    cotangent,
    lengths,
    owner_list,
    master,
    first_moment,
    second_moment,
    ema,
    left_basis,
    right_basis,
    gains,
    gain_first,
    gain_second,
):
    tensor_count = lax.axis_size("tensor")
    group_count = lax.axis_size("dp")
    head_cols = D // tensor_count
    ff_cols = FF // tensor_count
    share = frames_in.shape[0]
    owned_rows = master.shape[1]
    gathered = lax.all_gather(master.astype(jnp.bfloat16), "dp", axis=1, tiled=True)
    layers = jnp.take(gathered.reshape(2, group_count, owned_rows, -1), owner_list, axis=1).reshape(
        2, group_count * owned_rows, -1
    )

    def gather_rows(values):
        return lax.all_gather(values, "tensor", axis=0, tiled=True)

    def gather_grads(values):
        return lax.all_gather(values, "tensor", axis=0, tiled=True)

    def sum_rows(operand, weight):
        return lax.psum_scatter(
            row_term(operand, weight).astype(jnp.bfloat16),
            "tensor",
            scatter_dimension=0,
            tiled=True,
        ).astype(jnp.float32)

    def sum_back(operand, weight):
        return lax.psum_scatter(
            row_term(operand, weight).astype(jnp.bfloat16),
            "tensor",
            scatter_dimension=0,
            tiled=True,
        ).astype(jnp.float32)

    heads_path = (gather_rows, sum_rows, gather_grads, sum_back)
    rows_path = (keep_rows, dot_transposed, keep_rows, dot_transposed)

    def attend_global(queries, key_rows, value_rows):
        return global_attend(queries, key_rows, value_rows, lengths)

    def attend_global_back(queries, key_rows, value_rows, saved, grad_mixed):
        return global_attend_back(queries, key_rows, value_rows, lengths, saved, grad_mixed)

    global_matrices = split_layer(layers[0], 1, head_cols, ff_cols)
    global_out, global_kept = block_forward(
        frames_in.astype(jnp.float32),
        global_matrices,
        gains[0],
        gains[1],
        heads_path,
        attend_global,
    )
    local_in = (global_out[:, None, :] + code_emb.astype(jnp.float32)).reshape(share * CB, -1)
    local_layer = lax.all_gather(layers[1], "tensor", axis=1, tiled=True)
    local_matrices = split_layer(local_layer, tensor_count, head_cols, ff_cols)
    local_result, local_kept = block_forward(
        local_in, local_matrices, gains[2], gains[3], rows_path, local_attend
    )
    local_out = local_result.reshape(share, CB, -1).astype(jnp.bfloat16)
    frame_at = lax.axis_index("tensor") * share + jnp.arange(share, dtype=jnp.int32)
    item_at = frame_at // LMAX
    item_slots = jnp.arange(lengths.shape[0], dtype=jnp.int32)
    item_length = jnp.sum(
        jnp.where(item_at[:, None] == item_slots[None, :], lengths[None, :], 0), axis=1
    )
    valid = (frame_at % LMAX < item_length).astype(jnp.float32)
    grad_local = (cotangent.astype(jnp.float32) * valid[:, None, None]).reshape(share * CB, -1)
    grad_local_in, local_weight_grads, gain_c_grad, gain_d_grad = block_backward(
        grad_local, local_kept, local_matrices, gains[2], gains[3], rows_path, local_attend_back
    )
    grad_global_out = jnp.sum(grad_local_in.reshape(share, CB, -1), axis=1)
    input_grad, global_weight_grads, gain_a_grad, gain_b_grad = block_backward(
        grad_global_out,
        global_kept,
        global_matrices,
        gains[0],
        gains[1],
        heads_path,
        attend_global_back,
    )
    local_grads = join_layer(local_weight_grads, tensor_count)
    local_grads = lax.psum_scatter(
        local_grads.astype(jnp.bfloat16), "tensor", scatter_dimension=1, tiled=True
    ).astype(jnp.float32)
    layer_grads = jnp.stack([join_layer(global_weight_grads, 1), local_grads])
    slots = jnp.arange(group_count, dtype=jnp.int32)
    inverse = jnp.sum(jnp.where(owner_list[None, :] == slots[:, None], slots[None, :], 0), axis=1)
    ordered = jnp.take(
        layer_grads.reshape(2, group_count, owned_rows, -1), inverse, axis=1
    ).reshape(2, group_count * owned_rows, -1)
    weight_grads = lax.psum_scatter(
        ordered.astype(jnp.bfloat16), "dp", scatter_dimension=1, tiled=True
    ).astype(jnp.float32)
    gain_grads = lax.psum(
        jnp.stack([gain_a_grad, gain_b_grad, gain_c_grad, gain_d_grad]), ("dp", "tensor")
    )
    tile_count = right_basis.shape[1]
    turned_left = jnp.einsum("lab,lac->lbc", left_basis, weight_grads, precision=highest)
    rotated = jnp.einsum(
        "lbkc,lkce->lbke",
        turned_left.reshape(2, owned_rows, tile_count, -1),
        right_basis,
        precision=highest,
    ).reshape(weight_grads.shape)
    new_first = beta_first * first_moment + (1.0 - beta_first) * rotated
    new_second = beta_second * second_moment + (1.0 - beta_second) * rotated * rotated
    turned = new_first / (jnp.sqrt(new_second) + adam_eps)
    back_right = jnp.einsum(
        "lbke,lkce->lbkc",
        turned.reshape(2, owned_rows, tile_count, -1),
        right_basis,
        precision=highest,
    )
    back_full = jnp.einsum(
        "lab,lbc->lac", left_basis, back_right.reshape(weight_grads.shape), precision=highest
    )
    new_master = master - step_rate * back_full
    new_ema = ema_decay * ema + (1.0 - ema_decay) * new_master
    new_gain_first = beta_first * gain_first + (1.0 - beta_first) * gain_grads
    new_gain_second = beta_second * gain_second + (1.0 - beta_second) * gain_grads * gain_grads
    new_gains = gains - gain_rate * new_gain_first / (jnp.sqrt(new_gain_second) + adam_eps)
    return (
        local_out,
        input_grad,
        weight_grads,
        gain_grads,
        new_master,
        new_first,
        new_second,
        new_ema,
        new_gains,
        new_gain_first,
        new_gain_second,
    )


MIB = 1024 * 1024
VMEM_WHOLE = pl.BlockSpec(memory_space=pltpu.VMEM)
IN_SMEM = pl.BlockSpec(memory_space=pltpu.SMEM)
IN_HBM = pl.BlockSpec(memory_space=pl.ANY)


def shaped(shape, kind):
    return jax.ShapeDtypeStruct(shape, kind)


def cost(flops, moved, exps=0):
    return pl.CostEstimate(flops=int(flops), bytes_accessed=int(moved), transcendentals=int(exps))


weight_of = {
    "global_heads": 13,
    "global_ff": 12,
    "local_heads": 18,
    "local_ff": 34,
    "local_back": 90,
    "global_ff_back": 9,
    "global_ff_grads": 5,
    "global_heads_back": 12,
    "global_heads_grads": 5,
    "adam_update": 5,
}


def group_at(rel):
    mine = lax.axis_index("tensor")
    return 2 * ((mine // 2 + rel // 2) % 2) + (mine % 2 + rel % 2) % 2


def partner_of(hop):
    dp, tensor = lax.axis_index("dp"), lax.axis_index("tensor")
    if hop == "core":
        return {"tensor": tensor + 1 - 2 * (tensor % 2)}
    if hop == "x":
        return {"tensor": (tensor + 2) % 4}
    if hop == "y":
        return {"dp": dp + 1 - 2 * (dp % 2)}
    if hop == "z1":
        return {"dp": dp + 2 - 4 * ((dp // 2) % 2)}
    return {"dp": (dp + 4) % 8}


def greet(hops):
    barrier = pltpu.get_barrier_semaphore()
    for hop in hops:
        pl.semaphore_signal(
            barrier, inc=1, device_id=partner_of(hop), device_id_type=pl.DeviceIdType.MESH
        )
    pl.semaphore_wait(barrier, len(hops))


def to_partner(hop, source, target, send, recv):
    return pltpu.make_async_remote_copy(
        src_ref=source,
        dst_ref=target,
        send_sem=send,
        recv_sem=recv,
        device_id=partner_of(hop),
        device_id_type=pl.DeviceIdType.MESH,
    )


def part(array, begin, rows):
    return (array, begin, rows)


class Line:
    def __init__(self):
        self.token = None
        self.moves = ()
        self.arrived = []
        self.calls = 0

    def carry(self, *moves):
        self.moves = moves

    def run(self, body, args, in_specs, out_specs, out_shape, aliases=None, scratch_shapes=(), limit=32, hops=(), **rest):
        moves, self.moves = self.moves, ()
        sources, copies, landed = [], [], []
        for hop, *pieces in moves:
            offset = 0
            for piece in pieces:
                array, begin, rows = piece if isinstance(piece, tuple) else (piece, 0, piece.shape[0])
                which = next((at for at, one in enumerate(sources) if one is array), len(sources))
                if which == len(sources):
                    sources.append(array)
                copies.append((hop, which, begin, rows, len(landed), offset))
                offset += rows
            landed.append(shaped((offset,) + array.shape[1:], array.dtype))
        reach = list(hops) or list(dict.fromkeys(move[0] for move in moves))
        lead = 0 if self.token is None else 1
        inputs = lead + len(args)
        first_out = inputs + len(sources)
        outputs = len(out_shape)
        first_scratch = first_out + outputs + len(landed) + 1
        steps = rest.get("grid", (1,))[0]

        def inner(*refs):
            scratch = refs[first_scratch:]
            pending = []
            if copies:
                *scratch, send, recv = scratch
                for at, (hop, which, begin, rows, where, offset) in enumerate(copies):
                    pending.append(
                        to_partner(
                            hop,
                            refs[inputs + which].at[pl.ds(begin, rows)],
                            refs[first_out + outputs + where].at[pl.ds(offset, rows)],
                            send.at[at],
                            recv.at[at],
                        )
                    )

            def begin_all():
                greet(reach)
                for one in pending:
                    one.start()

            def end_all():
                for one in pending:
                    one.wait()

            at_ends = (lambda step, act: pl.when(pl.program_id(0) == step)(act)) if steps > 1 else (
                lambda step, act: act()
            )
            if pending:
                at_ends(0, begin_all)
            body(*refs[lead:inputs], *refs[first_out : first_out + outputs], *scratch)
            if pending:
                at_ends(steps - 1, end_all)

        extra = {}
        if reach:
            extra = {"collective_id": self.calls, "has_side_effects": True}
            self.calls += 1
        found = pl.pallas_call(
            inner,
            in_specs=[IN_HBM] * lead + list(in_specs) + [IN_HBM] * len(sources),
            out_specs=list(out_specs) + [IN_HBM] * (len(landed) + 1),
            out_shape=list(out_shape) + landed + [shaped((8, 128), jnp.float32)],
            scratch_shapes=list(scratch_shapes)
            + ([pltpu.SemaphoreType.DMA((len(copies),))] * 2 if copies else []),
            input_output_aliases={lead + at: to for at, to in (aliases or {}).items()},
            cost_estimate=cost(weight_of.get(rest["name"], 1.0) * 0.2e9, 1000),
            compiler_params=pltpu.CompilerParams(vmem_limit_bytes=limit * MIB, **extra),
            **rest,
        )(*([self.token] * lead), *args, *sources)
        self.token = found[-1]
        self.arrived = list(found[outputs:-1])
        return list(found[:outputs])


def lanes_of(source_ref, at, width):
    return pl.ds(pl.multiple_of(source_ref[at] * width, width), width)


def norm_rows(rows, gain):
    scale = lax.rsqrt(jnp.mean(rows * rows, axis=-1, keepdims=True) + norm_eps)
    return rows * scale * gain


def norm_rows_back(rows, gain, grad):
    scale = lax.rsqrt(jnp.mean(rows * rows, axis=-1, keepdims=True) + norm_eps)
    scaled = grad * gain
    inner = jnp.sum(scaled * rows, axis=-1, keepdims=True)
    grad_in = scale * scaled - rows * (scale * scale * scale) * inner / rows.shape[-1]
    return grad_in, jnp.sum(grad * rows * scale, axis=0, keepdims=True)


def gelu_both(upper):
    size = jnp.abs(upper)
    base = 1.0 + (0.3275911 / math.sqrt(2.0)) * size
    guess = pl.reciprocal(base, approx=True)
    ratio = guess * (2.0 - base * guess)
    bell = jnp.exp(-0.5 * upper * upper)
    series = ratio * (
        0.5 * 0.254829592
        + ratio
        * (
            -0.5 * 0.284496736
            + ratio * (0.5 * 1.421413741 + ratio * (-0.5 * 1.453152027 + ratio * (0.5 * 1.061405429)))
        )
    )
    tail = series * bell
    cdf = jnp.where(upper >= 0.0, 1.0 - tail, tail)
    density = bell * (1.0 / math.sqrt(2.0 * math.pi))
    return (upper * cdf).astype(jnp.bfloat16), (cdf + upper * density).astype(jnp.bfloat16)


def both(rows, near, far):
    depth = near.shape[0]
    return dot_rows(rows[:, :depth], near) + dot_rows(rows[:, depth:], far)


def prep_body(source_ref, frames_ref, gains_ref, rows_ref, gains_out_ref, normed_ref):
    owned = frames_ref.shape[1] // source_ref.shape[0]
    for at in range(source_ref.shape[0]):
        here = slice(at * owned, (at + 1) * owned)
        rows_ref[:, here] = frames_ref[:, lanes_of(source_ref, at, owned)]
        gains_out_ref[:, here] = gains_ref[:, lanes_of(source_ref, at, owned)]
    normed_ref[...] = norm_rows(rows_ref[...].astype(jnp.float32), gains_out_ref[0:1, :]).astype(
        jnp.bfloat16
    )


def prep(line, source, frames, gains):
    return line.run(
        prep_body,
        (source, frames, gains,),
        in_specs=[IN_SMEM, VMEM_WHOLE, VMEM_WHOLE],
        out_specs=[VMEM_WHOLE] * 3,
        out_shape=[
            shaped(frames.shape, jnp.bfloat16),
            shaped(gains.shape, jnp.float32),
            shaped(frames.shape, jnp.bfloat16),
        ],
        limit=(16),
        name="prep_rows",
    )


def merge_body(which, base_ref, one_ref, two_ref, three_ref, gains_ref, middle_ref, normed_ref=None):
    total = base_ref[...].astype(jnp.float32)
    for ref in (one_ref, two_ref, three_ref):
        total = total + ref[...].astype(jnp.float32)
    middle_ref[...] = total
    if normed_ref is not None:
        normed_ref[...] = norm_rows(total, gains_ref[which : which + 1, :]).astype(jnp.bfloat16)


def merge(line, base, terms, gains, which, normed=True):
    outs = [shaped(base.shape, jnp.float32)]
    if normed:
        outs.append(shaped(base.shape, jnp.bfloat16))
    return line.run(
        lambda *refs: merge_body(which, *refs),
        (base, *terms, gains,),
        in_specs=[VMEM_WHOLE] * 5,
        out_specs=[VMEM_WHOLE] * len(outs),
        out_shape=outs,
        limit=(16),
        name="merge_rows",
    )


def merge_back_body(
    which, rows_ref, one_ref, two_ref, three_ref, grad_ref, gains_ref, total_ref, small_ref, gain_ref
):
    grad = one_ref[...].astype(jnp.float32)
    for ref in (two_ref, three_ref):
        grad = grad + ref[...].astype(jnp.float32)
    part, gain_grad = norm_rows_back(
        rows_ref[...].astype(jnp.float32), gains_ref[which : which + 1, :], grad
    )
    total = grad_ref[...] + part
    total_ref[...] = total
    small_ref[...] = total.astype(jnp.bfloat16)
    gain_ref[...] = gain_grad


def merge_back(line, rows, terms, grad, gains, which):
    return line.run(
        lambda *refs: merge_back_body(which, *refs),
        (rows, *terms, grad, gains,),
        in_specs=[VMEM_WHOLE] * 6,
        out_specs=[VMEM_WHOLE] * 3,
        out_shape=[
            shaped(rows.shape, jnp.float32),
            shaped(rows.shape, jnp.bfloat16),
            shaped((1, rows.shape[1]), jnp.float32),
        ],
        limit=(16),
        name="merge_rows_back",
    )


def finish_body(
    source_ref, rows_ref, one_ref, two_ref, three_ref, grad_ref, gains_ref, gb_ref, gc_ref, gd_ref,
    out_ref, gain_ref,
):
    grad = one_ref[...].astype(jnp.float32)
    for ref in (two_ref, three_ref):
        grad = grad + ref[...].astype(jnp.float32)
    part, gain_grad = norm_rows_back(rows_ref[...].astype(jnp.float32), gains_ref[0:1, :], grad)
    total = grad_ref[...] + part
    owned = out_ref.shape[1] // source_ref.shape[0]
    for at in range(source_ref.shape[0]):
        here = slice(at * owned, (at + 1) * owned)
        there = lanes_of(source_ref, at, owned)
        out_ref[:, there] = total[:, here]
        gain_ref[0:1, there] = gain_grad[:, here]
        gain_ref[1:2, there] = gb_ref[:, here]
        gain_ref[2:3, there] = gc_ref[:, here]
        gain_ref[3:4, there] = gd_ref[:, here]


def finish(line, source, rows, terms, grad, gains, others):
    return line.run(
        finish_body,
        (source, rows, *terms, grad, gains, *others,),
        in_specs=[IN_SMEM] + [VMEM_WHOLE] * 9,
        out_specs=[VMEM_WHOLE] * 2,
        out_shape=[shaped(rows.shape, jnp.float32), shaped((4, rows.shape[1]), jnp.float32)],
        limit=(16),
        name="input_grad",
    )


def global_heads_body(
    info_ref, x0, x1, x2, x3, near_ref, far_ref, qkv_ref, mixed_ref, lse_ref, p0, p1, p2, p3, acc, lse_wide
):
    share = x0.shape[0]
    span = 4 * share
    width = mixed_ref.shape[1]
    length = info_ref[1]
    scale = HD ** (-0.5)
    for rel, x_ref in enumerate((x0, x1, x2, x3)):
        at = pl.ds(pl.multiple_of(group_at(rel) * share, share), share)
        full = both(x_ref[...], near_ref[:, : 3 * width], far_ref[:, : 3 * width])
        qkv_ref[at, :] = full.astype(jnp.bfloat16)
    acc[...] = jnp.zeros_like(acc)
    lse_wide[...] = jnp.zeros_like(lse_wide)
    head_of = lax.broadcasted_iota(jnp.int32, (1, width), 1) // HD
    lane = lax.broadcasted_iota(jnp.int32, (1, 128), 1)

    @pl.loop(0, width // HD)
    def per_head(head):
        own = head_of == head
        for block in range(4):
            rows = slice(block * share, (block + 1) * share)
            reach = (block + 1) * share
            query = jnp.where(own, qkv_ref[rows, :width] * scale, 0.0).astype(jnp.bfloat16)
            scores = dot_transposed(query, qkv_ref[:reach, width : 2 * width])
            row_at = block * share + lax.broadcasted_iota(jnp.int32, scores.shape, 0)
            col_at = lax.broadcasted_iota(jnp.int32, scores.shape, 1)
            scores = jnp.where((col_at <= row_at) & (col_at < length), scores, masked_fill)
            top = jnp.max(scores, axis=-1, keepdims=True)
            expanded = jnp.exp(scores - top)
            total = jnp.sum(expanded, axis=-1, keepdims=True)
            prob = (expanded * (1.0 / total)).astype(jnp.bfloat16)
            value = jnp.where(own, qkv_ref[:reach, 2 * width :], 0.0).astype(jnp.bfloat16)
            acc[rows, :] += dot_rows(prob, value)
            lse_wide[rows, :] = jnp.where(lane == head, top + jnp.log(total), lse_wide[rows, :])

    mixed_ref[...] = acc[...].astype(jnp.bfloat16)
    lse_ref[...] = jnp.transpose(lse_wide[...])[: lse_ref.shape[0], :]
    half = near_ref.shape[0]
    for rel, p_ref in enumerate((p0, p1, p2, p3)):
        at = pl.ds(pl.multiple_of(group_at(rel) * share, share), share)
        rows = mixed_ref[at, :]
        p_ref[:, :half] = dot_transposed(rows, near_ref[:, 3 * width :]).astype(jnp.bfloat16)
        p_ref[:, half:] = dot_transposed(rows, far_ref[:, 3 * width :]).astype(jnp.bfloat16)


def global_heads(line, info, rows, halves):
    share, width = rows[0].shape[0], halves[0].shape[1] // 4
    span = 4 * share
    return line.run(
        global_heads_body,
        (info, *rows, *halves,),
        in_specs=[IN_SMEM] + [VMEM_WHOLE] * 6,
        out_specs=[VMEM_WHOLE] * 7,
        out_shape=[
            shaped((span, 3 * width), jnp.bfloat16),
            shaped((span, width), jnp.bfloat16),
            shaped((8, span), jnp.float32),
        ]
        + [shaped((share, D), jnp.bfloat16)] * 4,
        scratch_shapes=[pltpu.VMEM((span, width), jnp.float32), pltpu.VMEM((span, 128), jnp.float32)],
        limit=(40),
        name="global_heads",
    )


def global_heads_back_body(
    info_ref, g0, g1, g2, g3, near_ref, far_ref, qkv_ref, mixed_ref, lse_ref, dqkv_ref, p0, p1, p2, p3,
    dmix, dq_t, dk_acc, dv_acc, center, k_t,
):
    share = g0.shape[0]
    width = mixed_ref.shape[1]
    heads = width // HD
    length = info_ref[1]
    scale = HD ** (-0.5)
    for rel, g_ref in enumerate((g0, g1, g2, g3)):
        at = pl.ds(pl.multiple_of(group_at(rel) * share, share), share)
        full = both(g_ref[...], near_ref[:, 3 * width :], far_ref[:, 3 * width :])
        dmix[at, :] = full.astype(jnp.bfloat16)
    head_of = lax.broadcasted_iota(jnp.int32, (1, width), 1) // HD
    pick = (
        lax.broadcasted_iota(jnp.int32, (8, width), 1) // HD
        == lax.broadcasted_iota(jnp.int32, (8, width), 0)
    ).astype(jnp.bfloat16)
    product = dmix[...].astype(jnp.float32) * mixed_ref[...].astype(jnp.float32)
    high = product.astype(jnp.bfloat16)
    low = (product - high.astype(jnp.float32)).astype(jnp.bfloat16)
    center[...] = dot_transposed(pick, high) + dot_transposed(pick, low)
    k_t[...] = jnp.transpose(qkv_ref[:, width : 2 * width])
    dq_t[...] = jnp.zeros_like(dq_t)
    dk_acc[...] = jnp.zeros_like(dk_acc)
    dv_acc[...] = jnp.zeros_like(dv_acc)
    for head in range(heads):
        own = head_of == head
        for block in range(4):
            rows = slice(block * share, (block + 1) * share)
            reach = (block + 1) * share
            query = jnp.where(own, qkv_ref[rows, :width] * scale, 0.0).astype(jnp.bfloat16)
            grad = jnp.where(own, dmix[rows, :], 0.0).astype(jnp.bfloat16)
            scores = dot_transposed(qkv_ref[:reach, width : 2 * width], query)
            key_at = lax.broadcasted_iota(jnp.int32, scores.shape, 0)
            row_at = block * share + lax.broadcasted_iota(jnp.int32, scores.shape, 1)
            prob = jnp.where(
                (key_at <= row_at) & (key_at < length),
                jnp.exp(scores - lse_ref[head : head + 1, rows]),
                0.0,
            )
            dprob = dot_transposed(qkv_ref[:reach, 2 * width :], grad)
            dscore = (prob * (dprob - center[head : head + 1, rows])).astype(jnp.bfloat16)
            dv_acc[:reach, :] += dot_rows(prob.astype(jnp.bfloat16), grad)
            dk_acc[:reach, :] += dot_rows(dscore, query)
            lanes = slice(head * HD, (head + 1) * HD)
            dq_t[lanes, rows] += dot_rows(k_t[lanes, :reach], dscore)
    dqkv_ref[:, :width] = (jnp.transpose(dq_t[...]) * scale).astype(jnp.bfloat16)
    dqkv_ref[:, width : 2 * width] = dk_acc[...].astype(jnp.bfloat16)
    dqkv_ref[:, 2 * width :] = dv_acc[...].astype(jnp.bfloat16)
    half = near_ref.shape[0]
    for rel, p_ref in enumerate((p0, p1, p2, p3)):
        at = pl.ds(pl.multiple_of(group_at(rel) * share, share), share)
        rows = dqkv_ref[at, :]
        p_ref[:, :half] = dot_transposed(rows, near_ref[:, : 3 * width]).astype(jnp.bfloat16)
        p_ref[:, half:] = dot_transposed(rows, far_ref[:, : 3 * width]).astype(jnp.bfloat16)


def global_heads_back(line, info, grads, halves, qkv, mixed, lse):
    share, width = grads[0].shape[0], mixed.shape[1]
    span = 4 * share
    return line.run(
        global_heads_back_body,
        (info, *grads, *halves, qkv, mixed, lse,),
        in_specs=[IN_SMEM] + [VMEM_WHOLE] * 9,
        out_specs=[VMEM_WHOLE] * 5,
        out_shape=[shaped((span, 3 * width), jnp.bfloat16)]
        + [shaped((share, D), jnp.bfloat16)] * 4,
        scratch_shapes=[
            pltpu.VMEM((span, width), jnp.bfloat16),
            pltpu.VMEM((width, span), jnp.float32),
            pltpu.VMEM((span, width), jnp.float32),
            pltpu.VMEM((span, width), jnp.float32),
            pltpu.VMEM((8, span), jnp.float32),
            pltpu.VMEM((width, span), jnp.bfloat16),
        ],
        limit=(40),
        name="global_heads_back",
    )


def global_grads_heads_body(
    info_ref, a0, a1, a2, a3, g0, g1, g2, g3, dqkv_ref, mixed_ref, near_ref, far_ref, a_t, g_t
):
    share = a0.shape[0]
    width = mixed_ref.shape[1]
    for rel in range(4):
        at = pl.ds(pl.multiple_of(group_at(rel) * share, share), share)
        a_t[:, at] = jnp.transpose((a0, a1, a2, a3)[rel][...])
        g_t[:, at] = jnp.transpose((g0, g1, g2, g3)[rel][...])

    for at in range(D // 256):
        rows = slice(at * 256, (at + 1) * 256)
        out_ref, begin = (near_ref, 0) if at * 256 < D // 2 else (far_ref, D // 2)
        there = slice(at * 256 - begin, at * 256 - begin + 256)
        out_ref[there, : 3 * width] = dot_rows(a_t[rows, :], dqkv_ref[...]).astype(jnp.bfloat16)
        out_ref[there, 3 * width :] = dot_rows(g_t[rows, :], mixed_ref[...]).astype(jnp.bfloat16)


def global_grads_heads(line, info, normed, grads, dqkv, mixed):
    span, width = mixed.shape
    return line.run(
        global_grads_heads_body,
        (info, *normed, *grads, dqkv, mixed,),
        in_specs=[IN_SMEM] + [VMEM_WHOLE] * 10,
        out_specs=[VMEM_WHOLE] * 2,
        out_shape=[shaped((D // 2, 4 * width), jnp.bfloat16)] * 2,
        scratch_shapes=[pltpu.VMEM((D, span), jnp.bfloat16)] * 2,
        limit=(40),
        name="global_heads_grads",
    )


def global_ff_body(x0, x1, x2, x3, up0, up1, down0, down1, active_ref, slope_ref, p0, p1, p2, p3, acc):
    step = pl.program_id(0)
    share = x0.shape[0]
    half = up0.shape[0]

    @pl.when(step == 0)
    def _():
        acc[...] = jnp.zeros_like(acc)

    for rel, x_ref in enumerate((x0, x1, x2, x3)):
        rows = slice(rel * share, (rel + 1) * share)
        active, slope = gelu_both(both(x_ref[...], up0[...], up1[...]))
        active_ref[rows, :] = active
        slope_ref[rows, :] = slope
        for at, down in enumerate((down0, down1)):
            lanes = slice(at * half, (at + 1) * half)
            acc[rows, lanes] += dot_transposed(active, down[...])

    @pl.when(step == pl.num_programs(0) - 1)
    def _():
        for rel, p_ref in enumerate((p0, p1, p2, p3)):
            p_ref[...] = acc[rel * share : (rel + 1) * share, :].astype(jnp.bfloat16)


def held(shape):
    return pl.BlockSpec(shape, lambda step: (0,) * len(shape), pipeline_mode=pl.Buffered(1))


def by_cols(shape):
    return pl.BlockSpec(shape, lambda step: (0, step))


def global_ff(line, rows, up, down, tile=256):
    share = rows[0].shape[0]
    span, hidden, half = 4 * share, up[0].shape[1], up[0].shape[0]
    return line.run(
        global_ff_body,
        (*rows, *up, *down,),
        grid=(hidden // tile,),
        in_specs=[held((share, D))] * 4 + [by_cols((half, tile))] * 4,
        out_specs=[by_cols((span, tile))] * 2 + [held((share, D))] * 4,
        out_shape=[shaped((span, hidden), jnp.bfloat16)] * 2
        + [shaped((share, D), jnp.bfloat16)] * 4,
        scratch_shapes=[pltpu.VMEM((span, D), jnp.float32)],
        limit=(40),
        name="global_ff",
    )


def global_ff_back_body(g0, g1, g2, g3, slope_ref, up0, up1, down0, down1, dup_ref, p0, p1, p2, p3, acc):
    step = pl.program_id(0)
    share = g0.shape[0]
    half = up0.shape[0]

    @pl.when(step == 0)
    def _():
        acc[...] = jnp.zeros_like(acc)

    for rel, g_ref in enumerate((g0, g1, g2, g3)):
        rows = slice(rel * share, (rel + 1) * share)
        grad = both(g_ref[...], down0[...], down1[...])
        dup = (grad * slope_ref[rows, :].astype(jnp.float32)).astype(jnp.bfloat16)
        dup_ref[rows, :] = dup
        for at, up in enumerate((up0, up1)):
            lanes = slice(at * half, (at + 1) * half)
            acc[rows, lanes] += dot_transposed(dup, up[...])

    @pl.when(step == pl.num_programs(0) - 1)
    def _():
        for rel, p_ref in enumerate((p0, p1, p2, p3)):
            p_ref[...] = acc[rel * share : (rel + 1) * share, :].astype(jnp.bfloat16)


def global_ff_back(line, grads, slope, up, down, tile=256):
    share = grads[0].shape[0]
    span, hidden, half = 4 * share, up[0].shape[1], up[0].shape[0]
    return line.run(
        global_ff_back_body,
        (*grads, slope, *up, *down,),
        grid=(hidden // tile,),
        in_specs=[held((share, D))] * 4 + [by_cols((span, tile))] + [by_cols((half, tile))] * 4,
        out_specs=[by_cols((span, tile))] + [held((share, D))] * 4,
        out_shape=[shaped((span, hidden), jnp.bfloat16)] + [shaped((share, D), jnp.bfloat16)] * 4,
        scratch_shapes=[pltpu.VMEM((span, D), jnp.float32)],
        limit=(40),
        name="global_ff_back",
    )


def outer_body(r0, r1, r2, r3, right_ref, near_ref, far_ref, left_t):
    share = r0.shape[0]

    @pl.when(pl.program_id(0) == 0)
    def _():
        for rel, ref in enumerate((r0, r1, r2, r3)):
            left_t[:, rel * share : (rel + 1) * share] = jnp.transpose(ref[...])

    for at in range(D // 256):
        rows = slice(at * 256, (at + 1) * 256)
        out_ref, begin = (near_ref, 0) if at * 256 < D // 2 else (far_ref, D // 2)
        out_ref[at * 256 - begin : at * 256 - begin + 256, :] = dot_rows(
            left_t[rows, :], right_ref[...]
        ).astype(jnp.bfloat16)


def global_outer(line, rows, right, tile=256):
    share = rows[0].shape[0]
    span, hidden = right.shape
    return line.run(
        outer_body,
        (*rows, right,),
        grid=(hidden // tile,),
        in_specs=[held((share, D))] * 4 + [by_cols((span, tile))],
        out_specs=[by_cols((D // 2, tile))] * 2,
        out_shape=[shaped((D // 2, hidden), jnp.bfloat16)] * 2,
        scratch_shapes=[pltpu.VMEM((D, span), jnp.bfloat16)],
        limit=(32),
        name="global_ff_grads",
    )


def head_sums(width):
    row_at = lax.broadcasted_iota(jnp.int32, (width, width), 0) // HD
    col_at = lax.broadcasted_iota(jnp.int32, (width, width), 1) // HD
    return (row_at == col_at).astype(jnp.bfloat16)


def over_heads(product, ones):
    high = product.astype(jnp.bfloat16)
    low = (product - high.astype(jnp.float32)).astype(jnp.bfloat16)
    return dot_rows(high, ones) + dot_rows(low, ones)


def frame_probs(queries, keys, ones):
    found = []
    for at in range(CB):
        scores = [over_heads(queries[at] * keys[c2], ones) * HD ** (-0.5) for c2 in range(at + 1)]
        top = scores[0]
        for one in scores[1:]:
            top = jnp.maximum(top, one)
        expanded = [jnp.exp(one - top) for one in scores]
        total = expanded[0]
        for one in expanded[1:]:
            total = total + one
        inverse = 1.0 / total
        found.append([one * inverse for one in expanded])
    return found


def rounded_f32(values):
    return values.astype(jnp.bfloat16).astype(jnp.float32)


def start_weights(parts, buffer, sems):
    for at, pair in enumerate(parts):
        for half, ref in enumerate(pair):
            pltpu.make_async_copy(ref, buffer.at[at, half], sems.at[at, half]).start()


def wait_weights(parts, buffer, sems, at):
    for half in range(2):
        pltpu.make_async_copy(parts[0][half], buffer.at[at, half], sems.at[at, half]).wait()


def local_heads_body(
    out_ref_in, code_ref, gains_ref, *refs
):
    count = 4
    parts = [refs[2 * at : 2 * at + 2] for at in range(count)]
    qkv_ref, mixed_ref, middle_ref, normed_b_ref, a_t_ref, normed_a, local_in, buffer, sems = refs[2 * count :]
    step = pl.program_id(0)
    frames = out_ref_in.shape[0]
    width = mixed_ref.shape[2]
    half = D // 2

    @pl.when(step == 0)
    def _():
        start_weights(parts, buffer, sems)
        for c in range(CB):
            rows = slice(c * frames, (c + 1) * frames)
            local_in[rows, :] = out_ref_in[...] + code_ref[rows, :].astype(jnp.float32)
            normed = norm_rows(local_in[rows, :], gains_ref[2:3, :]).astype(jnp.bfloat16)
            normed_a[rows, :] = normed
            a_t_ref[:, rows] = jnp.transpose(normed)
        middle_ref[...] = local_in[...]

    wait_weights(parts, buffer, sems, step)
    ones = head_sums(width)
    queries, keys, values = ([], [], [])
    for c in range(CB):
        rows = slice(c * frames, (c + 1) * frames)
        qkv = (
            dot_rows(normed_a[rows, :half], buffer[step, 0, :, : 3 * width])
            + dot_rows(normed_a[rows, half:], buffer[step, 1, :, : 3 * width])
        ).astype(jnp.bfloat16)
        qkv_ref[0, rows, :] = qkv
        queries.append(qkv[:, :width].astype(jnp.float32))
        keys.append(qkv[:, width : 2 * width].astype(jnp.float32))
        values.append(qkv[:, 2 * width :].astype(jnp.float32))
    prob = frame_probs(queries, keys, ones)
    for c in range(CB):
        rows = slice(c * frames, (c + 1) * frames)
        mix = rounded_f32(prob[c][0]) * values[0]
        for c2 in range(1, c + 1):
            mix = mix + rounded_f32(prob[c][c2]) * values[c2]
        mix = mix.astype(jnp.bfloat16)
        mixed_ref[0, rows, :] = mix
        for at in range(2):
            lanes = slice(at * half, (at + 1) * half)
            middle_ref[rows, lanes] += dot_transposed(mix, buffer[step, at, :, 3 * width :])

    @pl.when(step == count - 1)
    def _():
        for c in range(CB):
            rows = slice(c * frames, (c + 1) * frames)
            normed_b_ref[rows, :] = norm_rows(middle_ref[rows, :], gains_ref[3:4, :]).astype(
                jnp.bfloat16
            )


def local_heads(line, global_out, codes, gains, parts):
    frames = global_out.shape[0]
    rows = CB * frames
    width = parts[0][0].shape[1] // 4
    half = D // 2
    flat = [ref for pair in parts for ref in pair]
    return line.run(
        local_heads_body,
        (global_out, codes, gains, *flat),
        grid=(4,),
        in_specs=[held((frames, D)), held((rows, D)), held((4, D))] + [IN_HBM] * 8,
        out_specs=[
            pl.BlockSpec((1, rows, 3 * width), lambda step: (step, 0, 0)),
            pl.BlockSpec((1, rows, width), lambda step: (step, 0, 0)),
            held((rows, D)),
            held((rows, D)),
            held((D, rows)),
        ],
        out_shape=[
            shaped((4, rows, 3 * width), jnp.bfloat16),
            shaped((4, rows, width), jnp.bfloat16),
            shaped((rows, D), jnp.float32),
            shaped((rows, D), jnp.bfloat16),
            shaped((D, rows), jnp.bfloat16),
        ],
        scratch_shapes=[
            pltpu.VMEM((rows, D), jnp.bfloat16),
            pltpu.VMEM((rows, D), jnp.float32),
            pltpu.VMEM((4, 2, half, 4 * width), jnp.bfloat16),
            pltpu.SemaphoreType.DMA((4, 2)),
        ],
        limit=(52),
        name="local_heads",
    )


def local_ff_body(source_ref, normed_ref, middle_ref, *refs):
    count = 4
    ups = [refs[2 * at : 2 * at + 2] for at in range(count)]
    downs = [refs[2 * count + 2 * at : 2 * count + 2 * at + 2] for at in range(count)]
    active_ref, slope_ref, out_ref, b_t_ref, acc, up_buf, down_buf, up_sems, down_sems = refs[4 * count :]
    step = pl.program_id(0)
    rows_all = normed_ref.shape[0]
    frames = rows_all // CB
    half = D // 2
    tile = active_ref.shape[2]
    per = up_buf.shape[3] // tile
    group = step // per
    cols_at = pl.ds(pl.multiple_of((step % per) * tile, tile), tile)

    @pl.when(step == 0)
    def _():
        for at in range(count):
            start_weights_at(ups, up_buf, up_sems, at)
            start_weights_at(downs, down_buf, down_sems, at)
        b_t_ref[...] = jnp.transpose(normed_ref[...])
        acc[...] = middle_ref[...]

    @pl.when(step % per == 0)
    def _():
        wait_weights(ups, up_buf, up_sems, group)
        wait_weights(downs, down_buf, down_sems, group)

    for c in range(CB):
        rows = slice(c * frames, (c + 1) * frames)
        upper = dot_rows(normed_ref[rows, :half], up_buf[group, 0, :, cols_at]) + dot_rows(
            normed_ref[rows, half:], up_buf[group, 1, :, cols_at]
        )
        active, slope = gelu_both(upper)
        active_ref[0, rows, :] = active
        slope_ref[0, rows, :] = slope
        for at in range(2):
            lanes = slice(at * half, (at + 1) * half)
            acc[rows, lanes] += dot_transposed(active, down_buf[group, at, :, cols_at])

    @pl.when(step == pl.num_programs(0) - 1)
    def _():
        owned = D // source_ref.shape[0]
        for c in range(CB):
            rows = slice(c * frames, (c + 1) * frames)
            for at in range(source_ref.shape[0]):
                here = slice(at * owned, (at + 1) * owned)
                out_ref[c, :, lanes_of(source_ref, at, owned)] = acc[rows, here].astype(jnp.bfloat16)


def start_weights_at(parts, buffer, sems, at):
    for half in range(2):
        pltpu.make_async_copy(parts[at][half], buffer.at[at, half], sems.at[at, half]).start()


def local_ff(line, source, normed, middle, ups, downs, tile=512):
    rows = normed.shape[0]
    hidden = ups[0][0].shape[1]
    half = D // 2
    per = hidden // tile
    flat = [ref for pair in ups for ref in pair] + [ref for pair in downs for ref in pair]
    hidden_block = pl.BlockSpec((1, rows, tile), lambda step: (step // per, 0, step % per))
    return line.run(
        local_ff_body,
        (source, normed, middle, *flat,),
        grid=(4 * per,),
        in_specs=[IN_SMEM, held((rows, D)), held((rows, D))] + [IN_HBM] * 16,
        out_specs=[hidden_block, hidden_block, held((CB, rows // CB, D)), held((D, rows))],
        out_shape=[
            shaped((4, rows, hidden), jnp.bfloat16),
            shaped((4, rows, hidden), jnp.bfloat16),
            shaped((CB, rows // CB, D), jnp.bfloat16),
            shaped((D, rows), jnp.bfloat16),
        ],
        scratch_shapes=[
            pltpu.VMEM((rows, D), jnp.float32),
            pltpu.VMEM((4, 2, half, hidden), jnp.bfloat16),
            pltpu.VMEM((4, 2, half, hidden), jnp.bfloat16),
            pltpu.SemaphoreType.DMA((4, 2)),
            pltpu.SemaphoreType.DMA((4, 2)),
        ],
        limit=(56),
        name="local_ff",
    )


def seed_body(source_ref, count_ref, cot_ref, code_ref, grad_ref, grad_t_ref, codes_ref):
    frames = cot_ref.shape[1]
    owned = D // source_ref.shape[0]
    keep = lax.broadcasted_iota(jnp.int32, (frames, 1), 0) < count_ref[0]
    for c in range(CB):
        rows = slice(c * frames, (c + 1) * frames)
        for at in range(source_ref.shape[0]):
            here = slice(at * owned, (at + 1) * owned)
            values = cot_ref[c, :, lanes_of(source_ref, at, owned)].astype(jnp.float32)
            grad_ref[rows, here] = jnp.where(keep, values, 0.0).astype(jnp.bfloat16)
            codes_ref[rows, here] = code_ref[c, :, lanes_of(source_ref, at, owned)]
        grad_t_ref[:, rows] = jnp.transpose(grad_ref[rows, :])


def seed(line, source, count, cot, codes):
    frames = cot.shape[1]
    rows = CB * frames
    return line.run(
        seed_body,
        (source, count, cot, codes),
        in_specs=[IN_SMEM, IN_SMEM, VMEM_WHOLE, VMEM_WHOLE],
        out_specs=[VMEM_WHOLE] * 3,
        out_shape=[
            shaped((rows, D), jnp.bfloat16),
            shaped((D, rows), jnp.bfloat16),
            shaped((rows, D), jnp.bfloat16),
        ],
        limit=(24),
        name="seed_grads",
    )


def local_back_body(
    grad_h, grad_t_h, b_t_h, a_t_h, active_h, slope_h, qkv_h, mixed_h, middle_h, gout_h, codes_h, gains_ref, *refs
):
    heads_h, ups_h, downs_h, refs = refs[:8], refs[8:16], refs[16:24], refs[24:]
    total_ref, small_out_ref, gain_c_ref, gain_d_ref, *results_h = refs[:12]
    (
        grad_v, grad_t, other_t, weights, act, slp, dup, acc, mid, gout_v, codes_v,
        pair_out, pair_far, pair_near, head_out, head_far, head_near, x_in, y_far, y_near,
        sems, send, recv,
    ) = refs[12:]
    frames = gout_v.shape[0]
    rows_all = grad_v.shape[0]
    half = D // 2
    width = mixed_h.shape[2]
    scale = HD ** (-0.5)
    greet(("core", "x", "y"))

    def fetch(at, source, target):
        copy = pltpu.make_async_copy(source, target, sems.at[at])
        copy.start()
        return copy

    def give(at, hop, source, target):
        copy = to_partner(hop, source, target, send.at[at], recv.at[at])
        copy.start()
        return copy

    def fetch_ff(rel):
        found = [fetch(at, downs_h[2 * rel + at], weights.at[2 + at]) for at in range(2)]
        found.append(fetch(2, slope_h.at[rel], slp))
        return found + [fetch(3 + at, ups_h[2 * rel + at], weights.at[at]) for at in range(2)]

    order = (3, 1, 2, 0)
    waits = [fetch(5, grad_h, grad_v)] + fetch_ff(order[0])
    late = [fetch(6, grad_t_h, grad_t), fetch(7, active_h.at[order[0]], act), fetch(8, b_t_h, other_t)]
    later = [fetch(9, middle_h, mid), fetch(10, gout_h, gout_v), fetch(11, codes_h, codes_v)]
    acc[...] = jnp.zeros_like(acc)
    sent = []
    for step, rel in enumerate(order):
        for one in waits:
            one.wait()
        for tile in range(2):
            lanes = slice(tile * half, (tile + 1) * half)
            grad = dot_rows(grad_v[:, :half], weights[2, :, lanes]) + dot_rows(
                grad_v[:, half:], weights[3, :, lanes]
            )
            dup[:, lanes] = (grad * slp[:, lanes].astype(jnp.float32)).astype(jnp.bfloat16)
        for at in range(2):
            lanes = slice(at * half, (at + 1) * half)
            acc[:, lanes] += dot_transposed(dup[...], weights[at])
        if step < 3:
            waits = fetch_ff(order[step + 1])
        for one in late:
            one.wait()
        if step == 1:
            sent[0].wait_send()
        if step >= 2:
            sent[step - 2].wait_recv()
        met = (None, None, pair_far, pair_near)[step]
        for at in range(2):
            rows = slice(at * half, (at + 1) * half)
            for tile in range(2):
                lanes = slice(tile * half, (tile + 1) * half)
                down = dot_rows(grad_t[rows, :], act[:, lanes])
                up = dot_rows(other_t[rows, :], dup[:, lanes])
                if met is None:
                    pair_out[0, rows, lanes] = down.astype(jnp.bfloat16)
                    pair_out[1, rows, lanes] = up.astype(jnp.bfloat16)
                else:
                    met[0, rows, lanes] = (down + met[0, rows, lanes].astype(jnp.float32)).astype(jnp.bfloat16)
                    met[1, rows, lanes] = (up + met[1, rows, lanes].astype(jnp.float32)).astype(jnp.bfloat16)
        if step < 3:
            late = [fetch(7, active_h.at[order[step + 1]], act)]
        if step == 0:
            sent.append(give(0, "core", pair_out, pair_far))
        elif step == 1:
            sent.append(give(1, "core", pair_out, pair_near))
        elif step == 2:
            x_far = give(2, "x", pair_far.at[1, pl.ds(half, half)], x_in.at[pl.ds(half, half)])
            y_two = give(3, "y", pair_far.at[0, pl.ds(half, half)], y_far)
            x_near = give(4, "x", pair_far.at[1, pl.ds(0, half)], x_in.at[pl.ds(0, half)])
        else:
            y_zero = give(5, "y", pair_near.at[0, pl.ds(half, half)], y_near)

    def fetch_heads(rel):
        found = [fetch(at, heads_h[2 * rel + at], weights.at[at]) for at in range(2)]
        found.append(fetch(2, qkv_h.at[rel], act.at[:, pl.ds(0, 3 * width)]))
        return found + [fetch(3, mixed_h.at[rel], slp.at[:, pl.ds(0, width)])]

    waits = fetch_heads(order[0]) + [fetch(8, a_t_h, other_t)]
    sent[1].wait_send()
    for one in later:
        one.wait()
    total_gain = jnp.zeros((1, D), jnp.float32)
    for c in range(CB):
        rows = slice(c * frames, (c + 1) * frames)
        part_back, gain_grad = norm_rows_back(mid[rows, :], gains_ref[3:4, :], acc[rows, :])
        total = grad_v[rows, :].astype(jnp.float32) + part_back
        mid[rows, :] = total
        small = total.astype(jnp.bfloat16)
        grad_v[rows, :] = small
        grad_t[:, rows] = jnp.transpose(small)
        total_gain = total_gain + gain_grad
    gain_d_ref[...] = total_gain

    ones = head_sums(width)
    heads_sent = []

    def more(total, term):
        return term if total is None else total + term

    for step, rel in enumerate(order):
        for one in waits:
            one.wait()
        queries, keys, values, dmix = ([], [], [], [])
        back = rounded_f32(
            dot_rows(grad_v[:, :half], weights[0, :, 3 * width :])
            + dot_rows(grad_v[:, half:], weights[1, :, 3 * width :])
        )
        for c in range(CB):
            rows = slice(c * frames, (c + 1) * frames)
            qkv = act[rows, : 3 * width].astype(jnp.float32)
            queries.append(qkv[:, :width])
            keys.append(qkv[:, width : 2 * width])
            values.append(qkv[:, 2 * width :])
            dmix.append(back[rows, :])
        prob = frame_probs(queries, keys, ones)
        dq, dk, dv = ([None] * CB, [None] * CB, [None] * CB)
        for c in range(CB):
            dprob = [over_heads(dmix[c] * values[c2], ones) for c2 in range(c + 1)]
            center = prob[c][0] * dprob[0]
            for c2 in range(1, c + 1):
                center = center + prob[c][c2] * dprob[c2]
            for c2 in range(c + 1):
                dv[c2] = more(dv[c2], rounded_f32(prob[c][c2]) * dmix[c])
                dscore = rounded_f32(prob[c][c2] * (dprob[c2] - center))
                dq[c] = more(dq[c], dscore * keys[c2])
                dk[c2] = more(dk[c2], dscore * queries[c])
        for c in range(CB):
            rows = slice(c * frames, (c + 1) * frames)
            dup[rows, :width] = (dq[c] * scale).astype(jnp.bfloat16)
            dup[rows, width : 2 * width] = (dk[c] * scale).astype(jnp.bfloat16)
            dup[rows, 2 * width : 3 * width] = dv[c].astype(jnp.bfloat16)
        for at in range(2):
            lanes = slice(at * half, (at + 1) * half)
            term = dot_transposed(dup[:, : 3 * width], weights[at, :, : 3 * width])
            acc[:, lanes] = term if step == 0 else acc[:, lanes] + term
        if step == 1:
            heads_sent[0].wait_send()
        if step >= 2:
            heads_sent[step - 2].wait_recv()
        met = (None, None, head_far, head_near)[step]
        for at in range(2):
            rows = slice(at * half, (at + 1) * half)
            three = dot_rows(other_t[rows, :], dup[:, : 3 * width])
            one = dot_rows(grad_t[rows, :], slp[:, :width])
            if met is None:
                head_out[rows, : 3 * width] = three.astype(jnp.bfloat16)
                head_out[rows, 3 * width :] = one.astype(jnp.bfloat16)
            else:
                three = three + met[rows, : 3 * width].astype(jnp.float32)
                one = one + met[rows, 3 * width :].astype(jnp.float32)
                met[rows, : 3 * width] = three.astype(jnp.bfloat16)
                met[rows, 3 * width :] = one.astype(jnp.bfloat16)
        if step < 3:
            waits = fetch_heads(order[step + 1])
        if step == 0:
            heads_sent.append(give(6, "core", head_out, head_far))
        elif step == 1:
            heads_sent.append(give(7, "core", head_out, head_near))
    total_gain = jnp.zeros((1, D), jnp.float32)
    total = jnp.zeros((frames, D), jnp.float32)
    for c in range(CB):
        rows = slice(c * frames, (c + 1) * frames)
        local_in = gout_v[...] + codes_v[rows, :].astype(jnp.float32)
        part_back, gain_grad = norm_rows_back(local_in, gains_ref[2:3, :], acc[rows, :])
        total = total + (mid[rows, :] + part_back)
        total_gain = total_gain + gain_grad
    total_ref[...] = total
    small_out_ref[...] = total.astype(jnp.bfloat16)
    gain_c_ref[...] = total_gain

    heads_sent[1].wait_send()
    x_far.wait()
    x_near.wait()
    y_two.wait()
    y_zero.wait()

    def summed(one, two):
        return (one.astype(jnp.float32) + two.astype(jnp.float32)).astype(jnp.bfloat16)

    pair_near[1] = summed(pair_near[1], x_in[...])
    pair_far[0, :half, :] = summed(pair_far[0, :half, :], y_far[...])
    pair_near[0, :half, :] = summed(pair_near[0, :half, :], y_near[...])
    near, far = pl.ds(0, half), pl.ds(half, half)
    leaving = (
        pair_near.at[1, near], pair_near.at[1, far], pair_far.at[0, near], pair_near.at[0, near],
        head_far.at[near], head_far.at[far], head_near.at[near], head_near.at[far],
    )
    for one in [fetch(at, source, target) for at, (source, target) in enumerate(zip(leaving, results_h))]:
        one.wait()


def local_back(line, grad, grad_t, b_t, a_t, active, slope, qkv, mixed, middle, global_out, codes, gains, heads, ups, downs):
    rows, frames = grad.shape[0], global_out.shape[0]
    half = D // 2
    flat = [one for parts in (heads, ups, downs) for pair in parts for one in pair]
    columns = ups[0][0].shape[1]
    small = jnp.bfloat16
    return line.run(
        local_back_body,
        (grad, grad_t, b_t, a_t, active, slope, qkv, mixed, middle, global_out, codes, gains, *flat),
        in_specs=[IN_HBM] * 11 + [VMEM_WHOLE] + [IN_HBM] * 24,
        out_specs=[VMEM_WHOLE] * 4 + [IN_HBM] * 8,
        out_shape=[
            shaped((frames, D), jnp.float32),
            shaped((frames, D), small),
            shaped((1, D), jnp.float32),
            shaped((1, D), jnp.float32),
        ]
        + [shaped((half, columns), small)] * 8,
        scratch_shapes=[
            pltpu.VMEM((rows, D), small),
            pltpu.VMEM((D, rows), small),
            pltpu.VMEM((D, rows), small),
            pltpu.VMEM((4, half, columns), small),
            pltpu.VMEM((rows, columns), small),
            pltpu.VMEM((rows, columns), small),
            pltpu.VMEM((rows, columns), small),
            pltpu.VMEM((rows, D), jnp.float32),
            pltpu.VMEM((rows, D), jnp.float32),
            pltpu.VMEM((frames, D), jnp.float32),
            pltpu.VMEM((rows, D), small),
            pltpu.VMEM((2, D, columns), small),
            pltpu.VMEM((2, D, columns), small),
            pltpu.VMEM((2, D, columns), small),
            pltpu.VMEM((D, columns), small),
            pltpu.VMEM((D, columns), small),
            pltpu.VMEM((D, columns), small),
            pltpu.VMEM((D, columns), small),
            pltpu.VMEM((half, columns), small),
            pltpu.VMEM((half, columns), small),
            pltpu.SemaphoreType.DMA((12,)),
            pltpu.SemaphoreType.DMA((8,)),
            pltpu.SemaphoreType.DMA((8,)),
        ],
        hops=("core", "x", "y"),
        limit=58,
        name="local_back",
    )


def cast_body(*refs):
    count = len(refs) // 2
    for master_ref, out_ref in zip(refs[:count], refs[count:]):
        out_ref[...] = master_ref[0].astype(jnp.bfloat16)


def cast(line, master, which):
    owned, columns = master.shape[1], master.shape[2] // 3

    def spec(layer, third):
        return pl.BlockSpec((1, owned, columns), lambda step: (layer, 0, third))

    return line.run(
        cast_body,
        (master,) * len(which),
        grid=(1,),
        in_specs=[spec(*one) for one in which],
        out_specs=[held((owned, columns))] * len(which),
        out_shape=[shaped((owned, columns), jnp.bfloat16)] * len(which),
        limit=(24),
        name="cast_shard",
    )


def stack_body(one_ref, two_ref, out_ref):
    rows = one_ref.shape[0]
    out_ref[:rows, :] = one_ref[...]
    out_ref[rows:, :] = two_ref[...]


def stack_rows(line, parts):
    rows, columns = parts[0].shape
    return line.run(
        stack_body,
        tuple(parts),
        in_specs=[VMEM_WHOLE] * 2,
        out_specs=[VMEM_WHOLE],
        out_shape=[shaped((2 * rows, columns), jnp.bfloat16)],
        limit=(16),
        name="stack_shards",
    )[0]


def add_body(*refs):
    total = refs[0][...].astype(jnp.float32)
    for ref in refs[1:-1]:
        total = total + ref[...].astype(jnp.float32)
    refs[-1][...] = total.astype(jnp.bfloat16)


def add_rows(line, terms, part=0, parts=1):
    rows = min(term.shape[0] for term in terms) if parts == 1 else terms[0].shape[0] // parts
    columns = terms[0].shape[1]

    def spec(term):
        return pl.BlockSpec(
            (rows, columns), (lambda step: (part, 0)) if term.shape[0] > rows else (lambda step: (0, 0))
        )

    return line.run(
        add_body,
        tuple(terms),
        grid=(1,),
        in_specs=[spec(term) for term in terms],
        out_specs=[pl.BlockSpec((rows, columns), lambda step: (0, 0))],
        out_shape=[shaped((rows, columns), jnp.bfloat16)],
        limit=(24),
        name="add_terms",
    )[0]


def sum_pieces(line, terms, split=()):
    rows, columns = terms[0].shape[0] // 2, terms[0].shape[1]
    whole = len(terms)
    flat = list(terms) + [one for pair in split for one in pair]

    def body(*refs):
        for at, out_ref in enumerate(refs[-2:]):
            here = slice(at * rows, (at + 1) * rows)
            total = refs[0][here, :].astype(jnp.float32)
            for ref in refs[1:whole]:
                total = total + ref[here, :].astype(jnp.float32)
            for ref in refs[whole + at : -2 : 2]:
                total = total + ref[...].astype(jnp.float32)
            out_ref[...] = total.astype(jnp.bfloat16)

    return line.run(
        body,
        tuple(flat),
        in_specs=[VMEM_WHOLE] * len(flat),
        out_specs=[VMEM_WHOLE] * 2,
        out_shape=[shaped((rows, columns), jnp.bfloat16)] * 2,
        limit=24,
        name="sum_pieces",
    )


def pass_body(*refs):
    pass


def in_turn(line, *values):
    return line.run(
        pass_body,
        tuple(values),
        in_specs=[IN_HBM] * len(values),
        out_specs=[IN_HBM] * len(values),
        out_shape=[shaped(one.shape, one.dtype) for one in values],
        aliases={at: at for at in range(len(values))},
        name="in_turn",
    )


def split_dot(left, right):
    left_high = left.astype(jnp.bfloat16)
    left_low = (left - left_high.astype(jnp.float32)).astype(jnp.bfloat16)
    right_high = right.astype(jnp.bfloat16)
    right_low = (right - right_high.astype(jnp.float32)).astype(jnp.bfloat16)
    return (
        dot_rows(left_high, right_high) + dot_rows(left_high, right_low) + dot_rows(left_low, right_high)
    )


def adam_body(chained, one_ref, two_ref, left_ref, right_ref, master_ref, first_ref, second_ref, ema_ref, *refs):
    grads_ref, new_master_ref, new_first_ref, new_second_ref, new_ema_ref = refs[5:] if chained else refs
    left = left_ref[0]
    left_t = jnp.transpose(left)
    grads = one_ref[...].astype(jnp.float32) + two_ref[...].astype(jnp.float32)
    grads_ref[0] = grads
    turned_left = split_dot(left_t, grads)
    back = []
    for at in range(right_ref.shape[1]):
        tile = slice(at * 128, (at + 1) * 128)
        right = right_ref[0, at]
        rotated = split_dot(turned_left[:, tile], right)
        new_first = beta_first * first_ref[0, :, tile] + (1.0 - beta_first) * rotated
        new_second = beta_second * second_ref[0, :, tile] + (1.0 - beta_second) * rotated * rotated
        new_first_ref[0, :, tile] = new_first
        new_second_ref[0, :, tile] = new_second
        turned = new_first / (jnp.sqrt(new_second) + adam_eps)
        back.append(split_dot(turned, jnp.transpose(right)))
    back_full = split_dot(left, jnp.concatenate(back, axis=1))
    new_master = master_ref[0] - step_rate * back_full
    new_master_ref[0] = new_master
    new_ema_ref[0] = ema_decay * ema_ref[0] + (1.0 - ema_decay) * new_master


def adam(line, layer, third, pieces, left, right, master, first, second, ema, before, tile=256):
    owned, columns = pieces[0].shape
    steps = columns // tile
    first_step = third * steps

    def state(step):
        return (layer, 0, first_step + step)

    state_spec = pl.BlockSpec((1, owned, tile), state)
    chained = before is not None
    return line.run(
        lambda *refs: adam_body(chained, *refs),
        (*pieces, left, right, master, first, second, ema, *(before or ()),),
        grid=(steps,),
        in_specs=[by_cols((owned, tile))] * 2
        + [
            pl.BlockSpec((1,) + left.shape[1:], lambda step: (layer, 0, 0)),
            pl.BlockSpec(
                (1, tile // 128) + right.shape[2:], lambda step: (layer, first_step + step, 0, 0)
            ),
        ]
        + [state_spec] * 4
        + ([IN_HBM] * 5 if chained else []),
        out_specs=[state_spec] * 5,
        out_shape=[shaped(master.shape, jnp.float32)] * 5,
        aliases={8 + at: at for at in range(5)} if chained else {},
        limit=(32),
        name="adam_update",
    )


def hop_x(values):
    return lax.ppermute(values, "tensor", [(at, at ^ 2) for at in range(4)])


def hop_core(values):
    return lax.ppermute(values, "tensor", [(at, at ^ 1) for at in range(4)])


def hop_y(values):
    return lax.ppermute(values, "dp", [(at, at ^ 1) for at in range(8)])


def hop_z(values, step):
    return lax.ppermute(values, "dp", [(at, at ^ (2 * step)) for at in range(8)])


def total_everywhere(values):
    for hop in (hop_core, hop_x, hop_y):
        values = values + hop(values)
    for step in (1, 2):
        values = values + hop_z(values, step)
    return values


def shards_grid(
    frames_in,
    code_emb,
    cotangent,
    lengths,
    owner_list,
    master,
    first_moment,
    second_moment,
    ema,
    left_basis,
    right_basis,
    gains,
    gain_first,
    gain_second,
):
    share = frames_in.shape[0]
    owned = master.shape[1]
    groups = D // owned
    heads_w = D // lax.axis_size("tensor")
    ff_w = FF // lax.axis_size("tensor")
    my_dp = lax.axis_index("dp")
    my_group = lax.axis_index("tensor").astype(jnp.int32)

    rel = jnp.array([2 * z + y for y in range(2) for z in (0, 2, 1, 3)], jnp.int32)
    owner_at = my_dp ^ rel
    slots = jnp.arange(groups, dtype=jnp.int32)
    source = jnp.sum(
        jnp.where(owner_list[None, :] == owner_at[:, None], slots[None, :], 0), axis=1
    ).astype(jnp.int32)
    info = jnp.stack([my_group, lengths[0]])
    count = (lengths - my_group * share).astype(jnp.int32)

    line = Line()
    codes = jnp.transpose(code_emb, (1, 0, 2))

    (ga,) = cast(line, master, [(0, 0)])
    ga_z = hop_z(ga, 2)
    rows_in, gains_here, normed = prep(line, source, frames_in, gains)
    normed_x = hop_x(normed)
    la, gu, lu, gd, ld = cast(line, master, [(1, 0), (0, 1), (1, 1), (0, 2), (1, 2)])
    ga = stack_rows(line, [ga, ga_z])
    ga_z, la_z = hop_z(ga, 1), hop_z(la, 2)
    (normed_x,) = in_turn(line, normed_x)
    normed_a = [normed, hop_core(normed), normed_x, hop_core(normed_x)]
    ga = stack_rows(line, [ga, ga_z])
    la = stack_rows(line, [la, la_z])
    ga_far, la_z, gu_z = hop_y(ga), hop_z(la, 1), hop_z(gu, 2)
    la = stack_rows(line, [la, la_z])
    gu = stack_rows(line, [gu, gu_z])
    la_far, la_x, gu_z, lu_z = hop_y(la), hop_x(la), hop_z(gu, 1), hop_z(lu, 2)
    g_heads = (ga, ga_far)
    qkv, mixed, lse, *parts = global_heads(line, info, normed_a, g_heads)
    near_term, far_term = hop_core(parts[1]), hop_core(parts[3])
    gu = stack_rows(line, [gu, gu_z])
    lu = stack_rows(line, [lu, lu_z])
    gu_far, lu_z, gd_z = hop_y(gu), hop_z(lu, 1), hop_z(gd, 2)
    to_x = hop_x(add_rows(line, [parts[2], far_term]))
    la_far, la_x = in_turn(line, la_far, la_x)
    lu = stack_rows(line, [lu, lu_z])
    gd = stack_rows(line, [gd, gd_z])
    lu_far, gd_z, ld_z = hop_y(lu), hop_z(gd, 1), hop_z(ld, 2)
    middle, normed = merge(line, rows_in, (parts[0], near_term, to_x), gains_here, 1)
    normed_x = hop_x(normed)
    gd = stack_rows(line, [gd, gd_z])
    ld = stack_rows(line, [ld, ld_z])
    gd_far, ld_z = hop_y(gd), hop_z(ld, 1)
    (normed_x, la_far, lu) = in_turn(line, normed_x, la_far, lu)
    normed_b = [normed, hop_core(normed), normed_x, hop_core(normed_x)]
    la_far_x, lu_x = hop_x(la_far), hop_x(lu)
    grad, grad_t, codes_here = seed(line, source, count, jnp.transpose(cotangent, (1, 0, 2)), codes)
    ld = stack_rows(line, [ld, ld_z])
    ld_far, la_c, la_far_c = hop_y(ld), hop_core(la), hop_core(la_far)
    g_up, g_down = (gu, gu_far), (gd, gd_far)
    active, slope, *parts = global_ff(line, normed_b, g_up, g_down)
    near_term, far_term = hop_core(parts[1]), hop_core(parts[3])
    (lu_x, la_far_x, ld) = in_turn(line, lu_x, la_far_x, ld)
    lu_far_x = hop_y(lu_x)
    to_x = hop_x(add_rows(line, [parts[2], far_term]))
    ld_x = hop_x(ld)
    la_xc, la_far_xc = hop_core(la_x), hop_core(la_far_x)
    (global_out,) = merge(line, middle, (parts[0], near_term, to_x), gains_here, 1, normed=False)
    (ld_far, lu_far) = in_turn(line, ld_far, lu_far)

    l_heads = [(la, la_far), (la_c, la_far_c), (la_x, la_far_x), (la_xc, la_far_xc)]
    l_qkv, l_mixed, l_middle, l_normed_b, l_a_t = local_heads(
        line, global_out, codes_here, gains_here, l_heads
    )
    lu_c, lu_far_c, ld_c, ld_far_c = hop_core(lu), hop_core(lu_far), hop_core(ld), hop_core(ld_far)
    (ld_x, lu_far_x) = in_turn(line, ld_x, lu_far_x)
    ld_far_x = hop_y(ld_x)
    lu_xc, lu_far_xc, ld_xc = hop_core(lu_x), hop_core(lu_far_x), hop_core(ld_x)
    (ld_far_x,) = in_turn(line, ld_far_x)
    ld_far_xc = hop_core(ld_far_x)
    l_up = [(lu, lu_far), (lu_c, lu_far_c), (lu_x, lu_far_x), (lu_xc, lu_far_xc)]
    l_down = [(ld, ld_far), (ld_c, ld_far_c), (ld_x, ld_far_x), (ld_xc, ld_far_xc)]
    l_active, l_slope, local_out, l_b_t = local_ff(line, source, l_normed_b, l_middle, l_up, l_down)
    local_out = jnp.transpose(local_out, (1, 0, 2))

    (
        grad_global, small, gain_c, gain_d, u_near, u_far, d2, d0, h2_near, h2_far, h0_near, h0_far,
    ) = local_back(
        line, grad, grad_t, l_b_t, l_a_t, l_active, l_slope, l_qkv, l_mixed, l_middle, global_out, codes_here,
        gains_here, l_heads, l_up, l_down,
    )
    small_x = hop_x(small)
    u_far = hop_y(u_far)
    d2 = hop_x(d2)
    h2_far = hop_y(h2_far)

    def update(layer, third, pieces, before):
        return adam(
            line, layer, third, pieces, left_basis, right_basis, master, first_moment, second_moment, ema, before
        )

    def depth_first(terms, split=()):
        keep, send = sum_pieces(line, terms, split)
        return keep, hop_z(send, 1)

    def depth_second(keep, met):
        keep, send = sum_pieces(line, [keep, met])
        return keep, hop_z(send, 2)

    (small_x,) = in_turn(line, small_x)
    grad_rows = [small, hop_core(small), small_x, hop_core(small_x)]
    h0_far = hop_y(h0_far)
    grad_upper, *parts = global_ff_back(line, grad_rows, slope, g_up, g_down)
    near_term, far_term = hop_core(parts[1]), hop_core(parts[3])
    gd_near, gd_far = global_outer(line, grad_rows, active)
    gd_far = hop_y(gd_far)
    to_x = hop_x(add_rows(line, [parts[2], far_term]))
    ld = depth_first([d0, d2])
    lu = depth_first([u_near, u_far])
    gu_near, gu_far = global_outer(line, normed_b, grad_upper)
    gu_far = hop_y(gu_far)
    ld = depth_second(*ld)
    grad_middle, small, gain_b = merge_back(
        line, middle, (parts[0], near_term, to_x), grad_global, gains_here, 1
    )
    small_x = hop_x(small)
    h2 = hop_x(add_rows(line, [h2_near, h2_far]))
    lu = depth_second(*lu)
    found = update(1, 2, ld, None)
    (small_x,) = in_turn(line, small_x)
    grad_attn = [small, hop_core(small), small_x, hop_core(small_x)]
    grad_qkv, *parts = global_heads_back(line, info, grad_attn, g_heads, qkv, mixed, lse)
    near_term, far_term = hop_core(parts[1]), hop_core(parts[3])
    gh_near, gh_far = global_grads_heads(line, info, normed_a, grad_attn, grad_qkv, mixed)
    gh_far = hop_y(gh_far)
    to_x = hop_x(add_rows(line, [parts[2], far_term]))
    found = update(1, 1, lu, found)
    gd = depth_first([gd_near, gd_far])
    lh = depth_first([h0_near, h0_far, h2])
    input_grad, gain_grads = finish(
        line, source, rows_in, (parts[0], near_term, to_x), grad_middle, gains_here, (gain_b, gain_c, gain_d)
    )
    gain_grads = total_everywhere(gain_grads)
    gd = depth_second(*gd)
    lh = depth_second(*lh)
    gu = depth_first([gu_near, gu_far])
    found = update(0, 2, gd, found)
    found = update(1, 0, lh, found)
    gu = depth_second(*gu)
    gh = depth_first([gh_near, gh_far])
    found = update(0, 1, gu, found)
    gh = depth_second(*gh)
    found = update(0, 0, gh, found)
    weight_grads, new_master, new_first, new_second, new_ema = found
    new_gain_first = beta_first * gain_first + (1.0 - beta_first) * gain_grads
    new_gain_second = beta_second * gain_second + (1.0 - beta_second) * gain_grads * gain_grads
    new_gains = gains - gain_rate * new_gain_first / (jnp.sqrt(new_gain_second) + adam_eps)
    return (
        local_out,
        input_grad,
        weight_grads,
        gain_grads,
        new_master,
        new_first,
        new_second,
        new_ema,
        new_gains,
        new_gain_first,
        new_gain_second,
    )


def solution(mesh):
    fits = mesh.shape["dp"] == 8 and mesh.shape["tensor"] == 4
    return jax.shard_map(
        shards_grid if fits else shards_any,
        mesh=mesh,
        in_specs=(
            P(("dp", "tensor"), None),
            P(("dp", "tensor"), None, None),
            P(("dp", "tensor"), None, None),
            P("dp"),
            P(),
            P(None, "dp", "tensor"),
            P(None, "dp", "tensor"),
            P(None, "dp", "tensor"),
            P(None, "dp", "tensor"),
            P(None, "dp", "tensor"),
            P(None, "dp", None, "tensor"),
            P(),
            P(),
            P(),
        ),
        out_specs=(
            P(("dp", "tensor"), None, None),
            P(("dp", "tensor"), None),
            P(None, "dp", "tensor"),
            P(),
            P(None, "dp", "tensor"),
            P(None, "dp", "tensor"),
            P(None, "dp", "tensor"),
            P(None, "dp", "tensor"),
            P(),
            P(),
            P(),
        ),
        check_vma=False,
    )
```

```python
import math

import jax
import jax.numpy as jnp
from jax import lax
from jax.experimental import pallas as pl
from jax.experimental.pallas import tpu as pltpu
from jax.sharding import PartitionSpec as P

D = 1024
HD = 64
FF = 4096
CB = 3
LMAX = 1024


norm_eps = 1e-06
beta_first = 0.5
beta_second = 0.5
adam_eps = 1e-08
step_rate = 0.05
gain_rate = 0.4
ema_decay = 0.9
masked_fill = -1e30
highest = lax.Precision.HIGHEST


def dot_rows(left, right):
    return jnp.dot(left, right, preferred_element_type=jnp.float32)


def dot_transposed(left, right):
    return lax.dot_general(
        left, right, (((1,), (1,)), ((), ())), preferred_element_type=jnp.float32
    )


def dot_over_rows(left, right):
    return lax.dot_general(
        left, right, (((0,), (0,)), ((), ())), preferred_element_type=jnp.float32
    )


def keep_rows(values):
    return values


def row_term(operand, weight):
    return dot_transposed(operand, weight)


def rms_forward(rows_in, gain):
    return (
        rows_in * lax.rsqrt(jnp.mean(rows_in * rows_in, axis=-1, keepdims=True) + norm_eps) * gain
    )


def rms_backward(rows_in, gain, grad_out):
    width = rows_in.shape[-1]
    scale_rows = lax.rsqrt(jnp.mean(rows_in * rows_in, axis=-1, keepdims=True) + norm_eps)
    scaled_grad = grad_out * gain
    inner_total = jnp.sum(scaled_grad * rows_in, axis=-1, keepdims=True)
    grad_in = (
        scale_rows * scaled_grad
        - rows_in * (scale_rows * scale_rows * scale_rows) * inner_total / width
    )
    gain_grad = jnp.sum(grad_out * rows_in * scale_rows, axis=0)
    return (grad_in, gain_grad)


def gelu_slope(upper):
    normal_cdf = 0.5 * (1.0 + lax.erf(upper * (1.0 / math.sqrt(2.0))))
    density = jnp.exp(-0.5 * upper * upper) * (1.0 / math.sqrt(2.0 * math.pi))
    return normal_cdf + upper * density


def split_layer(layer_cols, groups, head_cols, ff_cols):
    width = layer_cols.shape[0]
    grouped = layer_cols.reshape(width, groups, -1)

    def columns(begin, extent):
        return grouped[:, :, begin : begin + extent].reshape(width, groups * extent)

    w_qkv = jnp.concatenate(
        [columns(0, head_cols), columns(head_cols, head_cols), columns(2 * head_cols, head_cols)],
        axis=1,
    )
    return (
        w_qkv,
        columns(3 * head_cols, head_cols),
        columns(4 * head_cols, ff_cols),
        columns(4 * head_cols + ff_cols, ff_cols),
    )


def join_layer(grad_parts, groups):
    grad_qkv, grad_out, grad_up, grad_down = grad_parts
    width = grad_qkv.shape[0]
    head_width = grad_qkv.shape[1] // 3
    pieces = [
        grad_qkv[:, 0:head_width],
        grad_qkv[:, head_width : 2 * head_width],
        grad_qkv[:, 2 * head_width :],
        grad_out,
        grad_up,
        grad_down,
    ]
    return jnp.concatenate([piece.reshape(width, groups, -1) for piece in pieces], axis=2).reshape(
        width, -1
    )


def global_scores(queries, key_rows, length):
    span = queries.shape[0]
    heads = queries.shape[1] // HD
    scores = jnp.einsum(
        "qhd,khd->hqk",
        queries.reshape(span, heads, HD),
        key_rows.reshape(span, heads, HD),
        preferred_element_type=jnp.float32,
    ) * HD ** (-0.5)
    rows_at = lax.broadcasted_iota(jnp.int32, (span, span), 0)
    cols_at = lax.broadcasted_iota(jnp.int32, (span, span), 1)
    allowed = (cols_at <= rows_at) & (cols_at < length)
    return jnp.where(allowed[None], scores, masked_fill)


def global_attend(queries, key_rows, value_rows, lengths):
    items = lengths.shape[0]
    span = queries.shape[0] // items
    heads = queries.shape[1] // HD

    def one_item(packed):
        item_query, item_key, item_value, length = packed
        scores = global_scores(item_query, item_key, length)
        row_max = jnp.max(scores, axis=-1, keepdims=True)
        expanded = jnp.exp(scores - row_max)
        row_total = jnp.sum(expanded, axis=-1, keepdims=True)
        probability = (expanded / row_total).astype(jnp.bfloat16)
        mixed = jnp.einsum(
            "hqk,khd->qhd",
            probability,
            item_value.reshape(span, heads, HD),
            preferred_element_type=jnp.float32,
        )
        return (
            mixed.reshape(span, -1).astype(jnp.bfloat16),
            (row_max + jnp.log(row_total))[..., 0],
        )

    mixed, log_total = lax.map(
        one_item,
        (
            queries.reshape(items, span, -1),
            key_rows.reshape(items, span, -1),
            value_rows.reshape(items, span, -1),
            lengths,
        ),
    )
    return (mixed.reshape(items * span, -1), log_total)


def global_attend_back(queries, key_rows, value_rows, lengths, log_total, grad_mixed):
    items = lengths.shape[0]
    span = queries.shape[0] // items
    heads = queries.shape[1] // HD
    scale_score = HD ** (-0.5)

    def one_item(packed):
        item_query, item_key, item_value, length, item_lse, item_grad = packed
        scores = global_scores(item_query, item_key, length)
        probability = jnp.exp(scores - item_lse[..., None])
        grad_heads = item_grad.reshape(span, heads, HD)
        query_heads = item_query.reshape(span, heads, HD)
        key_heads = item_key.reshape(span, heads, HD)
        value_heads = item_value.reshape(span, heads, HD)
        grad_value = jnp.einsum(
            "hqk,qhd->khd",
            probability.astype(jnp.bfloat16),
            grad_heads,
            preferred_element_type=jnp.float32,
        )
        grad_prob = jnp.einsum(
            "qhd,khd->hqk", grad_heads, value_heads, preferred_element_type=jnp.float32
        )
        center = jnp.sum(probability * grad_prob, axis=-1, keepdims=True)
        grad_scores = (probability * (grad_prob - center)).astype(jnp.bfloat16)
        grad_query = (
            jnp.einsum("hqk,khd->qhd", grad_scores, key_heads, preferred_element_type=jnp.float32)
            * scale_score
        )
        grad_key = (
            jnp.einsum("hqk,qhd->khd", grad_scores, query_heads, preferred_element_type=jnp.float32)
            * scale_score
        )
        return jnp.concatenate(
            [
                grad_query.reshape(span, -1),
                grad_key.reshape(span, -1),
                grad_value.reshape(span, -1),
            ],
            axis=1,
        ).astype(jnp.bfloat16)

    grads = lax.map(
        one_item,
        (
            queries.reshape(items, span, -1),
            key_rows.reshape(items, span, -1),
            value_rows.reshape(items, span, -1),
            lengths,
            log_total,
            grad_mixed.reshape(items, span, -1),
        ),
    )
    return grads.reshape(items * span, -1)


def local_probability(queries, key_rows):
    frame_count = queries.shape[0] // CB
    heads = queries.shape[1] // HD
    scores = jnp.einsum(
        "fqhd,fkhd->fhqk",
        queries.reshape(frame_count, CB, heads, HD),
        key_rows.reshape(frame_count, CB, heads, HD),
        preferred_element_type=jnp.float32,
    ) * HD ** (-0.5)
    rows_at = lax.broadcasted_iota(jnp.int32, (CB, CB), 0)
    cols_at = lax.broadcasted_iota(jnp.int32, (CB, CB), 1)
    scores = jnp.where(cols_at <= rows_at, scores, masked_fill)
    row_max = jnp.max(scores, axis=-1, keepdims=True)
    expanded = jnp.exp(scores - row_max)
    return expanded / jnp.sum(expanded, axis=-1, keepdims=True)


def local_attend(queries, key_rows, value_rows):
    frame_count = queries.shape[0] // CB
    heads = queries.shape[1] // HD
    probability = local_probability(queries, key_rows).astype(jnp.bfloat16)
    mixed = jnp.einsum(
        "fhqk,fkhd->fqhd",
        probability,
        value_rows.reshape(frame_count, CB, heads, HD),
        preferred_element_type=jnp.float32,
    )
    return (mixed.reshape(queries.shape[0], -1).astype(jnp.bfloat16), jnp.zeros((), jnp.float32))


def local_attend_back(queries, key_rows, value_rows, saved, grad_mixed):
    frame_count = queries.shape[0] // CB
    heads = queries.shape[1] // HD
    scale_score = HD ** (-0.5)
    probability = local_probability(queries, key_rows)
    grad_heads = grad_mixed.reshape(frame_count, CB, heads, HD)
    query_heads = queries.reshape(frame_count, CB, heads, HD)
    key_heads = key_rows.reshape(frame_count, CB, heads, HD)
    value_heads = value_rows.reshape(frame_count, CB, heads, HD)
    grad_value = jnp.einsum(
        "fhqk,fqhd->fkhd",
        probability.astype(jnp.bfloat16),
        grad_heads,
        preferred_element_type=jnp.float32,
    )
    grad_prob = jnp.einsum(
        "fqhd,fkhd->fhqk", grad_heads, value_heads, preferred_element_type=jnp.float32
    )
    center = jnp.sum(probability * grad_prob, axis=-1, keepdims=True)
    grad_scores = (probability * (grad_prob - center)).astype(jnp.bfloat16)
    grad_query = (
        jnp.einsum("fhqk,fkhd->fqhd", grad_scores, key_heads, preferred_element_type=jnp.float32)
        * scale_score
    )
    grad_key = (
        jnp.einsum("fhqk,fqhd->fkhd", grad_scores, query_heads, preferred_element_type=jnp.float32)
        * scale_score
    )
    total_rows = queries.shape[0]
    return jnp.concatenate(
        [
            grad_query.reshape(total_rows, -1),
            grad_key.reshape(total_rows, -1),
            grad_value.reshape(total_rows, -1),
        ],
        axis=1,
    ).astype(jnp.bfloat16)


def block_forward(rows_in, matrices, gain_a, gain_b, path, attend):
    gather_rows, sum_rows = (path[0], path[1])
    w_qkv, w_out, w_up, w_down = matrices
    normed_a = gather_rows(rms_forward(rows_in, gain_a).astype(jnp.bfloat16))
    projected = dot_rows(normed_a, w_qkv).astype(jnp.bfloat16)
    head_width = projected.shape[1] // 3
    mixed, saved = attend(
        projected[:, :head_width],
        projected[:, head_width : 2 * head_width],
        projected[:, 2 * head_width :],
    )
    middle = rows_in + sum_rows(mixed, w_out)
    normed_b = gather_rows(rms_forward(middle, gain_b).astype(jnp.bfloat16))
    upper = dot_rows(normed_b, w_up)
    active = jax.nn.gelu(upper, approximate=False).astype(jnp.bfloat16)
    result = middle + sum_rows(active, w_down)
    return (result, (rows_in, normed_a, projected, mixed, saved, middle, normed_b, upper, active))


def block_backward(grad_result, kept, matrices, gain_a, gain_b, path, attend_back):
    gather_grads, sum_back = (path[2], path[3])
    rows_in, normed_a, projected, mixed, saved, middle, normed_b, upper, active = kept
    w_qkv, w_out, w_up, w_down = matrices
    grad_branch = gather_grads(grad_result.astype(jnp.bfloat16))
    grad_down = dot_over_rows(grad_branch, active)
    grad_active = dot_rows(grad_branch, w_down)
    grad_upper = (grad_active * gelu_slope(upper)).astype(jnp.bfloat16)
    grad_up = dot_over_rows(normed_b, grad_upper)
    grad_normed_b = sum_back(grad_upper, w_up)
    grad_middle_part, gain_b_grad = rms_backward(middle, gain_b, grad_normed_b)
    grad_middle = grad_result + grad_middle_part
    grad_attn = gather_grads(grad_middle.astype(jnp.bfloat16))
    grad_out = dot_over_rows(grad_attn, mixed)
    grad_mixed = dot_rows(grad_attn, w_out).astype(jnp.bfloat16)
    head_width = projected.shape[1] // 3
    grad_qkv = attend_back(
        projected[:, :head_width],
        projected[:, head_width : 2 * head_width],
        projected[:, 2 * head_width :],
        saved,
        grad_mixed,
    )
    grad_weight_qkv = dot_over_rows(normed_a, grad_qkv)
    grad_normed_a = sum_back(grad_qkv, w_qkv)
    grad_rows_part, gain_a_grad = rms_backward(rows_in, gain_a, grad_normed_a)
    return (
        grad_middle + grad_rows_part,
        (grad_weight_qkv, grad_out, grad_up, grad_down),
        gain_a_grad,
        gain_b_grad,
    )


def shards_any(
    frames_in,
    code_emb,
    cotangent,
    lengths,
    owner_list,
    master,
    first_moment,
    second_moment,
    ema,
    left_basis,
    right_basis,
    gains,
    gain_first,
    gain_second,
):
    tensor_count = lax.axis_size("tensor")
    group_count = lax.axis_size("dp")
    head_cols = D // tensor_count
    ff_cols = FF // tensor_count
    share = frames_in.shape[0]
    owned_rows = master.shape[1]
    gathered = lax.all_gather(master.astype(jnp.bfloat16), "dp", axis=1, tiled=True)
    layers = jnp.take(gathered.reshape(2, group_count, owned_rows, -1), owner_list, axis=1).reshape(
        2, group_count * owned_rows, -1
    )

    def gather_rows(values):
        return lax.all_gather(values, "tensor", axis=0, tiled=True)

    def gather_grads(values):
        return lax.all_gather(values, "tensor", axis=0, tiled=True)

    def sum_rows(operand, weight):
        return lax.psum_scatter(
            row_term(operand, weight).astype(jnp.bfloat16),
            "tensor",
            scatter_dimension=0,
            tiled=True,
        ).astype(jnp.float32)

    def sum_back(operand, weight):
        return lax.psum_scatter(
            row_term(operand, weight).astype(jnp.bfloat16),
            "tensor",
            scatter_dimension=0,
            tiled=True,
        ).astype(jnp.float32)

    heads_path = (gather_rows, sum_rows, gather_grads, sum_back)
    rows_path = (keep_rows, dot_transposed, keep_rows, dot_transposed)

    def attend_global(queries, key_rows, value_rows):
        return global_attend(queries, key_rows, value_rows, lengths)

    def attend_global_back(queries, key_rows, value_rows, saved, grad_mixed):
        return global_attend_back(queries, key_rows, value_rows, lengths, saved, grad_mixed)

    global_matrices = split_layer(layers[0], 1, head_cols, ff_cols)
    global_out, global_kept = block_forward(
        frames_in.astype(jnp.float32),
        global_matrices,
        gains[0],
        gains[1],
        heads_path,
        attend_global,
    )
    local_in = (global_out[:, None, :] + code_emb.astype(jnp.float32)).reshape(share * CB, -1)
    local_layer = lax.all_gather(layers[1], "tensor", axis=1, tiled=True)
    local_matrices = split_layer(local_layer, tensor_count, head_cols, ff_cols)
    local_result, local_kept = block_forward(
        local_in, local_matrices, gains[2], gains[3], rows_path, local_attend
    )
    local_out = local_result.reshape(share, CB, -1).astype(jnp.bfloat16)
    frame_at = lax.axis_index("tensor") * share + jnp.arange(share, dtype=jnp.int32)
    item_at = frame_at // LMAX
    item_slots = jnp.arange(lengths.shape[0], dtype=jnp.int32)
    item_length = jnp.sum(
        jnp.where(item_at[:, None] == item_slots[None, :], lengths[None, :], 0), axis=1
    )
    valid = (frame_at % LMAX < item_length).astype(jnp.float32)
    grad_local = (cotangent.astype(jnp.float32) * valid[:, None, None]).reshape(share * CB, -1)
    grad_local_in, local_weight_grads, gain_c_grad, gain_d_grad = block_backward(
        grad_local, local_kept, local_matrices, gains[2], gains[3], rows_path, local_attend_back
    )
    grad_global_out = jnp.sum(grad_local_in.reshape(share, CB, -1), axis=1)
    input_grad, global_weight_grads, gain_a_grad, gain_b_grad = block_backward(
        grad_global_out,
        global_kept,
        global_matrices,
        gains[0],
        gains[1],
        heads_path,
        attend_global_back,
    )
    local_grads = join_layer(local_weight_grads, tensor_count)
    local_grads = lax.psum_scatter(
        local_grads.astype(jnp.bfloat16), "tensor", scatter_dimension=1, tiled=True
    ).astype(jnp.float32)
    layer_grads = jnp.stack([join_layer(global_weight_grads, 1), local_grads])
    slots = jnp.arange(group_count, dtype=jnp.int32)
    inverse = jnp.sum(jnp.where(owner_list[None, :] == slots[:, None], slots[None, :], 0), axis=1)
    ordered = jnp.take(
        layer_grads.reshape(2, group_count, owned_rows, -1), inverse, axis=1
    ).reshape(2, group_count * owned_rows, -1)
    weight_grads = lax.psum_scatter(
        ordered.astype(jnp.bfloat16), "dp", scatter_dimension=1, tiled=True
    ).astype(jnp.float32)
    gain_grads = lax.psum(
        jnp.stack([gain_a_grad, gain_b_grad, gain_c_grad, gain_d_grad]), ("dp", "tensor")
    )
    tile_count = right_basis.shape[1]
    turned_left = jnp.einsum("lab,lac->lbc", left_basis, weight_grads, precision=highest)
    rotated = jnp.einsum(
        "lbkc,lkce->lbke",
        turned_left.reshape(2, owned_rows, tile_count, -1),
        right_basis,
        precision=highest,
    ).reshape(weight_grads.shape)
    new_first = beta_first * first_moment + (1.0 - beta_first) * rotated
    new_second = beta_second * second_moment + (1.0 - beta_second) * rotated * rotated
    turned = new_first / (jnp.sqrt(new_second) + adam_eps)
    back_right = jnp.einsum(
        "lbke,lkce->lbkc",
        turned.reshape(2, owned_rows, tile_count, -1),
        right_basis,
        precision=highest,
    )
    back_full = jnp.einsum(
        "lab,lbc->lac", left_basis, back_right.reshape(weight_grads.shape), precision=highest
    )
    new_master = master - step_rate * back_full
    new_ema = ema_decay * ema + (1.0 - ema_decay) * new_master
    new_gain_first = beta_first * gain_first + (1.0 - beta_first) * gain_grads
    new_gain_second = beta_second * gain_second + (1.0 - beta_second) * gain_grads * gain_grads
    new_gains = gains - gain_rate * new_gain_first / (jnp.sqrt(new_gain_second) + adam_eps)
    return (
        local_out,
        input_grad,
        weight_grads,
        gain_grads,
        new_master,
        new_first,
        new_second,
        new_ema,
        new_gains,
        new_gain_first,
        new_gain_second,
    )


MIB = 1024 * 1024
VMEM_WHOLE = pl.BlockSpec(memory_space=pltpu.VMEM)
IN_SMEM = pl.BlockSpec(memory_space=pltpu.SMEM)
IN_HBM = pl.BlockSpec(memory_space=pl.ANY)


def shaped(shape, kind):
    return jax.ShapeDtypeStruct(shape, kind)


def cost(flops, moved, exps=0):
    return pl.CostEstimate(flops=int(flops), bytes_accessed=int(moved), transcendentals=int(exps))


weight_of = {
    "forward_global": 170,
    "local_heads": 18,
    "local_ff": 34,
    "local_back": 81,
    "backward_global": 90,
    "adam_update": 5,
}


def group_at(rel):
    mine = lax.axis_index("tensor")
    return 2 * ((mine // 2 + rel // 2) % 2) + (mine % 2 + rel % 2) % 2


def partner_of(hop):
    dp, tensor = lax.axis_index("dp"), lax.axis_index("tensor")
    if hop == "core":
        return {"tensor": tensor + 1 - 2 * (tensor % 2)}
    if hop == "x":
        return {"tensor": (tensor + 2) % 4}
    if hop == "y":
        return {"dp": dp + 1 - 2 * (dp % 2)}
    if hop == "z1":
        return {"dp": dp + 2 - 4 * ((dp // 2) % 2)}
    return {"dp": (dp + 4) % 8}


def greet(hops):
    barrier = pltpu.get_barrier_semaphore()
    for hop in hops:
        pl.semaphore_signal(
            barrier, inc=1, device_id=partner_of(hop), device_id_type=pl.DeviceIdType.MESH
        )
    pl.semaphore_wait(barrier, len(hops))


def to_partner(hop, source, target, send, recv):
    return pltpu.make_async_remote_copy(
        src_ref=source,
        dst_ref=target,
        send_sem=send,
        recv_sem=recv,
        device_id=partner_of(hop),
        device_id_type=pl.DeviceIdType.MESH,
    )


def part(array, begin, rows):
    return (array, begin, rows)


class Line:
    def __init__(self):
        self.token = None
        self.moves = ()
        self.arrived = []
        self.calls = 0

    def carry(self, *moves):
        self.moves = moves

    def run(self, body, args, in_specs, out_specs, out_shape, aliases=None, scratch_shapes=(), limit=32, hops=(), **rest):
        moves, self.moves = self.moves, ()
        sources, copies, landed = [], [], []
        for hop, *pieces in moves:
            offset = 0
            for piece in pieces:
                array, begin, rows = piece if isinstance(piece, tuple) else (piece, 0, piece.shape[0])
                which = next((at for at, one in enumerate(sources) if one is array), len(sources))
                if which == len(sources):
                    sources.append(array)
                copies.append((hop, which, begin, rows, len(landed), offset))
                offset += rows
            landed.append(shaped((offset,) + array.shape[1:], array.dtype))
        reach = list(hops) or list(dict.fromkeys(move[0] for move in moves))
        lead = 0 if self.token is None else 1
        inputs = lead + len(args)
        first_out = inputs + len(sources)
        outputs = len(out_shape)
        first_scratch = first_out + outputs + len(landed) + 1
        steps = rest.get("grid", (1,))[0]

        def inner(*refs):
            scratch = refs[first_scratch:]
            pending = []
            if copies:
                *scratch, send, recv = scratch
                for at, (hop, which, begin, rows, where, offset) in enumerate(copies):
                    pending.append(
                        to_partner(
                            hop,
                            refs[inputs + which].at[pl.ds(begin, rows)],
                            refs[first_out + outputs + where].at[pl.ds(offset, rows)],
                            send.at[at],
                            recv.at[at],
                        )
                    )

            def begin_all():
                greet(reach)
                for one in pending:
                    one.start()

            def end_all():
                for one in pending:
                    one.wait()

            at_ends = (lambda step, act: pl.when(pl.program_id(0) == step)(act)) if steps > 1 else (
                lambda step, act: act()
            )
            if pending:
                at_ends(0, begin_all)
            body(*refs[lead:inputs], *refs[first_out : first_out + outputs], *scratch)
            if pending:
                at_ends(steps - 1, end_all)

        extra = {}
        if reach:
            extra = {"collective_id": self.calls, "has_side_effects": True}
            self.calls += 1
        found = pl.pallas_call(
            inner,
            in_specs=[IN_HBM] * lead + list(in_specs) + [IN_HBM] * len(sources),
            out_specs=list(out_specs) + [IN_HBM] * (len(landed) + 1),
            out_shape=list(out_shape) + landed + [shaped((8, 128), jnp.float32)],
            scratch_shapes=list(scratch_shapes)
            + ([pltpu.SemaphoreType.DMA((len(copies),))] * 2 if copies else []),
            input_output_aliases={lead + at: to for at, to in (aliases or {}).items()},
            cost_estimate=cost(weight_of.get(rest["name"], 1.0) * 0.2e9, 1000),
            compiler_params=pltpu.CompilerParams(vmem_limit_bytes=limit * MIB, **extra),
            **rest,
        )(*([self.token] * lead), *args, *sources)
        self.token = found[-1]
        self.arrived = list(found[outputs:-1])
        return list(found[:outputs])


def lanes_of(source_ref, at, width):
    return pl.ds(pl.multiple_of(source_ref[at] * width, width), width)


def norm_rows(rows, gain):
    scale = lax.rsqrt(jnp.mean(rows * rows, axis=-1, keepdims=True) + norm_eps)
    return rows * scale * gain


def norm_rows_back(rows, gain, grad):
    scale = lax.rsqrt(jnp.mean(rows * rows, axis=-1, keepdims=True) + norm_eps)
    scaled = grad * gain
    inner = jnp.sum(scaled * rows, axis=-1, keepdims=True)
    grad_in = scale * scaled - rows * (scale * scale * scale) * inner / rows.shape[-1]
    return grad_in, jnp.sum(grad * rows * scale, axis=0, keepdims=True)


def gelu_both(upper):
    size = jnp.abs(upper)
    base = 1.0 + (0.3275911 / math.sqrt(2.0)) * size
    guess = pl.reciprocal(base, approx=True)
    ratio = guess * (2.0 - base * guess)
    bell = jnp.exp(-0.5 * upper * upper)
    series = ratio * (
        0.5 * 0.254829592
        + ratio
        * (
            -0.5 * 0.284496736
            + ratio * (0.5 * 1.421413741 + ratio * (-0.5 * 1.453152027 + ratio * (0.5 * 1.061405429)))
        )
    )
    tail = series * bell
    cdf = jnp.where(upper >= 0.0, 1.0 - tail, tail)
    density = bell * (1.0 / math.sqrt(2.0 * math.pi))
    return (upper * cdf).astype(jnp.bfloat16), (cdf + upper * density).astype(jnp.bfloat16)


def both(rows, near, far):
    depth = near.shape[0]
    return dot_rows(rows[:, :depth], near) + dot_rows(rows[:, depth:], far)


def held(shape):
    return pl.BlockSpec(shape, lambda step: (0,) * len(shape), pipeline_mode=pl.Buffered(1))


def by_cols(shape):
    return pl.BlockSpec(shape, lambda step: (0, step))


def prep_body(source_ref, frames_ref, gains_ref, *refs):
    masters, (rows_ref, gains_out_ref, normed_ref), shards = refs[:6], refs[6:9], refs[9:]
    for master_ref, shard_ref in zip(masters, shards):
        shard_ref[...] = master_ref[0].astype(jnp.bfloat16)
    owned = frames_ref.shape[1] // source_ref.shape[0]
    for at in range(source_ref.shape[0]):
        here = slice(at * owned, (at + 1) * owned)
        rows_ref[:, here] = frames_ref[:, lanes_of(source_ref, at, owned)]
        gains_out_ref[:, here] = gains_ref[:, lanes_of(source_ref, at, owned)]
    normed_ref[...] = norm_rows(rows_ref[...].astype(jnp.float32), gains_out_ref[0:1, :]).astype(
        jnp.bfloat16
    )


def prep(line, source, frames, gains, master):
    owned, columns = master.shape[1], master.shape[2] // 3

    def spec(layer, third):
        return pl.BlockSpec((1, owned, columns), lambda step: (layer, 0, third))

    shapes = [
        shaped(frames.shape, jnp.bfloat16),
        shaped(gains.shape, jnp.float32),
        shaped(frames.shape, jnp.bfloat16),
    ] + [shaped((owned, columns), jnp.bfloat16)] * 6
    found = line.run(
        prep_body,
        (source, frames, gains) + (master,) * 6,
        grid=(1,),
        in_specs=[IN_SMEM, held(frames.shape), held(gains.shape)]
        + [spec(layer, third) for layer in range(2) for third in range(3)],
        out_specs=[held(one.shape) for one in shapes],
        out_shape=shapes,
        limit=24,
        name="prep_rows",
    )
    return found[:3], found[3:]


def finish_body(source_ref, rows_ref, sum_ref, grad_ref, gains_ref, gb_ref, gc_ref, gd_ref, out_ref, gain_ref):
    back, gain_grad = norm_rows_back(rows_ref[...].astype(jnp.float32), gains_ref[0:1, :], sum_ref[...])
    total = grad_ref[...] + back
    owned = out_ref.shape[1] // source_ref.shape[0]
    for at in range(source_ref.shape[0]):
        here = slice(at * owned, (at + 1) * owned)
        there = lanes_of(source_ref, at, owned)
        out_ref[:, there] = total[:, here]
        gain_ref[0:1, there] = gain_grad[:, here]
        gain_ref[1:2, there] = gb_ref[:, here]
        gain_ref[2:3, there] = gc_ref[:, here]
        gain_ref[3:4, there] = gd_ref[:, here]


def finish(line, source, rows, total, grad, gains, others):
    return line.run(
        finish_body,
        (source, rows, total, grad, gains, *others),
        in_specs=[IN_SMEM] + [VMEM_WHOLE] * 7,
        out_specs=[VMEM_WHOLE] * 2,
        out_shape=[shaped(rows.shape, jnp.float32), shaped((4, rows.shape[1]), jnp.float32)],
        limit=16,
        name="input_grad",
    )


def forward_body(
    info_ref, rows_ref, normed_ref, gains_ref, ga_s, gu_s, gd_s, la_s, lu_s, ld_s,
    ga, gu, gd, la, lu, ld, qkv_ref, mixed_ref, lse_ref, middle_ref, out_ref, na_h, nb_h, active_h, slope_h,
    na, nb, a_v, u_v, d_v, acc, lse_wide, act, slp, parts, met_core, met_x, sends_x, sems, send, recv,
):
    share = rows_ref.shape[0]
    owned = ga_s.shape[0]
    half = D // 2
    width = mixed_ref.shape[1]
    span = 4 * share
    length = info_ref[1]
    scale = HD ** (-0.5)
    flying, filed, from_parts, numbers = [], [], [], []

    def fly(hop, source, target):
        at = len(numbers)
        copy = to_partner(hop, source, target, send.at[at], recv.at[at])
        copy.start()
        numbers.append(at)
        flying.append(copy)
        return copy

    def file(source, target):
        copy = pltpu.make_async_copy(source, target, sems.at[len(filed)])
        copy.start()
        filed.append(copy)
        return copy

    def first(shard, whole):
        return fly("z2", shard, whole.at[pl.ds(owned, owned)])

    def second(whole, begin=0):
        return fly("z1", whole.at[pl.ds(begin, 2 * owned)], whole.at[pl.ds(begin + 2 * owned, 2 * owned)])

    def across(whole):
        return fly("y", whole.at[pl.ds(0, half)], whole.at[pl.ds(half, half)])

    def over(hop, stack, begin, to, rows=half, start=0):
        here = pl.ds(start, rows)
        return fly(hop, stack.at[begin, here], stack.at[to, here])

    greet(("core", "x", "y", "z1", "z2"))
    ga_2 = first(ga_s, ga)
    normed_x = fly("x", normed_ref, na.at[pl.ds(2 * share, share)])
    normed_core = fly("core", normed_ref, na.at[pl.ds(share, share)])
    ld_x = fly("x", ld_s, ld.at[2, pl.ds(0, owned)])
    ld_y = fly("y", ld_s, ld.at[0, pl.ds(half, owned)])
    la_2 = first(la_s, la.at[0])
    own = [
        file(shard, whole.at[pl.ds(0, owned)])
        for shard, whole in ((ga_s, ga), (la_s, la.at[0]), (gu_s, gu), (gd_s, gd), (lu_s, lu.at[0]), (ld_s, ld.at[0]))
    ]
    na[pl.ds(0, share), :] = normed_ref[...]
    for one in own:
        one.wait()
    ga_2.wait_recv()
    ga_1 = second(ga)
    gu_2 = first(gu_s, gu)
    normed_x.wait_recv()
    normed_xc = fly("core", na.at[pl.ds(2 * share, share)], na.at[pl.ds(3 * share, share)])
    ld_x.wait_recv()
    ld_xy = fly("y", ld.at[2, pl.ds(0, owned)], ld.at[2, pl.ds(half, owned)])
    la_2.wait_recv()
    la_1 = second(la.at[0])
    gd_2 = first(gd_s, gd)
    ga_1.wait_recv()
    ga_y = across(ga)
    a_near = file(ga.at[pl.ds(0, half)], a_v.at[pl.ds(0, half)])
    gu_2.wait_recv()
    gu_1 = second(gu)
    lu_2 = first(lu_s, lu.at[0])
    la_1.wait_recv()
    la_x = over("x", la, 0, 2)
    la_y = across(la.at[0])
    la_c = over("core", la, 0, 1)
    gd_2.wait_recv()
    gd_1 = second(gd)
    gu_1.wait_recv()
    gu_y = across(gu)
    u_near = file(gu.at[pl.ds(0, half)], u_v.at[pl.ds(0, half)])
    normed_core.wait_recv()
    normed_xc.wait_recv()
    ga_y.wait_recv()
    a_far = file(ga.at[pl.ds(half, half)], a_v.at[pl.ds(half, half)])
    na_out = file(na, na_h)
    a_near.wait()
    a_far.wait()

    for rel in range(4):
        at = pl.ds(pl.multiple_of(group_at(rel) * share, share), share)
        full = both(na[rel * share : (rel + 1) * share, :], a_v[:half, : 3 * width], a_v[half:, : 3 * width])
        qkv_ref[at, :] = full.astype(jnp.bfloat16)
    acc[:, :width] = jnp.zeros((span, width), jnp.float32)
    lse_wide[...] = jnp.zeros_like(lse_wide)
    head_of = lax.broadcasted_iota(jnp.int32, (1, width), 1) // HD
    lane = lax.broadcasted_iota(jnp.int32, (1, 128), 1)

    def per_head(head):
        own_lanes = head_of == head
        for block in range(4):
            rows = slice(block * share, (block + 1) * share)
            reach = (block + 1) * share
            query = jnp.where(own_lanes, qkv_ref[rows, :width] * scale, 0.0).astype(jnp.bfloat16)
            scores = dot_transposed(query, qkv_ref[:reach, width : 2 * width])
            row_at = block * share + lax.broadcasted_iota(jnp.int32, scores.shape, 0)
            col_at = lax.broadcasted_iota(jnp.int32, scores.shape, 1)
            scores = jnp.where((col_at <= row_at) & (col_at < length), scores, masked_fill)
            top = jnp.max(scores, axis=-1, keepdims=True)
            expanded = jnp.exp(scores - top)
            total = jnp.sum(expanded, axis=-1, keepdims=True)
            prob = (expanded * (1.0 / total)).astype(jnp.bfloat16)
            value = jnp.where(own_lanes, qkv_ref[:reach, 2 * width :], 0.0).astype(jnp.bfloat16)
            acc[rows, :width] += dot_rows(prob, value)
            lse_wide[rows, :] = jnp.where(lane == head, top + jnp.log(total), lse_wide[rows, :])

    heads = width // HD
    pl.loop(0, heads // 2)(per_head)
    gd_1.wait_recv()
    gd_y = across(gd)
    d_near = file(gd.at[pl.ds(0, half)], d_v.at[pl.ds(0, half)])
    lu_2.wait_recv()
    lu_1 = second(lu.at[0])
    ld_y.wait_recv()
    ld_xy.wait_recv()
    ld_blocks = [(index, begin) for index in (0, 2) for begin in (0, half)]

    def ld_first(index, begin):
        return fly("z2", ld.at[index, pl.ds(begin, owned)], ld.at[index, pl.ds(begin + owned, owned)])

    ld_2 = [ld_first(*ld_blocks[0]), ld_first(*ld_blocks[1])]
    pl.loop(heads // 2, heads)(per_head)
    mixed_ref[...] = acc[:, :width].astype(jnp.bfloat16)
    lse_ref[...] = jnp.transpose(lse_wide[...])[: lse_ref.shape[0], :]

    def out_part(rel):
        at = pl.ds(pl.multiple_of(group_at(rel) * share, share), share)
        rows = mixed_ref[at, :]
        parts[rel, :, :half] = dot_transposed(rows, a_v[:half, 3 * width :]).astype(jnp.bfloat16)
        parts[rel, :, half:] = dot_transposed(rows, a_v[half:, 3 * width :]).astype(jnp.bfloat16)

    strip = share // 2
    strips = [pl.ds(at * strip, strip) for at in range(2)]

    def scatter(which, fill):
        fill(3)
        from_far = [fly("core", parts.at[3, rows], met_core.at[2 * which, rows]) for rows in strips]
        fill(2)
        fill(1)
        from_near = fly("core", parts.at[1], met_core.at[2 * which + 1])
        from_parts.extend(from_far + [from_near])
        fill(0)
        from_x = []
        for rows, one in zip(strips, from_far):
            one.wait_recv()
            total = parts[2, rows, :].astype(jnp.float32) + met_core[2 * which, rows, :].astype(jnp.float32)
            sends_x[which, rows, :] = total.astype(jnp.bfloat16)
            from_x.append(fly("x", sends_x.at[which, rows], met_x.at[which, rows]))
        from_near.wait_recv()
        return from_x

    def gathered(which, rows, base):
        return (
            base
            + parts[0, rows, :].astype(jnp.float32)
            + met_core[2 * which + 1, rows, :].astype(jnp.float32)
            + met_x[which, rows, :].astype(jnp.float32)
        )

    from_x = scatter(0, out_part)
    over_x = []
    for rows, one in zip(strips, from_x):
        one.wait_recv()
        total = gathered(0, rows, rows_ref[rows, :].astype(jnp.float32))
        middle_ref[rows, :] = total
        nb[rows, :] = norm_rows(total, gains_ref[1:2, :]).astype(jnp.bfloat16)
        over_x.append(fly("x", nb.at[rows], nb.at[pl.ds(2 * share + rows.start, strip)]))
    normed_core = fly("core", nb.at[pl.ds(0, share)], nb.at[pl.ds(share, share)])
    la_y.wait_recv()
    la_fx = over("x", la, 0, 2, start=half)
    la_fc = over("core", la, 0, 1, start=half)
    la_x.wait_recv()
    la_xc = over("core", la, 2, 3)
    lu_1.wait_recv()
    lu_x = over("x", lu, 0, 2)
    lu_y = across(lu.at[0])
    lu_c = over("core", lu, 0, 1)
    ld_1 = []
    for at in range(2):
        ld_2[at].wait_recv()
        index, begin = ld_blocks[at]
        ld_1.append(second(ld.at[index], begin))
        ld_2.append(ld_first(*ld_blocks[2 + at]))
    for one in over_x:
        one.wait_recv()
    normed_xc = fly("core", nb.at[pl.ds(2 * share, share)], nb.at[pl.ds(3 * share, share)])
    gu_y.wait_recv()
    u_far = file(gu.at[pl.ds(half, half)], u_v.at[pl.ds(half, half)])
    acc[...] = jnp.zeros_like(acc)
    normed_core.wait_recv()
    normed_xc.wait_recv()
    nb_out = file(nb, nb_h)
    gd_y.wait_recv()
    d_far = file(gd.at[pl.ds(half, half)], d_v.at[pl.ds(half, half)])
    for one in (u_near, u_far, d_near, d_far):
        one.wait()
    tile = 256
    hidden_out = []
    for at in range(u_v.shape[1] // tile):
        lanes = slice(at * tile, (at + 1) * tile)
        active, slope = gelu_both(both(nb[...], u_v[:half, lanes], u_v[half:, lanes]))
        act[:, lanes] = active
        slp[:, lanes] = slope
        for side in range(2):
            cols_at = slice(side * half, (side + 1) * half)
            acc[:, cols_at] += dot_transposed(active, d_v[side * half : (side + 1) * half, lanes])
        if at == 1:
            for which in (2, 3):
                ld_2[which].wait_recv()
                index, begin = ld_blocks[which]
                ld_1.append(second(ld.at[index], begin))
    hidden_out = [file(act, active_h), file(slp, slope_h)]

    def down_part(rel):
        parts[rel] = acc[rel * share : (rel + 1) * share, :].astype(jnp.bfloat16)

    for one in from_parts:
        one.wait_send()
        flying[:] = [other for other in flying if other is not one]
    from_x = scatter(1, down_part)
    la_fx.wait_recv()
    la_fxc = over("core", la, 2, 3, start=half)
    lu_x.wait_recv()
    lu_xy = across(lu.at[2])
    lu_xc = over("core", lu, 2, 3)
    for rows, one in zip(strips, from_x):
        one.wait_recv()
        out_ref[rows, :] = gathered(1, rows, middle_ref[rows, :])
    lu_y.wait_recv()
    lu_fc = over("core", lu, 0, 1, start=half)
    for one in ld_1[:2]:
        one.wait_recv()
    ld_c = over("core", ld, 0, 1, rows=D)
    for one in ld_1[2:]:
        one.wait_recv()
    ld_xc = over("core", ld, 2, 3, rows=D)
    lu_xy.wait_recv()
    lu_fxc = over("core", lu, 2, 3, start=half)
    for one in (la_c, la_fc, la_xc, la_fxc, lu_c, lu_fc, lu_xc, lu_fxc, ld_c, ld_xc):
        one.wait_recv()
    for one in [na_out, nb_out] + hidden_out:
        one.wait()
    for one in flying:
        one.wait_send()


def forward_global(line, info, rows, normed, gains, shards):
    share, owned = rows.shape[0], shards[0].shape[0]
    span, columns = 4 * share, shards[0].shape[1]
    width = columns // 4
    small = jnp.bfloat16
    weights = [shaped((D, columns), small)] * 3 + [shaped((4, D, columns), small)] * 3
    return line.run(
        forward_body,
        (info, rows, normed, gains, *shards),
        in_specs=[IN_SMEM] + [VMEM_WHOLE] * 3 + [IN_HBM] * 6,
        out_specs=[IN_HBM] * 6 + [VMEM_WHOLE] * 5 + [IN_HBM] * 4,
        out_shape=weights
        + [
            shaped((span, 3 * width), small),
            shaped((span, width), small),
            shaped((8, span), jnp.float32),
            shaped((share, D), jnp.float32),
            shaped((share, D), jnp.float32),
            shaped((span, D), small),
            shaped((span, D), small),
            shaped((span, columns), small),
            shaped((span, columns), small),
        ],
        scratch_shapes=[
            pltpu.VMEM((span, D), small),
            pltpu.VMEM((span, D), small),
            pltpu.VMEM((D, columns), small),
            pltpu.VMEM((D, columns), small),
            pltpu.VMEM((D, columns), small),
            pltpu.VMEM((span, D), jnp.float32),
            pltpu.VMEM((span, 128), jnp.float32),
            pltpu.VMEM((span, columns), small),
            pltpu.VMEM((span, columns), small),
            pltpu.VMEM((4, share, D), small),
            pltpu.VMEM((4, share, D), small),
            pltpu.VMEM((2, share, D), small),
            pltpu.VMEM((2, share, D), small),
            pltpu.SemaphoreType.DMA((20,)),
            pltpu.SemaphoreType.DMA((64,)),
            pltpu.SemaphoreType.DMA((64,)),
        ],
        hops=("core", "x", "y", "z1", "z2"),
        limit=56,
        name="forward_global",
    )


def backward_body(
    info_ref, small_ref, grad_ref, middle_ref, gains_ref, lse_ref, up_h, down_h, heads_h, active_h, slope_h,
    nb_h, na_h, qkv_h, mixed_h, u_near_h, u_far_h, d2_h, d0_h, h2_far_h, h0_far_h,
    mid_ref, sum_ref, gain_ref, gd_near_h, gd_met_h, gu_near_h, gu_far_h, gh_near_h, gh_far_h, lu_keep_h,
    lu_met_h, ld_keep_h, ld_met_h, h2_met_h, h0_met_h,
    rows_one, rows_two, up_v, down_v, heads_v, act, slp, dup, left_t, right_v, grads_v, qkv_v, mixed_v, dqkv,
    dmix, dq_t, dk_acc, dv_acc, center, k_t, parts, met_core, met_x, sends_x, u_v, u_met, d_v, d_met, z_met,
    sems, send, recv,
):
    share = small_ref.shape[0]
    half = D // 2
    quarter = half // 2
    owned = quarter // 2
    width = mixed_v.shape[1]
    heads = width // HD
    span = 4 * share
    length = info_ref[1]
    scale = HD ** (-0.5)
    numbers, flying, filed = [], [], []

    def fly(hop, source, target):
        at = len(numbers)
        copy = to_partner(hop, source, target, send.at[at], recv.at[at])
        copy.start()
        numbers.append(at)
        flying.append(copy)
        return copy

    def over(copy):
        copy.wait_send()
        flying[:] = [other for other in flying if other is not copy]

    def file(source, target):
        copy = pltpu.make_async_copy(source, target, sems.at[len(filed)])
        copy.start()
        filed.append(copy)
        return copy

    def block(rel):
        return slice(rel * share, (rel + 1) * share)

    def place(rel):
        return pl.ds(pl.multiple_of(group_at(rel) * share, share), share)

    def summed(*terms):
        total = terms[0].astype(jnp.float32)
        for term in terms[1:]:
            total = total + term.astype(jnp.float32)
        return total

    greet(("core", "x", "y", "z1", "z2"))
    small_x = fly("x", small_ref, rows_one.at[pl.ds(2 * share, share)])
    small_core = fly("core", small_ref, rows_one.at[pl.ds(share, share)])
    u_y = fly("y", u_far_h, u_met)
    d_first = fly("x", d2_h.at[pl.ds(0, quarter)], d_met.at[pl.ds(0, quarter)])
    h2_y = fly("y", h2_far_h, h2_met_h)
    h0_y = fly("y", h0_far_h, h0_met_h)
    first = [file(down_h, down_v), file(slope_h, slp), file(up_h, up_v)]
    active_in = file(active_h, act)
    nb_in = file(nb_h, right_v)
    u_in = file(u_near_h, u_v)
    attention_in = [file(heads_h, heads_v), file(qkv_h, qkv_v), file(mixed_h, mixed_v)]
    d_in = file(d0_h, d_v)
    rows_one[pl.ds(0, share), :] = small_ref[...]
    for one in first:
        one.wait()

    def ff_back(rel):
        rows = block(rel)
        for tile in range(2):
            lanes = slice(tile * half, (tile + 1) * half)
            grad = both(rows_one[rows, :], down_v[:half, lanes], down_v[half:, lanes])
            dup[rows, lanes] = (grad * slp[rows, lanes].astype(jnp.float32)).astype(jnp.bfloat16)
        for side in range(2):
            lanes = slice(side * half, (side + 1) * half)
            parts[rel, :, lanes] = dot_transposed(dup[rows, :], up_v[lanes, :]).astype(jnp.bfloat16)

    ff_back(0)
    small_core.wait_recv()
    ff_back(1)
    small_x.wait_recv()
    small_xc = fly("core", rows_one.at[pl.ds(2 * share, share)], rows_one.at[pl.ds(3 * share, share)])
    ff_back(2)
    small_xc.wait_recv()
    ff_back(3)
    strip = share // 2
    strips = [pl.ds(at * strip, strip) for at in range(2)]

    def scatter_start(which):
        from_far = [fly("core", parts.at[3, rows], met_core.at[2 * which, rows]) for rows in strips]
        return from_far, fly("core", parts.at[1], met_core.at[2 * which + 1])

    def scatter_on(which, from_far):
        from_x = []
        for rows, one in zip(strips, from_far):
            one.wait_recv()
            sends_x[which, rows, :] = summed(parts[2, rows, :], met_core[2 * which, rows, :]).astype(jnp.bfloat16)
            from_x.append(fly("x", sends_x.at[which, rows], met_x.at[which, rows]))
        return from_x

    def gathered(which, rows):
        return summed(parts[0, rows, :], met_core[2 * which + 1, rows, :], met_x[which, rows, :])

    from_far, from_near = scatter_start(0)
    for rel in range(4):
        left_t[:, block(rel)] = jnp.transpose(rows_one[block(rel), :])
    from_x = scatter_on(0, from_far)
    active_in.wait()
    for side in range(2):
        rows = slice(side * half, (side + 1) * half)
        for tile in range(2):
            lanes = slice(tile * half, (tile + 1) * half)
            grads_v[0, rows, lanes] = dot_rows(left_t[rows, :], act[:, lanes]).astype(jnp.bfloat16)
    gd_y = fly("y", grads_v.at[0, pl.ds(half, half)], gd_met_h)
    results = [file(grads_v.at[0, pl.ds(0, half)], gd_near_h)]
    from_near.wait_recv()
    gain_total = jnp.zeros((1, D), jnp.float32)
    over_x = []
    for rows, one in zip(strips, from_x):
        one.wait_recv()
        back, gain_grad = norm_rows_back(middle_ref[rows, :], gains_ref[1:2, :], gathered(0, rows))
        total = grad_ref[rows, :] + back
        mid_ref[rows, :] = total
        rows_two[rows, :] = total.astype(jnp.bfloat16)
        gain_total = gain_total + gain_grad
        over_x.append(fly("x", rows_two.at[rows], rows_two.at[pl.ds(2 * share + rows.start, strip)]))
    gain_ref[...] = gain_total
    small_core = fly("core", rows_two.at[pl.ds(0, share)], rows_two.at[pl.ds(share, share)])
    d_second = fly("x", d2_h.at[pl.ds(quarter, quarter)], d_met.at[pl.ds(quarter, quarter)])
    u_y.wait_recv()
    u_in.wait()
    u_v[...] = summed(u_v[...], u_met[...]).astype(jnp.bfloat16)
    u_1 = fly("z1", u_v.at[pl.ds(quarter, quarter)], z_met.at[0])
    nb_in.wait()
    left_t[...] = jnp.transpose(right_v[...])
    na_in = file(na_h, right_v)
    for side in range(2):
        rows = slice(side * half, (side + 1) * half)
        for tile in range(2):
            lanes = slice(tile * half, (tile + 1) * half)
            grads_v[1, rows, lanes] = dot_rows(left_t[rows, :], dup[:, lanes]).astype(jnp.bfloat16)
    results += [
        file(grads_v.at[1, pl.ds(0, half)], gu_near_h),
        file(grads_v.at[1, pl.ds(half, half)], gu_far_h),
    ]
    for one in attention_in:
        one.wait()

    def mix_back(rel):
        full = both(rows_two[block(rel), :], heads_v[:half, 3 * width :], heads_v[half:, 3 * width :])
        dmix[place(rel), :] = full.astype(jnp.bfloat16)

    head_of = lax.broadcasted_iota(jnp.int32, (1, width), 1) // HD
    pick = (
        lax.broadcasted_iota(jnp.int32, (8, width), 1) // HD
        == lax.broadcasted_iota(jnp.int32, (8, width), 0)
    ).astype(jnp.bfloat16)
    k_t[...] = jnp.transpose(qkv_v[:, width : 2 * width])
    dq_t[...] = jnp.zeros_like(dq_t)
    dk_acc[...] = jnp.zeros_like(dk_acc)
    dv_acc[...] = jnp.zeros_like(dv_acc)
    mix_back(0)
    small_core.wait_recv()
    mix_back(1)
    for one in over_x:
        one.wait_recv()
    small_xc = fly("core", rows_two.at[pl.ds(2 * share, share)], rows_two.at[pl.ds(3 * share, share)])
    mix_back(2)
    u_1.wait_recv()
    u_v[:quarter, :] = summed(u_v[:quarter, :], z_met[0]).astype(jnp.bfloat16)
    u_2 = fly("z2", u_v.at[pl.ds(owned, owned)], lu_met_h)
    results.append(file(u_v.at[pl.ds(0, owned)], lu_keep_h))
    small_xc.wait_recv()
    mix_back(3)
    product = dmix[...].astype(jnp.float32) * mixed_v[...].astype(jnp.float32)
    high = product.astype(jnp.bfloat16)
    low = (product - high.astype(jnp.float32)).astype(jnp.bfloat16)
    center[...] = dot_transposed(pick, high) + dot_transposed(pick, low)
    for head in range(heads):
        own_lanes = head_of == head
        for at in range(4):
            rows = block(at)
            reach = (at + 1) * share
            query = jnp.where(own_lanes, qkv_v[rows, :width] * scale, 0.0).astype(jnp.bfloat16)
            grad = jnp.where(own_lanes, dmix[rows, :], 0.0).astype(jnp.bfloat16)
            scores = dot_transposed(qkv_v[:reach, width : 2 * width], query)
            key_at = lax.broadcasted_iota(jnp.int32, scores.shape, 0)
            row_at = at * share + lax.broadcasted_iota(jnp.int32, scores.shape, 1)
            prob = jnp.where(
                (key_at <= row_at) & (key_at < length),
                jnp.exp(scores - lse_ref[head : head + 1, rows]),
                0.0,
            )
            dprob = dot_transposed(qkv_v[:reach, 2 * width :], grad)
            dscore = (prob * (dprob - center[head : head + 1, rows])).astype(jnp.bfloat16)
            dv_acc[:reach, :] += dot_rows(prob.astype(jnp.bfloat16), grad)
            dk_acc[:reach, :] += dot_rows(dscore, query)
            lanes = slice(head * HD, (head + 1) * HD)
            dq_t[lanes, rows] += dot_rows(k_t[lanes, :reach], dscore)
    dqkv[:, :width] = (jnp.transpose(dq_t[...]) * scale).astype(jnp.bfloat16)
    dqkv[:, width : 2 * width] = dk_acc[...].astype(jnp.bfloat16)
    dqkv[:, 2 * width :] = dv_acc[...].astype(jnp.bfloat16)
    d_in.wait()
    d_first.wait_recv()
    d_second.wait_recv()
    d_v[...] = summed(d_v[...], d_met[...]).astype(jnp.bfloat16)
    d_1 = fly("z1", d_v.at[pl.ds(quarter, quarter)], z_met.at[1])
    for one in from_far + [from_near]:
        over(one)

    def back_part(rel):
        rows = dqkv[place(rel), :]
        for side in range(2):
            lanes = slice(side * half, (side + 1) * half)
            parts[rel, :, lanes] = dot_transposed(rows, heads_v[lanes, : 3 * width]).astype(jnp.bfloat16)

    back_part(3)
    back_part(1)
    from_far, from_near = scatter_start(1)
    back_part(2)
    from_x = scatter_on(1, from_far)
    back_part(0)
    na_in.wait()
    for rel in range(4):
        left_t[:, place(rel)] = jnp.transpose(right_v[block(rel), :])
    over(gd_y)
    results[0].wait()
    for side in range(2):
        rows = slice(side * half, (side + 1) * half)
        grads_v[0, rows, : 3 * width] = dot_rows(left_t[rows, :], dqkv[...]).astype(jnp.bfloat16)
    for rel in range(4):
        left_t[:, place(rel)] = jnp.transpose(rows_two[block(rel), :])
    for side in range(2):
        rows = slice(side * half, (side + 1) * half)
        grads_v[0, rows, 3 * width :] = dot_rows(left_t[rows, :], mixed_v[...]).astype(jnp.bfloat16)
    results += [
        file(grads_v.at[0, pl.ds(0, half)], gh_near_h),
        file(grads_v.at[0, pl.ds(half, half)], gh_far_h),
    ]
    d_1.wait_recv()
    d_v[:quarter, :] = summed(d_v[:quarter, :], z_met[1]).astype(jnp.bfloat16)
    d_2 = fly("z2", d_v.at[pl.ds(owned, owned)], ld_met_h)
    results.append(file(d_v.at[pl.ds(0, owned)], ld_keep_h))
    from_near.wait_recv()
    for rows, one in zip(strips, from_x):
        one.wait_recv()
        sum_ref[rows, :] = gathered(1, rows)
    for one in (h2_y, h0_y, gd_y, u_2, d_2):
        one.wait_recv()
    for one in results[1:]:
        one.wait()
    for one in flying:
        one.wait_send()


def backward_global(line, info, small, grad, middle, gains, lse, weights, active, slope, nb, na, qkv, mixed, sums):
    share, columns = small.shape[0], active.shape[1]
    span, width = 4 * share, mixed.shape[1]
    half, owned = D // 2, D // 8
    low = jnp.bfloat16
    up, down, heads = weights
    return line.run(
        backward_body,
        (info, small, grad, middle, gains, lse, up, down, heads, active, slope, nb, na, qkv, mixed, *sums),
        in_specs=[IN_SMEM] + [VMEM_WHOLE] * 5 + [IN_HBM] * 15,
        out_specs=[VMEM_WHOLE] * 3 + [IN_HBM] * 12,
        out_shape=[
            shaped((share, D), jnp.float32),
            shaped((share, D), jnp.float32),
            shaped((1, D), jnp.float32),
        ]
        + [shaped((half, columns), low)] * 6
        + [shaped((owned, columns), low)] * 4
        + [shaped((half, columns), low)] * 2,
        scratch_shapes=[pltpu.VMEM((span, D), low)] * 2
        + [pltpu.VMEM((D, columns), low)] * 3
        + [pltpu.VMEM((span, columns), low)] * 3
        + [pltpu.VMEM((D, span), low), pltpu.VMEM((span, D), low), pltpu.VMEM((2, D, columns), low)]
        + [pltpu.VMEM((span, 3 * width), low), pltpu.VMEM((span, width), low), pltpu.VMEM((span, 3 * width), low)]
        + [
            pltpu.VMEM((span, width), low),
            pltpu.VMEM((width, span), jnp.float32),
            pltpu.VMEM((span, width), jnp.float32),
            pltpu.VMEM((span, width), jnp.float32),
            pltpu.VMEM((8, span), jnp.float32),
            pltpu.VMEM((width, span), low),
            pltpu.VMEM((4, share, D), low),
            pltpu.VMEM((4, share, D), low),
            pltpu.VMEM((2, share, D), low),
            pltpu.VMEM((2, share, D), low),
        ]
        + [pltpu.VMEM((half, columns), low)] * 4
        + [
            pltpu.VMEM((2, half // 2, columns), low),
            pltpu.SemaphoreType.DMA((24,)),
            pltpu.SemaphoreType.DMA((40,)),
            pltpu.SemaphoreType.DMA((40,)),
        ],
        hops=("core", "x", "y", "z1", "z2"),
        limit=56,
        name="backward_global",
    )


def head_sums(width):
    row_at = lax.broadcasted_iota(jnp.int32, (width, width), 0) // HD
    col_at = lax.broadcasted_iota(jnp.int32, (width, width), 1) // HD
    return (row_at == col_at).astype(jnp.bfloat16)


def over_heads(product, ones):
    high = product.astype(jnp.bfloat16)
    low = (product - high.astype(jnp.float32)).astype(jnp.bfloat16)
    return dot_rows(high, ones) + dot_rows(low, ones)


def frame_probs(queries, keys, ones):
    found = []
    for at in range(CB):
        scores = [over_heads(queries[at] * keys[c2], ones) * HD ** (-0.5) for c2 in range(at + 1)]
        top = scores[0]
        for one in scores[1:]:
            top = jnp.maximum(top, one)
        expanded = [jnp.exp(one - top) for one in scores]
        total = expanded[0]
        for one in expanded[1:]:
            total = total + one
        inverse = 1.0 / total
        found.append([one * inverse for one in expanded])
    return found


def rounded_f32(values):
    return values.astype(jnp.bfloat16).astype(jnp.float32)


def halves_of(stack):
    half = stack.shape[1] // 2
    return [(stack.at[at, pl.ds(0, half)], stack.at[at, pl.ds(half, half)]) for at in range(stack.shape[0])]


def start_weights(parts, buffer, sems):
    for at, pair in enumerate(parts):
        for half, ref in enumerate(pair):
            pltpu.make_async_copy(ref, buffer.at[at, half], sems.at[at, half]).start()


def wait_weights(parts, buffer, sems, at):
    for half in range(2):
        pltpu.make_async_copy(parts[0][half], buffer.at[at, half], sems.at[at, half]).wait()


def local_heads_body(
    out_ref_in, code_ref, gains_ref, *refs
):
    count = 4
    parts = halves_of(refs[0])
    qkv_ref, mixed_ref, middle_ref, normed_b_ref, a_t_ref, normed_a, local_in, buffer, sems = refs[1:]
    step = pl.program_id(0)
    frames = out_ref_in.shape[0]
    width = mixed_ref.shape[2]
    half = D // 2

    @pl.when(step == 0)
    def _():
        start_weights(parts, buffer, sems)
        for c in range(CB):
            rows = slice(c * frames, (c + 1) * frames)
            local_in[rows, :] = out_ref_in[...] + code_ref[rows, :].astype(jnp.float32)
            normed = norm_rows(local_in[rows, :], gains_ref[2:3, :]).astype(jnp.bfloat16)
            normed_a[rows, :] = normed
            a_t_ref[:, rows] = jnp.transpose(normed)
        middle_ref[...] = local_in[...]

    wait_weights(parts, buffer, sems, step)
    ones = head_sums(width)
    queries, keys, values = ([], [], [])
    for c in range(CB):
        rows = slice(c * frames, (c + 1) * frames)
        qkv = (
            dot_rows(normed_a[rows, :half], buffer[step, 0, :, : 3 * width])
            + dot_rows(normed_a[rows, half:], buffer[step, 1, :, : 3 * width])
        ).astype(jnp.bfloat16)
        qkv_ref[0, rows, :] = qkv
        queries.append(qkv[:, :width].astype(jnp.float32))
        keys.append(qkv[:, width : 2 * width].astype(jnp.float32))
        values.append(qkv[:, 2 * width :].astype(jnp.float32))
    prob = frame_probs(queries, keys, ones)
    for c in range(CB):
        rows = slice(c * frames, (c + 1) * frames)
        mix = rounded_f32(prob[c][0]) * values[0]
        for c2 in range(1, c + 1):
            mix = mix + rounded_f32(prob[c][c2]) * values[c2]
        mix = mix.astype(jnp.bfloat16)
        mixed_ref[0, rows, :] = mix
        for at in range(2):
            lanes = slice(at * half, (at + 1) * half)
            middle_ref[rows, lanes] += dot_transposed(mix, buffer[step, at, :, 3 * width :])

    @pl.when(step == count - 1)
    def _():
        for c in range(CB):
            rows = slice(c * frames, (c + 1) * frames)
            normed_b_ref[rows, :] = norm_rows(middle_ref[rows, :], gains_ref[3:4, :]).astype(
                jnp.bfloat16
            )


def local_heads(line, global_out, codes, gains, parts):
    frames = global_out.shape[0]
    rows = CB * frames
    width = parts.shape[2] // 4
    half = D // 2
    return line.run(
        local_heads_body,
        (global_out, codes, gains, parts),
        grid=(4,),
        in_specs=[held((frames, D)), held((rows, D)), held((4, D)), IN_HBM],
        out_specs=[
            pl.BlockSpec((1, rows, 3 * width), lambda step: (step, 0, 0)),
            pl.BlockSpec((1, rows, width), lambda step: (step, 0, 0)),
            held((rows, D)),
            held((rows, D)),
            held((D, rows)),
        ],
        out_shape=[
            shaped((4, rows, 3 * width), jnp.bfloat16),
            shaped((4, rows, width), jnp.bfloat16),
            shaped((rows, D), jnp.float32),
            shaped((rows, D), jnp.bfloat16),
            shaped((D, rows), jnp.bfloat16),
        ],
        scratch_shapes=[
            pltpu.VMEM((rows, D), jnp.bfloat16),
            pltpu.VMEM((rows, D), jnp.float32),
            pltpu.VMEM((4, 2, half, 4 * width), jnp.bfloat16),
            pltpu.SemaphoreType.DMA((4, 2)),
        ],
        limit=(52),
        name="local_heads",
    )


def local_ff_body(source_ref, normed_ref, middle_ref, *refs):
    count = 4
    ups, downs = halves_of(refs[0]), halves_of(refs[1])
    active_ref, slope_ref, out_ref, b_t_ref, acc, up_buf, down_buf, up_sems, down_sems = refs[2:]
    step = pl.program_id(0)
    rows_all = normed_ref.shape[0]
    frames = rows_all // CB
    half = D // 2
    tile = active_ref.shape[2]
    per = up_buf.shape[3] // tile
    group = step // per
    cols_at = pl.ds(pl.multiple_of((step % per) * tile, tile), tile)

    @pl.when(step == 0)
    def _():
        for at in range(count):
            start_weights_at(ups, up_buf, up_sems, at)
            start_weights_at(downs, down_buf, down_sems, at)
        b_t_ref[...] = jnp.transpose(normed_ref[...])
        acc[...] = middle_ref[...]

    @pl.when(step % per == 0)
    def _():
        wait_weights(ups, up_buf, up_sems, group)
        wait_weights(downs, down_buf, down_sems, group)

    for c in range(CB):
        rows = slice(c * frames, (c + 1) * frames)
        upper = dot_rows(normed_ref[rows, :half], up_buf[group, 0, :, cols_at]) + dot_rows(
            normed_ref[rows, half:], up_buf[group, 1, :, cols_at]
        )
        active, slope = gelu_both(upper)
        active_ref[0, rows, :] = active
        slope_ref[0, rows, :] = slope
        for at in range(2):
            lanes = slice(at * half, (at + 1) * half)
            acc[rows, lanes] += dot_transposed(active, down_buf[group, at, :, cols_at])

    @pl.when(step == pl.num_programs(0) - 1)
    def _():
        owned = D // source_ref.shape[0]
        for c in range(CB):
            rows = slice(c * frames, (c + 1) * frames)
            for at in range(source_ref.shape[0]):
                here = slice(at * owned, (at + 1) * owned)
                out_ref[c, :, lanes_of(source_ref, at, owned)] = acc[rows, here].astype(jnp.bfloat16)


def start_weights_at(parts, buffer, sems, at):
    for half in range(2):
        pltpu.make_async_copy(parts[at][half], buffer.at[at, half], sems.at[at, half]).start()


def local_ff(line, source, normed, middle, ups, downs, tile=512):
    rows = normed.shape[0]
    hidden = ups.shape[2]
    half = D // 2
    per = hidden // tile
    hidden_block = pl.BlockSpec((1, rows, tile), lambda step: (step // per, 0, step % per))
    return line.run(
        local_ff_body,
        (source, normed, middle, ups, downs),
        grid=(4 * per,),
        in_specs=[IN_SMEM, held((rows, D)), held((rows, D)), IN_HBM, IN_HBM],
        out_specs=[hidden_block, hidden_block, held((CB, rows // CB, D)), held((D, rows))],
        out_shape=[
            shaped((4, rows, hidden), jnp.bfloat16),
            shaped((4, rows, hidden), jnp.bfloat16),
            shaped((CB, rows // CB, D), jnp.bfloat16),
            shaped((D, rows), jnp.bfloat16),
        ],
        scratch_shapes=[
            pltpu.VMEM((rows, D), jnp.float32),
            pltpu.VMEM((4, 2, half, hidden), jnp.bfloat16),
            pltpu.VMEM((4, 2, half, hidden), jnp.bfloat16),
            pltpu.SemaphoreType.DMA((4, 2)),
            pltpu.SemaphoreType.DMA((4, 2)),
        ],
        limit=(56),
        name="local_ff",
    )


def seed_body(source_ref, count_ref, cot_ref, code_ref, grad_ref, grad_t_ref, codes_ref):
    frames = cot_ref.shape[1]
    owned = D // source_ref.shape[0]
    keep = lax.broadcasted_iota(jnp.int32, (frames, 1), 0) < count_ref[0]
    for c in range(CB):
        rows = slice(c * frames, (c + 1) * frames)
        for at in range(source_ref.shape[0]):
            here = slice(at * owned, (at + 1) * owned)
            values = cot_ref[c, :, lanes_of(source_ref, at, owned)].astype(jnp.float32)
            grad_ref[rows, here] = jnp.where(keep, values, 0.0).astype(jnp.bfloat16)
            codes_ref[rows, here] = code_ref[c, :, lanes_of(source_ref, at, owned)]
        grad_t_ref[:, rows] = jnp.transpose(grad_ref[rows, :])


def seed(line, source, count, cot, codes):
    frames = cot.shape[1]
    rows = CB * frames
    return line.run(
        seed_body,
        (source, count, cot, codes),
        in_specs=[IN_SMEM, IN_SMEM, VMEM_WHOLE, VMEM_WHOLE],
        out_specs=[VMEM_WHOLE] * 3,
        out_shape=[
            shaped((rows, D), jnp.bfloat16),
            shaped((D, rows), jnp.bfloat16),
            shaped((rows, D), jnp.bfloat16),
        ],
        limit=(24),
        name="seed_grads",
    )


def local_back_body(
    grad_h, grad_t_h, b_t_h, a_t_h, active_h, slope_h, qkv_h, mixed_h, middle_h, gout_h, codes_h, gains_ref, *refs
):
    heads_h, ups_h, downs_h = ([half for pair in halves_of(one) for half in pair] for one in refs[:3])
    refs = refs[3:]
    total_ref, small_out_ref, gain_c_ref, gain_d_ref, *results_h = refs[:12]
    (
        grad_v, grad_t, other_t, weights, act, slp, dup, acc, mid, gout_v, codes_v,
        pair_out, pair_far, pair_near, head_out, head_far, head_near, x_in, y_far, y_near,
        sems, send, recv,
    ) = refs[12:]
    frames = gout_v.shape[0]
    rows_all = grad_v.shape[0]
    half = D // 2
    width = mixed_h.shape[2]
    scale = HD ** (-0.5)
    greet(("core", "x", "y"))

    def fetch(at, source, target):
        copy = pltpu.make_async_copy(source, target, sems.at[at])
        copy.start()
        return copy

    def give(at, hop, source, target):
        copy = to_partner(hop, source, target, send.at[at], recv.at[at])
        copy.start()
        return copy

    def fetch_ff(rel):
        found = [fetch(at, downs_h[2 * rel + at], weights.at[2 + at]) for at in range(2)]
        found.append(fetch(2, slope_h.at[rel], slp))
        return found + [fetch(3 + at, ups_h[2 * rel + at], weights.at[at]) for at in range(2)]

    order = (3, 1, 2, 0)
    waits = [fetch(5, grad_h, grad_v)] + fetch_ff(order[0])
    late = [fetch(6, grad_t_h, grad_t), fetch(7, active_h.at[order[0]], act), fetch(8, b_t_h, other_t)]
    later = [fetch(9, middle_h, mid), fetch(10, gout_h, gout_v), fetch(11, codes_h, codes_v)]
    acc[...] = jnp.zeros_like(acc)
    sent = []
    for step, rel in enumerate(order):
        for one in waits:
            one.wait()
        for tile in range(2):
            lanes = slice(tile * half, (tile + 1) * half)
            grad = dot_rows(grad_v[:, :half], weights[2, :, lanes]) + dot_rows(
                grad_v[:, half:], weights[3, :, lanes]
            )
            dup[:, lanes] = (grad * slp[:, lanes].astype(jnp.float32)).astype(jnp.bfloat16)
        for at in range(2):
            lanes = slice(at * half, (at + 1) * half)
            acc[:, lanes] += dot_transposed(dup[...], weights[at])
        if step < 3:
            waits = fetch_ff(order[step + 1])
        for one in late:
            one.wait()
        if step == 1:
            sent[0].wait_send()
        if step >= 2:
            sent[step - 2].wait_recv()
        met = (None, None, pair_far, pair_near)[step]
        for at in range(2):
            rows = slice(at * half, (at + 1) * half)
            for tile in range(2):
                lanes = slice(tile * half, (tile + 1) * half)
                down = dot_rows(grad_t[rows, :], act[:, lanes])
                up = dot_rows(other_t[rows, :], dup[:, lanes])
                if met is None:
                    pair_out[0, rows, lanes] = down.astype(jnp.bfloat16)
                    pair_out[1, rows, lanes] = up.astype(jnp.bfloat16)
                else:
                    met[0, rows, lanes] = (down + met[0, rows, lanes].astype(jnp.float32)).astype(jnp.bfloat16)
                    met[1, rows, lanes] = (up + met[1, rows, lanes].astype(jnp.float32)).astype(jnp.bfloat16)
        if step < 3:
            late = [fetch(7, active_h.at[order[step + 1]], act)]
        if step == 0:
            sent.append(give(0, "core", pair_out, pair_far))
        elif step == 1:
            sent.append(give(1, "core", pair_out, pair_near))
        elif step == 2:
            x_far = give(2, "x", pair_far.at[1, pl.ds(half, half)], x_in.at[pl.ds(half, half)])
            y_two = give(3, "y", pair_far.at[0, pl.ds(half, half)], y_far)
            x_near = give(4, "x", pair_far.at[1, pl.ds(0, half)], x_in.at[pl.ds(0, half)])
        else:
            y_zero = give(5, "y", pair_near.at[0, pl.ds(half, half)], y_near)

    def fetch_heads(rel):
        found = [fetch(at, heads_h[2 * rel + at], weights.at[at]) for at in range(2)]
        found.append(fetch(2, qkv_h.at[rel], act.at[:, pl.ds(0, 3 * width)]))
        return found + [fetch(3, mixed_h.at[rel], slp.at[:, pl.ds(0, width)])]

    waits = fetch_heads(order[0]) + [fetch(8, a_t_h, other_t)]
    sent[1].wait_send()
    for one in later:
        one.wait()
    total_gain = jnp.zeros((1, D), jnp.float32)
    for c in range(CB):
        rows = slice(c * frames, (c + 1) * frames)
        part_back, gain_grad = norm_rows_back(mid[rows, :], gains_ref[3:4, :], acc[rows, :])
        total = grad_v[rows, :].astype(jnp.float32) + part_back
        mid[rows, :] = total
        small = total.astype(jnp.bfloat16)
        grad_v[rows, :] = small
        grad_t[:, rows] = jnp.transpose(small)
        total_gain = total_gain + gain_grad
    gain_d_ref[...] = total_gain

    ones = head_sums(width)
    heads_sent = []

    def more(total, term):
        return term if total is None else total + term

    for step, rel in enumerate(order):
        for one in waits:
            one.wait()
        queries, keys, values, dmix = ([], [], [], [])
        back = rounded_f32(
            dot_rows(grad_v[:, :half], weights[0, :, 3 * width :])
            + dot_rows(grad_v[:, half:], weights[1, :, 3 * width :])
        )
        for c in range(CB):
            rows = slice(c * frames, (c + 1) * frames)
            qkv = act[rows, : 3 * width].astype(jnp.float32)
            queries.append(qkv[:, :width])
            keys.append(qkv[:, width : 2 * width])
            values.append(qkv[:, 2 * width :])
            dmix.append(back[rows, :])
        prob = frame_probs(queries, keys, ones)
        dq, dk, dv = ([None] * CB, [None] * CB, [None] * CB)
        for c in range(CB):
            dprob = [over_heads(dmix[c] * values[c2], ones) for c2 in range(c + 1)]
            center = prob[c][0] * dprob[0]
            for c2 in range(1, c + 1):
                center = center + prob[c][c2] * dprob[c2]
            for c2 in range(c + 1):
                dv[c2] = more(dv[c2], rounded_f32(prob[c][c2]) * dmix[c])
                dscore = rounded_f32(prob[c][c2] * (dprob[c2] - center))
                dq[c] = more(dq[c], dscore * keys[c2])
                dk[c2] = more(dk[c2], dscore * queries[c])
        for c in range(CB):
            rows = slice(c * frames, (c + 1) * frames)
            dup[rows, :width] = (dq[c] * scale).astype(jnp.bfloat16)
            dup[rows, width : 2 * width] = (dk[c] * scale).astype(jnp.bfloat16)
            dup[rows, 2 * width : 3 * width] = dv[c].astype(jnp.bfloat16)
        for at in range(2):
            lanes = slice(at * half, (at + 1) * half)
            term = dot_transposed(dup[:, : 3 * width], weights[at, :, : 3 * width])
            acc[:, lanes] = term if step == 0 else acc[:, lanes] + term
        if step == 1:
            heads_sent[0].wait_send()
        if step >= 2:
            heads_sent[step - 2].wait_recv()
        met = (None, None, head_far, head_near)[step]
        for at in range(2):
            rows = slice(at * half, (at + 1) * half)
            three = dot_rows(other_t[rows, :], dup[:, : 3 * width])
            one = dot_rows(grad_t[rows, :], slp[:, :width])
            if met is None:
                head_out[rows, : 3 * width] = three.astype(jnp.bfloat16)
                head_out[rows, 3 * width :] = one.astype(jnp.bfloat16)
            else:
                three = three + met[rows, : 3 * width].astype(jnp.float32)
                one = one + met[rows, 3 * width :].astype(jnp.float32)
                met[rows, : 3 * width] = three.astype(jnp.bfloat16)
                met[rows, 3 * width :] = one.astype(jnp.bfloat16)
        if step < 3:
            waits = fetch_heads(order[step + 1])
        if step == 0:
            heads_sent.append(give(6, "core", head_out, head_far))
        elif step == 1:
            heads_sent.append(give(7, "core", head_out, head_near))
    total_gain = jnp.zeros((1, D), jnp.float32)
    total = jnp.zeros((frames, D), jnp.float32)
    for c in range(CB):
        rows = slice(c * frames, (c + 1) * frames)
        local_in = gout_v[...] + codes_v[rows, :].astype(jnp.float32)
        part_back, gain_grad = norm_rows_back(local_in, gains_ref[2:3, :], acc[rows, :])
        total = total + (mid[rows, :] + part_back)
        total_gain = total_gain + gain_grad
    total_ref[...] = total
    small_out_ref[...] = total.astype(jnp.bfloat16)
    gain_c_ref[...] = total_gain

    heads_sent[1].wait_send()
    x_far.wait()
    x_near.wait()
    y_two.wait()
    y_zero.wait()

    def summed(one, two):
        return (one.astype(jnp.float32) + two.astype(jnp.float32)).astype(jnp.bfloat16)

    pair_near[1] = summed(pair_near[1], x_in[...])
    pair_far[0, :half, :] = summed(pair_far[0, :half, :], y_far[...])
    pair_near[0, :half, :] = summed(pair_near[0, :half, :], y_near[...])
    near, far = pl.ds(0, half), pl.ds(half, half)
    leaving = (
        pair_near.at[1, near], pair_near.at[1, far], pair_far.at[0, near], pair_near.at[0, near],
        head_far.at[near], head_far.at[far], head_near.at[near], head_near.at[far],
    )
    for one in [fetch(at, source, target) for at, (source, target) in enumerate(zip(leaving, results_h))]:
        one.wait()


def local_back(line, grad, grad_t, b_t, a_t, active, slope, qkv, mixed, middle, global_out, codes, gains, heads, ups, downs):
    rows, frames = grad.shape[0], global_out.shape[0]
    half = D // 2
    columns = ups.shape[2]
    small = jnp.bfloat16
    return line.run(
        local_back_body,
        (grad, grad_t, b_t, a_t, active, slope, qkv, mixed, middle, global_out, codes, gains, heads, ups, downs),
        in_specs=[IN_HBM] * 11 + [VMEM_WHOLE] + [IN_HBM] * 3,
        out_specs=[VMEM_WHOLE] * 4 + [IN_HBM] * 8,
        out_shape=[
            shaped((frames, D), jnp.float32),
            shaped((frames, D), small),
            shaped((1, D), jnp.float32),
            shaped((1, D), jnp.float32),
        ]
        + [shaped((half, columns), small)] * 8,
        scratch_shapes=[
            pltpu.VMEM((rows, D), small),
            pltpu.VMEM((D, rows), small),
            pltpu.VMEM((D, rows), small),
            pltpu.VMEM((4, half, columns), small),
            pltpu.VMEM((rows, columns), small),
            pltpu.VMEM((rows, columns), small),
            pltpu.VMEM((rows, columns), small),
            pltpu.VMEM((rows, D), jnp.float32),
            pltpu.VMEM((rows, D), jnp.float32),
            pltpu.VMEM((frames, D), jnp.float32),
            pltpu.VMEM((rows, D), small),
            pltpu.VMEM((2, D, columns), small),
            pltpu.VMEM((2, D, columns), small),
            pltpu.VMEM((2, D, columns), small),
            pltpu.VMEM((D, columns), small),
            pltpu.VMEM((D, columns), small),
            pltpu.VMEM((D, columns), small),
            pltpu.VMEM((D, columns), small),
            pltpu.VMEM((half, columns), small),
            pltpu.VMEM((half, columns), small),
            pltpu.SemaphoreType.DMA((12,)),
            pltpu.SemaphoreType.DMA((8,)),
            pltpu.SemaphoreType.DMA((8,)),
        ],
        hops=("core", "x", "y"),
        limit=58,
        name="local_back",
    )


def add_body(*refs):
    total = refs[0][...].astype(jnp.float32)
    for ref in refs[1:-1]:
        total = total + ref[...].astype(jnp.float32)
    refs[-1][...] = total.astype(jnp.bfloat16)


def add_rows(line, terms, part=0, parts=1):
    rows = min(term.shape[0] for term in terms) if parts == 1 else terms[0].shape[0] // parts
    columns = terms[0].shape[1]

    def spec(term):
        return pl.BlockSpec(
            (rows, columns), (lambda step: (part, 0)) if term.shape[0] > rows else (lambda step: (0, 0))
        )

    return line.run(
        add_body,
        tuple(terms),
        grid=(1,),
        in_specs=[spec(term) for term in terms],
        out_specs=[pl.BlockSpec((rows, columns), lambda step: (0, 0))],
        out_shape=[shaped((rows, columns), jnp.bfloat16)],
        limit=(24),
        name="add_terms",
    )[0]


def sum_pieces(line, terms, split=()):
    rows, columns = terms[0].shape[0] // 2, terms[0].shape[1]
    whole = len(terms)
    flat = list(terms) + [one for pair in split for one in pair]

    def body(*refs):
        for at, out_ref in enumerate(refs[-2:]):
            here = slice(at * rows, (at + 1) * rows)
            total = refs[0][here, :].astype(jnp.float32)
            for ref in refs[1:whole]:
                total = total + ref[here, :].astype(jnp.float32)
            for ref in refs[whole + at : -2 : 2]:
                total = total + ref[...].astype(jnp.float32)
            out_ref[...] = total.astype(jnp.bfloat16)

    return line.run(
        body,
        tuple(flat),
        in_specs=[VMEM_WHOLE] * len(flat),
        out_specs=[VMEM_WHOLE] * 2,
        out_shape=[shaped((rows, columns), jnp.bfloat16)] * 2,
        limit=24,
        name="sum_pieces",
    )


def pass_body(*refs):
    pass


def in_turn(line, *values):
    return line.run(
        pass_body,
        tuple(values),
        in_specs=[IN_HBM] * len(values),
        out_specs=[IN_HBM] * len(values),
        out_shape=[shaped(one.shape, one.dtype) for one in values],
        aliases={at: at for at in range(len(values))},
        name="in_turn",
    )


def split_dot(left, right):
    left_high = left.astype(jnp.bfloat16)
    left_low = (left - left_high.astype(jnp.float32)).astype(jnp.bfloat16)
    right_high = right.astype(jnp.bfloat16)
    right_low = (right - right_high.astype(jnp.float32)).astype(jnp.bfloat16)
    return (
        dot_rows(left_high, right_high) + dot_rows(left_high, right_low) + dot_rows(left_low, right_high)
    )


def adam_body(chained, one_ref, two_ref, left_ref, right_ref, master_ref, first_ref, second_ref, ema_ref, *refs):
    grads_ref, new_master_ref, new_first_ref, new_second_ref, new_ema_ref = refs[5:] if chained else refs
    left = left_ref[0]
    left_t = jnp.transpose(left)
    grads = one_ref[...].astype(jnp.float32) + two_ref[...].astype(jnp.float32)
    grads_ref[0] = grads
    turned_left = split_dot(left_t, grads)
    back = []
    for at in range(right_ref.shape[1]):
        tile = slice(at * 128, (at + 1) * 128)
        right = right_ref[0, at]
        rotated = split_dot(turned_left[:, tile], right)
        new_first = beta_first * first_ref[0, :, tile] + (1.0 - beta_first) * rotated
        new_second = beta_second * second_ref[0, :, tile] + (1.0 - beta_second) * rotated * rotated
        new_first_ref[0, :, tile] = new_first
        new_second_ref[0, :, tile] = new_second
        turned = new_first / (jnp.sqrt(new_second) + adam_eps)
        back.append(split_dot(turned, jnp.transpose(right)))
    back_full = split_dot(left, jnp.concatenate(back, axis=1))
    new_master = master_ref[0] - step_rate * back_full
    new_master_ref[0] = new_master
    new_ema_ref[0] = ema_decay * ema_ref[0] + (1.0 - ema_decay) * new_master


def adam(line, layer, third, pieces, left, right, master, first, second, ema, before, tile=256):
    owned, columns = pieces[0].shape
    steps = columns // tile
    first_step = third * steps

    def state(step):
        return (layer, 0, first_step + step)

    state_spec = pl.BlockSpec((1, owned, tile), state)
    chained = before is not None
    return line.run(
        lambda *refs: adam_body(chained, *refs),
        (*pieces, left, right, master, first, second, ema, *(before or ()),),
        grid=(steps,),
        in_specs=[by_cols((owned, tile))] * 2
        + [
            pl.BlockSpec((1,) + left.shape[1:], lambda step: (layer, 0, 0)),
            pl.BlockSpec(
                (1, tile // 128) + right.shape[2:], lambda step: (layer, first_step + step, 0, 0)
            ),
        ]
        + [state_spec] * 4
        + ([IN_HBM] * 5 if chained else []),
        out_specs=[state_spec] * 5,
        out_shape=[shaped(master.shape, jnp.float32)] * 5,
        aliases={8 + at: at for at in range(5)} if chained else {},
        limit=(32),
        name="adam_update",
    )


def hop_x(values):
    return lax.ppermute(values, "tensor", [(at, at ^ 2) for at in range(4)])


def hop_core(values):
    return lax.ppermute(values, "tensor", [(at, at ^ 1) for at in range(4)])


def hop_y(values):
    return lax.ppermute(values, "dp", [(at, at ^ 1) for at in range(8)])


def hop_z(values, step):
    return lax.ppermute(values, "dp", [(at, at ^ (2 * step)) for at in range(8)])


def total_everywhere(values):
    for hop in (hop_core, hop_x, hop_y):
        values = values + hop(values)
    for step in (1, 2):
        values = values + hop_z(values, step)
    return values


def shards_grid(
    frames_in,
    code_emb,
    cotangent,
    lengths,
    owner_list,
    master,
    first_moment,
    second_moment,
    ema,
    left_basis,
    right_basis,
    gains,
    gain_first,
    gain_second,
):
    share = frames_in.shape[0]
    owned = master.shape[1]
    groups = D // owned
    heads_w = D // lax.axis_size("tensor")
    ff_w = FF // lax.axis_size("tensor")
    my_dp = lax.axis_index("dp")
    my_group = lax.axis_index("tensor").astype(jnp.int32)

    rel = jnp.array([2 * z + y for y in range(2) for z in (0, 2, 1, 3)], jnp.int32)
    owner_at = my_dp ^ rel
    slots = jnp.arange(groups, dtype=jnp.int32)
    source = jnp.sum(
        jnp.where(owner_list[None, :] == owner_at[:, None], slots[None, :], 0), axis=1
    ).astype(jnp.int32)
    info = jnp.stack([my_group, lengths[0]])
    count = (lengths - my_group * share).astype(jnp.int32)

    line = Line()
    codes = jnp.transpose(code_emb, (1, 0, 2))

    (rows_in, gains_here, normed), shards = prep(line, source, frames_in, gains, master)
    grad, grad_t, codes_here = seed(line, source, count, jnp.transpose(cotangent, (1, 0, 2)), codes)
    (
        g_heads, g_up, g_down, l_heads, l_up, l_down, qkv, mixed, lse, middle, global_out, normed_a, normed_b,
        active, slope,
    ) = forward_global(line, info, rows_in, normed, gains_here, shards)

    l_qkv, l_mixed, l_middle, l_normed_b, l_a_t = local_heads(
        line, global_out, codes_here, gains_here, l_heads
    )
    l_active, l_slope, local_out, l_b_t = local_ff(line, source, l_normed_b, l_middle, l_up, l_down)
    local_out = jnp.transpose(local_out, (1, 0, 2))

    (
        grad_global, small, gain_c, gain_d, u_near, u_far, d2, d0, h2_near, h2_far, h0_near, h0_far,
    ) = local_back(
        line, grad, grad_t, l_b_t, l_a_t, l_active, l_slope, l_qkv, l_mixed, l_middle, global_out, codes_here,
        gains_here, l_heads, l_up, l_down,
    )
    def update(layer, third, pieces, before):
        return adam(
            line, layer, third, pieces, left_basis, right_basis, master, first_moment, second_moment, ema, before
        )

    def depth_first(terms, split=()):
        keep, send = sum_pieces(line, terms, split)
        return keep, hop_z(send, 1)

    def depth_second(keep, met):
        keep, send = sum_pieces(line, [keep, met])
        return keep, hop_z(send, 2)

    (
        grad_middle, grad_sum, gain_b, gd_near, gd_met, gu_near, gu_far, gh_near, gh_far, lu_keep, lu_met, ld_keep,
        ld_met, h2_met, h0_met,
    ) = backward_global(
        line, info, small, grad_global, middle, gains_here, lse, (g_up, g_down, g_heads), active, slope, normed_b,
        normed_a, qkv, mixed, (u_near, u_far, d2, d0, h2_far, h0_far),
    )
    gu_met = hop_y(gu_far)
    gh_met = hop_y(gh_far)
    h2 = hop_x(add_rows(line, [h2_near, h2_met]))
    gd = depth_first([gd_near, gd_met])
    input_grad, gain_grads = finish(
        line, source, rows_in, grad_sum, grad_middle, gains_here, (gain_b, gain_c, gain_d)
    )
    gain_grads = total_everywhere(gain_grads)
    found = update(1, 1, (lu_keep, lu_met), None)
    gd = depth_second(*gd)
    found = update(1, 2, (ld_keep, ld_met), found)
    lh = depth_first([h0_near, h0_met, h2])
    gu = depth_first([gu_near, gu_met])
    found = update(0, 2, gd, found)
    lh = depth_second(*lh)
    gu = depth_second(*gu)
    gh = depth_first([gh_near, gh_met])
    found = update(1, 0, lh, found)
    found = update(0, 1, gu, found)
    gh = depth_second(*gh)
    found = update(0, 0, gh, found)
    weight_grads, new_master, new_first, new_second, new_ema = found
    new_gain_first = beta_first * gain_first + (1.0 - beta_first) * gain_grads
    new_gain_second = beta_second * gain_second + (1.0 - beta_second) * gain_grads * gain_grads
    new_gains = gains - gain_rate * new_gain_first / (jnp.sqrt(new_gain_second) + adam_eps)
    return (
        local_out,
        input_grad,
        weight_grads,
        gain_grads,
        new_master,
        new_first,
        new_second,
        new_ema,
        new_gains,
        new_gain_first,
        new_gain_second,
    )


def solution(mesh):
    fits = mesh.shape["dp"] == 8 and mesh.shape["tensor"] == 4
    return jax.shard_map(
        shards_grid if fits else shards_any,
        mesh=mesh,
        in_specs=(
            P(("dp", "tensor"), None),
            P(("dp", "tensor"), None, None),
            P(("dp", "tensor"), None, None),
            P("dp"),
            P(),
            P(None, "dp", "tensor"),
            P(None, "dp", "tensor"),
            P(None, "dp", "tensor"),
            P(None, "dp", "tensor"),
            P(None, "dp", "tensor"),
            P(None, "dp", None, "tensor"),
            P(),
            P(),
            P(),
        ),
        out_specs=(
            P(("dp", "tensor"), None, None),
            P(("dp", "tensor"), None),
            P(None, "dp", "tensor"),
            P(),
            P(None, "dp", "tensor"),
            P(None, "dp", "tensor"),
            P(None, "dp", "tensor"),
            P(None, "dp", "tensor"),
            P(),
            P(),
            P(),
        ),
        check_vma=False,
    )
```

```python
import math

import jax
import jax.numpy as jnp
from jax import lax
from jax.experimental import pallas as pl
from jax.experimental.pallas import tpu as pltpu
from jax.sharding import PartitionSpec as P

DP, TENSOR = "dp", "tensor"
D = 1024
HD = 64
FF = 4096
CB = 3
LMAX = 1024


norm_eps = 1e-06
beta_first = 0.5
beta_second = 0.5
adam_eps = 1e-08
step_rate = 0.05
gain_rate = 0.4
ema_decay = 0.9
masked_fill = -1e30
highest = lax.Precision.HIGHEST


def dot_rows(left, right):
    return jnp.dot(left, right, preferred_element_type=jnp.float32)


def dot_transposed(left, right):
    return lax.dot_general(
        left, right, (((1,), (1,)), ((), ())), preferred_element_type=jnp.float32
    )


def dot_over_rows(left, right):
    return lax.dot_general(
        left, right, (((0,), (0,)), ((), ())), preferred_element_type=jnp.float32
    )


def keep_rows(values):
    return values


def row_term(operand, weight):
    return dot_transposed(operand, weight)


def rms_forward(rows_in, gain):
    return (
        rows_in * lax.rsqrt(jnp.mean(rows_in * rows_in, axis=-1, keepdims=True) + norm_eps) * gain
    )


def rms_backward(rows_in, gain, grad_out):
    width = rows_in.shape[-1]
    scale_rows = lax.rsqrt(jnp.mean(rows_in * rows_in, axis=-1, keepdims=True) + norm_eps)
    scaled_grad = grad_out * gain
    inner_total = jnp.sum(scaled_grad * rows_in, axis=-1, keepdims=True)
    grad_in = (
        scale_rows * scaled_grad
        - rows_in * (scale_rows * scale_rows * scale_rows) * inner_total / width
    )
    gain_grad = jnp.sum(grad_out * rows_in * scale_rows, axis=0)
    return (grad_in, gain_grad)


def gelu_slope(upper):
    normal_cdf = 0.5 * (1.0 + lax.erf(upper * (1.0 / math.sqrt(2.0))))
    density = jnp.exp(-0.5 * upper * upper) * (1.0 / math.sqrt(2.0 * math.pi))
    return normal_cdf + upper * density


def split_layer(layer_cols, groups, head_cols, ff_cols):
    width = layer_cols.shape[0]
    grouped = layer_cols.reshape(width, groups, -1)

    def columns(begin, extent):
        return grouped[:, :, begin : begin + extent].reshape(width, groups * extent)

    w_qkv = jnp.concatenate(
        [columns(0, head_cols), columns(head_cols, head_cols), columns(2 * head_cols, head_cols)],
        axis=1,
    )
    return (
        w_qkv,
        columns(3 * head_cols, head_cols),
        columns(4 * head_cols, ff_cols),
        columns(4 * head_cols + ff_cols, ff_cols),
    )


def join_layer(grad_parts, groups):
    grad_qkv, grad_out, grad_up, grad_down = grad_parts
    width = grad_qkv.shape[0]
    head_width = grad_qkv.shape[1] // 3
    pieces = [
        grad_qkv[:, 0:head_width],
        grad_qkv[:, head_width : 2 * head_width],
        grad_qkv[:, 2 * head_width :],
        grad_out,
        grad_up,
        grad_down,
    ]
    return jnp.concatenate([piece.reshape(width, groups, -1) for piece in pieces], axis=2).reshape(
        width, -1
    )


def global_scores(queries, key_rows, length):
    span = queries.shape[0]
    heads = queries.shape[1] // HD
    scores = jnp.einsum(
        "qhd,khd->hqk",
        queries.reshape(span, heads, HD),
        key_rows.reshape(span, heads, HD),
        preferred_element_type=jnp.float32,
    ) * HD ** (-0.5)
    rows_at = lax.broadcasted_iota(jnp.int32, (span, span), 0)
    cols_at = lax.broadcasted_iota(jnp.int32, (span, span), 1)
    allowed = (cols_at <= rows_at) & (cols_at < length)
    return jnp.where(allowed[None], scores, masked_fill)


def global_attend(queries, key_rows, value_rows, lengths):
    items = lengths.shape[0]
    span = queries.shape[0] // items
    heads = queries.shape[1] // HD

    def one_item(packed):
        item_query, item_key, item_value, length = packed
        scores = global_scores(item_query, item_key, length)
        row_max = jnp.max(scores, axis=-1, keepdims=True)
        expanded = jnp.exp(scores - row_max)
        row_total = jnp.sum(expanded, axis=-1, keepdims=True)
        probability = (expanded / row_total).astype(jnp.bfloat16)
        mixed = jnp.einsum(
            "hqk,khd->qhd",
            probability,
            item_value.reshape(span, heads, HD),
            preferred_element_type=jnp.float32,
        )
        return (
            mixed.reshape(span, -1).astype(jnp.bfloat16),
            (row_max + jnp.log(row_total))[..., 0],
        )

    mixed, log_total = lax.map(
        one_item,
        (
            queries.reshape(items, span, -1),
            key_rows.reshape(items, span, -1),
            value_rows.reshape(items, span, -1),
            lengths,
        ),
    )
    return (mixed.reshape(items * span, -1), log_total)


def global_attend_back(queries, key_rows, value_rows, lengths, log_total, grad_mixed):
    items = lengths.shape[0]
    span = queries.shape[0] // items
    heads = queries.shape[1] // HD
    scale_score = HD ** (-0.5)

    def one_item(packed):
        item_query, item_key, item_value, length, item_lse, item_grad = packed
        scores = global_scores(item_query, item_key, length)
        probability = jnp.exp(scores - item_lse[..., None])
        grad_heads = item_grad.reshape(span, heads, HD)
        query_heads = item_query.reshape(span, heads, HD)
        key_heads = item_key.reshape(span, heads, HD)
        value_heads = item_value.reshape(span, heads, HD)
        grad_value = jnp.einsum(
            "hqk,qhd->khd",
            probability.astype(jnp.bfloat16),
            grad_heads,
            preferred_element_type=jnp.float32,
        )
        grad_prob = jnp.einsum(
            "qhd,khd->hqk", grad_heads, value_heads, preferred_element_type=jnp.float32
        )
        center = jnp.sum(probability * grad_prob, axis=-1, keepdims=True)
        grad_scores = (probability * (grad_prob - center)).astype(jnp.bfloat16)
        grad_query = (
            jnp.einsum("hqk,khd->qhd", grad_scores, key_heads, preferred_element_type=jnp.float32)
            * scale_score
        )
        grad_key = (
            jnp.einsum("hqk,qhd->khd", grad_scores, query_heads, preferred_element_type=jnp.float32)
            * scale_score
        )
        return jnp.concatenate(
            [
                grad_query.reshape(span, -1),
                grad_key.reshape(span, -1),
                grad_value.reshape(span, -1),
            ],
            axis=1,
        ).astype(jnp.bfloat16)

    grads = lax.map(
        one_item,
        (
            queries.reshape(items, span, -1),
            key_rows.reshape(items, span, -1),
            value_rows.reshape(items, span, -1),
            lengths,
            log_total,
            grad_mixed.reshape(items, span, -1),
        ),
    )
    return grads.reshape(items * span, -1)


def local_probability(queries, key_rows):
    frame_count = queries.shape[0] // CB
    heads = queries.shape[1] // HD
    scores = jnp.einsum(
        "fqhd,fkhd->fhqk",
        queries.reshape(frame_count, CB, heads, HD),
        key_rows.reshape(frame_count, CB, heads, HD),
        preferred_element_type=jnp.float32,
    ) * HD ** (-0.5)
    rows_at = lax.broadcasted_iota(jnp.int32, (CB, CB), 0)
    cols_at = lax.broadcasted_iota(jnp.int32, (CB, CB), 1)
    scores = jnp.where(cols_at <= rows_at, scores, masked_fill)
    row_max = jnp.max(scores, axis=-1, keepdims=True)
    expanded = jnp.exp(scores - row_max)
    return expanded / jnp.sum(expanded, axis=-1, keepdims=True)


def local_attend(queries, key_rows, value_rows):
    frame_count = queries.shape[0] // CB
    heads = queries.shape[1] // HD
    probability = local_probability(queries, key_rows).astype(jnp.bfloat16)
    mixed = jnp.einsum(
        "fhqk,fkhd->fqhd",
        probability,
        value_rows.reshape(frame_count, CB, heads, HD),
        preferred_element_type=jnp.float32,
    )
    return (mixed.reshape(queries.shape[0], -1).astype(jnp.bfloat16), jnp.zeros((), jnp.float32))


def local_attend_back(queries, key_rows, value_rows, saved, grad_mixed):
    frame_count = queries.shape[0] // CB
    heads = queries.shape[1] // HD
    scale_score = HD ** (-0.5)
    probability = local_probability(queries, key_rows)
    grad_heads = grad_mixed.reshape(frame_count, CB, heads, HD)
    query_heads = queries.reshape(frame_count, CB, heads, HD)
    key_heads = key_rows.reshape(frame_count, CB, heads, HD)
    value_heads = value_rows.reshape(frame_count, CB, heads, HD)
    grad_value = jnp.einsum(
        "fhqk,fqhd->fkhd",
        probability.astype(jnp.bfloat16),
        grad_heads,
        preferred_element_type=jnp.float32,
    )
    grad_prob = jnp.einsum(
        "fqhd,fkhd->fhqk", grad_heads, value_heads, preferred_element_type=jnp.float32
    )
    center = jnp.sum(probability * grad_prob, axis=-1, keepdims=True)
    grad_scores = (probability * (grad_prob - center)).astype(jnp.bfloat16)
    grad_query = (
        jnp.einsum("fhqk,fkhd->fqhd", grad_scores, key_heads, preferred_element_type=jnp.float32)
        * scale_score
    )
    grad_key = (
        jnp.einsum("fhqk,fqhd->fkhd", grad_scores, query_heads, preferred_element_type=jnp.float32)
        * scale_score
    )
    total_rows = queries.shape[0]
    return jnp.concatenate(
        [
            grad_query.reshape(total_rows, -1),
            grad_key.reshape(total_rows, -1),
            grad_value.reshape(total_rows, -1),
        ],
        axis=1,
    ).astype(jnp.bfloat16)


def block_forward(rows_in, matrices, gain_a, gain_b, path, attend):
    gather_rows, sum_rows = (path[0], path[1])
    w_qkv, w_out, w_up, w_down = matrices
    normed_a = gather_rows(rms_forward(rows_in, gain_a).astype(jnp.bfloat16))
    projected = dot_rows(normed_a, w_qkv).astype(jnp.bfloat16)
    head_width = projected.shape[1] // 3
    mixed, saved = attend(
        projected[:, :head_width],
        projected[:, head_width : 2 * head_width],
        projected[:, 2 * head_width :],
    )
    middle = rows_in + sum_rows(mixed, w_out)
    normed_b = gather_rows(rms_forward(middle, gain_b).astype(jnp.bfloat16))
    upper = dot_rows(normed_b, w_up)
    active = jax.nn.gelu(upper, approximate=False).astype(jnp.bfloat16)
    result = middle + sum_rows(active, w_down)
    return (result, (rows_in, normed_a, projected, mixed, saved, middle, normed_b, upper, active))


def block_backward(grad_result, kept, matrices, gain_a, gain_b, path, attend_back):
    gather_grads, sum_back = (path[2], path[3])
    rows_in, normed_a, projected, mixed, saved, middle, normed_b, upper, active = kept
    w_qkv, w_out, w_up, w_down = matrices
    grad_branch = gather_grads(grad_result.astype(jnp.bfloat16))
    grad_down = dot_over_rows(grad_branch, active)
    grad_active = dot_rows(grad_branch, w_down)
    grad_upper = (grad_active * gelu_slope(upper)).astype(jnp.bfloat16)
    grad_up = dot_over_rows(normed_b, grad_upper)
    grad_normed_b = sum_back(grad_upper, w_up)
    grad_middle_part, gain_b_grad = rms_backward(middle, gain_b, grad_normed_b)
    grad_middle = grad_result + grad_middle_part
    grad_attn = gather_grads(grad_middle.astype(jnp.bfloat16))
    grad_out = dot_over_rows(grad_attn, mixed)
    grad_mixed = dot_rows(grad_attn, w_out).astype(jnp.bfloat16)
    head_width = projected.shape[1] // 3
    grad_qkv = attend_back(
        projected[:, :head_width],
        projected[:, head_width : 2 * head_width],
        projected[:, 2 * head_width :],
        saved,
        grad_mixed,
    )
    grad_weight_qkv = dot_over_rows(normed_a, grad_qkv)
    grad_normed_a = sum_back(grad_qkv, w_qkv)
    grad_rows_part, gain_a_grad = rms_backward(rows_in, gain_a, grad_normed_a)
    return (
        grad_middle + grad_rows_part,
        (grad_weight_qkv, grad_out, grad_up, grad_down),
        gain_a_grad,
        gain_b_grad,
    )


def shards_any(
    frames_in,
    code_emb,
    cotangent,
    lengths,
    owner_list,
    master,
    first_moment,
    second_moment,
    ema,
    left_basis,
    right_basis,
    gains,
    gain_first,
    gain_second,
):
    tensor_count = lax.axis_size(TENSOR)
    group_count = lax.axis_size(DP)
    head_cols = D // tensor_count
    ff_cols = FF // tensor_count
    share = frames_in.shape[0]
    owned_rows = master.shape[1]
    gathered = lax.all_gather(master.astype(jnp.bfloat16), DP, axis=1, tiled=True)
    layers = jnp.take(gathered.reshape(2, group_count, owned_rows, -1), owner_list, axis=1).reshape(
        2, group_count * owned_rows, -1
    )

    def gather_rows(values):
        return lax.all_gather(values, TENSOR, axis=0, tiled=True)

    def gather_grads(values):
        return lax.all_gather(values, TENSOR, axis=0, tiled=True)

    def sum_rows(operand, weight):
        return lax.psum_scatter(
            row_term(operand, weight).astype(jnp.bfloat16),
            TENSOR,
            scatter_dimension=0,
            tiled=True,
        ).astype(jnp.float32)

    def sum_back(operand, weight):
        return lax.psum_scatter(
            row_term(operand, weight).astype(jnp.bfloat16),
            TENSOR,
            scatter_dimension=0,
            tiled=True,
        ).astype(jnp.float32)

    heads_path = (gather_rows, sum_rows, gather_grads, sum_back)
    rows_path = (keep_rows, dot_transposed, keep_rows, dot_transposed)

    def attend_global(queries, key_rows, value_rows):
        return global_attend(queries, key_rows, value_rows, lengths)

    def attend_global_back(queries, key_rows, value_rows, saved, grad_mixed):
        return global_attend_back(queries, key_rows, value_rows, lengths, saved, grad_mixed)

    global_matrices = split_layer(layers[0], 1, head_cols, ff_cols)
    global_out, global_kept = block_forward(
        frames_in.astype(jnp.float32),
        global_matrices,
        gains[0],
        gains[1],
        heads_path,
        attend_global,
    )
    local_in = (global_out[:, None, :] + code_emb.astype(jnp.float32)).reshape(share * CB, -1)
    local_layer = lax.all_gather(layers[1], TENSOR, axis=1, tiled=True)
    local_matrices = split_layer(local_layer, tensor_count, head_cols, ff_cols)
    local_result, local_kept = block_forward(
        local_in, local_matrices, gains[2], gains[3], rows_path, local_attend
    )
    local_out = local_result.reshape(share, CB, -1).astype(jnp.bfloat16)
    frame_at = lax.axis_index(TENSOR) * share + jnp.arange(share, dtype=jnp.int32)
    item_at = frame_at // LMAX
    item_slots = jnp.arange(lengths.shape[0], dtype=jnp.int32)
    item_length = jnp.sum(
        jnp.where(item_at[:, None] == item_slots[None, :], lengths[None, :], 0), axis=1
    )
    valid = (frame_at % LMAX < item_length).astype(jnp.float32)
    grad_local = (cotangent.astype(jnp.float32) * valid[:, None, None]).reshape(share * CB, -1)
    grad_local_in, local_weight_grads, gain_c_grad, gain_d_grad = block_backward(
        grad_local, local_kept, local_matrices, gains[2], gains[3], rows_path, local_attend_back
    )
    grad_global_out = jnp.sum(grad_local_in.reshape(share, CB, -1), axis=1)
    input_grad, global_weight_grads, gain_a_grad, gain_b_grad = block_backward(
        grad_global_out,
        global_kept,
        global_matrices,
        gains[0],
        gains[1],
        heads_path,
        attend_global_back,
    )
    local_grads = join_layer(local_weight_grads, tensor_count)
    local_grads = lax.psum_scatter(
        local_grads.astype(jnp.bfloat16), TENSOR, scatter_dimension=1, tiled=True
    ).astype(jnp.float32)
    layer_grads = jnp.stack([join_layer(global_weight_grads, 1), local_grads])
    slots = jnp.arange(group_count, dtype=jnp.int32)
    inverse = jnp.sum(jnp.where(owner_list[None, :] == slots[:, None], slots[None, :], 0), axis=1)
    ordered = jnp.take(
        layer_grads.reshape(2, group_count, owned_rows, -1), inverse, axis=1
    ).reshape(2, group_count * owned_rows, -1)
    weight_grads = lax.psum_scatter(
        ordered.astype(jnp.bfloat16), DP, scatter_dimension=1, tiled=True
    ).astype(jnp.float32)
    gain_grads = lax.psum(
        jnp.stack([gain_a_grad, gain_b_grad, gain_c_grad, gain_d_grad]), (DP, TENSOR)
    )
    tile_count = right_basis.shape[1]
    turned_left = jnp.einsum("lab,lac->lbc", left_basis, weight_grads, precision=highest)
    rotated = jnp.einsum(
        "lbkc,lkce->lbke",
        turned_left.reshape(2, owned_rows, tile_count, -1),
        right_basis,
        precision=highest,
    ).reshape(weight_grads.shape)
    new_first = beta_first * first_moment + (1.0 - beta_first) * rotated
    new_second = beta_second * second_moment + (1.0 - beta_second) * rotated * rotated
    turned = new_first / (jnp.sqrt(new_second) + adam_eps)
    back_right = jnp.einsum(
        "lbke,lkce->lbkc",
        turned.reshape(2, owned_rows, tile_count, -1),
        right_basis,
        precision=highest,
    )
    back_full = jnp.einsum(
        "lab,lbc->lac", left_basis, back_right.reshape(weight_grads.shape), precision=highest
    )
    new_master = master - step_rate * back_full
    new_ema = ema_decay * ema + (1.0 - ema_decay) * new_master
    new_gain_first = beta_first * gain_first + (1.0 - beta_first) * gain_grads
    new_gain_second = beta_second * gain_second + (1.0 - beta_second) * gain_grads * gain_grads
    new_gains = gains - gain_rate * new_gain_first / (jnp.sqrt(new_gain_second) + adam_eps)
    return (
        local_out,
        input_grad,
        weight_grads,
        gain_grads,
        new_master,
        new_first,
        new_second,
        new_ema,
        new_gains,
        new_gain_first,
        new_gain_second,
    )


MIB = 1024 * 1024
VMEM_WHOLE = pl.BlockSpec(memory_space=pltpu.VMEM)
IN_SMEM = pl.BlockSpec(memory_space=pltpu.SMEM)
IN_HBM = pl.BlockSpec(memory_space=pl.ANY)


def shaped(shape, kind):
    return jax.ShapeDtypeStruct(shape, kind)


def cost(flops, moved, exps=0):
    return pl.CostEstimate(flops=int(flops), bytes_accessed=int(moved), transcendentals=int(exps))


weight_of = {
    "forward_global": 170,
    "local_heads": 18,
    "local_ff": 34,
    "local_back": 81,
    "backward_global": 90,
    "last_transfers": 60,
    "adam_update": 5,
}


def group_at(rel):
    mine = lax.axis_index(TENSOR)
    return 2 * ((mine // 2 + rel // 2) % 2) + (mine % 2 + rel % 2) % 2


CORE, X, Y, Z1, Z2 = range(5)


def partner_of(hop):
    dp, tensor = lax.axis_index(DP), lax.axis_index(TENSOR)
    if hop == CORE:
        return {TENSOR: tensor + 1 - 2 * (tensor % 2)}
    if hop == X:
        return {TENSOR: (tensor + 2) % 4}
    if hop == Y:
        return {DP: dp + 1 - 2 * (dp % 2)}
    if hop == Z1:
        return {DP: dp + 2 - 4 * ((dp // 2) % 2)}
    return {DP: (dp + 4) % 8}


def greet(hops):
    barrier = pltpu.get_barrier_semaphore()
    for hop in hops:
        pl.semaphore_signal(
            barrier, inc=1, device_id=partner_of(hop), device_id_type=pl.DeviceIdType.MESH
        )
    pl.semaphore_wait(barrier, len(hops))


def to_partner(hop, source, target, send, recv):
    return pltpu.make_async_remote_copy(
        src_ref=source,
        dst_ref=target,
        send_sem=send,
        recv_sem=recv,
        device_id=partner_of(hop),
        device_id_type=pl.DeviceIdType.MESH,
    )


def part(array, begin, rows):
    return (array, begin, rows)


class Line:
    def __init__(self):
        self.token = None
        self.moves = ()
        self.arrived = []
        self.calls = 0

    def carry(self, *moves):
        self.moves = moves

    def run(self, body, args, in_specs, out_specs, out_shape, aliases=None, scratch_shapes=(), limit=32, hops=(), **rest):
        moves, self.moves = self.moves, ()
        sources, copies, landed = [], [], []
        for hop, *pieces in moves:
            offset = 0
            for piece in pieces:
                array, begin, rows = piece if isinstance(piece, tuple) else (piece, 0, piece.shape[0])
                which = next((at for at, one in enumerate(sources) if one is array), len(sources))
                if which == len(sources):
                    sources.append(array)
                copies.append((hop, which, begin, rows, len(landed), offset))
                offset += rows
            landed.append(shaped((offset,) + array.shape[1:], array.dtype))
        reach = list(hops) or list(dict.fromkeys(move[0] for move in moves))
        lead = 0 if self.token is None else 1
        inputs = lead + len(args)
        first_out = inputs + len(sources)
        outputs = len(out_shape)
        first_scratch = first_out + outputs + len(landed) + 1
        steps = rest.get("grid", (1,))[0]

        def inner(*refs):
            scratch = refs[first_scratch:]
            pending = []
            if copies:
                *scratch, send, recv = scratch
                for at, (hop, which, begin, rows, where, offset) in enumerate(copies):
                    pending.append(
                        to_partner(
                            hop,
                            refs[inputs + which].at[pl.ds(begin, rows)],
                            refs[first_out + outputs + where].at[pl.ds(offset, rows)],
                            send.at[at],
                            recv.at[at],
                        )
                    )

            def begin_all():
                greet(reach)
                for one in pending:
                    one.start()

            def end_all():
                for one in pending:
                    one.wait()

            at_ends = (lambda step, act: pl.when(pl.program_id(0) == step)(act)) if steps > 1 else (
                lambda step, act: act()
            )
            if pending:
                at_ends(0, begin_all)
            body(*refs[lead:inputs], *refs[first_out : first_out + outputs], *scratch)
            if pending:
                at_ends(steps - 1, end_all)

        extra = {}
        if reach:
            extra = {"collective_id": self.calls, "has_side_effects": True}
            self.calls += 1
        found = pl.pallas_call(
            inner,
            in_specs=[IN_HBM] * lead + list(in_specs) + [IN_HBM] * len(sources),
            out_specs=list(out_specs) + [IN_HBM] * (len(landed) + 1),
            out_shape=list(out_shape) + landed + [shaped((8, 128), jnp.float32)],
            scratch_shapes=list(scratch_shapes)
            + ([pltpu.SemaphoreType.DMA((len(copies),))] * 2 if copies else []),
            input_output_aliases={lead + at: to for at, to in (aliases or {}).items()},
            cost_estimate=cost(weight_of.get(rest["name"], 1.0) * 0.2e9, 1000),
            compiler_params=pltpu.CompilerParams(vmem_limit_bytes=limit * MIB, **extra),
            **rest,
        )(*([self.token] * lead), *args, *sources)
        self.token = found[-1]
        self.arrived = list(found[outputs:-1])
        return list(found[:outputs])


def lanes_of(source_ref, at, width):
    return pl.ds(pl.multiple_of(source_ref[at] * width, width), width)


def norm_rows(rows, gain):
    scale = lax.rsqrt(jnp.mean(rows * rows, axis=-1, keepdims=True) + norm_eps)
    return rows * scale * gain


def norm_rows_back(rows, gain, grad):
    scale = lax.rsqrt(jnp.mean(rows * rows, axis=-1, keepdims=True) + norm_eps)
    scaled = grad * gain
    inner = jnp.sum(scaled * rows, axis=-1, keepdims=True)
    grad_in = scale * scaled - rows * (scale * scale * scale) * inner / rows.shape[-1]
    return grad_in, jnp.sum(grad * rows * scale, axis=0, keepdims=True)


def gelu_both(upper):
    size = jnp.abs(upper)
    base = 1.0 + (0.3275911 / math.sqrt(2.0)) * size
    guess = pl.reciprocal(base, approx=True)
    ratio = guess * (2.0 - base * guess)
    bell = jnp.exp(-0.5 * upper * upper)
    series = ratio * (
        0.5 * 0.254829592
        + ratio
        * (
            -0.5 * 0.284496736
            + ratio * (0.5 * 1.421413741 + ratio * (-0.5 * 1.453152027 + ratio * (0.5 * 1.061405429)))
        )
    )
    tail = series * bell
    cdf = jnp.where(upper >= 0.0, 1.0 - tail, tail)
    density = bell * (1.0 / math.sqrt(2.0 * math.pi))
    return (upper * cdf).astype(jnp.bfloat16), (cdf + upper * density).astype(jnp.bfloat16)


def both(rows, near, far):
    depth = near.shape[0]
    return dot_rows(rows[:, :depth], near) + dot_rows(rows[:, depth:], far)


def held(shape):
    return pl.BlockSpec(shape, lambda step: (0,) * len(shape), pipeline_mode=pl.Buffered(1))


def by_cols(shape):
    return pl.BlockSpec(shape, lambda step: (0, step))


def prep_body(source_ref, frames_ref, gains_ref, *refs):
    masters, (rows_ref, gains_out_ref, normed_ref), shards = refs[:6], refs[6:9], refs[9:]
    for master_ref, shard_ref in zip(masters, shards):
        shard_ref[...] = master_ref[0].astype(jnp.bfloat16)
    owned = frames_ref.shape[1] // source_ref.shape[0]
    for at in range(source_ref.shape[0]):
        here = slice(at * owned, (at + 1) * owned)
        rows_ref[:, here] = frames_ref[:, lanes_of(source_ref, at, owned)]
        gains_out_ref[:, here] = gains_ref[:, lanes_of(source_ref, at, owned)]
    normed_ref[...] = norm_rows(rows_ref[...].astype(jnp.float32), gains_out_ref[0:1, :]).astype(
        jnp.bfloat16
    )


def prep(line, source, frames, gains, master):
    owned, columns = master.shape[1], master.shape[2] // 3

    def spec(layer, third):
        return pl.BlockSpec((1, owned, columns), lambda step: (layer, 0, third))

    shapes = [
        shaped(frames.shape, jnp.bfloat16),
        shaped(gains.shape, jnp.float32),
        shaped(frames.shape, jnp.bfloat16),
    ] + [shaped((owned, columns), jnp.bfloat16)] * 6
    found = line.run(
        prep_body,
        (source, frames, gains) + (master,) * 6,
        grid=(1,),
        in_specs=[IN_SMEM, held(frames.shape), held(gains.shape)]
        + [spec(layer, third) for layer in range(2) for third in range(3)],
        out_specs=[held(one.shape) for one in shapes],
        out_shape=shapes,
        limit=60,
        name="prep_rows",
    )
    return found[:3], found[3:]


def finish_body(source_ref, rows_ref, sum_ref, grad_ref, gains_ref, gb_ref, gc_ref, gd_ref, out_ref, gain_ref):
    back, gain_grad = norm_rows_back(rows_ref[...].astype(jnp.float32), gains_ref[0:1, :], sum_ref[...])
    total = grad_ref[...] + back
    owned = out_ref.shape[1] // source_ref.shape[0]
    for at in range(source_ref.shape[0]):
        here = slice(at * owned, (at + 1) * owned)
        there = lanes_of(source_ref, at, owned)
        out_ref[:, there] = total[:, here]
        gain_ref[0:1, there] = gain_grad[:, here]
        gain_ref[1:2, there] = gb_ref[:, here]
        gain_ref[2:3, there] = gc_ref[:, here]
        gain_ref[3:4, there] = gd_ref[:, here]


def finish(line, source, rows, total, grad, gains, others):
    return line.run(
        finish_body,
        (source, rows, total, grad, gains, *others),
        in_specs=[IN_SMEM] + [VMEM_WHOLE] * 7,
        out_specs=[VMEM_WHOLE] * 2,
        out_shape=[shaped(rows.shape, jnp.float32), shaped((4, rows.shape[1]), jnp.float32)],
        limit=60,
        name="input_grad",
    )


forward_order = (
    0, 12, 37, 4, 36, 50, 49, 66, 38, 8, 2, 1, 51, 43, 13, 15, 14, 24, 5, 3, 6, 16, 39, 9, 10, 67, 68, 18, 17,
    20, 85, 86, 45, 87, 44, 88, 69, 72, 52, 53, 73, 54, 74, 75, 55, 41, 22, 76, 56, 25, 7, 27, 26, 77, 62, 78,
    64, 63, 21, 40, 11, 19, 28, 70, 46, 65, 23, 71, 42, 89, 30, 32, 29, 90, 91, 92, 79, 57, 58, 80, 59, 81,
    60, 82, 61, 31, 34, 33, 83, 48, 84, 35, 47,
)


def forward_body(
    info_ref, rows_ref, normed_ref, gains_ref, ga_s, gu_s, gd_s, la_s, lu_s, ld_s,
    ga, gu, gd, la, lu, ld, qkv_ref, mixed_ref, lse_ref, middle_ref, out_ref, na_h, nb_h, active_h, slope_h,
    na, nb, a_v, u_v, d_v, acc, lse_wide, act, slp, parts, met_core, met_x, sends_x, sems, send, recv,
):
    share = rows_ref.shape[0]
    owned = ga_s.shape[0]
    half = D // 2
    width = mixed_ref.shape[1]
    span = 4 * share
    length = info_ref[1]
    scale = HD ** (-0.5)
    flying, filed, numbers = [], [], []

    def fly(hop, source, target):
        at = len(numbers)
        copy = to_partner(hop, source, target, send.at[at], recv.at[at])
        copy.start()
        numbers.append(at)
        flying.append(copy)
        return copy

    def file(source, target):
        copy = pltpu.make_async_copy(source, target, sems.at[len(filed)])
        copy.start()
        filed.append(copy)
        return copy

    quarter = half // 2
    arrived = set()
    named = {}

    def need(*names):
        for name in names:
            if name not in arrived:
                arrived.add(name)
                named[name].wait_recv()

    def same(hop, whole, begin, rows, shift):
        return lambda: fly(hop, whole.at[pl.ds(begin, rows)], whole.at[pl.ds(begin + shift, rows)])

    def level(hop, stack, begin, to, start, rows):
        here = pl.ds(start, rows)
        return lambda: fly(hop, stack.at[begin, here], stack.at[to, here])

    moves = {}
    for letter, shard, whole in (("A", ga_s, ga), ("U", gu_s, gu), ("D", gd_s, gd)):
        moves["g2" + letter] = (
            (lambda shard, whole: lambda: fly(Z2, shard, whole.at[pl.ds(owned, owned)]))(shard, whole),
            (),
        )
        moves["g1" + letter] = (same(Z1, whole, 0, quarter, quarter), ("g2" + letter, "own"))
        moves["gy0" + letter] = (same(Y, whole, 0, quarter, half), ("g2" + letter, "own"))
        moves["gy1" + letter] = (same(Y, whole, quarter, quarter, half), ("g1" + letter,))
    for letter, shard, stack in (("A", la_s, la), ("U", lu_s, lu)):
        near = stack.at[0]
        moves["l2" + letter] = (
            (lambda shard, near: lambda: fly(Z2, shard, near.at[pl.ds(owned, owned)]))(shard, near),
            (),
        )
        moves["l1" + letter] = (same(Z1, near, 0, quarter, quarter), ("l2" + letter, "own"))
        for at in range(2):
            source = ("l2" + letter, "own") if at == 0 else ("l1" + letter,)
            moves[f"ly{at}{letter}"] = (same(Y, near, at * quarter, quarter, half), source)
            moves[f"lx{at}{letter}"] = (level(X, stack, 0, 2, at * quarter, quarter), source)
            if letter == "A":
                moves[f"lf{at}{letter}"] = (
                    level(X, stack, 0, 2, half + at * quarter, quarter),
                    (f"ly{at}{letter}",),
                )
            else:
                moves[f"lf{at}{letter}"] = (
                    same(Y, stack.at[2], at * quarter, quarter, half),
                    (f"lx{at}{letter}",),
                )
        moves["cn" + letter] = (level(CORE, stack, 0, 1, 0, half), ("l2" + letter, "l1" + letter, "own"))
        moves["cf" + letter] = (level(CORE, stack, 0, 1, half, half), ("ly0" + letter, "ly1" + letter))
        moves["cx" + letter] = (level(CORE, stack, 2, 3, 0, half), ("lx0" + letter, "lx1" + letter))
        moves["cxf" + letter] = (level(CORE, stack, 2, 3, half, half), ("lf0" + letter, "lf1" + letter))
    moves["dx"] = (lambda: fly(X, ld_s, ld.at[2, pl.ds(0, owned)]), ())
    moves["dy"] = (lambda: fly(Y, ld_s, ld.at[0, pl.ds(half, owned)]), ())
    moves["dxy"] = (same(Y, ld.at[2], 0, owned, half), ("dx",))
    for at, source in enumerate((("own",), ("dy",), ("dx",), ("dxy",))):
        stack, begin = ld.at[2 * (at // 2)], half * (at % 2)
        moves[f"d2{at}"] = (same(Z2, stack, begin, owned, owned), source)
        moves[f"d1{at}"] = (same(Z1, stack, begin, quarter, quarter), (f"d2{at}",) + source)
    moves["cdn"] = (level(CORE, ld, 0, 1, 0, D), ("d10", "d11", "d20", "d21", "dy", "own"))
    moves["cdx"] = (level(CORE, ld, 2, 3, 0, D), ("d12", "d13", "d22", "d23", "dx", "dxy"))
    moves["nx"] = (lambda: fly(X, normed_ref, na.at[pl.ds(2 * share, share)]), ())
    moves["nc"] = (lambda: fly(CORE, normed_ref, na.at[pl.ds(share, share)]), ())
    moves["nxc"] = (same(CORE, na, 2 * share, share, share), ("nx",))
    strip = share // 2
    strips = [pl.ds(at * strip, strip) for at in range(2)]

    def sums_moves(far, near, over, which):
        for at, name in enumerate(far):
            moves[name] = (
                (lambda rows: lambda: fly(CORE, parts.at[3, rows], met_core.at[2 * which, rows]))(strips[at]),
                (),
            )
        moves[near] = (lambda: fly(CORE, parts.at[1], met_core.at[2 * which + 1]), ())
        for at, name in enumerate(over):
            moves[name] = (
                (lambda rows: lambda: fly(X, sends_x.at[which, rows], met_x.at[which, rows]))(strips[at]),
                (),
            )

    sums_moves(("c3a", "c3b"), "c1", ("sx0", "sx1"), 0)
    sums_moves(("e3a", "e3b"), "e1", ("tx0", "tx1"), 1)
    for at in range(2):
        moves[f"ox{at}"] = (same(X, nb, at * strip, strip, 2 * share), ())
    moves["oc"] = (same(CORE, nb, 0, share, share), ())
    moves["oxc"] = (same(CORE, nb, 2 * share, share, share), ("ox0", "ox1"))

    def do_own():
        copies = [
            file(shard, whole.at[pl.ds(0, owned)])
            for shard, whole in (
                (ga_s, ga), (la_s, la.at[0]), (gu_s, gu), (gd_s, gd), (lu_s, lu.at[0]), (ld_s, ld.at[0]),
            )
        ]
        na[pl.ds(0, share), :] = normed_ref[...]
        for one in copies:
            one.wait()

    def load(letter, whole, target):
        need("g2" + letter, "g1" + letter, "gy0" + letter, "gy1" + letter)
        return file(whole, target)

    def do_load_a():
        load("A", ga, a_v).wait()

    def do_qkv():
        need("nx", "nc", "nxc")
        outgoing.append(file(na, na_h))
        for rel in range(4):
            at = pl.ds(pl.multiple_of(group_at(rel) * share, share), share)
            full = both(
                na[rel * share : (rel + 1) * share, :], a_v[:half, : 3 * width], a_v[half:, : 3 * width]
            )
            qkv_ref[at, :] = full.astype(jnp.bfloat16)
        acc[:, :width] = jnp.zeros((span, width), jnp.float32)
        lse_wide[...] = jnp.zeros_like(lse_wide)

    head_of = lax.broadcasted_iota(jnp.int32, (1, width), 1) // HD
    lane = lax.broadcasted_iota(jnp.int32, (1, 128), 1)

    def do_head(head):
        own_lanes = head_of == head
        for block in range(4):
            rows = slice(block * share, (block + 1) * share)
            reach = (block + 1) * share
            query = jnp.where(own_lanes, qkv_ref[rows, :width] * scale, 0.0).astype(jnp.bfloat16)
            scores = dot_transposed(query, qkv_ref[:reach, width : 2 * width])
            row_at = block * share + lax.broadcasted_iota(jnp.int32, scores.shape, 0)
            col_at = lax.broadcasted_iota(jnp.int32, scores.shape, 1)
            scores = jnp.where((col_at <= row_at) & (col_at < length), scores, masked_fill)
            top = jnp.max(scores, axis=-1, keepdims=True)
            expanded = jnp.exp(scores - top)
            total = jnp.sum(expanded, axis=-1, keepdims=True)
            prob = (expanded * (1.0 / total)).astype(jnp.bfloat16)
            value = jnp.where(own_lanes, qkv_ref[:reach, 2 * width :], 0.0).astype(jnp.bfloat16)
            acc[rows, :width] += dot_rows(prob, value)
            lse_wide[rows, :] = jnp.where(lane == head, top + jnp.log(total), lse_wide[rows, :])

    def do_mix():
        mixed_ref[...] = acc[:, :width].astype(jnp.bfloat16)
        lse_ref[...] = jnp.transpose(lse_wide[...])[: lse_ref.shape[0], :]

    def out_part(rel):
        at = pl.ds(pl.multiple_of(group_at(rel) * share, share), share)
        rows = mixed_ref[at, :]
        parts[rel, :, :half] = dot_transposed(rows, a_v[:half, 3 * width :]).astype(jnp.bfloat16)
        parts[rel, :, half:] = dot_transposed(rows, a_v[half:, 3 * width :]).astype(jnp.bfloat16)

    def down_part(rel):
        parts[rel] = acc[rel * share : (rel + 1) * share, :].astype(jnp.bfloat16)

    def several(act_on, *values):
        def do():
            for value in values:
                act_on(value)

        return do

    def do_add(which, at, name):
        def do():
            need(name)
            rows = strips[at]
            total = parts[2, rows, :].astype(jnp.float32) + met_core[2 * which, rows, :].astype(jnp.float32)
            sends_x[which, rows, :] = total.astype(jnp.bfloat16)

        return do

    def gathered(which, rows, base):
        return (
            base
            + parts[0, rows, :].astype(jnp.float32)
            + met_core[2 * which + 1, rows, :].astype(jnp.float32)
            + met_x[which, rows, :].astype(jnp.float32)
        )

    def do_middle(at):
        def do():
            need("c1", f"sx{at}")
            rows = strips[at]
            total = gathered(0, rows, rows_ref[rows, :].astype(jnp.float32))
            middle_ref[rows, :] = total
            nb[rows, :] = norm_rows(total, gains_ref[1:2, :]).astype(jnp.bfloat16)

        return do

    def do_load_u():
        load("U", gu, u_v).wait()
        acc[...] = jnp.zeros_like(acc)

    def do_load_d():
        copy = load("D", gd, d_v)
        need("oc", "oxc", "ox0", "ox1")
        outgoing.append(file(nb, nb_h))
        copy.wait()

    def do_ff(at):
        lanes = slice(at * 256, (at + 1) * 256)
        active, slope = gelu_both(both(nb[...], u_v[:half, lanes], u_v[half:, lanes]))
        act[:, lanes] = active
        slp[:, lanes] = slope
        for side in range(2):
            cols_at = slice(side * half, (side + 1) * half)
            acc[:, cols_at] += dot_transposed(active, d_v[side * half : (side + 1) * half, lanes])

    def do_q3():
        outgoing.extend([file(act, active_h), file(slp, slope_h)])
        for name in ("c3a", "c3b", "c1"):
            named[name].wait_send()
            flying[:] = [other for other in flying if other is not named[name]]
        down_part(3)

    def do_result(at):
        def do():
            need("e1", f"tx{at}")
            rows = strips[at]
            out_ref[rows, :] = gathered(1, rows, middle_ref[rows, :])

        return do

    outgoing = []
    steps = {
        "own": do_own, "load_a": do_load_a, "qkv": do_qkv, "mix": do_mix, "load_u": do_load_u, "load_d": do_load_d,
        "p3": several(out_part, 3), "p2": several(out_part, 2, 1), "p0": several(out_part, 0),
        "s0": do_add(0, 0, "c3a"), "s1": do_add(0, 1, "c3b"), "m0": do_middle(0), "m1": do_middle(1),
        "q3": do_q3, "q1": several(down_part, 2, 1, 0), "t0": do_add(1, 0, "e3a"), "t1": do_add(1, 1, "e3b"),
        "r0": do_result(0), "r1": do_result(1),
    }
    for at in range(width // HD):
        steps[f"h{at}"] = several(do_head, at)
    for at in range(u_v.shape[1] // 256):
        steps[f"f{at}"] = several(do_ff, at)

    greet((CORE, X, Y, Z1, Z2))
    names = list(moves) + list(steps)
    for place in forward_order:
        name = names[place]
        if name in steps:
            steps[name]()
            arrived.add(name)
        else:
            start, before = moves[name]
            need(*before)
            named[name] = start()
    need(*named)
    for one in outgoing:
        one.wait()
    for one in flying:
        one.wait_send()


def forward_global(line, info, rows, normed, gains, shards):
    share, owned = rows.shape[0], shards[0].shape[0]
    span, columns = 4 * share, shards[0].shape[1]
    width = columns // 4
    small = jnp.bfloat16
    weights = [shaped((D, columns), small)] * 3 + [shaped((4, D, columns), small)] * 3
    return line.run(
        forward_body,
        (info, rows, normed, gains, *shards),
        in_specs=[IN_SMEM] + [VMEM_WHOLE] * 3 + [IN_HBM] * 6,
        out_specs=[IN_HBM] * 6 + [VMEM_WHOLE] * 5 + [IN_HBM] * 4,
        out_shape=weights
        + [
            shaped((span, 3 * width), small),
            shaped((span, width), small),
            shaped((8, span), jnp.float32),
            shaped((share, D), jnp.float32),
            shaped((share, D), jnp.float32),
            shaped((span, D), small),
            shaped((span, D), small),
            shaped((span, columns), small),
            shaped((span, columns), small),
        ],
        scratch_shapes=[
            pltpu.VMEM((span, D), small),
            pltpu.VMEM((span, D), small),
            pltpu.VMEM((D, columns), small),
            pltpu.VMEM((D, columns), small),
            pltpu.VMEM((D, columns), small),
            pltpu.VMEM((span, D), jnp.float32),
            pltpu.VMEM((span, 128), jnp.float32),
            pltpu.VMEM((span, columns), small),
            pltpu.VMEM((span, columns), small),
            pltpu.VMEM((4, share, D), small),
            pltpu.VMEM((4, share, D), small),
            pltpu.VMEM((2, share, D), small),
            pltpu.VMEM((2, share, D), small),
            pltpu.SemaphoreType.DMA((24,)),
            pltpu.SemaphoreType.DMA((96,)),
            pltpu.SemaphoreType.DMA((96,)),
        ],
        hops=(CORE, X, Y, Z1, Z2),
        limit=56,
        name="forward_global",
    )


def backward_body(
    info_ref, small_ref, grad_ref, middle_ref, gains_ref, lse_ref, up_h, down_h, heads_h, active_h, slope_h,
    nb_h, na_h, qkv_h, mixed_h, u_near_h, u_far_h, h2_far_h,
    h0_far_h, h2_near_h,
    mid_ref, sum_ref, gain_ref, gu_near_h, gu_met_h, gh_near_h, gh_far_h, lu_keep_h, lu_met_h, gd_keep_h,
    gd_met_h, h2_met_h, h_first_h, h2_first_h,
    rows_one, rows_two, up_v, down_v, heads_v, act, slp, dup, left_t, right_v, grads_v, qkv_v, mixed_v, dqkv,
    dmix, dq_t, dk_acc, dv_acc, center, k_t, parts, met_core, met_x, sends_x, u_v, u_met, d_v, d_met, z_met, h_v,
    sems, send, recv,
):
    share = small_ref.shape[0]
    half = D // 2
    quarter = half // 2
    owned = quarter // 2
    width = mixed_v.shape[1]
    heads = width // HD
    span = 4 * share
    length = info_ref[1]
    scale = HD ** (-0.5)
    numbers, flying, filed = [], [], []

    def fly(hop, source, target):
        at = len(numbers)
        copy = to_partner(hop, source, target, send.at[at], recv.at[at])
        copy.start()
        numbers.append(at)
        flying.append(copy)
        return copy

    def over(copy):
        copy.wait_send()
        flying[:] = [other for other in flying if other is not copy]

    def file(source, target):
        copy = pltpu.make_async_copy(source, target, sems.at[len(filed)])
        copy.start()
        filed.append(copy)
        return copy

    def block(rel):
        return slice(rel * share, (rel + 1) * share)

    def place(rel):
        return pl.ds(pl.multiple_of(group_at(rel) * share, share), share)

    def summed(*terms):
        total = terms[0].astype(jnp.float32)
        for term in terms[1:]:
            total = total + term.astype(jnp.float32)
        return total

    greet((CORE, X, Y, Z1, Z2))
    small_x = fly(X, small_ref, rows_one.at[pl.ds(2 * share, share)])
    small_core = fly(CORE, small_ref, rows_one.at[pl.ds(share, share)])
    u_y = fly(Y, u_far_h, u_met)
    h_first = fly(X, h2_far_h.at[pl.ds(0, quarter)], h_v.at[0])
    first = [file(down_h, down_v), file(slope_h, slp), file(up_h, up_v)]
    active_in = file(active_h, act)
    nb_in = file(nb_h, right_v)
    u_in = file(u_near_h, u_v)
    h_in = file(h0_far_h.at[pl.ds(0, quarter)], h_v.at[1])
    attention_in = [file(heads_h, heads_v), file(qkv_h, qkv_v), file(mixed_h, mixed_v)]
    rows_one[pl.ds(0, share), :] = small_ref[...]
    for one in first:
        one.wait()

    def ff_back(rel):
        rows = block(rel)
        for tile in range(2):
            lanes = slice(tile * half, (tile + 1) * half)
            grad = both(rows_one[rows, :], down_v[:half, lanes], down_v[half:, lanes])
            dup[rows, lanes] = (grad * slp[rows, lanes].astype(jnp.float32)).astype(jnp.bfloat16)
        for side in range(2):
            lanes = slice(side * half, (side + 1) * half)
            parts[rel, :, lanes] = dot_transposed(dup[rows, :], up_v[lanes, :]).astype(jnp.bfloat16)

    ff_back(0)
    small_core.wait_recv()
    ff_back(1)
    small_x.wait_recv()
    small_xc = fly(CORE, rows_one.at[pl.ds(2 * share, share)], rows_one.at[pl.ds(3 * share, share)])
    ff_back(2)
    small_xc.wait_recv()
    ff_back(3)
    strip = share // 2
    strips = [pl.ds(at * strip, strip) for at in range(2)]

    def scatter_start(which):
        from_far = [fly(CORE, parts.at[3, rows], met_core.at[2 * which, rows]) for rows in strips]
        return from_far, fly(CORE, parts.at[1], met_core.at[2 * which + 1])

    def scatter_on(which, from_far):
        from_x = []
        for rows, one in zip(strips, from_far):
            one.wait_recv()
            sends_x[which, rows, :] = summed(parts[2, rows, :], met_core[2 * which, rows, :]).astype(jnp.bfloat16)
            from_x.append(fly(X, sends_x.at[which, rows], met_x.at[which, rows]))
        return from_x

    def gathered(which, rows):
        return summed(parts[0, rows, :], met_core[2 * which + 1, rows, :], met_x[which, rows, :])

    from_far, from_near = scatter_start(0)
    for rel in range(4):
        left_t[:, block(rel)] = jnp.transpose(rows_one[block(rel), :])
    from_x = scatter_on(0, from_far)
    h_in.wait()
    h_first.wait_recv()
    h_v[1] = summed(h_v[0], h_v[1]).astype(jnp.bfloat16)
    h_y = fly(Y, h_v.at[1], h_first_h)
    active_in.wait()
    for side in range(2):
        rows = slice(side * half, (side + 1) * half)
        for tile in range(2):
            lanes = slice(tile * half, (tile + 1) * half)
            grads_v[0, rows, lanes] = dot_rows(left_t[rows, :], act[:, lanes]).astype(jnp.bfloat16)
    gd_y = fly(Y, grads_v.at[0, pl.ds(half, half)], d_met)
    results = []
    from_near.wait_recv()
    gain_total = jnp.zeros((1, D), jnp.float32)
    over_x = []
    for rows, one in zip(strips, from_x):
        one.wait_recv()
        back, gain_grad = norm_rows_back(middle_ref[rows, :], gains_ref[1:2, :], gathered(0, rows))
        total = grad_ref[rows, :] + back
        mid_ref[rows, :] = total
        rows_two[rows, :] = total.astype(jnp.bfloat16)
        gain_total = gain_total + gain_grad
        over_x.append(fly(X, rows_two.at[rows], rows_two.at[pl.ds(2 * share + rows.start, strip)]))
    gain_ref[...] = gain_total
    small_core = fly(CORE, rows_two.at[pl.ds(0, share)], rows_two.at[pl.ds(share, share)])
    h_second = fly(X, h2_far_h.at[pl.ds(quarter, quarter)], h2_met_h)
    h_third = fly(X, h2_near_h.at[pl.ds(0, quarter)], h2_first_h)
    u_y.wait_recv()
    u_in.wait()
    u_v[...] = summed(u_v[...], u_met[...]).astype(jnp.bfloat16)
    u_1 = fly(Z1, u_v.at[pl.ds(quarter, quarter)], z_met.at[0])
    nb_in.wait()
    left_t[...] = jnp.transpose(right_v[...])
    na_in = file(na_h, right_v)
    for side in range(2):
        rows = slice(side * half, (side + 1) * half)
        for tile in range(2):
            lanes = slice(tile * half, (tile + 1) * half)
            grads_v[1, rows, lanes] = dot_rows(left_t[rows, :], dup[:, lanes]).astype(jnp.bfloat16)
    gu_y = fly(Y, grads_v.at[1, pl.ds(half, half)], gu_met_h)
    results.append(file(grads_v.at[1, pl.ds(0, half)], gu_near_h))
    for one in attention_in:
        one.wait()

    def mix_back(rel):
        full = both(rows_two[block(rel), :], heads_v[:half, 3 * width :], heads_v[half:, 3 * width :])
        dmix[place(rel), :] = full.astype(jnp.bfloat16)

    head_of = lax.broadcasted_iota(jnp.int32, (1, width), 1) // HD
    pick = (
        lax.broadcasted_iota(jnp.int32, (8, width), 1) // HD
        == lax.broadcasted_iota(jnp.int32, (8, width), 0)
    ).astype(jnp.bfloat16)
    k_t[...] = jnp.transpose(qkv_v[:, width : 2 * width])
    dq_t[...] = jnp.zeros_like(dq_t)
    dk_acc[...] = jnp.zeros_like(dk_acc)
    dv_acc[...] = jnp.zeros_like(dv_acc)
    mix_back(0)
    small_core.wait_recv()
    mix_back(1)
    for one in over_x:
        one.wait_recv()
    small_xc = fly(CORE, rows_two.at[pl.ds(2 * share, share)], rows_two.at[pl.ds(3 * share, share)])
    mix_back(2)
    u_1.wait_recv()
    u_v[:quarter, :] = summed(u_v[:quarter, :], z_met[0]).astype(jnp.bfloat16)
    u_2 = fly(Z2, u_v.at[pl.ds(owned, owned)], lu_met_h)
    results.append(file(u_v.at[pl.ds(0, owned)], lu_keep_h))
    small_xc.wait_recv()
    mix_back(3)
    product = dmix[...].astype(jnp.float32) * mixed_v[...].astype(jnp.float32)
    high = product.astype(jnp.bfloat16)
    low = (product - high.astype(jnp.float32)).astype(jnp.bfloat16)
    center[...] = dot_transposed(pick, high) + dot_transposed(pick, low)
    for head in range(heads):
        own_lanes = head_of == head
        for at in range(4):
            rows = block(at)
            reach = (at + 1) * share
            query = jnp.where(own_lanes, qkv_v[rows, :width] * scale, 0.0).astype(jnp.bfloat16)
            grad = jnp.where(own_lanes, dmix[rows, :], 0.0).astype(jnp.bfloat16)
            scores = dot_transposed(qkv_v[:reach, width : 2 * width], query)
            key_at = lax.broadcasted_iota(jnp.int32, scores.shape, 0)
            row_at = at * share + lax.broadcasted_iota(jnp.int32, scores.shape, 1)
            prob = jnp.where(
                (key_at <= row_at) & (key_at < length),
                jnp.exp(scores - lse_ref[head : head + 1, rows]),
                0.0,
            )
            dprob = dot_transposed(qkv_v[:reach, 2 * width :], grad)
            dscore = (prob * (dprob - center[head : head + 1, rows])).astype(jnp.bfloat16)
            dv_acc[:reach, :] += dot_rows(prob.astype(jnp.bfloat16), grad)
            dk_acc[:reach, :] += dot_rows(dscore, query)
            lanes = slice(head * HD, (head + 1) * HD)
            dq_t[lanes, rows] += dot_rows(k_t[lanes, :reach], dscore)
    dqkv[:, :width] = (jnp.transpose(dq_t[...]) * scale).astype(jnp.bfloat16)
    dqkv[:, width : 2 * width] = dk_acc[...].astype(jnp.bfloat16)
    dqkv[:, 2 * width :] = dv_acc[...].astype(jnp.bfloat16)
    gd_y.wait_recv()
    d_v[...] = summed(grads_v[0, :half, :], d_met[...]).astype(jnp.bfloat16)
    d_1 = fly(Z1, d_v.at[pl.ds(quarter, quarter)], z_met.at[1])
    for one in from_far + [from_near]:
        over(one)

    def back_part(rel):
        rows = dqkv[place(rel), :]
        for side in range(2):
            lanes = slice(side * half, (side + 1) * half)
            parts[rel, :, lanes] = dot_transposed(rows, heads_v[lanes, : 3 * width]).astype(jnp.bfloat16)

    back_part(3)
    back_part(1)
    from_far, from_near = scatter_start(1)
    back_part(2)
    from_x = scatter_on(1, from_far)
    back_part(0)
    na_in.wait()
    for rel in range(4):
        left_t[:, place(rel)] = jnp.transpose(right_v[block(rel), :])
    over(gd_y)
    for side in range(2):
        rows = slice(side * half, (side + 1) * half)
        grads_v[0, rows, : 3 * width] = dot_rows(left_t[rows, :], dqkv[...]).astype(jnp.bfloat16)
    for rel in range(4):
        left_t[:, place(rel)] = jnp.transpose(rows_two[block(rel), :])
    for side in range(2):
        rows = slice(side * half, (side + 1) * half)
        grads_v[0, rows, 3 * width :] = dot_rows(left_t[rows, :], mixed_v[...]).astype(jnp.bfloat16)
    results += [
        file(grads_v.at[0, pl.ds(0, half)], gh_near_h),
        file(grads_v.at[0, pl.ds(half, half)], gh_far_h),
    ]
    d_1.wait_recv()
    d_v[:quarter, :] = summed(d_v[:quarter, :], z_met[1]).astype(jnp.bfloat16)
    d_2 = fly(Z2, d_v.at[pl.ds(owned, owned)], gd_met_h)
    results.append(file(d_v.at[pl.ds(0, owned)], gd_keep_h))
    from_near.wait_recv()
    for rows, one in zip(strips, from_x):
        one.wait_recv()
        sum_ref[rows, :] = gathered(1, rows)
    for one in (h_y, h_second, h_third, gu_y, u_2, d_2):
        one.wait_recv()
    for one in results:
        one.wait()
    for one in flying:
        one.wait_send()


def backward_global(line, info, small, grad, middle, gains, lse, weights, active, slope, nb, na, qkv, mixed, sums):
    share, columns = small.shape[0], active.shape[1]
    span, width = 4 * share, mixed.shape[1]
    half, owned = D // 2, D // 8
    low = jnp.bfloat16
    up, down, heads = weights
    return line.run(
        backward_body,
        (info, small, grad, middle, gains, lse, up, down, heads, active, slope, nb, na, qkv, mixed, *sums),
        in_specs=[IN_SMEM] + [VMEM_WHOLE] * 5 + [IN_HBM] * 14,
        out_specs=[VMEM_WHOLE] * 3 + [IN_HBM] * 11,
        out_shape=[
            shaped((share, D), jnp.float32),
            shaped((share, D), jnp.float32),
            shaped((1, D), jnp.float32),
        ]
        + [shaped((half, columns), low)] * 4
        + [shaped((owned, columns), low)] * 4
        + [shaped((half // 2, columns), low)] * 3,
        scratch_shapes=[pltpu.VMEM((span, D), low)] * 2
        + [pltpu.VMEM((D, columns), low)] * 3
        + [pltpu.VMEM((span, columns), low)] * 3
        + [pltpu.VMEM((D, span), low), pltpu.VMEM((span, D), low), pltpu.VMEM((2, D, columns), low)]
        + [pltpu.VMEM((span, 3 * width), low), pltpu.VMEM((span, width), low), pltpu.VMEM((span, 3 * width), low)]
        + [
            pltpu.VMEM((span, width), low),
            pltpu.VMEM((width, span), jnp.float32),
            pltpu.VMEM((span, width), jnp.float32),
            pltpu.VMEM((span, width), jnp.float32),
            pltpu.VMEM((8, span), jnp.float32),
            pltpu.VMEM((width, span), low),
            pltpu.VMEM((4, share, D), low),
            pltpu.VMEM((4, share, D), low),
            pltpu.VMEM((2, share, D), low),
            pltpu.VMEM((2, share, D), low),
        ]
        + [pltpu.VMEM((half, columns), low)] * 4
        + [
            pltpu.VMEM((2, half // 2, columns), low),
            pltpu.VMEM((2, half // 2, columns), low),
            pltpu.SemaphoreType.DMA((24,)),
            pltpu.SemaphoreType.DMA((40,)),
            pltpu.SemaphoreType.DMA((40,)),
        ],
        hops=(CORE, X, Y, Z1, Z2),
        limit=56,
        name="backward_global",
    )


def head_sums(width):
    row_at = lax.broadcasted_iota(jnp.int32, (width, width), 0) // HD
    col_at = lax.broadcasted_iota(jnp.int32, (width, width), 1) // HD
    return (row_at == col_at).astype(jnp.bfloat16)


def over_heads(product, ones):
    high = product.astype(jnp.bfloat16)
    low = (product - high.astype(jnp.float32)).astype(jnp.bfloat16)
    return dot_rows(high, ones) + dot_rows(low, ones)


def frame_probs(queries, keys, ones):
    found = []
    for at in range(CB):
        scores = [over_heads(queries[at] * keys[c2], ones) * HD ** (-0.5) for c2 in range(at + 1)]
        top = scores[0]
        for one in scores[1:]:
            top = jnp.maximum(top, one)
        expanded = [jnp.exp(one - top) for one in scores]
        total = expanded[0]
        for one in expanded[1:]:
            total = total + one
        inverse = 1.0 / total
        found.append([one * inverse for one in expanded])
    return found


def rounded_f32(values):
    return values.astype(jnp.bfloat16).astype(jnp.float32)


def halves_of(stack):
    half = stack.shape[1] // 2
    return [(stack.at[at, pl.ds(0, half)], stack.at[at, pl.ds(half, half)]) for at in range(stack.shape[0])]


def start_weights(parts, buffer, sems):
    for at, pair in enumerate(parts):
        for half, ref in enumerate(pair):
            pltpu.make_async_copy(ref, buffer.at[at, half], sems.at[at, half]).start()


def wait_weights(parts, buffer, sems, at):
    for half in range(2):
        pltpu.make_async_copy(parts[0][half], buffer.at[at, half], sems.at[at, half]).wait()


def local_heads_body(
    out_ref_in, code_ref, gains_ref, *refs
):
    count = 4
    parts = halves_of(refs[0])
    qkv_ref, mixed_ref, middle_ref, normed_b_ref, a_t_ref, normed_a, local_in, buffer, sems = refs[1:]
    step = pl.program_id(0)
    frames = out_ref_in.shape[0]
    width = mixed_ref.shape[2]
    half = D // 2

    @pl.when(step == 0)
    def _():
        start_weights(parts, buffer, sems)
        for c in range(CB):
            rows = slice(c * frames, (c + 1) * frames)
            local_in[rows, :] = out_ref_in[...] + code_ref[rows, :].astype(jnp.float32)
            normed = norm_rows(local_in[rows, :], gains_ref[2:3, :]).astype(jnp.bfloat16)
            normed_a[rows, :] = normed
            a_t_ref[:, rows] = jnp.transpose(normed)
        middle_ref[...] = local_in[...]

    wait_weights(parts, buffer, sems, step)
    ones = head_sums(width)
    queries, keys, values = ([], [], [])
    for c in range(CB):
        rows = slice(c * frames, (c + 1) * frames)
        qkv = (
            dot_rows(normed_a[rows, :half], buffer[step, 0, :, : 3 * width])
            + dot_rows(normed_a[rows, half:], buffer[step, 1, :, : 3 * width])
        ).astype(jnp.bfloat16)
        qkv_ref[0, rows, :] = qkv
        queries.append(qkv[:, :width].astype(jnp.float32))
        keys.append(qkv[:, width : 2 * width].astype(jnp.float32))
        values.append(qkv[:, 2 * width :].astype(jnp.float32))
    prob = frame_probs(queries, keys, ones)
    for c in range(CB):
        rows = slice(c * frames, (c + 1) * frames)
        mix = rounded_f32(prob[c][0]) * values[0]
        for c2 in range(1, c + 1):
            mix = mix + rounded_f32(prob[c][c2]) * values[c2]
        mix = mix.astype(jnp.bfloat16)
        mixed_ref[0, rows, :] = mix
        for at in range(2):
            lanes = slice(at * half, (at + 1) * half)
            middle_ref[rows, lanes] += dot_transposed(mix, buffer[step, at, :, 3 * width :])

    @pl.when(step == count - 1)
    def _():
        for c in range(CB):
            rows = slice(c * frames, (c + 1) * frames)
            normed_b_ref[rows, :] = norm_rows(middle_ref[rows, :], gains_ref[3:4, :]).astype(
                jnp.bfloat16
            )


def local_heads(line, global_out, codes, gains, parts):
    frames = global_out.shape[0]
    rows = CB * frames
    width = parts.shape[2] // 4
    half = D // 2
    return line.run(
        local_heads_body,
        (global_out, codes, gains, parts),
        grid=(4,),
        in_specs=[held((frames, D)), held((rows, D)), held((4, D)), IN_HBM],
        out_specs=[
            pl.BlockSpec((1, rows, 3 * width), lambda step: (step, 0, 0)),
            pl.BlockSpec((1, rows, width), lambda step: (step, 0, 0)),
            held((rows, D)),
            held((rows, D)),
            held((D, rows)),
        ],
        out_shape=[
            shaped((4, rows, 3 * width), jnp.bfloat16),
            shaped((4, rows, width), jnp.bfloat16),
            shaped((rows, D), jnp.float32),
            shaped((rows, D), jnp.bfloat16),
            shaped((D, rows), jnp.bfloat16),
        ],
        scratch_shapes=[
            pltpu.VMEM((rows, D), jnp.bfloat16),
            pltpu.VMEM((rows, D), jnp.float32),
            pltpu.VMEM((4, 2, half, 4 * width), jnp.bfloat16),
            pltpu.SemaphoreType.DMA((4, 2)),
        ],
        limit=52,
        name="local_heads",
    )


def local_ff_body(source_ref, normed_ref, middle_ref, *refs):
    count = 4
    ups, downs = halves_of(refs[0]), halves_of(refs[1])
    active_ref, slope_ref, out_ref, b_t_ref, acc, up_buf, down_buf, up_sems, down_sems = refs[2:]
    step = pl.program_id(0)
    rows_all = normed_ref.shape[0]
    frames = rows_all // CB
    half = D // 2
    tile = active_ref.shape[2]
    per = up_buf.shape[3] // tile
    group = step // per
    cols_at = pl.ds(pl.multiple_of((step % per) * tile, tile), tile)

    @pl.when(step == 0)
    def _():
        for at in range(count):
            start_weights_at(ups, up_buf, up_sems, at)
            start_weights_at(downs, down_buf, down_sems, at)
        b_t_ref[...] = jnp.transpose(normed_ref[...])
        acc[...] = middle_ref[...]

    @pl.when(step % per == 0)
    def _():
        wait_weights(ups, up_buf, up_sems, group)
        wait_weights(downs, down_buf, down_sems, group)

    for c in range(CB):
        rows = slice(c * frames, (c + 1) * frames)
        upper = dot_rows(normed_ref[rows, :half], up_buf[group, 0, :, cols_at]) + dot_rows(
            normed_ref[rows, half:], up_buf[group, 1, :, cols_at]
        )
        active, slope = gelu_both(upper)
        active_ref[0, rows, :] = active
        slope_ref[0, rows, :] = slope
        for at in range(2):
            lanes = slice(at * half, (at + 1) * half)
            acc[rows, lanes] += dot_transposed(active, down_buf[group, at, :, cols_at])

    @pl.when(step == pl.num_programs(0) - 1)
    def _():
        owned = D // source_ref.shape[0]
        for c in range(CB):
            rows = slice(c * frames, (c + 1) * frames)
            for at in range(source_ref.shape[0]):
                here = slice(at * owned, (at + 1) * owned)
                out_ref[c, :, lanes_of(source_ref, at, owned)] = acc[rows, here].astype(jnp.bfloat16)


def start_weights_at(parts, buffer, sems, at):
    for half in range(2):
        pltpu.make_async_copy(parts[at][half], buffer.at[at, half], sems.at[at, half]).start()


def local_ff(line, source, normed, middle, ups, downs, tile=512):
    rows = normed.shape[0]
    hidden = ups.shape[2]
    half = D // 2
    per = hidden // tile
    hidden_block = pl.BlockSpec((1, rows, tile), lambda step: (step // per, 0, step % per))
    return line.run(
        local_ff_body,
        (source, normed, middle, ups, downs),
        grid=(4 * per,),
        in_specs=[IN_SMEM, held((rows, D)), held((rows, D)), IN_HBM, IN_HBM],
        out_specs=[hidden_block, hidden_block, held((CB, rows // CB, D)), held((D, rows))],
        out_shape=[
            shaped((4, rows, hidden), jnp.bfloat16),
            shaped((4, rows, hidden), jnp.bfloat16),
            shaped((CB, rows // CB, D), jnp.bfloat16),
            shaped((D, rows), jnp.bfloat16),
        ],
        scratch_shapes=[
            pltpu.VMEM((rows, D), jnp.float32),
            pltpu.VMEM((4, 2, half, hidden), jnp.bfloat16),
            pltpu.VMEM((4, 2, half, hidden), jnp.bfloat16),
            pltpu.SemaphoreType.DMA((4, 2)),
            pltpu.SemaphoreType.DMA((4, 2)),
        ],
        limit=56,
        name="local_ff",
    )


def seed_body(source_ref, count_ref, cot_ref, code_ref, grad_ref, grad_t_ref, codes_ref):
    frames = cot_ref.shape[1]
    owned = D // source_ref.shape[0]
    keep = lax.broadcasted_iota(jnp.int32, (frames, 1), 0) < count_ref[0]
    for c in range(CB):
        rows = slice(c * frames, (c + 1) * frames)
        for at in range(source_ref.shape[0]):
            here = slice(at * owned, (at + 1) * owned)
            values = cot_ref[c, :, lanes_of(source_ref, at, owned)].astype(jnp.float32)
            grad_ref[rows, here] = jnp.where(keep, values, 0.0).astype(jnp.bfloat16)
            codes_ref[rows, here] = code_ref[c, :, lanes_of(source_ref, at, owned)]
        grad_t_ref[:, rows] = jnp.transpose(grad_ref[rows, :])


def seed(line, source, count, cot, codes):
    frames = cot.shape[1]
    rows = CB * frames
    return line.run(
        seed_body,
        (source, count, cot, codes),
        in_specs=[IN_SMEM, IN_SMEM, VMEM_WHOLE, VMEM_WHOLE],
        out_specs=[VMEM_WHOLE] * 3,
        out_shape=[
            shaped((rows, D), jnp.bfloat16),
            shaped((D, rows), jnp.bfloat16),
            shaped((rows, D), jnp.bfloat16),
        ],
        limit=60,
        name="seed_grads",
    )


def local_back_body(
    grad_h, grad_t_h, b_t_h, a_t_h, active_h, slope_h, qkv_h, mixed_h, middle_h, gout_h, codes_h, gains_ref, *refs
):
    heads_h, ups_h, downs_h = ([half for pair in halves_of(one) for half in pair] for one in refs[:3])
    refs = refs[3:]
    total_ref, small_out_ref, gain_c_ref, gain_d_ref, *results_h = refs[:12]
    (
        grad_v, grad_t, other_t, weights, act, slp, dup, acc, mid, gout_v, codes_v,
        pair_out, pair_far, pair_near, head_out, head_far, head_near, x_in, y_far, y_near,
        sems, send, recv,
    ) = refs[12:]
    frames = gout_v.shape[0]
    rows_all = grad_v.shape[0]
    half = D // 2
    width = mixed_h.shape[2]
    scale = HD ** (-0.5)
    greet((CORE, X, Y))

    def fetch(at, source, target):
        copy = pltpu.make_async_copy(source, target, sems.at[at])
        copy.start()
        return copy

    def give(at, hop, source, target):
        copy = to_partner(hop, source, target, send.at[at], recv.at[at])
        copy.start()
        return copy

    def fetch_ff(rel):
        found = [fetch(at, downs_h[2 * rel + at], weights.at[2 + at]) for at in range(2)]
        found.append(fetch(2, slope_h.at[rel], slp))
        return found + [fetch(3 + at, ups_h[2 * rel + at], weights.at[at]) for at in range(2)]

    order = (3, 2, 1, 0)
    waits = [fetch(5, grad_h, grad_v)] + fetch_ff(order[0])
    late = [fetch(6, grad_t_h, grad_t), fetch(7, active_h.at[order[0]], act), fetch(8, b_t_h, other_t)]
    later = [fetch(9, middle_h, mid), fetch(10, gout_h, gout_v), fetch(11, codes_h, codes_v)]
    acc[...] = jnp.zeros_like(acc)
    sent = []
    for step, rel in enumerate(order):
        for one in waits:
            one.wait()
        for tile in range(2):
            lanes = slice(tile * half, (tile + 1) * half)
            grad = dot_rows(grad_v[:, :half], weights[2, :, lanes]) + dot_rows(
                grad_v[:, half:], weights[3, :, lanes]
            )
            dup[:, lanes] = (grad * slp[:, lanes].astype(jnp.float32)).astype(jnp.bfloat16)
        for at in range(2):
            lanes = slice(at * half, (at + 1) * half)
            acc[:, lanes] += dot_transposed(dup[...], weights[at])
        if step < 3:
            waits = fetch_ff(order[step + 1])
        for one in late:
            one.wait()
        if step == 2:
            sent[0].wait_send()
        if step % 2 == 1:
            sent[step // 2].wait_recv()
        met = (None, pair_far, None, pair_near)[step]
        for at in range(2):
            rows = slice(at * half, (at + 1) * half)
            for tile in range(2):
                lanes = slice(tile * half, (tile + 1) * half)
                down = dot_rows(grad_t[rows, :], act[:, lanes])
                up = dot_rows(other_t[rows, :], dup[:, lanes])
                if met is None:
                    pair_out[0, rows, lanes] = down.astype(jnp.bfloat16)
                    pair_out[1, rows, lanes] = up.astype(jnp.bfloat16)
                else:
                    met[0, rows, lanes] = (down + met[0, rows, lanes].astype(jnp.float32)).astype(jnp.bfloat16)
                    met[1, rows, lanes] = (up + met[1, rows, lanes].astype(jnp.float32)).astype(jnp.bfloat16)
        if step < 3:
            late = [fetch(7, active_h.at[order[step + 1]], act)]
        if step == 0:
            sent.append(give(0, CORE, pair_out, pair_far))
        elif step == 2:
            sent.append(give(1, CORE, pair_out, pair_near))
        elif step == 1:
            x_far = give(2, X, pair_far.at[1, pl.ds(half, half)], x_in.at[pl.ds(half, half)])
            y_two = give(3, Y, pair_far.at[0, pl.ds(half, half)], y_far)
            x_near = give(4, X, pair_far.at[1, pl.ds(0, half)], x_in.at[pl.ds(0, half)])
        else:
            y_zero = give(5, Y, pair_near.at[0, pl.ds(half, half)], y_near)

    def fetch_heads(rel):
        found = [fetch(at, heads_h[2 * rel + at], weights.at[at]) for at in range(2)]
        found.append(fetch(2, qkv_h.at[rel], act.at[:, pl.ds(0, 3 * width)]))
        return found + [fetch(3, mixed_h.at[rel], slp.at[:, pl.ds(0, width)])]

    waits = fetch_heads(order[0]) + [fetch(8, a_t_h, other_t)]
    sent[1].wait_send()
    for one in later:
        one.wait()
    total_gain = jnp.zeros((1, D), jnp.float32)
    for c in range(CB):
        rows = slice(c * frames, (c + 1) * frames)
        part_back, gain_grad = norm_rows_back(mid[rows, :], gains_ref[3:4, :], acc[rows, :])
        total = grad_v[rows, :].astype(jnp.float32) + part_back
        mid[rows, :] = total
        small = total.astype(jnp.bfloat16)
        grad_v[rows, :] = small
        grad_t[:, rows] = jnp.transpose(small)
        total_gain = total_gain + gain_grad
    gain_d_ref[...] = total_gain

    ones = head_sums(width)
    heads_sent = []

    def more(total, term):
        return term if total is None else total + term

    for step, rel in enumerate(order):
        for one in waits:
            one.wait()
        queries, keys, values, dmix = ([], [], [], [])
        back = rounded_f32(
            dot_rows(grad_v[:, :half], weights[0, :, 3 * width :])
            + dot_rows(grad_v[:, half:], weights[1, :, 3 * width :])
        )
        for c in range(CB):
            rows = slice(c * frames, (c + 1) * frames)
            qkv = act[rows, : 3 * width].astype(jnp.float32)
            queries.append(qkv[:, :width])
            keys.append(qkv[:, width : 2 * width])
            values.append(qkv[:, 2 * width :])
            dmix.append(back[rows, :])
        prob = frame_probs(queries, keys, ones)
        dq, dk, dv = ([None] * CB, [None] * CB, [None] * CB)
        for c in range(CB):
            dprob = [over_heads(dmix[c] * values[c2], ones) for c2 in range(c + 1)]
            center = prob[c][0] * dprob[0]
            for c2 in range(1, c + 1):
                center = center + prob[c][c2] * dprob[c2]
            for c2 in range(c + 1):
                dv[c2] = more(dv[c2], rounded_f32(prob[c][c2]) * dmix[c])
                dscore = rounded_f32(prob[c][c2] * (dprob[c2] - center))
                dq[c] = more(dq[c], dscore * keys[c2])
                dk[c2] = more(dk[c2], dscore * queries[c])
        for c in range(CB):
            rows = slice(c * frames, (c + 1) * frames)
            dup[rows, :width] = (dq[c] * scale).astype(jnp.bfloat16)
            dup[rows, width : 2 * width] = (dk[c] * scale).astype(jnp.bfloat16)
            dup[rows, 2 * width : 3 * width] = dv[c].astype(jnp.bfloat16)
        for at in range(2):
            lanes = slice(at * half, (at + 1) * half)
            term = dot_transposed(dup[:, : 3 * width], weights[at, :, : 3 * width])
            acc[:, lanes] = term if step == 0 else acc[:, lanes] + term
        if step == 2:
            heads_sent[0].wait_send()
        if step % 2 == 1:
            heads_sent[step // 2].wait_recv()
        met = (None, head_far, None, head_near)[step]
        for at in range(2):
            rows = slice(at * half, (at + 1) * half)
            three = dot_rows(other_t[rows, :], dup[:, : 3 * width])
            one = dot_rows(grad_t[rows, :], slp[:, :width])
            if met is None:
                head_out[rows, : 3 * width] = three.astype(jnp.bfloat16)
                head_out[rows, 3 * width :] = one.astype(jnp.bfloat16)
            else:
                three = three + met[rows, : 3 * width].astype(jnp.float32)
                one = one + met[rows, 3 * width :].astype(jnp.float32)
                met[rows, : 3 * width] = three.astype(jnp.bfloat16)
                met[rows, 3 * width :] = one.astype(jnp.bfloat16)
        if step < 3:
            waits = fetch_heads(order[step + 1])
        if step == 0:
            heads_sent.append(give(6, CORE, head_out, head_far))
        elif step == 2:
            heads_sent.append(give(7, CORE, head_out, head_near))
    total_gain = jnp.zeros((1, D), jnp.float32)
    total = jnp.zeros((frames, D), jnp.float32)
    for c in range(CB):
        rows = slice(c * frames, (c + 1) * frames)
        local_in = gout_v[...] + codes_v[rows, :].astype(jnp.float32)
        part_back, gain_grad = norm_rows_back(local_in, gains_ref[2:3, :], acc[rows, :])
        total = total + (mid[rows, :] + part_back)
        total_gain = total_gain + gain_grad
    total_ref[...] = total
    small_out_ref[...] = total.astype(jnp.bfloat16)
    gain_c_ref[...] = total_gain

    heads_sent[1].wait_send()
    x_far.wait()
    x_near.wait()
    y_two.wait()
    y_zero.wait()

    def summed(one, two):
        return (one.astype(jnp.float32) + two.astype(jnp.float32)).astype(jnp.bfloat16)

    pair_near[1] = summed(pair_near[1], x_in[...])
    pair_far[0, :half, :] = summed(pair_far[0, :half, :], y_far[...])
    pair_near[0, :half, :] = summed(pair_near[0, :half, :], y_near[...])
    near, far = pl.ds(0, half), pl.ds(half, half)
    leaving = (
        pair_near.at[1, near], pair_near.at[1, far], pair_far.at[0, near], pair_near.at[0, near],
        head_far.at[near], head_far.at[far], head_near.at[near], head_near.at[far],
    )
    for one in [fetch(at, source, target) for at, (source, target) in enumerate(zip(leaving, results_h))]:
        one.wait()


def local_back(line, grad, grad_t, b_t, a_t, active, slope, qkv, mixed, middle, global_out, codes, gains, heads, ups, downs):
    rows, frames = grad.shape[0], global_out.shape[0]
    half = D // 2
    columns = ups.shape[2]
    small = jnp.bfloat16
    return line.run(
        local_back_body,
        (grad, grad_t, b_t, a_t, active, slope, qkv, mixed, middle, global_out, codes, gains, heads, ups, downs),
        in_specs=[IN_HBM] * 11 + [VMEM_WHOLE] + [IN_HBM] * 3,
        out_specs=[VMEM_WHOLE] * 4 + [IN_HBM] * 8,
        out_shape=[
            shaped((frames, D), jnp.float32),
            shaped((frames, D), small),
            shaped((1, D), jnp.float32),
            shaped((1, D), jnp.float32),
        ]
        + [shaped((half, columns), small)] * 8,
        scratch_shapes=[
            pltpu.VMEM((rows, D), small),
            pltpu.VMEM((D, rows), small),
            pltpu.VMEM((D, rows), small),
            pltpu.VMEM((4, half, columns), small),
            pltpu.VMEM((rows, columns), small),
            pltpu.VMEM((rows, columns), small),
            pltpu.VMEM((rows, columns), small),
            pltpu.VMEM((rows, D), jnp.float32),
            pltpu.VMEM((rows, D), jnp.float32),
            pltpu.VMEM((frames, D), jnp.float32),
            pltpu.VMEM((rows, D), small),
            pltpu.VMEM((2, D, columns), small),
            pltpu.VMEM((2, D, columns), small),
            pltpu.VMEM((2, D, columns), small),
            pltpu.VMEM((D, columns), small),
            pltpu.VMEM((D, columns), small),
            pltpu.VMEM((D, columns), small),
            pltpu.VMEM((D, columns), small),
            pltpu.VMEM((half, columns), small),
            pltpu.VMEM((half, columns), small),
            pltpu.SemaphoreType.DMA((12,)),
            pltpu.SemaphoreType.DMA((8,)),
            pltpu.SemaphoreType.DMA((8,)),
        ],
        hops=(CORE, X, Y),
        limit=58,
        name="local_back",
    )


def last_body(
    gains_ref, gu_near_h, gu_met_h, gh_near_h, gh_far_h, d0_h, d2_h, h0_near_h, h2_near_h, h0_far_h, h2_far_h,
    h_first_h, h2_first_h,
    gain_out_ref, gu_keep_h, gu_last_h, gh_keep_h, gh_last_h, d_keep_h, d_last_h, h_keep_h, h_send_h,
    gain_v, gain_met, held_v, met_v, extra_v, z_met, sems, send, recv,
):
    half = D // 2
    quarter = half // 2
    owned = quarter // 2
    flying, filed = [], []

    def fly(hop, source, target):
        at = len(flying)
        copy = to_partner(hop, source, target, send.at[at], recv.at[at])
        copy.start()
        flying.append(copy)
        return copy

    def file(source, target):
        copy = pltpu.make_async_copy(source, target, sems.at[len(filed)])
        copy.start()
        filed.append(copy)
        return copy

    def summed(*terms):
        total = terms[0].astype(jnp.float32)
        for term in terms[1:]:
            total = total + term.astype(jnp.float32)
        return total.astype(jnp.bfloat16)

    greet((CORE, X, Y, Z1, Z2))
    upper, lower = pl.ds(0, quarter), pl.ds(quarter, quarter)
    gain_core = fly(CORE, gains_ref, gain_met.at[0])
    gh_low, gh_up = [fly(Y, gh_far_h.at[rows], met_v.at[1, rows]) for rows in (lower, upper)]
    d_low, d_up = [fly(X, d2_h.at[rows], met_v.at[2, rows]) for rows in (lower, upper)]
    gu_in = [file(gu_near_h, held_v.at[0]), file(gu_met_h, met_v.at[0])]
    far_in = [file(h0_far_h.at[lower], extra_v.at[0, lower]), file(h2_far_h, extra_v.at[1, lower])]
    rest_in = [file(gh_near_h, held_v.at[1]), file(d0_h, held_v.at[2]), file(h0_near_h, held_v.at[3])]
    rest_in += [file(h2_first_h, met_v.at[3, upper]), file(h_first_h, extra_v.at[2, upper])]
    for one in gu_in:
        one.wait()
    held_v[0] = summed(held_v[0], met_v[0])
    gu_1 = fly(Z1, held_v.at[0, lower], z_met.at[0])
    gain_core.wait_recv()
    gain_v[0] = gains_ref[...] + gain_met[0]
    gain_x = fly(X, gain_v.at[0], gain_met.at[1])
    h_x = fly(X, h2_near_h.at[lower], met_v.at[3, lower])
    for one in far_in:
        one.wait()
    extra_v[0, quarter:, :] = summed(extra_v[0, quarter:, :], extra_v[1, quarter:, :])
    h_y = fly(Y, extra_v.at[0, lower], extra_v.at[2, lower])
    for one in rest_in:
        one.wait()
    done = []

    def add(at, first):
        rows = slice(0, quarter) if first else slice(quarter, half)
        held_v[at, rows, :] = summed(held_v[at, rows, :], met_v[at, rows, :])

    def second(at, first, last_h, keep_h):
        first.wait_recv()
        held_v[at, :quarter, :] = summed(held_v[at, :quarter, :], z_met[at])
        done.append(file(held_v.at[at, pl.ds(0, owned)], keep_h))
        return fly(Z2, held_v.at[at, pl.ds(owned, owned)], last_h)

    gh_low.wait_recv()
    add(1, False)
    gh_1 = fly(Z1, held_v.at[1, lower], z_met.at[1])
    d_low.wait_recv()
    add(2, False)
    gu_2 = second(0, gu_1, gu_last_h, gu_keep_h)
    gh_up.wait_recv()
    add(1, True)
    gh_2 = second(1, gh_1, gh_last_h, gh_keep_h)
    d_1 = fly(Z1, held_v.at[2, lower], z_met.at[2])
    d_up.wait_recv()
    add(2, True)
    gain_x.wait_recv()
    gain_v[1] = gain_v[0] + gain_met[1]
    gain_y = fly(Y, gain_v.at[1], gain_met.at[2])
    h_x.wait_recv()
    h_y.wait_recv()
    held_v[3] = summed(held_v[3], met_v[3], extra_v[2])
    done.append(file(held_v.at[3, upper], h_keep_h))
    done.append(file(held_v.at[3, lower], h_send_h))
    gain_y.wait_recv()
    gain_v[2] = gain_v[1] + gain_met[2]
    gain_1 = fly(Z1, gain_v.at[2], gain_met.at[3])
    d_1.wait_recv()
    held_v[2, :quarter, :] = summed(held_v[2, :quarter, :], z_met[2])
    done.append(file(held_v.at[2, pl.ds(0, owned)], d_keep_h))
    done.append(file(held_v.at[2, pl.ds(owned, owned)], d_last_h))
    gain_1.wait_recv()
    gain_v[3] = gain_v[2] + gain_met[3]
    gain_2 = fly(Z2, gain_v.at[3], gain_met.at[4])
    gain_2.wait_recv()
    gain_out_ref[...] = gain_v[3] + gain_met[4]
    for one in (gu_2, gh_2):
        one.wait_recv()
    for one in done:
        one.wait()
    for one in flying:
        one.wait_send()


def last_transfers(line, gains, parts):
    half, columns = parts[0].shape
    owned = half // 4
    low = jnp.bfloat16
    return line.run(
        last_body,
        (gains, *parts),
        in_specs=[VMEM_WHOLE] + [IN_HBM] * 12,
        out_specs=[VMEM_WHOLE] + [IN_HBM] * 8,
        out_shape=[shaped(gains.shape, jnp.float32)]
        + [shaped((owned, columns), low)] * 6
        + [shaped((2 * owned, columns), low)] * 2,
        scratch_shapes=[
            pltpu.VMEM((4,) + gains.shape, jnp.float32),
            pltpu.VMEM((5,) + gains.shape, jnp.float32),
            pltpu.VMEM((4, half, columns), low),
            pltpu.VMEM((4, half, columns), low),
            pltpu.VMEM((3, half, columns), low),
            pltpu.VMEM((3, half // 2, columns), low),
            pltpu.SemaphoreType.DMA((16,)),
            pltpu.SemaphoreType.DMA((16,)),
            pltpu.SemaphoreType.DMA((16,)),
        ],
        hops=(CORE, X, Y, Z1, Z2),
        limit=60,
        name="last_transfers",
    )


def add_body(*refs):
    total = refs[0][...].astype(jnp.float32)
    for ref in refs[1:-1]:
        total = total + ref[...].astype(jnp.float32)
    refs[-1][...] = total.astype(jnp.bfloat16)


def add_rows(line, terms, part=0, parts=1):
    rows = min(term.shape[0] for term in terms) if parts == 1 else terms[0].shape[0] // parts
    columns = terms[0].shape[1]

    def spec(term):
        return pl.BlockSpec(
            (rows, columns), (lambda step: (part, 0)) if term.shape[0] > rows else (lambda step: (0, 0))
        )

    return line.run(
        add_body,
        tuple(terms),
        grid=(1,),
        in_specs=[spec(term) for term in terms],
        out_specs=[pl.BlockSpec((rows, columns), lambda step: (0, 0))],
        out_shape=[shaped((rows, columns), jnp.bfloat16)],
        limit=24,
        name="add_terms",
    )[0]


def sum_pieces(line, terms, split=()):
    rows, columns = terms[0].shape[0] // 2, terms[0].shape[1]
    whole = len(terms)
    flat = list(terms) + [one for pair in split for one in pair]

    def body(*refs):
        for at, out_ref in enumerate(refs[-2:]):
            here = slice(at * rows, (at + 1) * rows)
            total = refs[0][here, :].astype(jnp.float32)
            for ref in refs[1:whole]:
                total = total + ref[here, :].astype(jnp.float32)
            for ref in refs[whole + at : -2 : 2]:
                total = total + ref[...].astype(jnp.float32)
            out_ref[...] = total.astype(jnp.bfloat16)

    return line.run(
        body,
        tuple(flat),
        in_specs=[VMEM_WHOLE] * len(flat),
        out_specs=[VMEM_WHOLE] * 2,
        out_shape=[shaped((rows, columns), jnp.bfloat16)] * 2,
        limit=24,
        name="sum_pieces",
    )


def pass_body(*refs):
    pass


def in_turn(line, *values):
    return line.run(
        pass_body,
        tuple(values),
        in_specs=[IN_HBM] * len(values),
        out_specs=[IN_HBM] * len(values),
        out_shape=[shaped(one.shape, one.dtype) for one in values],
        aliases={at: at for at in range(len(values))},
        name="in_turn",
    )


def split_dot(left, right):
    left_high = left.astype(jnp.bfloat16)
    left_low = (left - left_high.astype(jnp.float32)).astype(jnp.bfloat16)
    right_high = right.astype(jnp.bfloat16)
    right_low = (right - right_high.astype(jnp.float32)).astype(jnp.bfloat16)
    return (
        dot_rows(left_high, right_high) + dot_rows(left_high, right_low) + dot_rows(left_low, right_high)
    )


def adam_body(chained, one_ref, two_ref, left_ref, right_ref, master_ref, first_ref, second_ref, ema_ref, *refs):
    grads_ref, new_master_ref, new_first_ref, new_second_ref, new_ema_ref = refs[5:] if chained else refs
    left = left_ref[0]
    left_t = jnp.transpose(left)
    grads = one_ref[...].astype(jnp.float32) + two_ref[...].astype(jnp.float32)
    grads_ref[0] = grads
    turned_left = split_dot(left_t, grads)
    back = []
    for at in range(right_ref.shape[1]):
        tile = slice(at * 128, (at + 1) * 128)
        right = right_ref[0, at]
        rotated = split_dot(turned_left[:, tile], right)
        new_first = beta_first * first_ref[0, :, tile] + (1.0 - beta_first) * rotated
        new_second = beta_second * second_ref[0, :, tile] + (1.0 - beta_second) * rotated * rotated
        new_first_ref[0, :, tile] = new_first
        new_second_ref[0, :, tile] = new_second
        turned = new_first / (jnp.sqrt(new_second) + adam_eps)
        back.append(split_dot(turned, jnp.transpose(right)))
    back_full = split_dot(left, jnp.concatenate(back, axis=1))
    new_master = master_ref[0] - step_rate * back_full
    new_master_ref[0] = new_master
    new_ema_ref[0] = ema_decay * ema_ref[0] + (1.0 - ema_decay) * new_master


def adam(line, layer, third, pieces, left, right, master, first, second, ema, before, tile=512):
    owned, columns = pieces[0].shape
    steps = columns // tile
    first_step = third * steps

    def state(step):
        return (layer, 0, first_step + step)

    state_spec = pl.BlockSpec((1, owned, tile), state)
    chained = before is not None
    return line.run(
        lambda *refs: adam_body(chained, *refs),
        (*pieces, left, right, master, first, second, ema, *(before or ()),),
        grid=(steps,),
        in_specs=[by_cols((owned, tile))] * 2
        + [
            pl.BlockSpec((1,) + left.shape[1:], lambda step: (layer, 0, 0)),
            pl.BlockSpec(
                (1, tile // 128) + right.shape[2:], lambda step: (layer, first_step + step, 0, 0)
            ),
        ]
        + [state_spec] * 4
        + ([IN_HBM] * 5 if chained else []),
        out_specs=[state_spec] * 5,
        out_shape=[shaped(master.shape, jnp.float32)] * 5,
        aliases={8 + at: at for at in range(5)} if chained else {},
        limit=32,
        name="adam_update",
    )


def hop_x(values):
    return lax.ppermute(values, TENSOR, [(at, at ^ 2) for at in range(4)])


def hop_core(values):
    return lax.ppermute(values, TENSOR, [(at, at ^ 1) for at in range(4)])


def hop_y(values):
    return lax.ppermute(values, DP, [(at, at ^ 1) for at in range(8)])


def hop_z(values, step):
    return lax.ppermute(values, DP, [(at, at ^ (2 * step)) for at in range(8)])


def shards_grid(
    frames_in,
    code_emb,
    cotangent,
    lengths,
    owner_list,
    master,
    first_moment,
    second_moment,
    ema,
    left_basis,
    right_basis,
    gains,
    gain_first,
    gain_second,
):
    share = frames_in.shape[0]
    owned = master.shape[1]
    groups = D // owned
    heads_w = D // lax.axis_size(TENSOR)
    ff_w = FF // lax.axis_size(TENSOR)
    my_dp = lax.axis_index(DP)
    my_group = lax.axis_index(TENSOR).astype(jnp.int32)

    rel = jnp.array([2 * z + y for y in range(2) for z in (0, 2, 1, 3)], jnp.int32)
    owner_at = my_dp ^ rel
    slots = jnp.arange(groups, dtype=jnp.int32)
    source = jnp.sum(
        jnp.where(owner_list[None, :] == owner_at[:, None], slots[None, :], 0), axis=1
    ).astype(jnp.int32)
    info = jnp.stack([my_group, lengths[0]])
    count = (lengths - my_group * share).astype(jnp.int32)

    line = Line()
    codes = jnp.transpose(code_emb, (1, 0, 2))

    (rows_in, gains_here, normed), shards = prep(line, source, frames_in, gains, master)
    grad, grad_t, codes_here = seed(line, source, count, jnp.transpose(cotangent, (1, 0, 2)), codes)
    (
        g_heads, g_up, g_down, l_heads, l_up, l_down, qkv, mixed, lse, middle, global_out, normed_a, normed_b,
        active, slope,
    ) = forward_global(line, info, rows_in, normed, gains_here, shards)

    l_qkv, l_mixed, l_middle, l_normed_b, l_a_t = local_heads(
        line, global_out, codes_here, gains_here, l_heads
    )
    l_active, l_slope, local_out, l_b_t = local_ff(line, source, l_normed_b, l_middle, l_up, l_down)
    local_out = jnp.transpose(local_out, (1, 0, 2))

    (
        grad_global, small, gain_c, gain_d, u_near, u_far, d2, d0, h2_near, h2_far, h0_near, h0_far,
    ) = local_back(
        line, grad, grad_t, l_b_t, l_a_t, l_active, l_slope, l_qkv, l_mixed, l_middle, global_out, codes_here,
        gains_here, l_heads, l_up, l_down,
    )
    def update(layer, third, pieces, before):
        return adam(
            line, layer, third, pieces, left_basis, right_basis, master, first_moment, second_moment, ema, before
        )

    def depth_second(keep, met):
        keep, send = sum_pieces(line, [keep, met])
        return keep, hop_z(send, 2)

    (
        grad_middle, grad_sum, gain_b, gu_near, gu_met, gh_near, gh_far, lu_keep, lu_met, gd_keep, gd_met, h2_met,
        h_first, h2_first,
    ) = backward_global(
        line, info, small, grad_global, middle, gains_here, lse, (g_up, g_down, g_heads), active, slope, normed_b,
        normed_a, qkv, mixed, (u_near, u_far, h2_far, h0_far, h2_near),
    )
    input_grad, gain_grads = finish(
        line, source, rows_in, grad_sum, grad_middle, gains_here, (gain_b, gain_c, gain_d)
    )
    (
        gain_grads, gu_keep, gu_met, gh_keep, gh_met, ld_keep, ld_send, lh_keep, lh_send,
    ) = last_transfers(
        line,
        gain_grads,
        (gu_near, gu_met, gh_near, gh_far, d0, d2, h0_near, h2_near, h0_far, h2_met, h_first, h2_first),
    )
    lh_met = hop_z(lh_send, 1)
    ld_met = hop_z(ld_send, 2)
    found = update(1, 1, (lu_keep, lu_met), None)
    found = update(0, 2, (gd_keep, gd_met), found)
    found = update(0, 1, (gu_keep, gu_met), found)
    lh = depth_second(lh_keep, lh_met)
    found = update(0, 0, (gh_keep, gh_met), found)
    found = update(1, 2, (ld_keep, ld_met), found)
    found = update(1, 0, lh, found)
    weight_grads, new_master, new_first, new_second, new_ema = found
    new_gain_first = beta_first * gain_first + (1.0 - beta_first) * gain_grads
    new_gain_second = beta_second * gain_second + (1.0 - beta_second) * gain_grads * gain_grads
    new_gains = gains - gain_rate * new_gain_first / (jnp.sqrt(new_gain_second) + adam_eps)
    return (
        local_out,
        input_grad,
        weight_grads,
        gain_grads,
        new_master,
        new_first,
        new_second,
        new_ema,
        new_gains,
        new_gain_first,
        new_gain_second,
    )


def solution(mesh):
    fits = mesh.shape[DP] == 8 and mesh.shape[TENSOR] == 4
    return jax.shard_map(
        shards_grid if fits else shards_any,
        mesh=mesh,
        in_specs=(
            P((DP, TENSOR), None),
            P((DP, TENSOR), None, None),
            P((DP, TENSOR), None, None),
            P(DP),
            P(),
            P(None, DP, TENSOR),
            P(None, DP, TENSOR),
            P(None, DP, TENSOR),
            P(None, DP, TENSOR),
            P(None, DP, TENSOR),
            P(None, DP, None, TENSOR),
            P(),
            P(),
            P(),
        ),
        out_specs=(
            P((DP, TENSOR), None, None),
            P((DP, TENSOR), None),
            P(None, DP, TENSOR),
            P(),
            P(None, DP, TENSOR),
            P(None, DP, TENSOR),
            P(None, DP, TENSOR),
            P(None, DP, TENSOR),
            P(),
            P(),
            P(),
        ),
        check_vma=False,
    )
```

```python
import math

import jax
import jax.numpy as jnp
from jax import lax
from jax.experimental import pallas as pl
from jax.experimental.pallas import tpu as pltpu
from jax.sharding import PartitionSpec as P

DP, TENSOR = "dp", "tensor"
D = 1024
HD = 64
FF = 4096
CB = 3
LMAX = 1024


norm_eps = 1e-06
beta_first = 0.5
beta_second = 0.5
adam_eps = 1e-08
step_rate = 0.05
gain_rate = 0.4
ema_decay = 0.9
masked_fill = -1e30
highest = lax.Precision.HIGHEST


def dot_rows(left, right):
    return jnp.dot(left, right, preferred_element_type=jnp.float32)


def dot_transposed(left, right):
    return lax.dot_general(
        left, right, (((1,), (1,)), ((), ())), preferred_element_type=jnp.float32
    )


def dot_over_rows(left, right):
    return lax.dot_general(
        left, right, (((0,), (0,)), ((), ())), preferred_element_type=jnp.float32
    )


def keep_rows(values):
    return values


def row_term(operand, weight):
    return dot_transposed(operand, weight)


def rms_forward(rows_in, gain):
    return (
        rows_in * lax.rsqrt(jnp.mean(rows_in * rows_in, axis=-1, keepdims=True) + norm_eps) * gain
    )


def rms_backward(rows_in, gain, grad_out):
    width = rows_in.shape[-1]
    scale_rows = lax.rsqrt(jnp.mean(rows_in * rows_in, axis=-1, keepdims=True) + norm_eps)
    scaled_grad = grad_out * gain
    inner_total = jnp.sum(scaled_grad * rows_in, axis=-1, keepdims=True)
    grad_in = (
        scale_rows * scaled_grad
        - rows_in * (scale_rows * scale_rows * scale_rows) * inner_total / width
    )
    gain_grad = jnp.sum(grad_out * rows_in * scale_rows, axis=0)
    return (grad_in, gain_grad)


def gelu_slope(upper):
    normal_cdf = 0.5 * (1.0 + lax.erf(upper * (1.0 / math.sqrt(2.0))))
    density = jnp.exp(-0.5 * upper * upper) * (1.0 / math.sqrt(2.0 * math.pi))
    return normal_cdf + upper * density


def split_layer(layer_cols, groups, head_cols, ff_cols):
    width = layer_cols.shape[0]
    grouped = layer_cols.reshape(width, groups, -1)

    def columns(begin, extent):
        return grouped[:, :, begin : begin + extent].reshape(width, groups * extent)

    w_qkv = jnp.concatenate(
        [columns(0, head_cols), columns(head_cols, head_cols), columns(2 * head_cols, head_cols)],
        axis=1,
    )
    return (
        w_qkv,
        columns(3 * head_cols, head_cols),
        columns(4 * head_cols, ff_cols),
        columns(4 * head_cols + ff_cols, ff_cols),
    )


def join_layer(grad_parts, groups):
    grad_qkv, grad_out, grad_up, grad_down = grad_parts
    width = grad_qkv.shape[0]
    head_width = grad_qkv.shape[1] // 3
    pieces = [
        grad_qkv[:, 0:head_width],
        grad_qkv[:, head_width : 2 * head_width],
        grad_qkv[:, 2 * head_width :],
        grad_out,
        grad_up,
        grad_down,
    ]
    return jnp.concatenate([piece.reshape(width, groups, -1) for piece in pieces], axis=2).reshape(
        width, -1
    )


def global_scores(queries, key_rows, length):
    span = queries.shape[0]
    heads = queries.shape[1] // HD
    scores = jnp.einsum(
        "qhd,khd->hqk",
        queries.reshape(span, heads, HD),
        key_rows.reshape(span, heads, HD),
        preferred_element_type=jnp.float32,
    ) * HD ** (-0.5)
    rows_at = lax.broadcasted_iota(jnp.int32, (span, span), 0)
    cols_at = lax.broadcasted_iota(jnp.int32, (span, span), 1)
    allowed = (cols_at <= rows_at) & (cols_at < length)
    return jnp.where(allowed[None], scores, masked_fill)


def global_attend(queries, key_rows, value_rows, lengths):
    items = lengths.shape[0]
    span = queries.shape[0] // items
    heads = queries.shape[1] // HD

    def one_item(packed):
        item_query, item_key, item_value, length = packed
        scores = global_scores(item_query, item_key, length)
        row_max = jnp.max(scores, axis=-1, keepdims=True)
        expanded = jnp.exp(scores - row_max)
        row_total = jnp.sum(expanded, axis=-1, keepdims=True)
        probability = (expanded / row_total).astype(jnp.bfloat16)
        mixed = jnp.einsum(
            "hqk,khd->qhd",
            probability,
            item_value.reshape(span, heads, HD),
            preferred_element_type=jnp.float32,
        )
        return (
            mixed.reshape(span, -1).astype(jnp.bfloat16),
            (row_max + jnp.log(row_total))[..., 0],
        )

    mixed, log_total = lax.map(
        one_item,
        (
            queries.reshape(items, span, -1),
            key_rows.reshape(items, span, -1),
            value_rows.reshape(items, span, -1),
            lengths,
        ),
    )
    return (mixed.reshape(items * span, -1), log_total)


def global_attend_back(queries, key_rows, value_rows, lengths, log_total, grad_mixed):
    items = lengths.shape[0]
    span = queries.shape[0] // items
    heads = queries.shape[1] // HD
    scale_score = HD ** (-0.5)

    def one_item(packed):
        item_query, item_key, item_value, length, item_lse, item_grad = packed
        scores = global_scores(item_query, item_key, length)
        probability = jnp.exp(scores - item_lse[..., None])
        grad_heads = item_grad.reshape(span, heads, HD)
        query_heads = item_query.reshape(span, heads, HD)
        key_heads = item_key.reshape(span, heads, HD)
        value_heads = item_value.reshape(span, heads, HD)
        grad_value = jnp.einsum(
            "hqk,qhd->khd",
            probability.astype(jnp.bfloat16),
            grad_heads,
            preferred_element_type=jnp.float32,
        )
        grad_prob = jnp.einsum(
            "qhd,khd->hqk", grad_heads, value_heads, preferred_element_type=jnp.float32
        )
        center = jnp.sum(probability * grad_prob, axis=-1, keepdims=True)
        grad_scores = (probability * (grad_prob - center)).astype(jnp.bfloat16)
        grad_query = (
            jnp.einsum("hqk,khd->qhd", grad_scores, key_heads, preferred_element_type=jnp.float32)
            * scale_score
        )
        grad_key = (
            jnp.einsum("hqk,qhd->khd", grad_scores, query_heads, preferred_element_type=jnp.float32)
            * scale_score
        )
        return jnp.concatenate(
            [
                grad_query.reshape(span, -1),
                grad_key.reshape(span, -1),
                grad_value.reshape(span, -1),
            ],
            axis=1,
        ).astype(jnp.bfloat16)

    grads = lax.map(
        one_item,
        (
            queries.reshape(items, span, -1),
            key_rows.reshape(items, span, -1),
            value_rows.reshape(items, span, -1),
            lengths,
            log_total,
            grad_mixed.reshape(items, span, -1),
        ),
    )
    return grads.reshape(items * span, -1)


def local_probability(queries, key_rows):
    frame_count = queries.shape[0] // CB
    heads = queries.shape[1] // HD
    scores = jnp.einsum(
        "fqhd,fkhd->fhqk",
        queries.reshape(frame_count, CB, heads, HD),
        key_rows.reshape(frame_count, CB, heads, HD),
        preferred_element_type=jnp.float32,
    ) * HD ** (-0.5)
    rows_at = lax.broadcasted_iota(jnp.int32, (CB, CB), 0)
    cols_at = lax.broadcasted_iota(jnp.int32, (CB, CB), 1)
    scores = jnp.where(cols_at <= rows_at, scores, masked_fill)
    row_max = jnp.max(scores, axis=-1, keepdims=True)
    expanded = jnp.exp(scores - row_max)
    return expanded / jnp.sum(expanded, axis=-1, keepdims=True)


def local_attend(queries, key_rows, value_rows):
    frame_count = queries.shape[0] // CB
    heads = queries.shape[1] // HD
    probability = local_probability(queries, key_rows).astype(jnp.bfloat16)
    mixed = jnp.einsum(
        "fhqk,fkhd->fqhd",
        probability,
        value_rows.reshape(frame_count, CB, heads, HD),
        preferred_element_type=jnp.float32,
    )
    return (mixed.reshape(queries.shape[0], -1).astype(jnp.bfloat16), jnp.zeros((), jnp.float32))


def local_attend_back(queries, key_rows, value_rows, saved, grad_mixed):
    frame_count = queries.shape[0] // CB
    heads = queries.shape[1] // HD
    scale_score = HD ** (-0.5)
    probability = local_probability(queries, key_rows)
    grad_heads = grad_mixed.reshape(frame_count, CB, heads, HD)
    query_heads = queries.reshape(frame_count, CB, heads, HD)
    key_heads = key_rows.reshape(frame_count, CB, heads, HD)
    value_heads = value_rows.reshape(frame_count, CB, heads, HD)
    grad_value = jnp.einsum(
        "fhqk,fqhd->fkhd",
        probability.astype(jnp.bfloat16),
        grad_heads,
        preferred_element_type=jnp.float32,
    )
    grad_prob = jnp.einsum(
        "fqhd,fkhd->fhqk", grad_heads, value_heads, preferred_element_type=jnp.float32
    )
    center = jnp.sum(probability * grad_prob, axis=-1, keepdims=True)
    grad_scores = (probability * (grad_prob - center)).astype(jnp.bfloat16)
    grad_query = (
        jnp.einsum("fhqk,fkhd->fqhd", grad_scores, key_heads, preferred_element_type=jnp.float32)
        * scale_score
    )
    grad_key = (
        jnp.einsum("fhqk,fqhd->fkhd", grad_scores, query_heads, preferred_element_type=jnp.float32)
        * scale_score
    )
    total_rows = queries.shape[0]
    return jnp.concatenate(
        [
            grad_query.reshape(total_rows, -1),
            grad_key.reshape(total_rows, -1),
            grad_value.reshape(total_rows, -1),
        ],
        axis=1,
    ).astype(jnp.bfloat16)


def block_forward(rows_in, matrices, gain_a, gain_b, path, attend):
    gather_rows, sum_rows = (path[0], path[1])
    w_qkv, w_out, w_up, w_down = matrices
    normed_a = gather_rows(rms_forward(rows_in, gain_a).astype(jnp.bfloat16))
    projected = dot_rows(normed_a, w_qkv).astype(jnp.bfloat16)
    head_width = projected.shape[1] // 3
    mixed, saved = attend(
        projected[:, :head_width],
        projected[:, head_width : 2 * head_width],
        projected[:, 2 * head_width :],
    )
    middle = rows_in + sum_rows(mixed, w_out)
    normed_b = gather_rows(rms_forward(middle, gain_b).astype(jnp.bfloat16))
    upper = dot_rows(normed_b, w_up)
    active = jax.nn.gelu(upper, approximate=False).astype(jnp.bfloat16)
    result = middle + sum_rows(active, w_down)
    return (result, (rows_in, normed_a, projected, mixed, saved, middle, normed_b, upper, active))


def block_backward(grad_result, kept, matrices, gain_a, gain_b, path, attend_back):
    gather_grads, sum_back = (path[2], path[3])
    rows_in, normed_a, projected, mixed, saved, middle, normed_b, upper, active = kept
    w_qkv, w_out, w_up, w_down = matrices
    grad_branch = gather_grads(grad_result.astype(jnp.bfloat16))
    grad_down = dot_over_rows(grad_branch, active)
    grad_active = dot_rows(grad_branch, w_down)
    grad_upper = (grad_active * gelu_slope(upper)).astype(jnp.bfloat16)
    grad_up = dot_over_rows(normed_b, grad_upper)
    grad_normed_b = sum_back(grad_upper, w_up)
    grad_middle_part, gain_b_grad = rms_backward(middle, gain_b, grad_normed_b)
    grad_middle = grad_result + grad_middle_part
    grad_attn = gather_grads(grad_middle.astype(jnp.bfloat16))
    grad_out = dot_over_rows(grad_attn, mixed)
    grad_mixed = dot_rows(grad_attn, w_out).astype(jnp.bfloat16)
    head_width = projected.shape[1] // 3
    grad_qkv = attend_back(
        projected[:, :head_width],
        projected[:, head_width : 2 * head_width],
        projected[:, 2 * head_width :],
        saved,
        grad_mixed,
    )
    grad_weight_qkv = dot_over_rows(normed_a, grad_qkv)
    grad_normed_a = sum_back(grad_qkv, w_qkv)
    grad_rows_part, gain_a_grad = rms_backward(rows_in, gain_a, grad_normed_a)
    return (
        grad_middle + grad_rows_part,
        (grad_weight_qkv, grad_out, grad_up, grad_down),
        gain_a_grad,
        gain_b_grad,
    )


def shards_any(
    frames_in,
    code_emb,
    cotangent,
    lengths,
    owner_list,
    master,
    first_moment,
    second_moment,
    ema,
    left_basis,
    right_basis,
    gains,
    gain_first,
    gain_second,
):
    tensor_count = lax.axis_size(TENSOR)
    group_count = lax.axis_size(DP)
    head_cols = D // tensor_count
    ff_cols = FF // tensor_count
    share = frames_in.shape[0]
    owned_rows = master.shape[1]
    gathered = lax.all_gather(master.astype(jnp.bfloat16), DP, axis=1, tiled=True)
    layers = jnp.take(gathered.reshape(2, group_count, owned_rows, -1), owner_list, axis=1).reshape(
        2, group_count * owned_rows, -1
    )

    def gather_rows(values):
        return lax.all_gather(values, TENSOR, axis=0, tiled=True)

    def gather_grads(values):
        return lax.all_gather(values, TENSOR, axis=0, tiled=True)

    def sum_rows(operand, weight):
        return lax.psum_scatter(
            row_term(operand, weight).astype(jnp.bfloat16),
            TENSOR,
            scatter_dimension=0,
            tiled=True,
        ).astype(jnp.float32)

    def sum_back(operand, weight):
        return lax.psum_scatter(
            row_term(operand, weight).astype(jnp.bfloat16),
            TENSOR,
            scatter_dimension=0,
            tiled=True,
        ).astype(jnp.float32)

    heads_path = (gather_rows, sum_rows, gather_grads, sum_back)
    rows_path = (keep_rows, dot_transposed, keep_rows, dot_transposed)

    def attend_global(queries, key_rows, value_rows):
        return global_attend(queries, key_rows, value_rows, lengths)

    def attend_global_back(queries, key_rows, value_rows, saved, grad_mixed):
        return global_attend_back(queries, key_rows, value_rows, lengths, saved, grad_mixed)

    global_matrices = split_layer(layers[0], 1, head_cols, ff_cols)
    global_out, global_kept = block_forward(
        frames_in.astype(jnp.float32),
        global_matrices,
        gains[0],
        gains[1],
        heads_path,
        attend_global,
    )
    local_in = (global_out[:, None, :] + code_emb.astype(jnp.float32)).reshape(share * CB, -1)
    local_layer = lax.all_gather(layers[1], TENSOR, axis=1, tiled=True)
    local_matrices = split_layer(local_layer, tensor_count, head_cols, ff_cols)
    local_result, local_kept = block_forward(
        local_in, local_matrices, gains[2], gains[3], rows_path, local_attend
    )
    local_out = local_result.reshape(share, CB, -1).astype(jnp.bfloat16)
    frame_at = lax.axis_index(TENSOR) * share + jnp.arange(share, dtype=jnp.int32)
    item_at = frame_at // LMAX
    item_slots = jnp.arange(lengths.shape[0], dtype=jnp.int32)
    item_length = jnp.sum(
        jnp.where(item_at[:, None] == item_slots[None, :], lengths[None, :], 0), axis=1
    )
    valid = (frame_at % LMAX < item_length).astype(jnp.float32)
    grad_local = (cotangent.astype(jnp.float32) * valid[:, None, None]).reshape(share * CB, -1)
    grad_local_in, local_weight_grads, gain_c_grad, gain_d_grad = block_backward(
        grad_local, local_kept, local_matrices, gains[2], gains[3], rows_path, local_attend_back
    )
    grad_global_out = jnp.sum(grad_local_in.reshape(share, CB, -1), axis=1)
    input_grad, global_weight_grads, gain_a_grad, gain_b_grad = block_backward(
        grad_global_out,
        global_kept,
        global_matrices,
        gains[0],
        gains[1],
        heads_path,
        attend_global_back,
    )
    local_grads = join_layer(local_weight_grads, tensor_count)
    local_grads = lax.psum_scatter(
        local_grads.astype(jnp.bfloat16), TENSOR, scatter_dimension=1, tiled=True
    ).astype(jnp.float32)
    layer_grads = jnp.stack([join_layer(global_weight_grads, 1), local_grads])
    slots = jnp.arange(group_count, dtype=jnp.int32)
    inverse = jnp.sum(jnp.where(owner_list[None, :] == slots[:, None], slots[None, :], 0), axis=1)
    ordered = jnp.take(
        layer_grads.reshape(2, group_count, owned_rows, -1), inverse, axis=1
    ).reshape(2, group_count * owned_rows, -1)
    weight_grads = lax.psum_scatter(
        ordered.astype(jnp.bfloat16), DP, scatter_dimension=1, tiled=True
    ).astype(jnp.float32)
    gain_grads = lax.psum(
        jnp.stack([gain_a_grad, gain_b_grad, gain_c_grad, gain_d_grad]), (DP, TENSOR)
    )
    tile_count = right_basis.shape[1]
    turned_left = jnp.einsum("lab,lac->lbc", left_basis, weight_grads, precision=highest)
    rotated = jnp.einsum(
        "lbkc,lkce->lbke",
        turned_left.reshape(2, owned_rows, tile_count, -1),
        right_basis,
        precision=highest,
    ).reshape(weight_grads.shape)
    new_first = beta_first * first_moment + (1.0 - beta_first) * rotated
    new_second = beta_second * second_moment + (1.0 - beta_second) * rotated * rotated
    turned = new_first / (jnp.sqrt(new_second) + adam_eps)
    back_right = jnp.einsum(
        "lbke,lkce->lbkc",
        turned.reshape(2, owned_rows, tile_count, -1),
        right_basis,
        precision=highest,
    )
    back_full = jnp.einsum(
        "lab,lbc->lac", left_basis, back_right.reshape(weight_grads.shape), precision=highest
    )
    new_master = master - step_rate * back_full
    new_ema = ema_decay * ema + (1.0 - ema_decay) * new_master
    new_gain_first = beta_first * gain_first + (1.0 - beta_first) * gain_grads
    new_gain_second = beta_second * gain_second + (1.0 - beta_second) * gain_grads * gain_grads
    new_gains = gains - gain_rate * new_gain_first / (jnp.sqrt(new_gain_second) + adam_eps)
    return (
        local_out,
        input_grad,
        weight_grads,
        gain_grads,
        new_master,
        new_first,
        new_second,
        new_ema,
        new_gains,
        new_gain_first,
        new_gain_second,
    )


MIB = 1024 * 1024
VMEM_WHOLE = pl.BlockSpec(memory_space=pltpu.VMEM)
IN_SMEM = pl.BlockSpec(memory_space=pltpu.SMEM)
IN_HBM = pl.BlockSpec(memory_space=pl.ANY)


def shaped(shape, kind):
    return jax.ShapeDtypeStruct(shape, kind)


def cost(flops, moved, exps=0):
    return pl.CostEstimate(flops=int(flops), bytes_accessed=int(moved), transcendentals=int(exps))


weight_of = {
    "forward_global": 170,
    "local_heads": 18,
    "local_ff": 34,
    "local_back": 81,
    "backward_global": 90,
    "last_transfers": 60,
    "adam_update": 5,
}


def group_at(rel):
    mine = lax.axis_index(TENSOR)
    return 2 * ((mine // 2 + rel // 2) % 2) + (mine % 2 + rel % 2) % 2


CORE, X, Y, Z1, Z2 = range(5)


def partner_of(hop):
    dp, tensor = lax.axis_index(DP), lax.axis_index(TENSOR)
    if hop == CORE:
        return {TENSOR: tensor + 1 - 2 * (tensor % 2)}
    if hop == X:
        return {TENSOR: (tensor + 2) % 4}
    if hop == Y:
        return {DP: dp + 1 - 2 * (dp % 2)}
    if hop == Z1:
        return {DP: dp + 2 - 4 * ((dp // 2) % 2)}
    return {DP: (dp + 4) % 8}


def greet(hops):
    barrier = pltpu.get_barrier_semaphore()
    for hop in hops:
        pl.semaphore_signal(
            barrier, inc=1, device_id=partner_of(hop), device_id_type=pl.DeviceIdType.MESH
        )
    pl.semaphore_wait(barrier, len(hops))


def to_partner(hop, source, target, send, recv):
    return pltpu.make_async_remote_copy(
        src_ref=source,
        dst_ref=target,
        send_sem=send,
        recv_sem=recv,
        device_id=partner_of(hop),
        device_id_type=pl.DeviceIdType.MESH,
    )


def part(array, begin, rows):
    return (array, begin, rows)


class Line:
    def __init__(self):
        self.token = None
        self.moves = ()
        self.arrived = []
        self.calls = 0

    def carry(self, *moves):
        self.moves = moves

    def run(self, body, args, in_specs, out_specs, out_shape, aliases=None, scratch_shapes=(), limit=32, hops=(), **rest):
        moves, self.moves = self.moves, ()
        sources, copies, landed = [], [], []
        for hop, *pieces in moves:
            offset = 0
            for piece in pieces:
                array, begin, rows = piece if isinstance(piece, tuple) else (piece, 0, piece.shape[0])
                which = next((at for at, one in enumerate(sources) if one is array), len(sources))
                if which == len(sources):
                    sources.append(array)
                copies.append((hop, which, begin, rows, len(landed), offset))
                offset += rows
            landed.append(shaped((offset,) + array.shape[1:], array.dtype))
        reach = list(hops) or list(dict.fromkeys(move[0] for move in moves))
        lead = 0 if self.token is None else 1
        inputs = lead + len(args)
        first_out = inputs + len(sources)
        outputs = len(out_shape)
        first_scratch = first_out + outputs + len(landed) + 1
        steps = rest.get("grid", (1,))[0]

        def inner(*refs):
            scratch = refs[first_scratch:]
            pending = []
            if copies:
                *scratch, send, recv = scratch
                for at, (hop, which, begin, rows, where, offset) in enumerate(copies):
                    pending.append(
                        to_partner(
                            hop,
                            refs[inputs + which].at[pl.ds(begin, rows)],
                            refs[first_out + outputs + where].at[pl.ds(offset, rows)],
                            send.at[at],
                            recv.at[at],
                        )
                    )

            def begin_all():
                greet(reach)
                for one in pending:
                    one.start()

            def end_all():
                for one in pending:
                    one.wait()

            at_ends = (lambda step, act: pl.when(pl.program_id(0) == step)(act)) if steps > 1 else (
                lambda step, act: act()
            )
            if pending:
                at_ends(0, begin_all)
            body(*refs[lead:inputs], *refs[first_out : first_out + outputs], *scratch)
            if pending:
                at_ends(steps - 1, end_all)

        extra = {}
        if reach:
            extra = {"collective_id": self.calls, "has_side_effects": True}
            self.calls += 1
        found = pl.pallas_call(
            inner,
            in_specs=[IN_HBM] * lead + list(in_specs) + [IN_HBM] * len(sources),
            out_specs=list(out_specs) + [IN_HBM] * (len(landed) + 1),
            out_shape=list(out_shape) + landed + [shaped((8, 128), jnp.float32)],
            scratch_shapes=list(scratch_shapes)
            + ([pltpu.SemaphoreType.DMA((len(copies),))] * 2 if copies else []),
            input_output_aliases={lead + at: to for at, to in (aliases or {}).items()},
            cost_estimate=cost(weight_of.get(rest["name"], 1.0) * 0.2e9, 1000),
            compiler_params=pltpu.CompilerParams(vmem_limit_bytes=limit * MIB, **extra),
            **rest,
        )(*([self.token] * lead), *args, *sources)
        self.token = found[-1]
        self.arrived = list(found[outputs:-1])
        return list(found[:outputs])


def lanes_of(source_ref, at, width):
    return pl.ds(pl.multiple_of(source_ref[at] * width, width), width)


def norm_rows(rows, gain):
    scale = lax.rsqrt(jnp.mean(rows * rows, axis=-1, keepdims=True) + norm_eps)
    return rows * scale * gain


def norm_rows_back(rows, gain, grad):
    scale = lax.rsqrt(jnp.mean(rows * rows, axis=-1, keepdims=True) + norm_eps)
    scaled = grad * gain
    inner = jnp.sum(scaled * rows, axis=-1, keepdims=True)
    grad_in = scale * scaled - rows * (scale * scale * scale) * inner / rows.shape[-1]
    return grad_in, jnp.sum(grad * rows * scale, axis=0, keepdims=True)


def gelu_both(upper):
    size = jnp.abs(upper)
    base = 1.0 + (0.3275911 / math.sqrt(2.0)) * size
    guess = pl.reciprocal(base, approx=True)
    ratio = guess * (2.0 - base * guess)
    bell = jnp.exp(-0.5 * upper * upper)
    series = ratio * (
        0.5 * 0.254829592
        + ratio
        * (
            -0.5 * 0.284496736
            + ratio * (0.5 * 1.421413741 + ratio * (-0.5 * 1.453152027 + ratio * (0.5 * 1.061405429)))
        )
    )
    tail = series * bell
    cdf = jnp.where(upper >= 0.0, 1.0 - tail, tail)
    density = bell * (1.0 / math.sqrt(2.0 * math.pi))
    return (upper * cdf).astype(jnp.bfloat16), (cdf + upper * density).astype(jnp.bfloat16)


def both(rows, near, far):
    depth = near.shape[0]
    return dot_rows(rows[:, :depth], near) + dot_rows(rows[:, depth:], far)


def held(shape):
    return pl.BlockSpec(shape, lambda step: (0,) * len(shape), pipeline_mode=pl.Buffered(1))


def by_cols(shape):
    return pl.BlockSpec(shape, lambda step: (0, step))


def prep_body(source_ref, frames_ref, gains_ref, *refs):
    masters, (rows_ref, gains_out_ref, normed_ref), shards = refs[:6], refs[6:9], refs[9:]
    for master_ref, shard_ref in zip(masters, shards):
        shard_ref[...] = master_ref[0].astype(jnp.bfloat16)
    owned = frames_ref.shape[1] // source_ref.shape[0]
    for at in range(source_ref.shape[0]):
        here = slice(at * owned, (at + 1) * owned)
        rows_ref[:, here] = frames_ref[:, lanes_of(source_ref, at, owned)]
        gains_out_ref[:, here] = gains_ref[:, lanes_of(source_ref, at, owned)]
    normed_ref[...] = norm_rows(rows_ref[...].astype(jnp.float32), gains_out_ref[0:1, :]).astype(
        jnp.bfloat16
    )


def prep(line, source, frames, gains, master):
    owned, columns = master.shape[1], master.shape[2] // 3

    def spec(layer, third):
        return pl.BlockSpec((1, owned, columns), lambda step: (layer, 0, third))

    shapes = [
        shaped(frames.shape, jnp.bfloat16),
        shaped(gains.shape, jnp.float32),
        shaped(frames.shape, jnp.bfloat16),
    ] + [shaped((owned, columns), jnp.bfloat16)] * 6
    found = line.run(
        prep_body,
        (source, frames, gains) + (master,) * 6,
        grid=(1,),
        in_specs=[IN_SMEM, held(frames.shape), held(gains.shape)]
        + [spec(layer, third) for layer in range(2) for third in range(3)],
        out_specs=[held(one.shape) for one in shapes],
        out_shape=shapes,
        limit=60,
        name="prep_rows",
    )
    return found[:3], found[3:]


def finish_body(source_ref, rows_ref, sum_ref, grad_ref, gains_ref, gb_ref, gc_ref, gd_ref, out_ref, gain_ref):
    back, gain_grad = norm_rows_back(rows_ref[...].astype(jnp.float32), gains_ref[0:1, :], sum_ref[...])
    total = grad_ref[...] + back
    owned = out_ref.shape[1] // source_ref.shape[0]
    for at in range(source_ref.shape[0]):
        here = slice(at * owned, (at + 1) * owned)
        there = lanes_of(source_ref, at, owned)
        out_ref[:, there] = total[:, here]
        gain_ref[0:1, there] = gain_grad[:, here]
        gain_ref[1:2, there] = gb_ref[:, here]
        gain_ref[2:3, there] = gc_ref[:, here]
        gain_ref[3:4, there] = gd_ref[:, here]


def finish(line, source, rows, total, grad, gains, others):
    return line.run(
        finish_body,
        (source, rows, total, grad, gains, *others),
        in_specs=[IN_SMEM] + [VMEM_WHOLE] * 7,
        out_specs=[VMEM_WHOLE] * 2,
        out_shape=[shaped(rows.shape, jnp.float32), shaped((4, rows.shape[1]), jnp.float32)],
        limit=60,
        name="input_grad",
    )


forward_order = (
    0, 12, 37, 4, 36, 50, 49, 66, 38, 8, 2, 1, 51, 43, 13, 15, 14, 24, 5, 3, 6, 16, 39, 9, 10, 67, 68, 18, 17,
    20, 85, 86, 45, 87, 44, 88, 69, 72, 52, 53, 73, 54, 74, 75, 55, 41, 22, 76, 56, 25, 7, 27, 26, 77, 62, 78,
    64, 63, 21, 40, 11, 19, 28, 70, 46, 65, 23, 71, 42, 89, 30, 32, 29, 90, 91, 92, 79, 57, 58, 80, 59, 81,
    60, 82, 61, 31, 34, 33, 83, 48, 84, 35, 47,
)


def forward_body(
    info_ref, rows_ref, normed_ref, gains_ref, ga_s, gu_s, gd_s, la_s, lu_s, ld_s,
    ga, gu, gd, la, lu, ld, qkv_ref, mixed_ref, lse_ref, middle_ref, out_ref, na_h, nb_h, active_h, slope_h,
    na, nb, a_v, u_v, d_v, acc, lse_wide, act, slp, parts, met_core, met_x, sends_x, sems, send, recv,
):
    share = rows_ref.shape[0]
    owned = ga_s.shape[0]
    half = D // 2
    width = mixed_ref.shape[1]
    span = 4 * share
    length = info_ref[1]
    scale = HD ** (-0.5)
    flying, filed, numbers = [], [], []

    def fly(hop, source, target):
        at = len(numbers)
        copy = to_partner(hop, source, target, send.at[at], recv.at[at])
        copy.start()
        numbers.append(at)
        flying.append(copy)
        return copy

    def file(source, target):
        copy = pltpu.make_async_copy(source, target, sems.at[len(filed)])
        copy.start()
        filed.append(copy)
        return copy

    quarter = half // 2
    arrived = set()
    named = {}

    def need(*names):
        for name in names:
            if name not in arrived:
                arrived.add(name)
                named[name].wait_recv()

    def same(hop, whole, begin, rows, shift):
        return lambda: fly(hop, whole.at[pl.ds(begin, rows)], whole.at[pl.ds(begin + shift, rows)])

    def level(hop, stack, begin, to, start, rows):
        here = pl.ds(start, rows)
        return lambda: fly(hop, stack.at[begin, here], stack.at[to, here])

    moves = {}
    for letter, shard, whole in (("A", ga_s, ga), ("U", gu_s, gu), ("D", gd_s, gd)):
        moves["g2" + letter] = (
            (lambda shard, whole: lambda: fly(Z2, shard, whole.at[pl.ds(owned, owned)]))(shard, whole),
            (),
        )
        moves["g1" + letter] = (same(Z1, whole, 0, quarter, quarter), ("g2" + letter, "own"))
        moves["gy0" + letter] = (same(Y, whole, 0, quarter, half), ("g2" + letter, "own"))
        moves["gy1" + letter] = (same(Y, whole, quarter, quarter, half), ("g1" + letter,))
    for letter, shard, stack in (("A", la_s, la), ("U", lu_s, lu)):
        near = stack.at[0]
        moves["l2" + letter] = (
            (lambda shard, near: lambda: fly(Z2, shard, near.at[pl.ds(owned, owned)]))(shard, near),
            (),
        )
        moves["l1" + letter] = (same(Z1, near, 0, quarter, quarter), ("l2" + letter, "own"))
        for at in range(2):
            source = ("l2" + letter, "own") if at == 0 else ("l1" + letter,)
            moves[f"ly{at}{letter}"] = (same(Y, near, at * quarter, quarter, half), source)
            moves[f"lx{at}{letter}"] = (level(X, stack, 0, 2, at * quarter, quarter), source)
            if letter == "A":
                moves[f"lf{at}{letter}"] = (
                    level(X, stack, 0, 2, half + at * quarter, quarter),
                    (f"ly{at}{letter}",),
                )
            else:
                moves[f"lf{at}{letter}"] = (
                    same(Y, stack.at[2], at * quarter, quarter, half),
                    (f"lx{at}{letter}",),
                )
        moves["cn" + letter] = (level(CORE, stack, 0, 1, 0, half), ("l2" + letter, "l1" + letter, "own"))
        moves["cf" + letter] = (level(CORE, stack, 0, 1, half, half), ("ly0" + letter, "ly1" + letter))
        moves["cx" + letter] = (level(CORE, stack, 2, 3, 0, half), ("lx0" + letter, "lx1" + letter))
        moves["cxf" + letter] = (level(CORE, stack, 2, 3, half, half), ("lf0" + letter, "lf1" + letter))
    moves["dx"] = (lambda: fly(X, ld_s, ld.at[2, pl.ds(0, owned)]), ())
    moves["dy"] = (lambda: fly(Y, ld_s, ld.at[0, pl.ds(half, owned)]), ())
    moves["dxy"] = (same(Y, ld.at[2], 0, owned, half), ("dx",))
    for at, source in enumerate((("own",), ("dy",), ("dx",), ("dxy",))):
        stack, begin = ld.at[2 * (at // 2)], half * (at % 2)
        moves[f"d2{at}"] = (same(Z2, stack, begin, owned, owned), source)
        moves[f"d1{at}"] = (same(Z1, stack, begin, quarter, quarter), (f"d2{at}",) + source)
    moves["cdn"] = (level(CORE, ld, 0, 1, 0, D), ("d10", "d11", "d20", "d21", "dy", "own"))
    moves["cdx"] = (level(CORE, ld, 2, 3, 0, D), ("d12", "d13", "d22", "d23", "dx", "dxy"))
    moves["nx"] = (lambda: fly(X, normed_ref, na.at[pl.ds(2 * share, share)]), ())
    moves["nc"] = (lambda: fly(CORE, normed_ref, na.at[pl.ds(share, share)]), ())
    moves["nxc"] = (same(CORE, na, 2 * share, share, share), ("nx",))
    strip = share // 2
    strips = [pl.ds(at * strip, strip) for at in range(2)]

    def sums_moves(far, near, over, which):
        for at, name in enumerate(far):
            moves[name] = (
                (lambda rows: lambda: fly(CORE, parts.at[3, rows], met_core.at[2 * which, rows]))(strips[at]),
                (),
            )
        moves[near] = (lambda: fly(CORE, parts.at[1], met_core.at[2 * which + 1]), ())
        for at, name in enumerate(over):
            moves[name] = (
                (lambda rows: lambda: fly(X, sends_x.at[which, rows], met_x.at[which, rows]))(strips[at]),
                (),
            )

    sums_moves(("c3a", "c3b"), "c1", ("sx0", "sx1"), 0)
    sums_moves(("e3a", "e3b"), "e1", ("tx0", "tx1"), 1)
    for at in range(2):
        moves[f"ox{at}"] = (same(X, nb, at * strip, strip, 2 * share), ())
    moves["oc"] = (same(CORE, nb, 0, share, share), ())
    moves["oxc"] = (same(CORE, nb, 2 * share, share, share), ("ox0", "ox1"))

    def do_own():
        copies = [
            file(shard, whole.at[pl.ds(0, owned)])
            for shard, whole in (
                (ga_s, ga), (la_s, la.at[0]), (gu_s, gu), (gd_s, gd), (lu_s, lu.at[0]), (ld_s, ld.at[0]),
            )
        ]
        na[pl.ds(0, share), :] = normed_ref[...]
        for one in copies:
            one.wait()

    def load(letter, whole, target):
        need("g2" + letter, "g1" + letter, "gy0" + letter, "gy1" + letter)
        return file(whole, target)

    def do_load_a():
        load("A", ga, a_v).wait()

    def do_qkv():
        need("nx", "nc", "nxc")
        outgoing.append(file(na, na_h))
        for rel in range(4):
            at = pl.ds(pl.multiple_of(group_at(rel) * share, share), share)
            full = both(
                na[rel * share : (rel + 1) * share, :], a_v[:half, : 3 * width], a_v[half:, : 3 * width]
            )
            qkv_ref[at, :] = full.astype(jnp.bfloat16)
        acc[:, :width] = jnp.zeros((span, width), jnp.float32)
        lse_wide[...] = jnp.zeros_like(lse_wide)

    head_of = lax.broadcasted_iota(jnp.int32, (1, width), 1) // HD
    lane = lax.broadcasted_iota(jnp.int32, (1, 128), 1)

    def do_head(head):
        own_lanes = head_of == head
        for block in range(4):
            rows = slice(block * share, (block + 1) * share)
            reach = (block + 1) * share
            query = jnp.where(own_lanes, qkv_ref[rows, :width] * scale, 0.0).astype(jnp.bfloat16)
            scores = dot_transposed(query, qkv_ref[:reach, width : 2 * width])
            row_at = block * share + lax.broadcasted_iota(jnp.int32, scores.shape, 0)
            col_at = lax.broadcasted_iota(jnp.int32, scores.shape, 1)
            scores = jnp.where((col_at <= row_at) & (col_at < length), scores, masked_fill)
            top = jnp.max(scores, axis=-1, keepdims=True)
            expanded = jnp.exp(scores - top)
            total = jnp.sum(expanded, axis=-1, keepdims=True)
            prob = (expanded * (1.0 / total)).astype(jnp.bfloat16)
            value = jnp.where(own_lanes, qkv_ref[:reach, 2 * width :], 0.0).astype(jnp.bfloat16)
            acc[rows, :width] += dot_rows(prob, value)
            lse_wide[rows, :] = jnp.where(lane == head, top + jnp.log(total), lse_wide[rows, :])

    def do_mix():
        mixed_ref[...] = acc[:, :width].astype(jnp.bfloat16)
        lse_ref[...] = jnp.transpose(lse_wide[...])[: lse_ref.shape[0], :]

    def out_part(rel):
        at = pl.ds(pl.multiple_of(group_at(rel) * share, share), share)
        rows = mixed_ref[at, :]
        parts[rel, :, :half] = dot_transposed(rows, a_v[:half, 3 * width :]).astype(jnp.bfloat16)
        parts[rel, :, half:] = dot_transposed(rows, a_v[half:, 3 * width :]).astype(jnp.bfloat16)

    def down_part(rel):
        parts[rel] = acc[rel * share : (rel + 1) * share, :].astype(jnp.bfloat16)

    def several(act_on, *values):
        def do():
            for value in values:
                act_on(value)

        return do

    def do_add(which, at, name):
        def do():
            need(name)
            rows = strips[at]
            total = parts[2, rows, :].astype(jnp.float32) + met_core[2 * which, rows, :].astype(jnp.float32)
            sends_x[which, rows, :] = total.astype(jnp.bfloat16)

        return do

    def gathered(which, rows, base):
        return (
            base
            + parts[0, rows, :].astype(jnp.float32)
            + met_core[2 * which + 1, rows, :].astype(jnp.float32)
            + met_x[which, rows, :].astype(jnp.float32)
        )

    def do_middle(at):
        def do():
            need("c1", f"sx{at}")
            rows = strips[at]
            total = gathered(0, rows, rows_ref[rows, :].astype(jnp.float32))
            middle_ref[rows, :] = total
            nb[rows, :] = norm_rows(total, gains_ref[1:2, :]).astype(jnp.bfloat16)

        return do

    def do_load_u():
        load("U", gu, u_v).wait()
        acc[...] = jnp.zeros_like(acc)

    def do_load_d():
        copy = load("D", gd, d_v)
        need("oc", "oxc", "ox0", "ox1")
        outgoing.append(file(nb, nb_h))
        copy.wait()

    def do_ff(at):
        lanes = slice(at * 256, (at + 1) * 256)
        active, slope = gelu_both(both(nb[...], u_v[:half, lanes], u_v[half:, lanes]))
        act[:, lanes] = active
        slp[:, lanes] = slope
        for side in range(2):
            cols_at = slice(side * half, (side + 1) * half)
            acc[:, cols_at] += dot_transposed(active, d_v[side * half : (side + 1) * half, lanes])

    def do_q3():
        outgoing.extend([file(act, active_h), file(slp, slope_h)])
        for name in ("c3a", "c3b", "c1"):
            named[name].wait_send()
            flying[:] = [other for other in flying if other is not named[name]]
        down_part(3)

    def do_result(at):
        def do():
            need("e1", f"tx{at}")
            rows = strips[at]
            out_ref[rows, :] = gathered(1, rows, middle_ref[rows, :])

        return do

    outgoing = []
    steps = {
        "own": do_own, "load_a": do_load_a, "qkv": do_qkv, "mix": do_mix, "load_u": do_load_u, "load_d": do_load_d,
        "p3": several(out_part, 3), "p2": several(out_part, 2, 1), "p0": several(out_part, 0),
        "s0": do_add(0, 0, "c3a"), "s1": do_add(0, 1, "c3b"), "m0": do_middle(0), "m1": do_middle(1),
        "q3": do_q3, "q1": several(down_part, 2, 1, 0), "t0": do_add(1, 0, "e3a"), "t1": do_add(1, 1, "e3b"),
        "r0": do_result(0), "r1": do_result(1),
    }
    for at in range(width // HD):
        steps[f"h{at}"] = several(do_head, at)
    for at in range(u_v.shape[1] // 256):
        steps[f"f{at}"] = several(do_ff, at)

    greet((CORE, X, Y, Z1, Z2))
    names = list(moves) + list(steps)
    for place in forward_order:
        name = names[place]
        if name in steps:
            steps[name]()
            arrived.add(name)
        else:
            start, before = moves[name]
            need(*before)
            named[name] = start()
    need(*named)
    for one in outgoing:
        one.wait()
    for one in flying:
        one.wait_send()


def forward_global(line, info, rows, normed, gains, shards):
    share, owned = rows.shape[0], shards[0].shape[0]
    span, columns = 4 * share, shards[0].shape[1]
    width = columns // 4
    small = jnp.bfloat16
    weights = [shaped((D, columns), small)] * 3 + [shaped((4, D, columns), small)] * 3
    return line.run(
        forward_body,
        (info, rows, normed, gains, *shards),
        in_specs=[IN_SMEM] + [VMEM_WHOLE] * 3 + [IN_HBM] * 6,
        out_specs=[IN_HBM] * 6 + [VMEM_WHOLE] * 5 + [IN_HBM] * 4,
        out_shape=weights
        + [
            shaped((span, 3 * width), small),
            shaped((span, width), small),
            shaped((8, span), jnp.float32),
            shaped((share, D), jnp.float32),
            shaped((share, D), jnp.float32),
            shaped((span, D), small),
            shaped((span, D), small),
            shaped((span, columns), small),
            shaped((span, columns), small),
        ],
        scratch_shapes=[
            pltpu.VMEM((span, D), small),
            pltpu.VMEM((span, D), small),
            pltpu.VMEM((D, columns), small),
            pltpu.VMEM((D, columns), small),
            pltpu.VMEM((D, columns), small),
            pltpu.VMEM((span, D), jnp.float32),
            pltpu.VMEM((span, 128), jnp.float32),
            pltpu.VMEM((span, columns), small),
            pltpu.VMEM((span, columns), small),
            pltpu.VMEM((4, share, D), small),
            pltpu.VMEM((4, share, D), small),
            pltpu.VMEM((2, share, D), small),
            pltpu.VMEM((2, share, D), small),
            pltpu.SemaphoreType.DMA((24,)),
            pltpu.SemaphoreType.DMA((96,)),
            pltpu.SemaphoreType.DMA((96,)),
        ],
        hops=(CORE, X, Y, Z1, Z2),
        limit=56,
        name="forward_global",
    )


def backward_body(
    info_ref, small_ref, grad_ref, middle_ref, gains_ref, lse_ref, up_h, down_h, heads_h, active_h, slope_h,
    nb_h, na_h, qkv_h, mixed_h, u_near_h, u_far_h, h2_far_h,
    h0_far_h, h2_near_h,
    mid_ref, sum_ref, gain_ref, gu_near_h, gu_met_h, gh_near_h, gh_far_h, lu_keep_h, lu_met_h, gd_keep_h,
    gd_met_h, h2_met_h, h_first_h, h2_first_h,
    rows_one, rows_two, up_v, down_v, heads_v, act, slp, dup, left_t, right_v, grads_v, qkv_v, mixed_v, dqkv,
    dmix, dq_t, dk_acc, dv_acc, center, k_t, parts, met_core, met_x, sends_x, u_v, u_met, d_v, d_met, z_met, h_v,
    sems, send, recv,
):
    share = small_ref.shape[0]
    half = D // 2
    quarter = half // 2
    owned = quarter // 2
    width = mixed_v.shape[1]
    heads = width // HD
    span = 4 * share
    length = info_ref[1]
    scale = HD ** (-0.5)
    numbers, flying, filed = [], [], []

    def fly(hop, source, target):
        at = len(numbers)
        copy = to_partner(hop, source, target, send.at[at], recv.at[at])
        copy.start()
        numbers.append(at)
        flying.append(copy)
        return copy

    def over(copy):
        copy.wait_send()
        flying[:] = [other for other in flying if other is not copy]

    def file(source, target):
        copy = pltpu.make_async_copy(source, target, sems.at[len(filed)])
        copy.start()
        filed.append(copy)
        return copy

    def block(rel):
        return slice(rel * share, (rel + 1) * share)

    def place(rel):
        return pl.ds(pl.multiple_of(group_at(rel) * share, share), share)

    def summed(*terms):
        total = terms[0].astype(jnp.float32)
        for term in terms[1:]:
            total = total + term.astype(jnp.float32)
        return total

    greet((CORE, X, Y, Z1, Z2))
    small_x = fly(X, small_ref, rows_one.at[pl.ds(2 * share, share)])
    small_core = fly(CORE, small_ref, rows_one.at[pl.ds(share, share)])
    u_y = fly(Y, u_far_h, u_met)
    h_first = fly(X, h2_far_h.at[pl.ds(0, quarter)], h_v.at[0])
    first = [file(down_h, down_v), file(slope_h, slp), file(up_h, up_v)]
    active_in = file(active_h, act)
    nb_in = file(nb_h, right_v)
    u_in = file(u_near_h, u_v)
    h_in = file(h0_far_h.at[pl.ds(0, quarter)], h_v.at[1])
    attention_in = [file(heads_h, heads_v), file(qkv_h, qkv_v), file(mixed_h, mixed_v)]
    rows_one[pl.ds(0, share), :] = small_ref[...]
    for one in first:
        one.wait()

    def ff_back(rel):
        rows = block(rel)
        for tile in range(2):
            lanes = slice(tile * half, (tile + 1) * half)
            grad = both(rows_one[rows, :], down_v[:half, lanes], down_v[half:, lanes])
            dup[rows, lanes] = (grad * slp[rows, lanes].astype(jnp.float32)).astype(jnp.bfloat16)
        for side in range(2):
            lanes = slice(side * half, (side + 1) * half)
            parts[rel, :, lanes] = dot_transposed(dup[rows, :], up_v[lanes, :]).astype(jnp.bfloat16)

    ff_back(0)
    small_core.wait_recv()
    ff_back(1)
    small_x.wait_recv()
    small_xc = fly(CORE, rows_one.at[pl.ds(2 * share, share)], rows_one.at[pl.ds(3 * share, share)])
    ff_back(2)
    small_xc.wait_recv()
    ff_back(3)
    strip = share // 2
    strips = [pl.ds(at * strip, strip) for at in range(2)]

    def scatter_start(which):
        from_far = [fly(CORE, parts.at[3, rows], met_core.at[2 * which, rows]) for rows in strips]
        return from_far, fly(CORE, parts.at[1], met_core.at[2 * which + 1])

    def scatter_on(which, from_far):
        from_x = []
        for rows, one in zip(strips, from_far):
            one.wait_recv()
            sends_x[which, rows, :] = summed(parts[2, rows, :], met_core[2 * which, rows, :]).astype(jnp.bfloat16)
            from_x.append(fly(X, sends_x.at[which, rows], met_x.at[which, rows]))
        return from_x

    def gathered(which, rows):
        return summed(parts[0, rows, :], met_core[2 * which + 1, rows, :], met_x[which, rows, :])

    from_far, from_near = scatter_start(0)
    for rel in range(4):
        left_t[:, block(rel)] = jnp.transpose(rows_one[block(rel), :])
    from_x = scatter_on(0, from_far)
    h_in.wait()
    h_first.wait_recv()
    h_v[1] = summed(h_v[0], h_v[1]).astype(jnp.bfloat16)
    h_y = fly(Y, h_v.at[1], h_first_h)
    active_in.wait()
    for side in range(2):
        rows = slice(side * half, (side + 1) * half)
        for tile in range(2):
            lanes = slice(tile * half, (tile + 1) * half)
            grads_v[0, rows, lanes] = dot_rows(left_t[rows, :], act[:, lanes]).astype(jnp.bfloat16)
    gd_y = fly(Y, grads_v.at[0, pl.ds(half, half)], d_met)
    results = []
    from_near.wait_recv()
    gain_total = jnp.zeros((1, D), jnp.float32)
    over_x = []
    for rows, one in zip(strips, from_x):
        one.wait_recv()
        back, gain_grad = norm_rows_back(middle_ref[rows, :], gains_ref[1:2, :], gathered(0, rows))
        total = grad_ref[rows, :] + back
        mid_ref[rows, :] = total
        rows_two[rows, :] = total.astype(jnp.bfloat16)
        gain_total = gain_total + gain_grad
        over_x.append(fly(X, rows_two.at[rows], rows_two.at[pl.ds(2 * share + rows.start, strip)]))
    gain_ref[...] = gain_total
    small_core = fly(CORE, rows_two.at[pl.ds(0, share)], rows_two.at[pl.ds(share, share)])
    h_second = fly(X, h2_far_h.at[pl.ds(quarter, quarter)], h2_met_h)
    h_third = fly(X, h2_near_h.at[pl.ds(0, quarter)], h2_first_h)
    u_y.wait_recv()
    u_in.wait()
    u_v[...] = summed(u_v[...], u_met[...]).astype(jnp.bfloat16)
    u_1 = fly(Z1, u_v.at[pl.ds(quarter, quarter)], z_met.at[0])
    nb_in.wait()
    left_t[...] = jnp.transpose(right_v[...])
    na_in = file(na_h, right_v)
    for side in range(2):
        rows = slice(side * half, (side + 1) * half)
        for tile in range(2):
            lanes = slice(tile * half, (tile + 1) * half)
            grads_v[1, rows, lanes] = dot_rows(left_t[rows, :], dup[:, lanes]).astype(jnp.bfloat16)
    gu_y = fly(Y, grads_v.at[1, pl.ds(half, half)], gu_met_h)
    results.append(file(grads_v.at[1, pl.ds(0, half)], gu_near_h))
    for one in attention_in:
        one.wait()

    def mix_back(rel):
        full = both(rows_two[block(rel), :], heads_v[:half, 3 * width :], heads_v[half:, 3 * width :])
        dmix[place(rel), :] = full.astype(jnp.bfloat16)

    head_of = lax.broadcasted_iota(jnp.int32, (1, width), 1) // HD
    pick = (
        lax.broadcasted_iota(jnp.int32, (8, width), 1) // HD
        == lax.broadcasted_iota(jnp.int32, (8, width), 0)
    ).astype(jnp.bfloat16)
    k_t[...] = jnp.transpose(qkv_v[:, width : 2 * width])
    dq_t[...] = jnp.zeros_like(dq_t)
    dk_acc[...] = jnp.zeros_like(dk_acc)
    dv_acc[...] = jnp.zeros_like(dv_acc)
    mix_back(0)
    small_core.wait_recv()
    mix_back(1)
    for one in over_x:
        one.wait_recv()
    small_xc = fly(CORE, rows_two.at[pl.ds(2 * share, share)], rows_two.at[pl.ds(3 * share, share)])
    mix_back(2)
    u_1.wait_recv()
    u_v[:quarter, :] = summed(u_v[:quarter, :], z_met[0]).astype(jnp.bfloat16)
    u_2 = fly(Z2, u_v.at[pl.ds(owned, owned)], lu_met_h)
    results.append(file(u_v.at[pl.ds(0, owned)], lu_keep_h))
    small_xc.wait_recv()
    mix_back(3)
    product = dmix[...].astype(jnp.float32) * mixed_v[...].astype(jnp.float32)
    high = product.astype(jnp.bfloat16)
    low = (product - high.astype(jnp.float32)).astype(jnp.bfloat16)
    center[...] = dot_transposed(pick, high) + dot_transposed(pick, low)
    for head in range(heads):
        own_lanes = head_of == head
        for at in range(4):
            rows = block(at)
            reach = (at + 1) * share
            query = jnp.where(own_lanes, qkv_v[rows, :width] * scale, 0.0).astype(jnp.bfloat16)
            grad = jnp.where(own_lanes, dmix[rows, :], 0.0).astype(jnp.bfloat16)
            scores = dot_transposed(qkv_v[:reach, width : 2 * width], query)
            key_at = lax.broadcasted_iota(jnp.int32, scores.shape, 0)
            row_at = at * share + lax.broadcasted_iota(jnp.int32, scores.shape, 1)
            prob = jnp.where(
                (key_at <= row_at) & (key_at < length),
                jnp.exp(scores - lse_ref[head : head + 1, rows]),
                0.0,
            )
            dprob = dot_transposed(qkv_v[:reach, 2 * width :], grad)
            dscore = (prob * (dprob - center[head : head + 1, rows])).astype(jnp.bfloat16)
            dv_acc[:reach, :] += dot_rows(prob.astype(jnp.bfloat16), grad)
            dk_acc[:reach, :] += dot_rows(dscore, query)
            lanes = slice(head * HD, (head + 1) * HD)
            dq_t[lanes, rows] += dot_rows(k_t[lanes, :reach], dscore)
    dqkv[:, :width] = (jnp.transpose(dq_t[...]) * scale).astype(jnp.bfloat16)
    dqkv[:, width : 2 * width] = dk_acc[...].astype(jnp.bfloat16)
    dqkv[:, 2 * width :] = dv_acc[...].astype(jnp.bfloat16)
    gd_y.wait_recv()
    d_v[...] = summed(grads_v[0, :half, :], d_met[...]).astype(jnp.bfloat16)
    d_1 = fly(Z1, d_v.at[pl.ds(quarter, quarter)], z_met.at[1])
    for one in from_far + [from_near]:
        over(one)

    def back_part(rel):
        rows = dqkv[place(rel), :]
        for side in range(2):
            lanes = slice(side * half, (side + 1) * half)
            parts[rel, :, lanes] = dot_transposed(rows, heads_v[lanes, : 3 * width]).astype(jnp.bfloat16)

    back_part(3)
    back_part(1)
    from_far, from_near = scatter_start(1)
    back_part(2)
    from_x = scatter_on(1, from_far)
    back_part(0)
    na_in.wait()
    for rel in range(4):
        left_t[:, place(rel)] = jnp.transpose(right_v[block(rel), :])
    over(gd_y)
    for side in range(2):
        rows = slice(side * half, (side + 1) * half)
        grads_v[0, rows, : 3 * width] = dot_rows(left_t[rows, :], dqkv[...]).astype(jnp.bfloat16)
    for rel in range(4):
        left_t[:, place(rel)] = jnp.transpose(rows_two[block(rel), :])
    for side in range(2):
        rows = slice(side * half, (side + 1) * half)
        grads_v[0, rows, 3 * width :] = dot_rows(left_t[rows, :], mixed_v[...]).astype(jnp.bfloat16)
    results += [
        file(grads_v.at[0, pl.ds(0, half)], gh_near_h),
        file(grads_v.at[0, pl.ds(half, half)], gh_far_h),
    ]
    d_1.wait_recv()
    d_v[:quarter, :] = summed(d_v[:quarter, :], z_met[1]).astype(jnp.bfloat16)
    d_2 = fly(Z2, d_v.at[pl.ds(owned, owned)], gd_met_h)
    results.append(file(d_v.at[pl.ds(0, owned)], gd_keep_h))
    from_near.wait_recv()
    for rows, one in zip(strips, from_x):
        one.wait_recv()
        sum_ref[rows, :] = gathered(1, rows)
    for one in (h_y, h_second, h_third, gu_y, u_2, d_2):
        one.wait_recv()
    for one in results:
        one.wait()
    for one in flying:
        one.wait_send()


def backward_global(line, info, small, grad, middle, gains, lse, weights, active, slope, nb, na, qkv, mixed, sums):
    share, columns = small.shape[0], active.shape[1]
    span, width = 4 * share, mixed.shape[1]
    half, owned = D // 2, D // 8
    low = jnp.bfloat16
    up, down, heads = weights
    return line.run(
        backward_body,
        (info, small, grad, middle, gains, lse, up, down, heads, active, slope, nb, na, qkv, mixed, *sums),
        in_specs=[IN_SMEM] + [VMEM_WHOLE] * 5 + [IN_HBM] * 14,
        out_specs=[VMEM_WHOLE] * 3 + [IN_HBM] * 11,
        out_shape=[
            shaped((share, D), jnp.float32),
            shaped((share, D), jnp.float32),
            shaped((1, D), jnp.float32),
        ]
        + [shaped((half, columns), low)] * 4
        + [shaped((owned, columns), low)] * 4
        + [shaped((half // 2, columns), low)] * 3,
        scratch_shapes=[pltpu.VMEM((span, D), low)] * 2
        + [pltpu.VMEM((D, columns), low)] * 3
        + [pltpu.VMEM((span, columns), low)] * 3
        + [pltpu.VMEM((D, span), low), pltpu.VMEM((span, D), low), pltpu.VMEM((2, D, columns), low)]
        + [pltpu.VMEM((span, 3 * width), low), pltpu.VMEM((span, width), low), pltpu.VMEM((span, 3 * width), low)]
        + [
            pltpu.VMEM((span, width), low),
            pltpu.VMEM((width, span), jnp.float32),
            pltpu.VMEM((span, width), jnp.float32),
            pltpu.VMEM((span, width), jnp.float32),
            pltpu.VMEM((8, span), jnp.float32),
            pltpu.VMEM((width, span), low),
            pltpu.VMEM((4, share, D), low),
            pltpu.VMEM((4, share, D), low),
            pltpu.VMEM((2, share, D), low),
            pltpu.VMEM((2, share, D), low),
        ]
        + [pltpu.VMEM((half, columns), low)] * 4
        + [
            pltpu.VMEM((2, half // 2, columns), low),
            pltpu.VMEM((2, half // 2, columns), low),
            pltpu.SemaphoreType.DMA((24,)),
            pltpu.SemaphoreType.DMA((40,)),
            pltpu.SemaphoreType.DMA((40,)),
        ],
        hops=(CORE, X, Y, Z1, Z2),
        limit=56,
        name="backward_global",
    )


def head_sums(width):
    row_at = lax.broadcasted_iota(jnp.int32, (width, width), 0) // HD
    col_at = lax.broadcasted_iota(jnp.int32, (width, width), 1) // HD
    return (row_at == col_at).astype(jnp.bfloat16)


def over_heads(product, ones):
    high = product.astype(jnp.bfloat16)
    low = (product - high.astype(jnp.float32)).astype(jnp.bfloat16)
    return dot_rows(high, ones) + dot_rows(low, ones)


def frame_probs(queries, keys, ones):
    found = []
    for at in range(CB):
        scores = [over_heads(queries[at] * keys[c2], ones) * HD ** (-0.5) for c2 in range(at + 1)]
        top = scores[0]
        for one in scores[1:]:
            top = jnp.maximum(top, one)
        expanded = [jnp.exp(one - top) for one in scores]
        total = expanded[0]
        for one in expanded[1:]:
            total = total + one
        inverse = 1.0 / total
        found.append([one * inverse for one in expanded])
    return found


def rounded_f32(values):
    return values.astype(jnp.bfloat16).astype(jnp.float32)


def halves_of(stack):
    half = stack.shape[1] // 2
    return [(stack.at[at, pl.ds(0, half)], stack.at[at, pl.ds(half, half)]) for at in range(stack.shape[0])]


def start_weights(parts, buffer, sems):
    for at, pair in enumerate(parts):
        for half, ref in enumerate(pair):
            pltpu.make_async_copy(ref, buffer.at[at, half], sems.at[at, half]).start()


def wait_weights(parts, buffer, sems, at):
    for half in range(2):
        pltpu.make_async_copy(parts[0][half], buffer.at[at, half], sems.at[at, half]).wait()


def local_heads_body(
    out_ref_in, code_ref, gains_ref, *refs
):
    count = 4
    parts = halves_of(refs[0])
    qkv_ref, mixed_ref, middle_ref, normed_b_ref, a_t_ref, normed_a, local_in, buffer, sems = refs[1:]
    step = pl.program_id(0)
    frames = out_ref_in.shape[0]
    width = mixed_ref.shape[2]
    half = D // 2

    @pl.when(step == 0)
    def _():
        start_weights(parts, buffer, sems)
        for c in range(CB):
            rows = slice(c * frames, (c + 1) * frames)
            local_in[rows, :] = out_ref_in[...] + code_ref[rows, :].astype(jnp.float32)
            normed = norm_rows(local_in[rows, :], gains_ref[2:3, :]).astype(jnp.bfloat16)
            normed_a[rows, :] = normed
            a_t_ref[:, rows] = jnp.transpose(normed)
        middle_ref[...] = local_in[...]

    wait_weights(parts, buffer, sems, step)
    ones = head_sums(width)
    queries, keys, values = ([], [], [])
    for c in range(CB):
        rows = slice(c * frames, (c + 1) * frames)
        qkv = (
            dot_rows(normed_a[rows, :half], buffer[step, 0, :, : 3 * width])
            + dot_rows(normed_a[rows, half:], buffer[step, 1, :, : 3 * width])
        ).astype(jnp.bfloat16)
        qkv_ref[0, rows, :] = qkv
        queries.append(qkv[:, :width].astype(jnp.float32))
        keys.append(qkv[:, width : 2 * width].astype(jnp.float32))
        values.append(qkv[:, 2 * width :].astype(jnp.float32))
    prob = frame_probs(queries, keys, ones)
    for c in range(CB):
        rows = slice(c * frames, (c + 1) * frames)
        mix = rounded_f32(prob[c][0]) * values[0]
        for c2 in range(1, c + 1):
            mix = mix + rounded_f32(prob[c][c2]) * values[c2]
        mix = mix.astype(jnp.bfloat16)
        mixed_ref[0, rows, :] = mix
        for at in range(2):
            lanes = slice(at * half, (at + 1) * half)
            middle_ref[rows, lanes] += dot_transposed(mix, buffer[step, at, :, 3 * width :])

    @pl.when(step == count - 1)
    def _():
        for c in range(CB):
            rows = slice(c * frames, (c + 1) * frames)
            normed_b_ref[rows, :] = norm_rows(middle_ref[rows, :], gains_ref[3:4, :]).astype(
                jnp.bfloat16
            )


def local_heads(line, global_out, codes, gains, parts):
    frames = global_out.shape[0]
    rows = CB * frames
    width = parts.shape[2] // 4
    half = D // 2
    return line.run(
        local_heads_body,
        (global_out, codes, gains, parts),
        grid=(4,),
        in_specs=[held((frames, D)), held((rows, D)), held((4, D)), IN_HBM],
        out_specs=[
            pl.BlockSpec((1, rows, 3 * width), lambda step: (step, 0, 0)),
            pl.BlockSpec((1, rows, width), lambda step: (step, 0, 0)),
            held((rows, D)),
            held((rows, D)),
            held((D, rows)),
        ],
        out_shape=[
            shaped((4, rows, 3 * width), jnp.bfloat16),
            shaped((4, rows, width), jnp.bfloat16),
            shaped((rows, D), jnp.float32),
            shaped((rows, D), jnp.bfloat16),
            shaped((D, rows), jnp.bfloat16),
        ],
        scratch_shapes=[
            pltpu.VMEM((rows, D), jnp.bfloat16),
            pltpu.VMEM((rows, D), jnp.float32),
            pltpu.VMEM((4, 2, half, 4 * width), jnp.bfloat16),
            pltpu.SemaphoreType.DMA((4, 2)),
        ],
        limit=52,
        name="local_heads",
    )


def local_ff_body(source_ref, normed_ref, middle_ref, *refs):
    count = 4
    ups, downs = halves_of(refs[0]), halves_of(refs[1])
    active_ref, slope_ref, out_ref, b_t_ref, acc, up_buf, down_buf, up_sems, down_sems = refs[2:]
    step = pl.program_id(0)
    rows_all = normed_ref.shape[0]
    frames = rows_all // CB
    half = D // 2
    tile = active_ref.shape[2]
    per = up_buf.shape[3] // tile
    group = step // per

    @pl.when(step == 0)
    def _():
        for at in range(count):
            start_weights_at(ups, up_buf, up_sems, at)
            start_weights_at(downs, down_buf, down_sems, at)
        b_t_ref[...] = jnp.transpose(normed_ref[...])
        acc[...] = middle_ref[...]

    @pl.when(step % per == 0)
    def _():
        wait_weights(ups, up_buf, up_sems, group)
        wait_weights(downs, down_buf, down_sems, group)

    piece = 512
    pieces = [
        (slice(begin, begin + rows_all), pl.ds(pl.multiple_of((step % per) * tile + at * piece, piece), piece), at)
        for at in range(tile // piece)
        for begin in (0,)
    ]

    def raised(rows, lanes):
        return dot_rows(normed_ref[rows, :half], up_buf[group, 0, :, lanes]) + dot_rows(
            normed_ref[rows, half:], up_buf[group, 1, :, lanes]
        )

    upper = raised(*pieces[0][:2])
    for at, (rows, lanes, place) in enumerate(pieces):
        coming = raised(*pieces[at + 1][:2]) if at + 1 < len(pieces) else None
        active, slope = gelu_both(upper)
        here = slice(place * piece, (place + 1) * piece)
        active_ref[0, rows, here] = active
        slope_ref[0, rows, here] = slope
        for side in range(2):
            sides = slice(side * half, (side + 1) * half)
            acc[rows, sides] += dot_transposed(active, down_buf[group, side, :, lanes])
        upper = coming

    @pl.when(step == pl.num_programs(0) - 1)
    def _():
        owned = D // source_ref.shape[0]
        for c in range(CB):
            rows = slice(c * frames, (c + 1) * frames)
            for at in range(source_ref.shape[0]):
                here = slice(at * owned, (at + 1) * owned)
                out_ref[c, :, lanes_of(source_ref, at, owned)] = acc[rows, here].astype(jnp.bfloat16)


def start_weights_at(parts, buffer, sems, at):
    for half in range(2):
        pltpu.make_async_copy(parts[at][half], buffer.at[at, half], sems.at[at, half]).start()


def local_ff(line, source, normed, middle, ups, downs, tile=1024):
    rows = normed.shape[0]
    hidden = ups.shape[2]
    half = D // 2
    per = hidden // tile
    hidden_block = pl.BlockSpec((1, rows, tile), lambda step: (step // per, 0, step % per))
    return line.run(
        local_ff_body,
        (source, normed, middle, ups, downs),
        grid=(4 * per,),
        in_specs=[IN_SMEM, held((rows, D)), held((rows, D)), IN_HBM, IN_HBM],
        out_specs=[hidden_block, hidden_block, held((CB, rows // CB, D)), held((D, rows))],
        out_shape=[
            shaped((4, rows, hidden), jnp.bfloat16),
            shaped((4, rows, hidden), jnp.bfloat16),
            shaped((CB, rows // CB, D), jnp.bfloat16),
            shaped((D, rows), jnp.bfloat16),
        ],
        scratch_shapes=[
            pltpu.VMEM((rows, D), jnp.float32),
            pltpu.VMEM((4, 2, half, hidden), jnp.bfloat16),
            pltpu.VMEM((4, 2, half, hidden), jnp.bfloat16),
            pltpu.SemaphoreType.DMA((4, 2)),
            pltpu.SemaphoreType.DMA((4, 2)),
        ],
        limit=56,
        name="local_ff",
    )


def seed_body(source_ref, count_ref, cot_ref, code_ref, grad_ref, grad_t_ref, codes_ref):
    frames = cot_ref.shape[1]
    owned = D // source_ref.shape[0]
    keep = lax.broadcasted_iota(jnp.int32, (frames, 1), 0) < count_ref[0]
    for c in range(CB):
        rows = slice(c * frames, (c + 1) * frames)
        for at in range(source_ref.shape[0]):
            here = slice(at * owned, (at + 1) * owned)
            values = cot_ref[c, :, lanes_of(source_ref, at, owned)].astype(jnp.float32)
            grad_ref[rows, here] = jnp.where(keep, values, 0.0).astype(jnp.bfloat16)
            codes_ref[rows, here] = code_ref[c, :, lanes_of(source_ref, at, owned)]
        grad_t_ref[:, rows] = jnp.transpose(grad_ref[rows, :])


def seed(line, source, count, cot, codes):
    frames = cot.shape[1]
    rows = CB * frames
    return line.run(
        seed_body,
        (source, count, cot, codes),
        in_specs=[IN_SMEM, IN_SMEM, VMEM_WHOLE, VMEM_WHOLE],
        out_specs=[VMEM_WHOLE] * 3,
        out_shape=[
            shaped((rows, D), jnp.bfloat16),
            shaped((D, rows), jnp.bfloat16),
            shaped((rows, D), jnp.bfloat16),
        ],
        limit=60,
        name="seed_grads",
    )


def local_back_body(
    grad_h, grad_t_h, b_t_h, a_t_h, active_h, slope_h, qkv_h, mixed_h, middle_h, gout_h, codes_h, gains_ref, *refs
):
    heads_h, ups_h, downs_h = ([half for pair in halves_of(one) for half in pair] for one in refs[:3])
    refs = refs[3:]
    total_ref, small_out_ref, gain_c_ref, gain_d_ref, *results_h = refs[:12]
    (
        grad_v, grad_t, other_t, weights, act, slp, dup, acc, mid, gout_v, codes_v,
        pair_out, pair_far, pair_near, head_out, head_far, head_near, x_in, y_far, y_near,
        sems, send, recv,
    ) = refs[12:]
    frames = gout_v.shape[0]
    rows_all = grad_v.shape[0]
    half = D // 2
    width = mixed_h.shape[2]
    scale = HD ** (-0.5)
    greet((CORE, X, Y))

    def fetch(at, source, target):
        copy = pltpu.make_async_copy(source, target, sems.at[at])
        copy.start()
        return copy

    def give(at, hop, source, target):
        copy = to_partner(hop, source, target, send.at[at], recv.at[at])
        copy.start()
        return copy

    def fetch_ff(rel):
        found = [fetch(at, downs_h[2 * rel + at], weights.at[2 + at]) for at in range(2)]
        found.append(fetch(2, slope_h.at[rel], slp))
        return found + [fetch(3 + at, ups_h[2 * rel + at], weights.at[at]) for at in range(2)]

    order = (3, 2, 1, 0)
    waits = [fetch(5, grad_h, grad_v)] + fetch_ff(order[0])
    late = [fetch(6, grad_t_h, grad_t), fetch(7, active_h.at[order[0]], act), fetch(8, b_t_h, other_t)]
    later = [fetch(9, middle_h, mid), fetch(10, gout_h, gout_v), fetch(11, codes_h, codes_v)]
    acc[...] = jnp.zeros_like(acc)
    sent = []
    for step, rel in enumerate(order):
        for one in waits:
            one.wait()
        for tile in range(2):
            lanes = slice(tile * half, (tile + 1) * half)
            grad = dot_rows(grad_v[:, :half], weights[2, :, lanes]) + dot_rows(
                grad_v[:, half:], weights[3, :, lanes]
            )
            dup[:, lanes] = (grad * slp[:, lanes].astype(jnp.float32)).astype(jnp.bfloat16)
        for at in range(2):
            lanes = slice(at * half, (at + 1) * half)
            acc[:, lanes] += dot_transposed(dup[...], weights[at])
        if step < 3:
            waits = fetch_ff(order[step + 1])
        for one in late:
            one.wait()
        if step == 2:
            sent[0].wait_send()
        if step % 2 == 1:
            sent[step // 2].wait_recv()
        met = (None, pair_far, None, pair_near)[step]
        for at in range(2):
            rows = slice(at * half, (at + 1) * half)
            for tile in range(2):
                lanes = slice(tile * half, (tile + 1) * half)
                down = dot_rows(grad_t[rows, :], act[:, lanes])
                up = dot_rows(other_t[rows, :], dup[:, lanes])
                if met is None:
                    pair_out[0, rows, lanes] = down.astype(jnp.bfloat16)
                    pair_out[1, rows, lanes] = up.astype(jnp.bfloat16)
                else:
                    met[0, rows, lanes] = (down + met[0, rows, lanes].astype(jnp.float32)).astype(jnp.bfloat16)
                    met[1, rows, lanes] = (up + met[1, rows, lanes].astype(jnp.float32)).astype(jnp.bfloat16)
        if step < 3:
            late = [fetch(7, active_h.at[order[step + 1]], act)]
        if step == 0:
            sent.append(give(0, CORE, pair_out, pair_far))
        elif step == 2:
            sent.append(give(1, CORE, pair_out, pair_near))
        elif step == 1:
            x_far = give(2, X, pair_far.at[1, pl.ds(half, half)], x_in.at[pl.ds(half, half)])
            y_two = give(3, Y, pair_far.at[0, pl.ds(half, half)], y_far)
            x_near = give(4, X, pair_far.at[1, pl.ds(0, half)], x_in.at[pl.ds(0, half)])
        else:
            y_zero = give(5, Y, pair_near.at[0, pl.ds(half, half)], y_near)

    def fetch_heads(rel):
        found = [fetch(at, heads_h[2 * rel + at], weights.at[at]) for at in range(2)]
        found.append(fetch(2, qkv_h.at[rel], act.at[:, pl.ds(0, 3 * width)]))
        return found + [fetch(3, mixed_h.at[rel], slp.at[:, pl.ds(0, width)])]

    waits = fetch_heads(order[0]) + [fetch(8, a_t_h, other_t)]
    sent[1].wait_send()
    for one in later:
        one.wait()
    total_gain = jnp.zeros((1, D), jnp.float32)
    for c in range(CB):
        rows = slice(c * frames, (c + 1) * frames)
        part_back, gain_grad = norm_rows_back(mid[rows, :], gains_ref[3:4, :], acc[rows, :])
        total = grad_v[rows, :].astype(jnp.float32) + part_back
        mid[rows, :] = total
        small = total.astype(jnp.bfloat16)
        grad_v[rows, :] = small
        grad_t[:, rows] = jnp.transpose(small)
        total_gain = total_gain + gain_grad
    gain_d_ref[...] = total_gain

    ones = head_sums(width)
    heads_sent = []

    def more(total, term):
        return term if total is None else total + term

    for step, rel in enumerate(order):
        for one in waits:
            one.wait()
        queries, keys, values, dmix = ([], [], [], [])
        back = rounded_f32(
            dot_rows(grad_v[:, :half], weights[0, :, 3 * width :])
            + dot_rows(grad_v[:, half:], weights[1, :, 3 * width :])
        )
        for c in range(CB):
            rows = slice(c * frames, (c + 1) * frames)
            qkv = act[rows, : 3 * width].astype(jnp.float32)
            queries.append(qkv[:, :width])
            keys.append(qkv[:, width : 2 * width])
            values.append(qkv[:, 2 * width :])
            dmix.append(back[rows, :])
        prob = frame_probs(queries, keys, ones)
        dq, dk, dv = ([None] * CB, [None] * CB, [None] * CB)
        for c in range(CB):
            dprob = [over_heads(dmix[c] * values[c2], ones) for c2 in range(c + 1)]
            center = prob[c][0] * dprob[0]
            for c2 in range(1, c + 1):
                center = center + prob[c][c2] * dprob[c2]
            for c2 in range(c + 1):
                dv[c2] = more(dv[c2], rounded_f32(prob[c][c2]) * dmix[c])
                dscore = rounded_f32(prob[c][c2] * (dprob[c2] - center))
                dq[c] = more(dq[c], dscore * keys[c2])
                dk[c2] = more(dk[c2], dscore * queries[c])
        for c in range(CB):
            rows = slice(c * frames, (c + 1) * frames)
            dup[rows, :width] = (dq[c] * scale).astype(jnp.bfloat16)
            dup[rows, width : 2 * width] = (dk[c] * scale).astype(jnp.bfloat16)
            dup[rows, 2 * width : 3 * width] = dv[c].astype(jnp.bfloat16)
        for at in range(2):
            lanes = slice(at * half, (at + 1) * half)
            term = dot_transposed(dup[:, : 3 * width], weights[at, :, : 3 * width])
            acc[:, lanes] = term if step == 0 else acc[:, lanes] + term
        if step == 2:
            heads_sent[0].wait_send()
        if step % 2 == 1:
            heads_sent[step // 2].wait_recv()
        met = (None, head_far, None, head_near)[step]
        for at in range(2):
            rows = slice(at * half, (at + 1) * half)
            three = dot_rows(other_t[rows, :], dup[:, : 3 * width])
            one = dot_rows(grad_t[rows, :], slp[:, :width])
            if met is None:
                head_out[rows, : 3 * width] = three.astype(jnp.bfloat16)
                head_out[rows, 3 * width :] = one.astype(jnp.bfloat16)
            else:
                three = three + met[rows, : 3 * width].astype(jnp.float32)
                one = one + met[rows, 3 * width :].astype(jnp.float32)
                met[rows, : 3 * width] = three.astype(jnp.bfloat16)
                met[rows, 3 * width :] = one.astype(jnp.bfloat16)
        if step < 3:
            waits = fetch_heads(order[step + 1])
        if step == 0:
            heads_sent.append(give(6, CORE, head_out, head_far))
        elif step == 2:
            heads_sent.append(give(7, CORE, head_out, head_near))
    total_gain = jnp.zeros((1, D), jnp.float32)
    total = jnp.zeros((frames, D), jnp.float32)
    for c in range(CB):
        rows = slice(c * frames, (c + 1) * frames)
        local_in = gout_v[...] + codes_v[rows, :].astype(jnp.float32)
        part_back, gain_grad = norm_rows_back(local_in, gains_ref[2:3, :], acc[rows, :])
        total = total + (mid[rows, :] + part_back)
        total_gain = total_gain + gain_grad
    total_ref[...] = total
    small_out_ref[...] = total.astype(jnp.bfloat16)
    gain_c_ref[...] = total_gain

    heads_sent[1].wait_send()
    x_far.wait()
    x_near.wait()
    y_two.wait()
    y_zero.wait()

    def summed(one, two):
        return (one.astype(jnp.float32) + two.astype(jnp.float32)).astype(jnp.bfloat16)

    pair_near[1] = summed(pair_near[1], x_in[...])
    pair_far[0, :half, :] = summed(pair_far[0, :half, :], y_far[...])
    pair_near[0, :half, :] = summed(pair_near[0, :half, :], y_near[...])
    near, far = pl.ds(0, half), pl.ds(half, half)
    leaving = (
        pair_near.at[1, near], pair_near.at[1, far], pair_far.at[0, near], pair_near.at[0, near],
        head_far.at[near], head_far.at[far], head_near.at[near], head_near.at[far],
    )
    for one in [fetch(at, source, target) for at, (source, target) in enumerate(zip(leaving, results_h))]:
        one.wait()


def local_back(line, grad, grad_t, b_t, a_t, active, slope, qkv, mixed, middle, global_out, codes, gains, heads, ups, downs):
    rows, frames = grad.shape[0], global_out.shape[0]
    half = D // 2
    columns = ups.shape[2]
    small = jnp.bfloat16
    return line.run(
        local_back_body,
        (grad, grad_t, b_t, a_t, active, slope, qkv, mixed, middle, global_out, codes, gains, heads, ups, downs),
        in_specs=[IN_HBM] * 11 + [VMEM_WHOLE] + [IN_HBM] * 3,
        out_specs=[VMEM_WHOLE] * 4 + [IN_HBM] * 8,
        out_shape=[
            shaped((frames, D), jnp.float32),
            shaped((frames, D), small),
            shaped((1, D), jnp.float32),
            shaped((1, D), jnp.float32),
        ]
        + [shaped((half, columns), small)] * 8,
        scratch_shapes=[
            pltpu.VMEM((rows, D), small),
            pltpu.VMEM((D, rows), small),
            pltpu.VMEM((D, rows), small),
            pltpu.VMEM((4, half, columns), small),
            pltpu.VMEM((rows, columns), small),
            pltpu.VMEM((rows, columns), small),
            pltpu.VMEM((rows, columns), small),
            pltpu.VMEM((rows, D), jnp.float32),
            pltpu.VMEM((rows, D), jnp.float32),
            pltpu.VMEM((frames, D), jnp.float32),
            pltpu.VMEM((rows, D), small),
            pltpu.VMEM((2, D, columns), small),
            pltpu.VMEM((2, D, columns), small),
            pltpu.VMEM((2, D, columns), small),
            pltpu.VMEM((D, columns), small),
            pltpu.VMEM((D, columns), small),
            pltpu.VMEM((D, columns), small),
            pltpu.VMEM((D, columns), small),
            pltpu.VMEM((half, columns), small),
            pltpu.VMEM((half, columns), small),
            pltpu.SemaphoreType.DMA((12,)),
            pltpu.SemaphoreType.DMA((8,)),
            pltpu.SemaphoreType.DMA((8,)),
        ],
        hops=(CORE, X, Y),
        limit=58,
        name="local_back",
    )


def last_body(
    gains_ref, gu_near_h, gu_met_h, gh_near_h, gh_far_h, d0_h, d2_h, h0_near_h, h2_near_h, h0_far_h, h2_far_h,
    h_first_h, h2_first_h,
    gain_out_ref, gu_keep_h, gu_last_h, gh_keep_h, gh_last_h, d_keep_h, d_last_h, h_keep_h, h_send_h,
    gain_v, gain_met, held_v, met_v, extra_v, z_met, sems, send, recv,
):
    half = D // 2
    quarter = half // 2
    owned = quarter // 2
    flying, filed = [], []

    def fly(hop, source, target):
        at = len(flying)
        copy = to_partner(hop, source, target, send.at[at], recv.at[at])
        copy.start()
        flying.append(copy)
        return copy

    def file(source, target):
        copy = pltpu.make_async_copy(source, target, sems.at[len(filed)])
        copy.start()
        filed.append(copy)
        return copy

    def summed(*terms):
        total = terms[0].astype(jnp.float32)
        for term in terms[1:]:
            total = total + term.astype(jnp.float32)
        return total.astype(jnp.bfloat16)

    greet((CORE, X, Y, Z1, Z2))
    upper, lower = pl.ds(0, quarter), pl.ds(quarter, quarter)
    gain_core = fly(CORE, gains_ref, gain_met.at[0])
    gh_low = fly(Y, gh_far_h.at[lower], met_v.at[1, lower])
    d_low = fly(X, d2_h.at[lower], met_v.at[2, lower])
    gu_in = [file(gu_near_h, held_v.at[0]), file(gu_met_h, met_v.at[0])]
    far_in = [file(h0_far_h.at[lower], extra_v.at[0, lower]), file(h2_far_h, extra_v.at[1, lower])]
    rest_in = [file(gh_near_h, held_v.at[1]), file(d0_h, held_v.at[2]), file(h0_near_h, held_v.at[3])]
    rest_in += [file(h2_first_h, met_v.at[3, upper]), file(h_first_h, extra_v.at[2, upper])]
    gain_core.wait_recv()
    gain_v[0] = gains_ref[...] + gain_met[0]
    gain_1 = fly(Z1, gain_v.at[0], gain_met.at[1])
    for one in gu_in:
        one.wait()
    held_v[0] = summed(held_v[0], met_v[0])
    gu_1 = fly(Z1, held_v.at[0, lower], z_met.at[0])
    gain_1.wait_recv()
    gain_v[1] = gain_v[0] + gain_met[1]
    gain_2 = fly(Z2, gain_v.at[1], gain_met.at[2])
    gh_up = fly(Y, gh_far_h.at[upper], met_v.at[1, upper])
    gain_2.wait_recv()
    gain_v[2] = gain_v[1] + gain_met[2]
    gain_x = fly(X, gain_v.at[2], gain_met.at[3])
    d_up = fly(X, d2_h.at[upper], met_v.at[2, upper])
    h_x = fly(X, h2_near_h.at[lower], met_v.at[3, lower])
    for one in far_in:
        one.wait()
    extra_v[0, quarter:, :] = summed(extra_v[0, quarter:, :], extra_v[1, quarter:, :])
    for one in rest_in:
        one.wait()
    done = []

    def add(at, first):
        rows = slice(0, quarter) if first else slice(quarter, half)
        held_v[at, rows, :] = summed(held_v[at, rows, :], met_v[at, rows, :])

    def second(at, first, last_h, keep_h):
        first.wait_recv()
        held_v[at, :quarter, :] = summed(held_v[at, :quarter, :], z_met[at])
        done.append(file(held_v.at[at, pl.ds(0, owned)], keep_h))
        return fly(Z2, held_v.at[at, pl.ds(owned, owned)], last_h)

    gh_low.wait_recv()
    add(1, False)
    gh_1 = fly(Z1, held_v.at[1, lower], z_met.at[1])
    d_low.wait_recv()
    add(2, False)
    gain_x.wait_recv()
    gain_v[3] = gain_v[2] + gain_met[3]
    gain_y = fly(Y, gain_v.at[3], gain_met.at[4])
    h_y = fly(Y, extra_v.at[0, lower], extra_v.at[2, lower])
    gu_2 = second(0, gu_1, gu_last_h, gu_keep_h)
    gh_up.wait_recv()
    add(1, True)
    gh_2 = second(1, gh_1, gh_last_h, gh_keep_h)
    d_1 = fly(Z1, held_v.at[2, lower], z_met.at[2])
    d_up.wait_recv()
    add(2, True)
    gain_y.wait_recv()
    gain_out_ref[...] = gain_v[3] + gain_met[4]
    h_x.wait_recv()
    h_y.wait_recv()
    held_v[3] = summed(held_v[3], met_v[3], extra_v[2])
    done.append(file(held_v.at[3, upper], h_keep_h))
    done.append(file(held_v.at[3, lower], h_send_h))
    d_1.wait_recv()
    held_v[2, :quarter, :] = summed(held_v[2, :quarter, :], z_met[2])
    done.append(file(held_v.at[2, pl.ds(0, owned)], d_keep_h))
    done.append(file(held_v.at[2, pl.ds(owned, owned)], d_last_h))
    for one in (gu_2, gh_2):
        one.wait_recv()
    for one in done:
        one.wait()
    for one in flying:
        one.wait_send()


def last_transfers(line, gains, parts):
    half, columns = parts[0].shape
    owned = half // 4
    low = jnp.bfloat16
    return line.run(
        last_body,
        (gains, *parts),
        in_specs=[VMEM_WHOLE] + [IN_HBM] * 12,
        out_specs=[VMEM_WHOLE] + [IN_HBM] * 8,
        out_shape=[shaped(gains.shape, jnp.float32)]
        + [shaped((owned, columns), low)] * 6
        + [shaped((2 * owned, columns), low)] * 2,
        scratch_shapes=[
            pltpu.VMEM((4,) + gains.shape, jnp.float32),
            pltpu.VMEM((5,) + gains.shape, jnp.float32),
            pltpu.VMEM((4, half, columns), low),
            pltpu.VMEM((4, half, columns), low),
            pltpu.VMEM((3, half, columns), low),
            pltpu.VMEM((3, half // 2, columns), low),
            pltpu.SemaphoreType.DMA((16,)),
            pltpu.SemaphoreType.DMA((16,)),
            pltpu.SemaphoreType.DMA((16,)),
        ],
        hops=(CORE, X, Y, Z1, Z2),
        limit=60,
        name="last_transfers",
    )


def add_body(*refs):
    total = refs[0][...].astype(jnp.float32)
    for ref in refs[1:-1]:
        total = total + ref[...].astype(jnp.float32)
    refs[-1][...] = total.astype(jnp.bfloat16)


def add_rows(line, terms, part=0, parts=1):
    rows = min(term.shape[0] for term in terms) if parts == 1 else terms[0].shape[0] // parts
    columns = terms[0].shape[1]

    def spec(term):
        return pl.BlockSpec(
            (rows, columns), (lambda step: (part, 0)) if term.shape[0] > rows else (lambda step: (0, 0))
        )

    return line.run(
        add_body,
        tuple(terms),
        grid=(1,),
        in_specs=[spec(term) for term in terms],
        out_specs=[pl.BlockSpec((rows, columns), lambda step: (0, 0))],
        out_shape=[shaped((rows, columns), jnp.bfloat16)],
        limit=24,
        name="add_terms",
    )[0]


def sum_pieces(line, terms, split=()):
    rows, columns = terms[0].shape[0] // 2, terms[0].shape[1]
    whole = len(terms)
    flat = list(terms) + [one for pair in split for one in pair]

    def body(*refs):
        for at, out_ref in enumerate(refs[-2:]):
            here = slice(at * rows, (at + 1) * rows)
            total = refs[0][here, :].astype(jnp.float32)
            for ref in refs[1:whole]:
                total = total + ref[here, :].astype(jnp.float32)
            for ref in refs[whole + at : -2 : 2]:
                total = total + ref[...].astype(jnp.float32)
            out_ref[...] = total.astype(jnp.bfloat16)

    return line.run(
        body,
        tuple(flat),
        in_specs=[VMEM_WHOLE] * len(flat),
        out_specs=[VMEM_WHOLE] * 2,
        out_shape=[shaped((rows, columns), jnp.bfloat16)] * 2,
        limit=24,
        name="sum_pieces",
    )


def pass_body(*refs):
    pass


def in_turn(line, *values):
    return line.run(
        pass_body,
        tuple(values),
        in_specs=[IN_HBM] * len(values),
        out_specs=[IN_HBM] * len(values),
        out_shape=[shaped(one.shape, one.dtype) for one in values],
        aliases={at: at for at in range(len(values))},
        name="in_turn",
    )


def split_dot(left, right):
    left_high = left.astype(jnp.bfloat16)
    left_low = (left - left_high.astype(jnp.float32)).astype(jnp.bfloat16)
    right_high = right.astype(jnp.bfloat16)
    right_low = (right - right_high.astype(jnp.float32)).astype(jnp.bfloat16)
    return (
        dot_rows(left_high, right_high) + dot_rows(left_high, right_low) + dot_rows(left_low, right_high)
    )


def adam_body(chained, one_ref, two_ref, left_ref, right_ref, master_ref, first_ref, second_ref, ema_ref, *refs):
    grads_ref, new_master_ref, new_first_ref, new_second_ref, new_ema_ref = refs[5:] if chained else refs
    left = left_ref[0]
    left_t = jnp.transpose(left)
    grads = one_ref[...].astype(jnp.float32) + two_ref[...].astype(jnp.float32)
    grads_ref[0] = grads
    turned_left = split_dot(left_t, grads)
    back = []
    for at in range(right_ref.shape[1]):
        tile = slice(at * 128, (at + 1) * 128)
        right = right_ref[0, at]
        rotated = split_dot(turned_left[:, tile], right)
        new_first = beta_first * first_ref[0, :, tile] + (1.0 - beta_first) * rotated
        new_second = beta_second * second_ref[0, :, tile] + (1.0 - beta_second) * rotated * rotated
        new_first_ref[0, :, tile] = new_first
        new_second_ref[0, :, tile] = new_second
        turned = new_first / (jnp.sqrt(new_second) + adam_eps)
        back.append(split_dot(turned, jnp.transpose(right)))
    back_full = split_dot(left, jnp.concatenate(back, axis=1))
    new_master = master_ref[0] - step_rate * back_full
    new_master_ref[0] = new_master
    new_ema_ref[0] = ema_decay * ema_ref[0] + (1.0 - ema_decay) * new_master


def adam(line, layer, third, pieces, left, right, master, first, second, ema, before, tile=512):
    owned, columns = pieces[0].shape
    steps = columns // tile
    first_step = third * steps

    def state(step):
        return (layer, 0, first_step + step)

    state_spec = pl.BlockSpec((1, owned, tile), state)
    chained = before is not None
    return line.run(
        lambda *refs: adam_body(chained, *refs),
        (*pieces, left, right, master, first, second, ema, *(before or ()),),
        grid=(steps,),
        in_specs=[by_cols((owned, tile))] * 2
        + [
            pl.BlockSpec((1,) + left.shape[1:], lambda step: (layer, 0, 0)),
            pl.BlockSpec(
                (1, tile // 128) + right.shape[2:], lambda step: (layer, first_step + step, 0, 0)
            ),
        ]
        + [state_spec] * 4
        + ([IN_HBM] * 5 if chained else []),
        out_specs=[state_spec] * 5,
        out_shape=[shaped(master.shape, jnp.float32)] * 5,
        aliases={8 + at: at for at in range(5)} if chained else {},
        limit=32,
        name="adam_update",
    )


def hop_x(values):
    return lax.ppermute(values, TENSOR, [(at, at ^ 2) for at in range(4)])


def hop_core(values):
    return lax.ppermute(values, TENSOR, [(at, at ^ 1) for at in range(4)])


def hop_y(values):
    return lax.ppermute(values, DP, [(at, at ^ 1) for at in range(8)])


def hop_z(values, step):
    return lax.ppermute(values, DP, [(at, at ^ (2 * step)) for at in range(8)])


def shards_grid(
    frames_in,
    code_emb,
    cotangent,
    lengths,
    owner_list,
    master,
    first_moment,
    second_moment,
    ema,
    left_basis,
    right_basis,
    gains,
    gain_first,
    gain_second,
):
    share = frames_in.shape[0]
    owned = master.shape[1]
    groups = D // owned
    heads_w = D // lax.axis_size(TENSOR)
    ff_w = FF // lax.axis_size(TENSOR)
    my_dp = lax.axis_index(DP)
    my_group = lax.axis_index(TENSOR).astype(jnp.int32)

    rel = jnp.array([2 * z + y for y in range(2) for z in (0, 2, 1, 3)], jnp.int32)
    owner_at = my_dp ^ rel
    slots = jnp.arange(groups, dtype=jnp.int32)
    source = jnp.sum(
        jnp.where(owner_list[None, :] == owner_at[:, None], slots[None, :], 0), axis=1
    ).astype(jnp.int32)
    info = jnp.stack([my_group, lengths[0]])
    count = (lengths - my_group * share).astype(jnp.int32)

    line = Line()
    codes = jnp.transpose(code_emb, (1, 0, 2))

    (rows_in, gains_here, normed), shards = prep(line, source, frames_in, gains, master)
    grad, grad_t, codes_here = seed(line, source, count, jnp.transpose(cotangent, (1, 0, 2)), codes)
    (
        g_heads, g_up, g_down, l_heads, l_up, l_down, qkv, mixed, lse, middle, global_out, normed_a, normed_b,
        active, slope,
    ) = forward_global(line, info, rows_in, normed, gains_here, shards)

    l_qkv, l_mixed, l_middle, l_normed_b, l_a_t = local_heads(
        line, global_out, codes_here, gains_here, l_heads
    )
    l_active, l_slope, local_out, l_b_t = local_ff(line, source, l_normed_b, l_middle, l_up, l_down)
    local_out = jnp.transpose(local_out, (1, 0, 2))

    (
        grad_global, small, gain_c, gain_d, u_near, u_far, d2, d0, h2_near, h2_far, h0_near, h0_far,
    ) = local_back(
        line, grad, grad_t, l_b_t, l_a_t, l_active, l_slope, l_qkv, l_mixed, l_middle, global_out, codes_here,
        gains_here, l_heads, l_up, l_down,
    )
    def update(layer, third, pieces, before):
        return adam(
            line, layer, third, pieces, left_basis, right_basis, master, first_moment, second_moment, ema, before
        )

    def depth_second(keep, met):
        keep, send = sum_pieces(line, [keep, met])
        return keep, hop_z(send, 2)

    (
        grad_middle, grad_sum, gain_b, gu_near, gu_met, gh_near, gh_far, lu_keep, lu_met, gd_keep, gd_met, h2_met,
        h_first, h2_first,
    ) = backward_global(
        line, info, small, grad_global, middle, gains_here, lse, (g_up, g_down, g_heads), active, slope, normed_b,
        normed_a, qkv, mixed, (u_near, u_far, h2_far, h0_far, h2_near),
    )
    input_grad, gain_grads = finish(
        line, source, rows_in, grad_sum, grad_middle, gains_here, (gain_b, gain_c, gain_d)
    )
    (
        gain_grads, gu_keep, gu_met, gh_keep, gh_met, ld_keep, ld_send, lh_keep, lh_send,
    ) = last_transfers(
        line,
        gain_grads,
        (gu_near, gu_met, gh_near, gh_far, d0, d2, h0_near, h2_near, h0_far, h2_met, h_first, h2_first),
    )
    lh_met = hop_z(lh_send, 1)
    ld_met = hop_z(ld_send, 2)
    found = update(1, 1, (lu_keep, lu_met), None)
    found = update(0, 2, (gd_keep, gd_met), found)
    found = update(0, 1, (gu_keep, gu_met), found)
    lh = depth_second(lh_keep, lh_met)
    found = update(0, 0, (gh_keep, gh_met), found)
    found = update(1, 2, (ld_keep, ld_met), found)
    found = update(1, 0, lh, found)
    weight_grads, new_master, new_first, new_second, new_ema = found
    new_gain_first = beta_first * gain_first + (1.0 - beta_first) * gain_grads
    new_gain_second = beta_second * gain_second + (1.0 - beta_second) * gain_grads * gain_grads
    new_gains = gains - gain_rate * new_gain_first / (jnp.sqrt(new_gain_second) + adam_eps)
    return (
        local_out,
        input_grad,
        weight_grads,
        gain_grads,
        new_master,
        new_first,
        new_second,
        new_ema,
        new_gains,
        new_gain_first,
        new_gain_second,
    )


def solution(mesh):
    fits = mesh.shape[DP] == 8 and mesh.shape[TENSOR] == 4
    return jax.shard_map(
        shards_grid if fits else shards_any,
        mesh=mesh,
        in_specs=(
            P((DP, TENSOR), None),
            P((DP, TENSOR), None, None),
            P((DP, TENSOR), None, None),
            P(DP),
            P(),
            P(None, DP, TENSOR),
            P(None, DP, TENSOR),
            P(None, DP, TENSOR),
            P(None, DP, TENSOR),
            P(None, DP, TENSOR),
            P(None, DP, None, TENSOR),
            P(),
            P(),
            P(),
        ),
        out_specs=(
            P((DP, TENSOR), None, None),
            P((DP, TENSOR), None),
            P(None, DP, TENSOR),
            P(),
            P(None, DP, TENSOR),
            P(None, DP, TENSOR),
            P(None, DP, TENSOR),
            P(None, DP, TENSOR),
            P(),
            P(),
            P(),
        ),
        check_vma=False,
    )
```

```python
import math

import jax
import jax.numpy as jnp
from jax import lax
from jax.experimental import pallas as pl
from jax.experimental.pallas import tpu as pltpu
from jax.sharding import PartitionSpec as P

DP, TENSOR = "dp", "tensor"
D = 1024
HD = 64
FF = 4096
CB = 3
LMAX = 1024


norm_eps = 1e-06
beta_first = 0.5
beta_second = 0.5
adam_eps = 1e-08
step_rate = 0.05
gain_rate = 0.4
ema_decay = 0.9
masked_fill = -1e30
highest = lax.Precision.HIGHEST


def dot_rows(left, right):
    return jnp.dot(left, right, preferred_element_type=jnp.float32)


def dot_transposed(left, right):
    return lax.dot_general(
        left, right, (((1,), (1,)), ((), ())), preferred_element_type=jnp.float32
    )


def dot_over_rows(left, right):
    return lax.dot_general(
        left, right, (((0,), (0,)), ((), ())), preferred_element_type=jnp.float32
    )


def keep_rows(values):
    return values


def row_term(operand, weight):
    return dot_transposed(operand, weight)


def rms_forward(rows_in, gain):
    return (
        rows_in * lax.rsqrt(jnp.mean(rows_in * rows_in, axis=-1, keepdims=True) + norm_eps) * gain
    )


def rms_backward(rows_in, gain, grad_out):
    width = rows_in.shape[-1]
    scale_rows = lax.rsqrt(jnp.mean(rows_in * rows_in, axis=-1, keepdims=True) + norm_eps)
    scaled_grad = grad_out * gain
    inner_total = jnp.sum(scaled_grad * rows_in, axis=-1, keepdims=True)
    grad_in = (
        scale_rows * scaled_grad
        - rows_in * (scale_rows * scale_rows * scale_rows) * inner_total / width
    )
    gain_grad = jnp.sum(grad_out * rows_in * scale_rows, axis=0)
    return (grad_in, gain_grad)


def gelu_slope(upper):
    normal_cdf = 0.5 * (1.0 + lax.erf(upper * (1.0 / math.sqrt(2.0))))
    density = jnp.exp(-0.5 * upper * upper) * (1.0 / math.sqrt(2.0 * math.pi))
    return normal_cdf + upper * density


def split_layer(layer_cols, groups, head_cols, ff_cols):
    width = layer_cols.shape[0]
    grouped = layer_cols.reshape(width, groups, -1)

    def columns(begin, extent):
        return grouped[:, :, begin : begin + extent].reshape(width, groups * extent)

    w_qkv = jnp.concatenate(
        [columns(0, head_cols), columns(head_cols, head_cols), columns(2 * head_cols, head_cols)],
        axis=1,
    )
    return (
        w_qkv,
        columns(3 * head_cols, head_cols),
        columns(4 * head_cols, ff_cols),
        columns(4 * head_cols + ff_cols, ff_cols),
    )


def join_layer(grad_parts, groups):
    grad_qkv, grad_out, grad_up, grad_down = grad_parts
    width = grad_qkv.shape[0]
    head_width = grad_qkv.shape[1] // 3
    pieces = [
        grad_qkv[:, 0:head_width],
        grad_qkv[:, head_width : 2 * head_width],
        grad_qkv[:, 2 * head_width :],
        grad_out,
        grad_up,
        grad_down,
    ]
    return jnp.concatenate([piece.reshape(width, groups, -1) for piece in pieces], axis=2).reshape(
        width, -1
    )


def global_scores(queries, key_rows, length):
    span = queries.shape[0]
    heads = queries.shape[1] // HD
    scores = jnp.einsum(
        "qhd,khd->hqk",
        queries.reshape(span, heads, HD),
        key_rows.reshape(span, heads, HD),
        preferred_element_type=jnp.float32,
    ) * HD ** (-0.5)
    rows_at = lax.broadcasted_iota(jnp.int32, (span, span), 0)
    cols_at = lax.broadcasted_iota(jnp.int32, (span, span), 1)
    allowed = (cols_at <= rows_at) & (cols_at < length)
    return jnp.where(allowed[None], scores, masked_fill)


def global_attend(queries, key_rows, value_rows, lengths):
    items = lengths.shape[0]
    span = queries.shape[0] // items
    heads = queries.shape[1] // HD

    def one_item(packed):
        item_query, item_key, item_value, length = packed
        scores = global_scores(item_query, item_key, length)
        row_max = jnp.max(scores, axis=-1, keepdims=True)
        expanded = jnp.exp(scores - row_max)
        row_total = jnp.sum(expanded, axis=-1, keepdims=True)
        probability = (expanded / row_total).astype(jnp.bfloat16)
        mixed = jnp.einsum(
            "hqk,khd->qhd",
            probability,
            item_value.reshape(span, heads, HD),
            preferred_element_type=jnp.float32,
        )
        return (
            mixed.reshape(span, -1).astype(jnp.bfloat16),
            (row_max + jnp.log(row_total))[..., 0],
        )

    mixed, log_total = lax.map(
        one_item,
        (
            queries.reshape(items, span, -1),
            key_rows.reshape(items, span, -1),
            value_rows.reshape(items, span, -1),
            lengths,
        ),
    )
    return (mixed.reshape(items * span, -1), log_total)


def global_attend_back(queries, key_rows, value_rows, lengths, log_total, grad_mixed):
    items = lengths.shape[0]
    span = queries.shape[0] // items
    heads = queries.shape[1] // HD
    scale_score = HD ** (-0.5)

    def one_item(packed):
        item_query, item_key, item_value, length, item_lse, item_grad = packed
        scores = global_scores(item_query, item_key, length)
        probability = jnp.exp(scores - item_lse[..., None])
        grad_heads = item_grad.reshape(span, heads, HD)
        query_heads = item_query.reshape(span, heads, HD)
        key_heads = item_key.reshape(span, heads, HD)
        value_heads = item_value.reshape(span, heads, HD)
        grad_value = jnp.einsum(
            "hqk,qhd->khd",
            probability.astype(jnp.bfloat16),
            grad_heads,
            preferred_element_type=jnp.float32,
        )
        grad_prob = jnp.einsum(
            "qhd,khd->hqk", grad_heads, value_heads, preferred_element_type=jnp.float32
        )
        center = jnp.sum(probability * grad_prob, axis=-1, keepdims=True)
        grad_scores = (probability * (grad_prob - center)).astype(jnp.bfloat16)
        grad_query = (
            jnp.einsum("hqk,khd->qhd", grad_scores, key_heads, preferred_element_type=jnp.float32)
            * scale_score
        )
        grad_key = (
            jnp.einsum("hqk,qhd->khd", grad_scores, query_heads, preferred_element_type=jnp.float32)
            * scale_score
        )
        return jnp.concatenate(
            [
                grad_query.reshape(span, -1),
                grad_key.reshape(span, -1),
                grad_value.reshape(span, -1),
            ],
            axis=1,
        ).astype(jnp.bfloat16)

    grads = lax.map(
        one_item,
        (
            queries.reshape(items, span, -1),
            key_rows.reshape(items, span, -1),
            value_rows.reshape(items, span, -1),
            lengths,
            log_total,
            grad_mixed.reshape(items, span, -1),
        ),
    )
    return grads.reshape(items * span, -1)


def local_probability(queries, key_rows):
    frame_count = queries.shape[0] // CB
    heads = queries.shape[1] // HD
    scores = jnp.einsum(
        "fqhd,fkhd->fhqk",
        queries.reshape(frame_count, CB, heads, HD),
        key_rows.reshape(frame_count, CB, heads, HD),
        preferred_element_type=jnp.float32,
    ) * HD ** (-0.5)
    rows_at = lax.broadcasted_iota(jnp.int32, (CB, CB), 0)
    cols_at = lax.broadcasted_iota(jnp.int32, (CB, CB), 1)
    scores = jnp.where(cols_at <= rows_at, scores, masked_fill)
    row_max = jnp.max(scores, axis=-1, keepdims=True)
    expanded = jnp.exp(scores - row_max)
    return expanded / jnp.sum(expanded, axis=-1, keepdims=True)


def local_attend(queries, key_rows, value_rows):
    frame_count = queries.shape[0] // CB
    heads = queries.shape[1] // HD
    probability = local_probability(queries, key_rows).astype(jnp.bfloat16)
    mixed = jnp.einsum(
        "fhqk,fkhd->fqhd",
        probability,
        value_rows.reshape(frame_count, CB, heads, HD),
        preferred_element_type=jnp.float32,
    )
    return (mixed.reshape(queries.shape[0], -1).astype(jnp.bfloat16), jnp.zeros((), jnp.float32))


def local_attend_back(queries, key_rows, value_rows, saved, grad_mixed):
    frame_count = queries.shape[0] // CB
    heads = queries.shape[1] // HD
    scale_score = HD ** (-0.5)
    probability = local_probability(queries, key_rows)
    grad_heads = grad_mixed.reshape(frame_count, CB, heads, HD)
    query_heads = queries.reshape(frame_count, CB, heads, HD)
    key_heads = key_rows.reshape(frame_count, CB, heads, HD)
    value_heads = value_rows.reshape(frame_count, CB, heads, HD)
    grad_value = jnp.einsum(
        "fhqk,fqhd->fkhd",
        probability.astype(jnp.bfloat16),
        grad_heads,
        preferred_element_type=jnp.float32,
    )
    grad_prob = jnp.einsum(
        "fqhd,fkhd->fhqk", grad_heads, value_heads, preferred_element_type=jnp.float32
    )
    center = jnp.sum(probability * grad_prob, axis=-1, keepdims=True)
    grad_scores = (probability * (grad_prob - center)).astype(jnp.bfloat16)
    grad_query = (
        jnp.einsum("fhqk,fkhd->fqhd", grad_scores, key_heads, preferred_element_type=jnp.float32)
        * scale_score
    )
    grad_key = (
        jnp.einsum("fhqk,fqhd->fkhd", grad_scores, query_heads, preferred_element_type=jnp.float32)
        * scale_score
    )
    total_rows = queries.shape[0]
    return jnp.concatenate(
        [
            grad_query.reshape(total_rows, -1),
            grad_key.reshape(total_rows, -1),
            grad_value.reshape(total_rows, -1),
        ],
        axis=1,
    ).astype(jnp.bfloat16)


def block_forward(rows_in, matrices, gain_a, gain_b, path, attend):
    gather_rows, sum_rows = (path[0], path[1])
    w_qkv, w_out, w_up, w_down = matrices
    normed_a = gather_rows(rms_forward(rows_in, gain_a).astype(jnp.bfloat16))
    projected = dot_rows(normed_a, w_qkv).astype(jnp.bfloat16)
    head_width = projected.shape[1] // 3
    mixed, saved = attend(
        projected[:, :head_width],
        projected[:, head_width : 2 * head_width],
        projected[:, 2 * head_width :],
    )
    middle = rows_in + sum_rows(mixed, w_out)
    normed_b = gather_rows(rms_forward(middle, gain_b).astype(jnp.bfloat16))
    upper = dot_rows(normed_b, w_up)
    active = jax.nn.gelu(upper, approximate=False).astype(jnp.bfloat16)
    result = middle + sum_rows(active, w_down)
    return (result, (rows_in, normed_a, projected, mixed, saved, middle, normed_b, upper, active))


def block_backward(grad_result, kept, matrices, gain_a, gain_b, path, attend_back):
    gather_grads, sum_back = (path[2], path[3])
    rows_in, normed_a, projected, mixed, saved, middle, normed_b, upper, active = kept
    w_qkv, w_out, w_up, w_down = matrices
    grad_branch = gather_grads(grad_result.astype(jnp.bfloat16))
    grad_down = dot_over_rows(grad_branch, active)
    grad_active = dot_rows(grad_branch, w_down)
    grad_upper = (grad_active * gelu_slope(upper)).astype(jnp.bfloat16)
    grad_up = dot_over_rows(normed_b, grad_upper)
    grad_normed_b = sum_back(grad_upper, w_up)
    grad_middle_part, gain_b_grad = rms_backward(middle, gain_b, grad_normed_b)
    grad_middle = grad_result + grad_middle_part
    grad_attn = gather_grads(grad_middle.astype(jnp.bfloat16))
    grad_out = dot_over_rows(grad_attn, mixed)
    grad_mixed = dot_rows(grad_attn, w_out).astype(jnp.bfloat16)
    head_width = projected.shape[1] // 3
    grad_qkv = attend_back(
        projected[:, :head_width],
        projected[:, head_width : 2 * head_width],
        projected[:, 2 * head_width :],
        saved,
        grad_mixed,
    )
    grad_weight_qkv = dot_over_rows(normed_a, grad_qkv)
    grad_normed_a = sum_back(grad_qkv, w_qkv)
    grad_rows_part, gain_a_grad = rms_backward(rows_in, gain_a, grad_normed_a)
    return (
        grad_middle + grad_rows_part,
        (grad_weight_qkv, grad_out, grad_up, grad_down),
        gain_a_grad,
        gain_b_grad,
    )


def shards_any(
    frames_in,
    code_emb,
    cotangent,
    lengths,
    owner_list,
    master,
    first_moment,
    second_moment,
    ema,
    left_basis,
    right_basis,
    gains,
    gain_first,
    gain_second,
):
    tensor_count = lax.axis_size(TENSOR)
    group_count = lax.axis_size(DP)
    head_cols = D // tensor_count
    ff_cols = FF // tensor_count
    share = frames_in.shape[0]
    owned_rows = master.shape[1]
    gathered = lax.all_gather(master.astype(jnp.bfloat16), DP, axis=1, tiled=True)
    layers = jnp.take(gathered.reshape(2, group_count, owned_rows, -1), owner_list, axis=1).reshape(
        2, group_count * owned_rows, -1
    )

    def gather_rows(values):
        return lax.all_gather(values, TENSOR, axis=0, tiled=True)

    def gather_grads(values):
        return lax.all_gather(values, TENSOR, axis=0, tiled=True)

    def sum_rows(operand, weight):
        return lax.psum_scatter(
            row_term(operand, weight).astype(jnp.bfloat16),
            TENSOR,
            scatter_dimension=0,
            tiled=True,
        ).astype(jnp.float32)

    def sum_back(operand, weight):
        return lax.psum_scatter(
            row_term(operand, weight).astype(jnp.bfloat16),
            TENSOR,
            scatter_dimension=0,
            tiled=True,
        ).astype(jnp.float32)

    heads_path = (gather_rows, sum_rows, gather_grads, sum_back)
    rows_path = (keep_rows, dot_transposed, keep_rows, dot_transposed)

    def attend_global(queries, key_rows, value_rows):
        return global_attend(queries, key_rows, value_rows, lengths)

    def attend_global_back(queries, key_rows, value_rows, saved, grad_mixed):
        return global_attend_back(queries, key_rows, value_rows, lengths, saved, grad_mixed)

    global_matrices = split_layer(layers[0], 1, head_cols, ff_cols)
    global_out, global_kept = block_forward(
        frames_in.astype(jnp.float32),
        global_matrices,
        gains[0],
        gains[1],
        heads_path,
        attend_global,
    )
    local_in = (global_out[:, None, :] + code_emb.astype(jnp.float32)).reshape(share * CB, -1)
    local_layer = lax.all_gather(layers[1], TENSOR, axis=1, tiled=True)
    local_matrices = split_layer(local_layer, tensor_count, head_cols, ff_cols)
    local_result, local_kept = block_forward(
        local_in, local_matrices, gains[2], gains[3], rows_path, local_attend
    )
    local_out = local_result.reshape(share, CB, -1).astype(jnp.bfloat16)
    frame_at = lax.axis_index(TENSOR) * share + jnp.arange(share, dtype=jnp.int32)
    item_at = frame_at // LMAX
    item_slots = jnp.arange(lengths.shape[0], dtype=jnp.int32)
    item_length = jnp.sum(
        jnp.where(item_at[:, None] == item_slots[None, :], lengths[None, :], 0), axis=1
    )
    valid = (frame_at % LMAX < item_length).astype(jnp.float32)
    grad_local = (cotangent.astype(jnp.float32) * valid[:, None, None]).reshape(share * CB, -1)
    grad_local_in, local_weight_grads, gain_c_grad, gain_d_grad = block_backward(
        grad_local, local_kept, local_matrices, gains[2], gains[3], rows_path, local_attend_back
    )
    grad_global_out = jnp.sum(grad_local_in.reshape(share, CB, -1), axis=1)
    input_grad, global_weight_grads, gain_a_grad, gain_b_grad = block_backward(
        grad_global_out,
        global_kept,
        global_matrices,
        gains[0],
        gains[1],
        heads_path,
        attend_global_back,
    )
    local_grads = join_layer(local_weight_grads, tensor_count)
    local_grads = lax.psum_scatter(
        local_grads.astype(jnp.bfloat16), TENSOR, scatter_dimension=1, tiled=True
    ).astype(jnp.float32)
    layer_grads = jnp.stack([join_layer(global_weight_grads, 1), local_grads])
    slots = jnp.arange(group_count, dtype=jnp.int32)
    inverse = jnp.sum(jnp.where(owner_list[None, :] == slots[:, None], slots[None, :], 0), axis=1)
    ordered = jnp.take(
        layer_grads.reshape(2, group_count, owned_rows, -1), inverse, axis=1
    ).reshape(2, group_count * owned_rows, -1)
    weight_grads = lax.psum_scatter(
        ordered.astype(jnp.bfloat16), DP, scatter_dimension=1, tiled=True
    ).astype(jnp.float32)
    gain_grads = lax.psum(
        jnp.stack([gain_a_grad, gain_b_grad, gain_c_grad, gain_d_grad]), (DP, TENSOR)
    )
    tile_count = right_basis.shape[1]
    turned_left = jnp.einsum("lab,lac->lbc", left_basis, weight_grads, precision=highest)
    rotated = jnp.einsum(
        "lbkc,lkce->lbke",
        turned_left.reshape(2, owned_rows, tile_count, -1),
        right_basis,
        precision=highest,
    ).reshape(weight_grads.shape)
    new_first = beta_first * first_moment + (1.0 - beta_first) * rotated
    new_second = beta_second * second_moment + (1.0 - beta_second) * rotated * rotated
    turned = new_first / (jnp.sqrt(new_second) + adam_eps)
    back_right = jnp.einsum(
        "lbke,lkce->lbkc",
        turned.reshape(2, owned_rows, tile_count, -1),
        right_basis,
        precision=highest,
    )
    back_full = jnp.einsum(
        "lab,lbc->lac", left_basis, back_right.reshape(weight_grads.shape), precision=highest
    )
    new_master = master - step_rate * back_full
    new_ema = ema_decay * ema + (1.0 - ema_decay) * new_master
    new_gain_first = beta_first * gain_first + (1.0 - beta_first) * gain_grads
    new_gain_second = beta_second * gain_second + (1.0 - beta_second) * gain_grads * gain_grads
    new_gains = gains - gain_rate * new_gain_first / (jnp.sqrt(new_gain_second) + adam_eps)
    return (
        local_out,
        input_grad,
        weight_grads,
        gain_grads,
        new_master,
        new_first,
        new_second,
        new_ema,
        new_gains,
        new_gain_first,
        new_gain_second,
    )


MIB = 1024 * 1024
VMEM_WHOLE = pl.BlockSpec(memory_space=pltpu.VMEM)
IN_SMEM = pl.BlockSpec(memory_space=pltpu.SMEM)
IN_HBM = pl.BlockSpec(memory_space=pl.ANY)


def shaped(shape, kind):
    return jax.ShapeDtypeStruct(shape, kind)


def cost(flops, moved, exps=0):
    return pl.CostEstimate(flops=int(flops), bytes_accessed=int(moved), transcendentals=int(exps))


weight_of = {
    "forward_global": 170,
    "local_heads": 18,
    "local_ff": 34,
    "local_back": 81,
    "backward_global": 90,
    "last_transfers": 60,
    "adam_update": 5,
}


def group_at(rel):
    mine = lax.axis_index(TENSOR)
    return 2 * ((mine // 2 + rel // 2) % 2) + (mine % 2 + rel % 2) % 2


CORE, X, Y, Z1, Z2 = range(5)


def partner_of(hop):
    dp, tensor = lax.axis_index(DP), lax.axis_index(TENSOR)
    if hop == CORE:
        return {TENSOR: tensor + 1 - 2 * (tensor % 2)}
    if hop == X:
        return {TENSOR: (tensor + 2) % 4}
    if hop == Y:
        return {DP: dp + 1 - 2 * (dp % 2)}
    if hop == Z1:
        return {DP: dp + 2 - 4 * ((dp // 2) % 2)}
    return {DP: (dp + 4) % 8}


def greet(hops):
    barrier = pltpu.get_barrier_semaphore()
    for hop in hops:
        pl.semaphore_signal(
            barrier, inc=1, device_id=partner_of(hop), device_id_type=pl.DeviceIdType.MESH
        )
    pl.semaphore_wait(barrier, len(hops))


def to_partner(hop, source, target, send, recv):
    return pltpu.make_async_remote_copy(
        src_ref=source,
        dst_ref=target,
        send_sem=send,
        recv_sem=recv,
        device_id=partner_of(hop),
        device_id_type=pl.DeviceIdType.MESH,
    )


def part(array, begin, rows):
    return (array, begin, rows)


class Line:
    def __init__(self):
        self.token = None
        self.moves = ()
        self.arrived = []
        self.calls = 0

    def carry(self, *moves):
        self.moves = moves

    def run(self, body, args, in_specs, out_specs, out_shape, aliases=None, scratch_shapes=(), limit=32, hops=(), **rest):
        moves, self.moves = self.moves, ()
        sources, copies, landed = [], [], []
        for hop, *pieces in moves:
            offset = 0
            for piece in pieces:
                array, begin, rows = piece if isinstance(piece, tuple) else (piece, 0, piece.shape[0])
                which = next((at for at, one in enumerate(sources) if one is array), len(sources))
                if which == len(sources):
                    sources.append(array)
                copies.append((hop, which, begin, rows, len(landed), offset))
                offset += rows
            landed.append(shaped((offset,) + array.shape[1:], array.dtype))
        reach = list(hops) or list(dict.fromkeys(move[0] for move in moves))
        lead = 0 if self.token is None else 1
        inputs = lead + len(args)
        first_out = inputs + len(sources)
        outputs = len(out_shape)
        first_scratch = first_out + outputs + len(landed) + 1
        steps = rest.get("grid", (1,))[0]

        def inner(*refs):
            scratch = refs[first_scratch:]
            pending = []
            if copies:
                *scratch, send, recv = scratch
                for at, (hop, which, begin, rows, where, offset) in enumerate(copies):
                    pending.append(
                        to_partner(
                            hop,
                            refs[inputs + which].at[pl.ds(begin, rows)],
                            refs[first_out + outputs + where].at[pl.ds(offset, rows)],
                            send.at[at],
                            recv.at[at],
                        )
                    )

            def begin_all():
                greet(reach)
                for one in pending:
                    one.start()

            def end_all():
                for one in pending:
                    one.wait()

            at_ends = (lambda step, act: pl.when(pl.program_id(0) == step)(act)) if steps > 1 else (
                lambda step, act: act()
            )
            if pending:
                at_ends(0, begin_all)
            body(*refs[lead:inputs], *refs[first_out : first_out + outputs], *scratch)
            if pending:
                at_ends(steps - 1, end_all)

        extra = {}
        if reach:
            extra = {"collective_id": self.calls, "has_side_effects": True}
            self.calls += 1
        found = pl.pallas_call(
            inner,
            in_specs=[IN_HBM] * lead + list(in_specs) + [IN_HBM] * len(sources),
            out_specs=list(out_specs) + [IN_HBM] * (len(landed) + 1),
            out_shape=list(out_shape) + landed + [shaped((8, 128), jnp.float32)],
            scratch_shapes=list(scratch_shapes)
            + ([pltpu.SemaphoreType.DMA((len(copies),))] * 2 if copies else []),
            input_output_aliases={lead + at: to for at, to in (aliases or {}).items()},
            cost_estimate=cost(weight_of.get(rest["name"], 1.0) * 0.2e9, 1000),
            compiler_params=pltpu.CompilerParams(vmem_limit_bytes=limit * MIB, **extra),
            **rest,
        )(*([self.token] * lead), *args, *sources)
        self.token = found[-1]
        self.arrived = list(found[outputs:-1])
        return list(found[:outputs])


def lanes_of(source_ref, at, width):
    return pl.ds(pl.multiple_of(source_ref[at] * width, width), width)


def norm_rows(rows, gain):
    scale = lax.rsqrt(jnp.mean(rows * rows, axis=-1, keepdims=True) + norm_eps)
    return rows * scale * gain


def norm_rows_back(rows, gain, grad):
    scale = lax.rsqrt(jnp.mean(rows * rows, axis=-1, keepdims=True) + norm_eps)
    scaled = grad * gain
    inner = jnp.sum(scaled * rows, axis=-1, keepdims=True)
    grad_in = scale * scaled - rows * (scale * scale * scale) * inner / rows.shape[-1]
    return grad_in, jnp.sum(grad * rows * scale, axis=0, keepdims=True)


def gelu_both(upper):
    size = jnp.abs(upper)
    base = 1.0 + (0.3275911 / math.sqrt(2.0)) * size
    guess = pl.reciprocal(base, approx=True)
    ratio = guess * (2.0 - base * guess)
    bell = jnp.exp(-0.5 * upper * upper)
    series = ratio * (
        0.5 * 0.254829592
        + ratio
        * (
            -0.5 * 0.284496736
            + ratio * (0.5 * 1.421413741 + ratio * (-0.5 * 1.453152027 + ratio * (0.5 * 1.061405429)))
        )
    )
    tail = series * bell
    cdf = jnp.where(upper >= 0.0, 1.0 - tail, tail)
    density = bell * (1.0 / math.sqrt(2.0 * math.pi))
    return (upper * cdf).astype(jnp.bfloat16), (cdf + upper * density).astype(jnp.bfloat16)


def both(rows, near, far):
    depth = near.shape[0]
    return dot_rows(rows[:, :depth], near) + dot_rows(rows[:, depth:], far)


def held(shape):
    return pl.BlockSpec(shape, lambda step: (0,) * len(shape), pipeline_mode=pl.Buffered(1))


def by_cols(shape):
    return pl.BlockSpec(shape, lambda step: (0, step))


def prep_body(source_ref, frames_ref, gains_ref, *refs):
    masters, (rows_ref, gains_out_ref, normed_ref), shards = refs[:6], refs[6:9], refs[9:]
    for master_ref, shard_ref in zip(masters, shards):
        shard_ref[...] = master_ref[0].astype(jnp.bfloat16)
    owned = frames_ref.shape[1] // source_ref.shape[0]
    for at in range(source_ref.shape[0]):
        here = slice(at * owned, (at + 1) * owned)
        rows_ref[:, here] = frames_ref[:, lanes_of(source_ref, at, owned)]
        gains_out_ref[:, here] = gains_ref[:, lanes_of(source_ref, at, owned)]
    normed_ref[...] = norm_rows(rows_ref[...].astype(jnp.float32), gains_out_ref[0:1, :]).astype(
        jnp.bfloat16
    )


def prep(line, source, frames, gains, master):
    owned, columns = master.shape[1], master.shape[2] // 3

    def spec(layer, third):
        return pl.BlockSpec((1, owned, columns), lambda step: (layer, 0, third))

    shapes = [
        shaped(frames.shape, jnp.bfloat16),
        shaped(gains.shape, jnp.float32),
        shaped(frames.shape, jnp.bfloat16),
    ] + [shaped((owned, columns), jnp.bfloat16)] * 6
    found = line.run(
        prep_body,
        (source, frames, gains) + (master,) * 6,
        grid=(1,),
        in_specs=[IN_SMEM, held(frames.shape), held(gains.shape)]
        + [spec(layer, third) for layer in range(2) for third in range(3)],
        out_specs=[held(one.shape) for one in shapes],
        out_shape=shapes,
        limit=60,
        name="prep_rows",
    )
    return found[:3], found[3:]


def finish_body(source_ref, rows_ref, sum_ref, grad_ref, gains_ref, gb_ref, gc_ref, gd_ref, out_ref, gain_ref):
    back, gain_grad = norm_rows_back(rows_ref[...].astype(jnp.float32), gains_ref[0:1, :], sum_ref[...])
    total = grad_ref[...] + back
    owned = out_ref.shape[1] // source_ref.shape[0]
    for at in range(source_ref.shape[0]):
        here = slice(at * owned, (at + 1) * owned)
        there = lanes_of(source_ref, at, owned)
        out_ref[:, there] = total[:, here]
        gain_ref[0:1, there] = gain_grad[:, here]
        gain_ref[1:2, there] = gb_ref[:, here]
        gain_ref[2:3, there] = gc_ref[:, here]
        gain_ref[3:4, there] = gd_ref[:, here]


def finish(line, source, rows, total, grad, gains, others):
    return line.run(
        finish_body,
        (source, rows, total, grad, gains, *others),
        in_specs=[IN_SMEM] + [VMEM_WHOLE] * 7,
        out_specs=[VMEM_WHOLE] * 2,
        out_shape=[shaped(rows.shape, jnp.float32), shaped((4, rows.shape[1]), jnp.float32)],
        limit=60,
        name="input_grad",
    )


forward_order = (
    0, 12, 37, 4, 36, 50, 49, 66, 38, 8, 2, 1, 51, 43, 13, 15, 14, 24, 5, 3, 6, 16, 39, 9, 10, 67, 68, 18, 17,
    20, 85, 86, 45, 87, 44, 88, 69, 72, 52, 53, 73, 54, 74, 75, 55, 41, 22, 76, 56, 25, 7, 27, 26, 77, 62, 78,
    64, 63, 21, 40, 11, 19, 28, 70, 46, 65, 23, 71, 42, 89, 30, 32, 29, 90, 91, 92, 79, 57, 58, 80, 59, 81,
    60, 82, 61, 31, 34, 33, 83, 48, 84, 35, 47,
)


def forward_body(
    info_ref, rows_ref, normed_ref, gains_ref, ga_s, gu_s, gd_s, la_s, lu_s, ld_s,
    ga, gu, gd, la, lu, ld, qkv_ref, mixed_ref, lse_ref, middle_ref, out_ref, na_h, nb_h, active_h, slope_h,
    na, nb, a_v, u_v, d_v, acc, lse_wide, act, slp, parts, met_core, met_x, sends_x, sems, send, recv,
):
    share = rows_ref.shape[0]
    owned = ga_s.shape[0]
    half = D // 2
    width = mixed_ref.shape[1]
    span = 4 * share
    length = info_ref[1]
    scale = HD ** (-0.5)
    flying, filed, numbers = [], [], []

    def fly(hop, source, target):
        at = len(numbers)
        copy = to_partner(hop, source, target, send.at[at], recv.at[at])
        copy.start()
        numbers.append(at)
        flying.append(copy)
        return copy

    def file(source, target):
        copy = pltpu.make_async_copy(source, target, sems.at[len(filed)])
        copy.start()
        filed.append(copy)
        return copy

    quarter = half // 2
    arrived = set()
    named = {}

    def need(*names):
        for name in names:
            if name not in arrived:
                arrived.add(name)
                named[name].wait_recv()

    def same(hop, whole, begin, rows, shift):
        return lambda: fly(hop, whole.at[pl.ds(begin, rows)], whole.at[pl.ds(begin + shift, rows)])

    def level(hop, stack, begin, to, start, rows):
        here = pl.ds(start, rows)
        return lambda: fly(hop, stack.at[begin, here], stack.at[to, here])

    moves = {}
    for letter, shard, whole in (("A", ga_s, ga), ("U", gu_s, gu), ("D", gd_s, gd)):
        moves["g2" + letter] = (
            (lambda shard, whole: lambda: fly(Z2, shard, whole.at[pl.ds(owned, owned)]))(shard, whole),
            (),
        )
        moves["g1" + letter] = (same(Z1, whole, 0, quarter, quarter), ("g2" + letter, "own"))
        moves["gy0" + letter] = (same(Y, whole, 0, quarter, half), ("g2" + letter, "own"))
        moves["gy1" + letter] = (same(Y, whole, quarter, quarter, half), ("g1" + letter,))
    for letter, shard, stack in (("A", la_s, la), ("U", lu_s, lu)):
        near = stack.at[0]
        moves["l2" + letter] = (
            (lambda shard, near: lambda: fly(Z2, shard, near.at[pl.ds(owned, owned)]))(shard, near),
            (),
        )
        moves["l1" + letter] = (same(Z1, near, 0, quarter, quarter), ("l2" + letter, "own"))
        for at in range(2):
            source = ("l2" + letter, "own") if at == 0 else ("l1" + letter,)
            moves[f"ly{at}{letter}"] = (same(Y, near, at * quarter, quarter, half), source)
            moves[f"lx{at}{letter}"] = (level(X, stack, 0, 2, at * quarter, quarter), source)
            if letter == "A":
                moves[f"lf{at}{letter}"] = (
                    level(X, stack, 0, 2, half + at * quarter, quarter),
                    (f"ly{at}{letter}",),
                )
            else:
                moves[f"lf{at}{letter}"] = (
                    same(Y, stack.at[2], at * quarter, quarter, half),
                    (f"lx{at}{letter}",),
                )
        moves["cn" + letter] = (level(CORE, stack, 0, 1, 0, half), ("l2" + letter, "l1" + letter, "own"))
        moves["cf" + letter] = (level(CORE, stack, 0, 1, half, half), ("ly0" + letter, "ly1" + letter))
        moves["cx" + letter] = (level(CORE, stack, 2, 3, 0, half), ("lx0" + letter, "lx1" + letter))
        moves["cxf" + letter] = (level(CORE, stack, 2, 3, half, half), ("lf0" + letter, "lf1" + letter))
    moves["dx"] = (lambda: fly(X, ld_s, ld.at[2, pl.ds(0, owned)]), ())
    moves["dy"] = (lambda: fly(Y, ld_s, ld.at[0, pl.ds(half, owned)]), ())
    moves["dxy"] = (same(Y, ld.at[2], 0, owned, half), ("dx",))
    for at, source in enumerate((("own",), ("dy",), ("dx",), ("dxy",))):
        stack, begin = ld.at[2 * (at // 2)], half * (at % 2)
        moves[f"d2{at}"] = (same(Z2, stack, begin, owned, owned), source)
        moves[f"d1{at}"] = (same(Z1, stack, begin, quarter, quarter), (f"d2{at}",) + source)
    moves["cdn"] = (level(CORE, ld, 0, 1, 0, D), ("d10", "d11", "d20", "d21", "dy", "own"))
    moves["cdx"] = (level(CORE, ld, 2, 3, 0, D), ("d12", "d13", "d22", "d23", "dx", "dxy"))
    moves["nx"] = (lambda: fly(X, normed_ref, na.at[pl.ds(2 * share, share)]), ())
    moves["nc"] = (lambda: fly(CORE, normed_ref, na.at[pl.ds(share, share)]), ())
    moves["nxc"] = (same(CORE, na, 2 * share, share, share), ("nx",))
    strip = share // 2
    strips = [pl.ds(at * strip, strip) for at in range(2)]

    def sums_moves(far, near, over, which):
        for at, name in enumerate(far):
            moves[name] = (
                (lambda rows: lambda: fly(CORE, parts.at[3, rows], met_core.at[2 * which, rows]))(strips[at]),
                (),
            )
        moves[near] = (lambda: fly(CORE, parts.at[1], met_core.at[2 * which + 1]), ())
        for at, name in enumerate(over):
            moves[name] = (
                (lambda rows: lambda: fly(X, sends_x.at[which, rows], met_x.at[which, rows]))(strips[at]),
                (),
            )

    sums_moves(("c3a", "c3b"), "c1", ("sx0", "sx1"), 0)
    sums_moves(("e3a", "e3b"), "e1", ("tx0", "tx1"), 1)
    for at in range(2):
        moves[f"ox{at}"] = (same(X, nb, at * strip, strip, 2 * share), ())
    moves["oc"] = (same(CORE, nb, 0, share, share), ())
    moves["oxc"] = (same(CORE, nb, 2 * share, share, share), ("ox0", "ox1"))

    def do_own():
        copies = [
            file(shard, whole.at[pl.ds(0, owned)])
            for shard, whole in (
                (ga_s, ga), (la_s, la.at[0]), (gu_s, gu), (gd_s, gd), (lu_s, lu.at[0]), (ld_s, ld.at[0]),
            )
        ]
        na[pl.ds(0, share), :] = normed_ref[...]
        for one in copies:
            one.wait()

    def load(letter, whole, target):
        need("g2" + letter, "g1" + letter, "gy0" + letter, "gy1" + letter)
        return file(whole, target)

    def do_load_a():
        load("A", ga, a_v).wait()

    def do_qkv():
        need("nx", "nc", "nxc")
        outgoing.append(file(na, na_h))
        for rel in range(4):
            at = pl.ds(pl.multiple_of(group_at(rel) * share, share), share)
            full = both(
                na[rel * share : (rel + 1) * share, :], a_v[:half, : 3 * width], a_v[half:, : 3 * width]
            )
            qkv_ref[at, :] = full.astype(jnp.bfloat16)
        acc[:, :width] = jnp.zeros((span, width), jnp.float32)
        lse_wide[...] = jnp.zeros_like(lse_wide)

    head_of = lax.broadcasted_iota(jnp.int32, (1, width), 1) // HD
    lane = lax.broadcasted_iota(jnp.int32, (1, 128), 1)

    def do_head(head):
        own_lanes = head_of == head
        for block in range(4):
            rows = slice(block * share, (block + 1) * share)
            reach = (block + 1) * share
            query = jnp.where(own_lanes, qkv_ref[rows, :width] * scale, 0.0).astype(jnp.bfloat16)
            scores = dot_transposed(query, qkv_ref[:reach, width : 2 * width])
            row_at = block * share + lax.broadcasted_iota(jnp.int32, scores.shape, 0)
            col_at = lax.broadcasted_iota(jnp.int32, scores.shape, 1)
            scores = jnp.where((col_at <= row_at) & (col_at < length), scores, masked_fill)
            top = jnp.max(scores, axis=-1, keepdims=True)
            expanded = jnp.exp(scores - top)
            total = jnp.sum(expanded, axis=-1, keepdims=True)
            prob = (expanded * (1.0 / total)).astype(jnp.bfloat16)
            value = jnp.where(own_lanes, qkv_ref[:reach, 2 * width :], 0.0).astype(jnp.bfloat16)
            acc[rows, :width] += dot_rows(prob, value)
            lse_wide[rows, :] = jnp.where(lane == head, top + jnp.log(total), lse_wide[rows, :])

    def do_mix():
        mixed_ref[...] = acc[:, :width].astype(jnp.bfloat16)
        lse_ref[...] = jnp.transpose(lse_wide[...])[: lse_ref.shape[0], :]

    def out_part(rel):
        at = pl.ds(pl.multiple_of(group_at(rel) * share, share), share)
        rows = mixed_ref[at, :]
        parts[rel, :, :half] = dot_transposed(rows, a_v[:half, 3 * width :]).astype(jnp.bfloat16)
        parts[rel, :, half:] = dot_transposed(rows, a_v[half:, 3 * width :]).astype(jnp.bfloat16)

    def down_part(rel):
        parts[rel] = acc[rel * share : (rel + 1) * share, :].astype(jnp.bfloat16)

    def several(act_on, *values):
        def do():
            for value in values:
                act_on(value)

        return do

    def do_add(which, at, name):
        def do():
            need(name)
            rows = strips[at]
            total = parts[2, rows, :].astype(jnp.float32) + met_core[2 * which, rows, :].astype(jnp.float32)
            sends_x[which, rows, :] = total.astype(jnp.bfloat16)

        return do

    def gathered(which, rows, base):
        return (
            base
            + parts[0, rows, :].astype(jnp.float32)
            + met_core[2 * which + 1, rows, :].astype(jnp.float32)
            + met_x[which, rows, :].astype(jnp.float32)
        )

    def do_middle(at):
        def do():
            need("c1", f"sx{at}")
            rows = strips[at]
            total = gathered(0, rows, rows_ref[rows, :].astype(jnp.float32))
            middle_ref[rows, :] = total
            nb[rows, :] = norm_rows(total, gains_ref[1:2, :]).astype(jnp.bfloat16)

        return do

    def do_load_u():
        load("U", gu, u_v).wait()
        acc[...] = jnp.zeros_like(acc)

    def do_load_d():
        copy = load("D", gd, d_v)
        need("oc", "oxc", "ox0", "ox1")
        outgoing.append(file(nb, nb_h))
        copy.wait()

    def do_ff(at):
        lanes = slice(at * 256, (at + 1) * 256)
        active, slope = gelu_both(both(nb[...], u_v[:half, lanes], u_v[half:, lanes]))
        act[:, lanes] = active
        slp[:, lanes] = slope
        for side in range(2):
            cols_at = slice(side * half, (side + 1) * half)
            acc[:, cols_at] += dot_transposed(active, d_v[side * half : (side + 1) * half, lanes])

    def do_q3():
        outgoing.extend([file(act, active_h), file(slp, slope_h)])
        for name in ("c3a", "c3b", "c1"):
            named[name].wait_send()
            flying[:] = [other for other in flying if other is not named[name]]
        down_part(3)

    def do_result(at):
        def do():
            need("e1", f"tx{at}")
            rows = strips[at]
            out_ref[rows, :] = gathered(1, rows, middle_ref[rows, :])

        return do

    outgoing = []
    steps = {
        "own": do_own, "load_a": do_load_a, "qkv": do_qkv, "mix": do_mix, "load_u": do_load_u, "load_d": do_load_d,
        "p3": several(out_part, 3), "p2": several(out_part, 2, 1), "p0": several(out_part, 0),
        "s0": do_add(0, 0, "c3a"), "s1": do_add(0, 1, "c3b"), "m0": do_middle(0), "m1": do_middle(1),
        "q3": do_q3, "q1": several(down_part, 2, 1, 0), "t0": do_add(1, 0, "e3a"), "t1": do_add(1, 1, "e3b"),
        "r0": do_result(0), "r1": do_result(1),
    }
    for at in range(width // HD):
        steps[f"h{at}"] = several(do_head, at)
    for at in range(u_v.shape[1] // 256):
        steps[f"f{at}"] = several(do_ff, at)

    greet((CORE, X, Y, Z1, Z2))
    names = list(moves) + list(steps)
    for place in forward_order:
        name = names[place]
        if name in steps:
            steps[name]()
            arrived.add(name)
        else:
            start, before = moves[name]
            need(*before)
            named[name] = start()
    need(*named)
    for one in outgoing:
        one.wait()
    for one in flying:
        one.wait_send()


def forward_global(line, info, rows, normed, gains, shards):
    share, owned = rows.shape[0], shards[0].shape[0]
    span, columns = 4 * share, shards[0].shape[1]
    width = columns // 4
    small = jnp.bfloat16
    weights = [shaped((D, columns), small)] * 3 + [shaped((4, D, columns), small)] * 3
    return line.run(
        forward_body,
        (info, rows, normed, gains, *shards),
        in_specs=[IN_SMEM] + [VMEM_WHOLE] * 3 + [IN_HBM] * 6,
        out_specs=[IN_HBM] * 6 + [VMEM_WHOLE] * 5 + [IN_HBM] * 4,
        out_shape=weights
        + [
            shaped((span, 3 * width), small),
            shaped((span, width), small),
            shaped((8, span), jnp.float32),
            shaped((share, D), jnp.float32),
            shaped((share, D), jnp.float32),
            shaped((span, D), small),
            shaped((span, D), small),
            shaped((span, columns), small),
            shaped((span, columns), small),
        ],
        scratch_shapes=[
            pltpu.VMEM((span, D), small),
            pltpu.VMEM((span, D), small),
            pltpu.VMEM((D, columns), small),
            pltpu.VMEM((D, columns), small),
            pltpu.VMEM((D, columns), small),
            pltpu.VMEM((span, D), jnp.float32),
            pltpu.VMEM((span, 128), jnp.float32),
            pltpu.VMEM((span, columns), small),
            pltpu.VMEM((span, columns), small),
            pltpu.VMEM((4, share, D), small),
            pltpu.VMEM((4, share, D), small),
            pltpu.VMEM((2, share, D), small),
            pltpu.VMEM((2, share, D), small),
            pltpu.SemaphoreType.DMA((24,)),
            pltpu.SemaphoreType.DMA((96,)),
            pltpu.SemaphoreType.DMA((96,)),
        ],
        hops=(CORE, X, Y, Z1, Z2),
        limit=56,
        name="forward_global",
    )


def backward_body(
    info_ref, small_ref, grad_ref, middle_ref, gains_ref, lse_ref, up_h, down_h, heads_h, active_h, slope_h,
    nb_h, na_h, qkv_h, mixed_h, u_near_h, u_far_h, h2_far_h,
    h0_far_h, h2_near_h,
    mid_ref, sum_ref, gain_ref, gu_near_h, gu_met_h, gh_near_h, gh_far_h, lu_keep_h, lu_met_h, gd_keep_h,
    gd_met_h, h2_met_h, h_first_h, h2_first_h,
    rows_one, rows_two, up_v, down_v, heads_v, act, slp, dup, left_t, right_v, grads_v, qkv_v, mixed_v, dqkv,
    dmix, dq_t, dk_acc, dv_acc, center, k_t, parts, met_core, met_x, sends_x, u_v, u_met, d_v, d_met, z_met, h_v,
    sems, send, recv,
):
    share = small_ref.shape[0]
    half = D // 2
    quarter = half // 2
    owned = quarter // 2
    width = mixed_v.shape[1]
    heads = width // HD
    span = 4 * share
    length = info_ref[1]
    scale = HD ** (-0.5)
    numbers, flying, filed = [], [], []

    def fly(hop, source, target):
        at = len(numbers)
        copy = to_partner(hop, source, target, send.at[at], recv.at[at])
        copy.start()
        numbers.append(at)
        flying.append(copy)
        return copy

    def over(copy):
        copy.wait_send()
        flying[:] = [other for other in flying if other is not copy]

    def file(source, target):
        copy = pltpu.make_async_copy(source, target, sems.at[len(filed)])
        copy.start()
        filed.append(copy)
        return copy

    def block(rel):
        return slice(rel * share, (rel + 1) * share)

    def place(rel):
        return pl.ds(pl.multiple_of(group_at(rel) * share, share), share)

    def summed(*terms):
        total = terms[0].astype(jnp.float32)
        for term in terms[1:]:
            total = total + term.astype(jnp.float32)
        return total

    greet((CORE, X, Y, Z1, Z2))
    small_x = fly(X, small_ref, rows_one.at[pl.ds(2 * share, share)])
    small_core = fly(CORE, small_ref, rows_one.at[pl.ds(share, share)])
    u_y = fly(Y, u_far_h, u_met)
    h_first = fly(X, h2_far_h.at[pl.ds(0, quarter)], h_v.at[0])
    first = [file(down_h, down_v), file(slope_h, slp), file(up_h, up_v)]
    active_in = file(active_h, act)
    nb_in = file(nb_h, right_v)
    u_in = file(u_near_h, u_v)
    h_in = file(h0_far_h.at[pl.ds(0, quarter)], h_v.at[1])
    attention_in = [file(heads_h, heads_v), file(qkv_h, qkv_v), file(mixed_h, mixed_v)]
    rows_one[pl.ds(0, share), :] = small_ref[...]
    for one in first:
        one.wait()

    def ff_back(rel):
        rows = block(rel)
        for tile in range(2):
            lanes = slice(tile * half, (tile + 1) * half)
            grad = both(rows_one[rows, :], down_v[:half, lanes], down_v[half:, lanes])
            dup[rows, lanes] = (grad * slp[rows, lanes].astype(jnp.float32)).astype(jnp.bfloat16)
        for side in range(2):
            lanes = slice(side * half, (side + 1) * half)
            parts[rel, :, lanes] = dot_transposed(dup[rows, :], up_v[lanes, :]).astype(jnp.bfloat16)

    ff_back(0)
    small_core.wait_recv()
    ff_back(1)
    small_x.wait_recv()
    small_xc = fly(CORE, rows_one.at[pl.ds(2 * share, share)], rows_one.at[pl.ds(3 * share, share)])
    ff_back(2)
    small_xc.wait_recv()
    ff_back(3)
    strip = share // 2
    strips = [pl.ds(at * strip, strip) for at in range(2)]

    def scatter_start(which):
        from_far = [fly(CORE, parts.at[3, rows], met_core.at[2 * which, rows]) for rows in strips]
        return from_far, fly(CORE, parts.at[1], met_core.at[2 * which + 1])

    def scatter_on(which, from_far):
        from_x = []
        for rows, one in zip(strips, from_far):
            one.wait_recv()
            sends_x[which, rows, :] = summed(parts[2, rows, :], met_core[2 * which, rows, :]).astype(jnp.bfloat16)
            from_x.append(fly(X, sends_x.at[which, rows], met_x.at[which, rows]))
        return from_x

    def gathered(which, rows):
        return summed(parts[0, rows, :], met_core[2 * which + 1, rows, :], met_x[which, rows, :])

    from_far, from_near = scatter_start(0)
    for rel in range(4):
        left_t[:, block(rel)] = jnp.transpose(rows_one[block(rel), :])
    from_x = scatter_on(0, from_far)
    h_in.wait()
    h_first.wait_recv()
    h_v[1] = summed(h_v[0], h_v[1]).astype(jnp.bfloat16)
    h_y = fly(Y, h_v.at[1], h_first_h)
    active_in.wait()
    for side in range(2):
        rows = slice(side * half, (side + 1) * half)
        for tile in range(2):
            lanes = slice(tile * half, (tile + 1) * half)
            grads_v[0, rows, lanes] = dot_rows(left_t[rows, :], act[:, lanes]).astype(jnp.bfloat16)
    gd_y = fly(Y, grads_v.at[0, pl.ds(half, half)], d_met)
    results = []
    from_near.wait_recv()
    gain_total = jnp.zeros((1, D), jnp.float32)
    over_x = []
    for rows, one in zip(strips, from_x):
        one.wait_recv()
        back, gain_grad = norm_rows_back(middle_ref[rows, :], gains_ref[1:2, :], gathered(0, rows))
        total = grad_ref[rows, :] + back
        mid_ref[rows, :] = total
        rows_two[rows, :] = total.astype(jnp.bfloat16)
        gain_total = gain_total + gain_grad
        over_x.append(fly(X, rows_two.at[rows], rows_two.at[pl.ds(2 * share + rows.start, strip)]))
    gain_ref[...] = gain_total
    small_core = fly(CORE, rows_two.at[pl.ds(0, share)], rows_two.at[pl.ds(share, share)])
    h_second = fly(X, h2_far_h.at[pl.ds(quarter, quarter)], h2_met_h)
    h_third = fly(X, h2_near_h.at[pl.ds(0, quarter)], h2_first_h)
    u_y.wait_recv()
    u_in.wait()
    u_v[...] = summed(u_v[...], u_met[...]).astype(jnp.bfloat16)
    u_1 = fly(Z1, u_v.at[pl.ds(quarter, quarter)], z_met.at[0])
    nb_in.wait()
    left_t[...] = jnp.transpose(right_v[...])
    na_in = file(na_h, right_v)
    for side in range(2):
        rows = slice(side * half, (side + 1) * half)
        for tile in range(2):
            lanes = slice(tile * half, (tile + 1) * half)
            grads_v[1, rows, lanes] = dot_rows(left_t[rows, :], dup[:, lanes]).astype(jnp.bfloat16)
    gu_y = fly(Y, grads_v.at[1, pl.ds(half, half)], gu_met_h)
    results.append(file(grads_v.at[1, pl.ds(0, half)], gu_near_h))
    for one in attention_in:
        one.wait()

    def mix_back(rel):
        full = both(rows_two[block(rel), :], heads_v[:half, 3 * width :], heads_v[half:, 3 * width :])
        dmix[place(rel), :] = full.astype(jnp.bfloat16)

    head_of = lax.broadcasted_iota(jnp.int32, (1, width), 1) // HD
    pick = (
        lax.broadcasted_iota(jnp.int32, (8, width), 1) // HD
        == lax.broadcasted_iota(jnp.int32, (8, width), 0)
    ).astype(jnp.bfloat16)
    k_t[...] = jnp.transpose(qkv_v[:, width : 2 * width])
    dq_t[...] = jnp.zeros_like(dq_t)
    dk_acc[...] = jnp.zeros_like(dk_acc)
    dv_acc[...] = jnp.zeros_like(dv_acc)
    mix_back(0)
    small_core.wait_recv()
    mix_back(1)
    for one in over_x:
        one.wait_recv()
    small_xc = fly(CORE, rows_two.at[pl.ds(2 * share, share)], rows_two.at[pl.ds(3 * share, share)])
    mix_back(2)
    u_1.wait_recv()
    u_v[:quarter, :] = summed(u_v[:quarter, :], z_met[0]).astype(jnp.bfloat16)
    u_2 = fly(Z2, u_v.at[pl.ds(owned, owned)], lu_met_h)
    results.append(file(u_v.at[pl.ds(0, owned)], lu_keep_h))
    small_xc.wait_recv()
    mix_back(3)
    product = dmix[...].astype(jnp.float32) * mixed_v[...].astype(jnp.float32)
    high = product.astype(jnp.bfloat16)
    low = (product - high.astype(jnp.float32)).astype(jnp.bfloat16)
    center[...] = dot_transposed(pick, high) + dot_transposed(pick, low)
    for head in range(heads):
        own_lanes = head_of == head
        for at in range(4):
            rows = block(at)
            reach = (at + 1) * share
            query = jnp.where(own_lanes, qkv_v[rows, :width] * scale, 0.0).astype(jnp.bfloat16)
            grad = jnp.where(own_lanes, dmix[rows, :], 0.0).astype(jnp.bfloat16)
            scores = dot_transposed(qkv_v[:reach, width : 2 * width], query)
            key_at = lax.broadcasted_iota(jnp.int32, scores.shape, 0)
            row_at = at * share + lax.broadcasted_iota(jnp.int32, scores.shape, 1)
            prob = jnp.where(
                (key_at <= row_at) & (key_at < length),
                jnp.exp(scores - lse_ref[head : head + 1, rows]),
                0.0,
            )
            dprob = dot_transposed(qkv_v[:reach, 2 * width :], grad)
            dscore = (prob * (dprob - center[head : head + 1, rows])).astype(jnp.bfloat16)
            dv_acc[:reach, :] += dot_rows(prob.astype(jnp.bfloat16), grad)
            dk_acc[:reach, :] += dot_rows(dscore, query)
            lanes = slice(head * HD, (head + 1) * HD)
            dq_t[lanes, rows] += dot_rows(k_t[lanes, :reach], dscore)
    dqkv[:, :width] = (jnp.transpose(dq_t[...]) * scale).astype(jnp.bfloat16)
    dqkv[:, width : 2 * width] = dk_acc[...].astype(jnp.bfloat16)
    dqkv[:, 2 * width :] = dv_acc[...].astype(jnp.bfloat16)
    gd_y.wait_recv()
    d_v[...] = summed(grads_v[0, :half, :], d_met[...]).astype(jnp.bfloat16)
    d_1 = fly(Z1, d_v.at[pl.ds(quarter, quarter)], z_met.at[1])
    for one in from_far + [from_near]:
        over(one)

    def back_part(rel):
        rows = dqkv[place(rel), :]
        for side in range(2):
            lanes = slice(side * half, (side + 1) * half)
            parts[rel, :, lanes] = dot_transposed(rows, heads_v[lanes, : 3 * width]).astype(jnp.bfloat16)

    back_part(3)
    back_part(1)
    from_far, from_near = scatter_start(1)
    back_part(2)
    from_x = scatter_on(1, from_far)
    back_part(0)
    na_in.wait()
    for rel in range(4):
        left_t[:, place(rel)] = jnp.transpose(right_v[block(rel), :])
    over(gd_y)
    for side in range(2):
        rows = slice(side * half, (side + 1) * half)
        grads_v[0, rows, : 3 * width] = dot_rows(left_t[rows, :], dqkv[...]).astype(jnp.bfloat16)
    for rel in range(4):
        left_t[:, place(rel)] = jnp.transpose(rows_two[block(rel), :])
    for side in range(2):
        rows = slice(side * half, (side + 1) * half)
        grads_v[0, rows, 3 * width :] = dot_rows(left_t[rows, :], mixed_v[...]).astype(jnp.bfloat16)
    results += [
        file(grads_v.at[0, pl.ds(0, half)], gh_near_h),
        file(grads_v.at[0, pl.ds(half, half)], gh_far_h),
    ]
    d_1.wait_recv()
    d_v[:quarter, :] = summed(d_v[:quarter, :], z_met[1]).astype(jnp.bfloat16)
    d_2 = fly(Z2, d_v.at[pl.ds(owned, owned)], gd_met_h)
    results.append(file(d_v.at[pl.ds(0, owned)], gd_keep_h))
    from_near.wait_recv()
    for rows, one in zip(strips, from_x):
        one.wait_recv()
        sum_ref[rows, :] = gathered(1, rows)
    for one in (h_y, h_second, h_third, gu_y, u_2, d_2):
        one.wait_recv()
    for one in results:
        one.wait()
    for one in flying:
        one.wait_send()


def backward_global(line, info, small, grad, middle, gains, lse, weights, active, slope, nb, na, qkv, mixed, sums):
    share, columns = small.shape[0], active.shape[1]
    span, width = 4 * share, mixed.shape[1]
    half, owned = D // 2, D // 8
    low = jnp.bfloat16
    up, down, heads = weights
    return line.run(
        backward_body,
        (info, small, grad, middle, gains, lse, up, down, heads, active, slope, nb, na, qkv, mixed, *sums),
        in_specs=[IN_SMEM] + [VMEM_WHOLE] * 5 + [IN_HBM] * 14,
        out_specs=[VMEM_WHOLE] * 3 + [IN_HBM] * 11,
        out_shape=[
            shaped((share, D), jnp.float32),
            shaped((share, D), jnp.float32),
            shaped((1, D), jnp.float32),
        ]
        + [shaped((half, columns), low)] * 4
        + [shaped((owned, columns), low)] * 4
        + [shaped((half // 2, columns), low)] * 3,
        scratch_shapes=[pltpu.VMEM((span, D), low)] * 2
        + [pltpu.VMEM((D, columns), low)] * 3
        + [pltpu.VMEM((span, columns), low)] * 3
        + [pltpu.VMEM((D, span), low), pltpu.VMEM((span, D), low), pltpu.VMEM((2, D, columns), low)]
        + [pltpu.VMEM((span, 3 * width), low), pltpu.VMEM((span, width), low), pltpu.VMEM((span, 3 * width), low)]
        + [
            pltpu.VMEM((span, width), low),
            pltpu.VMEM((width, span), jnp.float32),
            pltpu.VMEM((span, width), jnp.float32),
            pltpu.VMEM((span, width), jnp.float32),
            pltpu.VMEM((8, span), jnp.float32),
            pltpu.VMEM((width, span), low),
            pltpu.VMEM((4, share, D), low),
            pltpu.VMEM((4, share, D), low),
            pltpu.VMEM((2, share, D), low),
            pltpu.VMEM((2, share, D), low),
        ]
        + [pltpu.VMEM((half, columns), low)] * 4
        + [
            pltpu.VMEM((2, half // 2, columns), low),
            pltpu.VMEM((2, half // 2, columns), low),
            pltpu.SemaphoreType.DMA((24,)),
            pltpu.SemaphoreType.DMA((40,)),
            pltpu.SemaphoreType.DMA((40,)),
        ],
        hops=(CORE, X, Y, Z1, Z2),
        limit=56,
        name="backward_global",
    )


def head_sums(width):
    row_at = lax.broadcasted_iota(jnp.int32, (width, width), 0) // HD
    col_at = lax.broadcasted_iota(jnp.int32, (width, width), 1) // HD
    return (row_at == col_at).astype(jnp.bfloat16)


def over_heads(product, ones):
    high = product.astype(jnp.bfloat16)
    low = (product - high.astype(jnp.float32)).astype(jnp.bfloat16)
    return dot_rows(high, ones) + dot_rows(low, ones)


def frame_probs(queries, keys, ones):
    found = []
    for at in range(CB):
        scores = [over_heads(queries[at] * keys[c2], ones) * HD ** (-0.5) for c2 in range(at + 1)]
        top = scores[0]
        for one in scores[1:]:
            top = jnp.maximum(top, one)
        expanded = [jnp.exp(one - top) for one in scores]
        total = expanded[0]
        for one in expanded[1:]:
            total = total + one
        inverse = 1.0 / total
        found.append([one * inverse for one in expanded])
    return found


def rounded_f32(values):
    return values.astype(jnp.bfloat16).astype(jnp.float32)


def halves_of(stack):
    half = stack.shape[1] // 2
    return [(stack.at[at, pl.ds(0, half)], stack.at[at, pl.ds(half, half)]) for at in range(stack.shape[0])]


def start_weights(parts, buffer, sems):
    for at, pair in enumerate(parts):
        for half, ref in enumerate(pair):
            pltpu.make_async_copy(ref, buffer.at[at, half], sems.at[at, half]).start()


def wait_weights(parts, buffer, sems, at):
    for half in range(2):
        pltpu.make_async_copy(parts[0][half], buffer.at[at, half], sems.at[at, half]).wait()


def local_heads_body(
    out_ref_in, code_ref, gains_ref, *refs
):
    count = 4
    parts = halves_of(refs[0])
    qkv_ref, mixed_ref, middle_ref, normed_b_ref, a_t_ref, normed_a, local_in, buffer, sems = refs[1:]
    step = pl.program_id(0)
    frames = out_ref_in.shape[0]
    width = mixed_ref.shape[2]
    half = D // 2

    @pl.when(step == 0)
    def _():
        start_weights(parts, buffer, sems)
        for c in range(CB):
            rows = slice(c * frames, (c + 1) * frames)
            local_in[rows, :] = out_ref_in[...] + code_ref[rows, :].astype(jnp.float32)
            normed = norm_rows(local_in[rows, :], gains_ref[2:3, :]).astype(jnp.bfloat16)
            normed_a[rows, :] = normed
            a_t_ref[:, rows] = jnp.transpose(normed)
        middle_ref[...] = local_in[...]

    wait_weights(parts, buffer, sems, step)
    ones = head_sums(width)
    queries, keys, values = ([], [], [])
    for c in range(CB):
        rows = slice(c * frames, (c + 1) * frames)
        qkv = (
            dot_rows(normed_a[rows, :half], buffer[step, 0, :, : 3 * width])
            + dot_rows(normed_a[rows, half:], buffer[step, 1, :, : 3 * width])
        ).astype(jnp.bfloat16)
        qkv_ref[0, rows, :] = qkv
        queries.append(qkv[:, :width].astype(jnp.float32))
        keys.append(qkv[:, width : 2 * width].astype(jnp.float32))
        values.append(qkv[:, 2 * width :].astype(jnp.float32))
    prob = frame_probs(queries, keys, ones)
    for c in range(CB):
        rows = slice(c * frames, (c + 1) * frames)
        mix = rounded_f32(prob[c][0]) * values[0]
        for c2 in range(1, c + 1):
            mix = mix + rounded_f32(prob[c][c2]) * values[c2]
        mix = mix.astype(jnp.bfloat16)
        mixed_ref[0, rows, :] = mix
        for at in range(2):
            lanes = slice(at * half, (at + 1) * half)
            middle_ref[rows, lanes] += dot_transposed(mix, buffer[step, at, :, 3 * width :])

    @pl.when(step == count - 1)
    def _():
        for c in range(CB):
            rows = slice(c * frames, (c + 1) * frames)
            normed_b_ref[rows, :] = norm_rows(middle_ref[rows, :], gains_ref[3:4, :]).astype(
                jnp.bfloat16
            )


def local_heads(line, global_out, codes, gains, parts):
    frames = global_out.shape[0]
    rows = CB * frames
    width = parts.shape[2] // 4
    half = D // 2
    return line.run(
        local_heads_body,
        (global_out, codes, gains, parts),
        grid=(4,),
        in_specs=[held((frames, D)), held((rows, D)), held((4, D)), IN_HBM],
        out_specs=[
            pl.BlockSpec((1, rows, 3 * width), lambda step: (step, 0, 0)),
            pl.BlockSpec((1, rows, width), lambda step: (step, 0, 0)),
            held((rows, D)),
            held((rows, D)),
            held((D, rows)),
        ],
        out_shape=[
            shaped((4, rows, 3 * width), jnp.bfloat16),
            shaped((4, rows, width), jnp.bfloat16),
            shaped((rows, D), jnp.float32),
            shaped((rows, D), jnp.bfloat16),
            shaped((D, rows), jnp.bfloat16),
        ],
        scratch_shapes=[
            pltpu.VMEM((rows, D), jnp.bfloat16),
            pltpu.VMEM((rows, D), jnp.float32),
            pltpu.VMEM((4, 2, half, 4 * width), jnp.bfloat16),
            pltpu.SemaphoreType.DMA((4, 2)),
        ],
        limit=52,
        name="local_heads",
    )


def local_ff_body(source_ref, normed_ref, middle_ref, *refs):
    count = 4
    ups, downs = halves_of(refs[0]), halves_of(refs[1])
    active_ref, slope_ref, out_ref, b_t_ref, acc, up_buf, down_buf, up_sems, down_sems = refs[2:]
    step = pl.program_id(0)
    rows_all = normed_ref.shape[0]
    frames = rows_all // CB
    half = D // 2
    tile = active_ref.shape[2]
    per = up_buf.shape[3] // tile
    group = step // per

    @pl.when(step == 0)
    def _():
        for at in range(count):
            start_weights_at(ups, up_buf, up_sems, at)
            start_weights_at(downs, down_buf, down_sems, at)
        b_t_ref[...] = jnp.transpose(normed_ref[...])
        acc[...] = middle_ref[...]

    @pl.when(step % per == 0)
    def _():
        wait_weights(ups, up_buf, up_sems, group)
        wait_weights(downs, down_buf, down_sems, group)

    piece = 512
    pieces = [
        (slice(begin, begin + rows_all), pl.ds(pl.multiple_of((step % per) * tile + at * piece, piece), piece), at)
        for at in range(tile // piece)
        for begin in (0,)
    ]

    def raised(rows, lanes):
        return dot_rows(normed_ref[rows, :half], up_buf[group, 0, :, lanes]) + dot_rows(
            normed_ref[rows, half:], up_buf[group, 1, :, lanes]
        )

    upper = raised(*pieces[0][:2])
    for at, (rows, lanes, place) in enumerate(pieces):
        coming = raised(*pieces[at + 1][:2]) if at + 1 < len(pieces) else None
        active, slope = gelu_both(upper)
        here = slice(place * piece, (place + 1) * piece)
        active_ref[0, rows, here] = active
        slope_ref[0, rows, here] = slope
        for side in range(2):
            sides = slice(side * half, (side + 1) * half)
            acc[rows, sides] += dot_transposed(active, down_buf[group, side, :, lanes])
        upper = coming

    @pl.when(step == pl.num_programs(0) - 1)
    def _():
        owned = D // source_ref.shape[0]
        for c in range(CB):
            rows = slice(c * frames, (c + 1) * frames)
            for at in range(source_ref.shape[0]):
                here = slice(at * owned, (at + 1) * owned)
                out_ref[c, :, lanes_of(source_ref, at, owned)] = acc[rows, here].astype(jnp.bfloat16)


def start_weights_at(parts, buffer, sems, at):
    for half in range(2):
        pltpu.make_async_copy(parts[at][half], buffer.at[at, half], sems.at[at, half]).start()


def local_ff(line, source, normed, middle, ups, downs, tile=1024):
    rows = normed.shape[0]
    hidden = ups.shape[2]
    half = D // 2
    per = hidden // tile
    hidden_block = pl.BlockSpec((1, rows, tile), lambda step: (step // per, 0, step % per))
    return line.run(
        local_ff_body,
        (source, normed, middle, ups, downs),
        grid=(4 * per,),
        in_specs=[IN_SMEM, held((rows, D)), held((rows, D)), IN_HBM, IN_HBM],
        out_specs=[hidden_block, hidden_block, held((CB, rows // CB, D)), held((D, rows))],
        out_shape=[
            shaped((4, rows, hidden), jnp.bfloat16),
            shaped((4, rows, hidden), jnp.bfloat16),
            shaped((CB, rows // CB, D), jnp.bfloat16),
            shaped((D, rows), jnp.bfloat16),
        ],
        scratch_shapes=[
            pltpu.VMEM((rows, D), jnp.float32),
            pltpu.VMEM((4, 2, half, hidden), jnp.bfloat16),
            pltpu.VMEM((4, 2, half, hidden), jnp.bfloat16),
            pltpu.SemaphoreType.DMA((4, 2)),
            pltpu.SemaphoreType.DMA((4, 2)),
        ],
        limit=56,
        name="local_ff",
    )


def seed_body(source_ref, count_ref, cot_ref, code_ref, grad_ref, grad_t_ref, codes_ref):
    frames = cot_ref.shape[1]
    owned = D // source_ref.shape[0]
    keep = lax.broadcasted_iota(jnp.int32, (frames, 1), 0) < count_ref[0]
    for c in range(CB):
        rows = slice(c * frames, (c + 1) * frames)
        for at in range(source_ref.shape[0]):
            here = slice(at * owned, (at + 1) * owned)
            values = cot_ref[c, :, lanes_of(source_ref, at, owned)].astype(jnp.float32)
            grad_ref[rows, here] = jnp.where(keep, values, 0.0).astype(jnp.bfloat16)
            codes_ref[rows, here] = code_ref[c, :, lanes_of(source_ref, at, owned)]
        grad_t_ref[:, rows] = jnp.transpose(grad_ref[rows, :])


def seed(line, source, count, cot, codes):
    frames = cot.shape[1]
    rows = CB * frames
    return line.run(
        seed_body,
        (source, count, cot, codes),
        in_specs=[IN_SMEM, IN_SMEM, VMEM_WHOLE, VMEM_WHOLE],
        out_specs=[VMEM_WHOLE] * 3,
        out_shape=[
            shaped((rows, D), jnp.bfloat16),
            shaped((D, rows), jnp.bfloat16),
            shaped((rows, D), jnp.bfloat16),
        ],
        limit=60,
        name="seed_grads",
    )


def local_back_body(
    grad_h, grad_t_h, b_t_h, a_t_h, active_h, slope_h, qkv_h, mixed_h, middle_h, gout_h, codes_h, gains_ref, *refs
):
    heads_h, ups_h, downs_h = ([half for pair in halves_of(one) for half in pair] for one in refs[:3])
    refs = refs[3:]
    total_ref, small_out_ref, gain_c_ref, gain_d_ref, *results_h = refs[:12]
    (
        grad_v, grad_t, other_t, weights, act, slp, dup, acc, mid, gout_v, codes_v,
        pair_out, pair_far, pair_near, head_out, head_far, head_near, x_in, y_far, y_near,
        sems, send, recv,
    ) = refs[12:]
    frames = gout_v.shape[0]
    rows_all = grad_v.shape[0]
    half = D // 2
    width = mixed_h.shape[2]
    scale = HD ** (-0.5)
    greet((CORE, X, Y))

    def fetch(at, source, target):
        copy = pltpu.make_async_copy(source, target, sems.at[at])
        copy.start()
        return copy

    def give(at, hop, source, target):
        copy = to_partner(hop, source, target, send.at[at], recv.at[at])
        copy.start()
        return copy

    def fetch_ff(rel):
        found = [fetch(at, downs_h[2 * rel + at], weights.at[2 + at]) for at in range(2)]
        found.append(fetch(2, slope_h.at[rel], slp))
        return found + [fetch(3 + at, ups_h[2 * rel + at], weights.at[at]) for at in range(2)]

    order = (3, 2, 1, 0)
    waits = [fetch(5, grad_h, grad_v)] + fetch_ff(order[0])
    late = [fetch(6, grad_t_h, grad_t), fetch(7, active_h.at[order[0]], act), fetch(8, b_t_h, other_t)]
    later = [fetch(9, middle_h, mid), fetch(10, gout_h, gout_v), fetch(11, codes_h, codes_v)]
    acc[...] = jnp.zeros_like(acc)
    sent = []
    for step, rel in enumerate(order):
        for one in waits:
            one.wait()
        for tile in range(2):
            lanes = slice(tile * half, (tile + 1) * half)
            grad = dot_rows(grad_v[:, :half], weights[2, :, lanes]) + dot_rows(
                grad_v[:, half:], weights[3, :, lanes]
            )
            dup[:, lanes] = (grad * slp[:, lanes].astype(jnp.float32)).astype(jnp.bfloat16)
        for at in range(2):
            lanes = slice(at * half, (at + 1) * half)
            acc[:, lanes] += dot_transposed(dup[...], weights[at])
        if step < 3:
            waits = fetch_ff(order[step + 1])
        for one in late:
            one.wait()
        if step == 2:
            sent[0].wait_send()
        if step % 2 == 1:
            sent[step // 2].wait_recv()
        met = (None, pair_far, None, pair_near)[step]
        for at in range(2):
            rows = slice(at * half, (at + 1) * half)
            for tile in range(2):
                lanes = slice(tile * half, (tile + 1) * half)
                down = dot_rows(grad_t[rows, :], act[:, lanes])
                up = dot_rows(other_t[rows, :], dup[:, lanes])
                if met is None:
                    pair_out[0, rows, lanes] = down.astype(jnp.bfloat16)
                    pair_out[1, rows, lanes] = up.astype(jnp.bfloat16)
                else:
                    met[0, rows, lanes] = (down + met[0, rows, lanes].astype(jnp.float32)).astype(jnp.bfloat16)
                    met[1, rows, lanes] = (up + met[1, rows, lanes].astype(jnp.float32)).astype(jnp.bfloat16)
        if step < 3:
            late = [fetch(7, active_h.at[order[step + 1]], act)]
        if step == 0:
            sent.append(give(0, CORE, pair_out, pair_far))
        elif step == 2:
            sent.append(give(1, CORE, pair_out, pair_near))
        elif step == 1:
            x_far = give(2, X, pair_far.at[1, pl.ds(half, half)], x_in.at[pl.ds(half, half)])
            y_two = give(3, Y, pair_far.at[0, pl.ds(half, half)], y_far)
            x_near = give(4, X, pair_far.at[1, pl.ds(0, half)], x_in.at[pl.ds(0, half)])
        else:
            y_zero = give(5, Y, pair_near.at[0, pl.ds(half, half)], y_near)

    def fetch_heads(rel):
        found = [fetch(at, heads_h[2 * rel + at], weights.at[at]) for at in range(2)]
        found.append(fetch(2, qkv_h.at[rel], act.at[:, pl.ds(0, 3 * width)]))
        return found + [fetch(3, mixed_h.at[rel], slp.at[:, pl.ds(0, width)])]

    waits = fetch_heads(order[0]) + [fetch(8, a_t_h, other_t)]
    sent[1].wait_send()
    for one in later:
        one.wait()
    total_gain = jnp.zeros((1, D), jnp.float32)
    for c in range(CB):
        rows = slice(c * frames, (c + 1) * frames)
        part_back, gain_grad = norm_rows_back(mid[rows, :], gains_ref[3:4, :], acc[rows, :])
        total = grad_v[rows, :].astype(jnp.float32) + part_back
        mid[rows, :] = total
        small = total.astype(jnp.bfloat16)
        grad_v[rows, :] = small
        grad_t[:, rows] = jnp.transpose(small)
        total_gain = total_gain + gain_grad
    gain_d_ref[...] = total_gain

    ones = head_sums(width)
    heads_sent = []

    def more(total, term):
        return term if total is None else total + term

    for step, rel in enumerate(order):
        for one in waits:
            one.wait()
        queries, keys, values, dmix = ([], [], [], [])
        back = rounded_f32(
            dot_rows(grad_v[:, :half], weights[0, :, 3 * width :])
            + dot_rows(grad_v[:, half:], weights[1, :, 3 * width :])
        )
        for c in range(CB):
            rows = slice(c * frames, (c + 1) * frames)
            qkv = act[rows, : 3 * width].astype(jnp.float32)
            queries.append(qkv[:, :width])
            keys.append(qkv[:, width : 2 * width])
            values.append(qkv[:, 2 * width :])
            dmix.append(back[rows, :])
        prob = frame_probs(queries, keys, ones)
        dq, dk, dv = ([None] * CB, [None] * CB, [None] * CB)
        for c in range(CB):
            dprob = [over_heads(dmix[c] * values[c2], ones) for c2 in range(c + 1)]
            center = prob[c][0] * dprob[0]
            for c2 in range(1, c + 1):
                center = center + prob[c][c2] * dprob[c2]
            for c2 in range(c + 1):
                dv[c2] = more(dv[c2], rounded_f32(prob[c][c2]) * dmix[c])
                dscore = rounded_f32(prob[c][c2] * (dprob[c2] - center))
                dq[c] = more(dq[c], dscore * keys[c2])
                dk[c2] = more(dk[c2], dscore * queries[c])
        for c in range(CB):
            rows = slice(c * frames, (c + 1) * frames)
            dup[rows, :width] = (dq[c] * scale).astype(jnp.bfloat16)
            dup[rows, width : 2 * width] = (dk[c] * scale).astype(jnp.bfloat16)
            dup[rows, 2 * width : 3 * width] = dv[c].astype(jnp.bfloat16)
        for at in range(2):
            lanes = slice(at * half, (at + 1) * half)
            term = dot_transposed(dup[:, : 3 * width], weights[at, :, : 3 * width])
            acc[:, lanes] = term if step == 0 else acc[:, lanes] + term
        if step == 2:
            heads_sent[0].wait_send()
        if step % 2 == 1:
            heads_sent[step // 2].wait_recv()
        met = (None, head_far, None, head_near)[step]
        for at in range(2):
            rows = slice(at * half, (at + 1) * half)
            three = dot_rows(other_t[rows, :], dup[:, : 3 * width])
            one = dot_rows(grad_t[rows, :], slp[:, :width])
            if met is None:
                head_out[rows, : 3 * width] = three.astype(jnp.bfloat16)
                head_out[rows, 3 * width :] = one.astype(jnp.bfloat16)
            else:
                three = three + met[rows, : 3 * width].astype(jnp.float32)
                one = one + met[rows, 3 * width :].astype(jnp.float32)
                met[rows, : 3 * width] = three.astype(jnp.bfloat16)
                met[rows, 3 * width :] = one.astype(jnp.bfloat16)
        if step < 3:
            waits = fetch_heads(order[step + 1])
        if step == 0:
            heads_sent.append(give(6, CORE, head_out, head_far))
        elif step == 2:
            heads_sent.append(give(7, CORE, head_out, head_near))
    total_gain = jnp.zeros((1, D), jnp.float32)
    total = jnp.zeros((frames, D), jnp.float32)
    for c in range(CB):
        rows = slice(c * frames, (c + 1) * frames)
        local_in = gout_v[...] + codes_v[rows, :].astype(jnp.float32)
        part_back, gain_grad = norm_rows_back(local_in, gains_ref[2:3, :], acc[rows, :])
        total = total + (mid[rows, :] + part_back)
        total_gain = total_gain + gain_grad
    total_ref[...] = total
    small_out_ref[...] = total.astype(jnp.bfloat16)
    gain_c_ref[...] = total_gain

    heads_sent[1].wait_send()
    x_far.wait()
    x_near.wait()
    y_two.wait()
    y_zero.wait()

    def summed(one, two):
        return (one.astype(jnp.float32) + two.astype(jnp.float32)).astype(jnp.bfloat16)

    pair_near[1] = summed(pair_near[1], x_in[...])
    pair_far[0, :half, :] = summed(pair_far[0, :half, :], y_far[...])
    pair_near[0, :half, :] = summed(pair_near[0, :half, :], y_near[...])
    near, far = pl.ds(0, half), pl.ds(half, half)
    leaving = (
        pair_near.at[1, near], pair_near.at[1, far], pair_far.at[0, near], pair_near.at[0, near],
        head_far.at[near], head_far.at[far], head_near.at[near], head_near.at[far],
    )
    for one in [fetch(at, source, target) for at, (source, target) in enumerate(zip(leaving, results_h))]:
        one.wait()


def local_back(line, grad, grad_t, b_t, a_t, active, slope, qkv, mixed, middle, global_out, codes, gains, heads, ups, downs):
    rows, frames = grad.shape[0], global_out.shape[0]
    half = D // 2
    columns = ups.shape[2]
    small = jnp.bfloat16
    return line.run(
        local_back_body,
        (grad, grad_t, b_t, a_t, active, slope, qkv, mixed, middle, global_out, codes, gains, heads, ups, downs),
        in_specs=[IN_HBM] * 11 + [VMEM_WHOLE] + [IN_HBM] * 3,
        out_specs=[VMEM_WHOLE] * 4 + [IN_HBM] * 8,
        out_shape=[
            shaped((frames, D), jnp.float32),
            shaped((frames, D), small),
            shaped((1, D), jnp.float32),
            shaped((1, D), jnp.float32),
        ]
        + [shaped((half, columns), small)] * 8,
        scratch_shapes=[
            pltpu.VMEM((rows, D), small),
            pltpu.VMEM((D, rows), small),
            pltpu.VMEM((D, rows), small),
            pltpu.VMEM((4, half, columns), small),
            pltpu.VMEM((rows, columns), small),
            pltpu.VMEM((rows, columns), small),
            pltpu.VMEM((rows, columns), small),
            pltpu.VMEM((rows, D), jnp.float32),
            pltpu.VMEM((rows, D), jnp.float32),
            pltpu.VMEM((frames, D), jnp.float32),
            pltpu.VMEM((rows, D), small),
            pltpu.VMEM((2, D, columns), small),
            pltpu.VMEM((2, D, columns), small),
            pltpu.VMEM((2, D, columns), small),
            pltpu.VMEM((D, columns), small),
            pltpu.VMEM((D, columns), small),
            pltpu.VMEM((D, columns), small),
            pltpu.VMEM((D, columns), small),
            pltpu.VMEM((half, columns), small),
            pltpu.VMEM((half, columns), small),
            pltpu.SemaphoreType.DMA((12,)),
            pltpu.SemaphoreType.DMA((8,)),
            pltpu.SemaphoreType.DMA((8,)),
        ],
        hops=(CORE, X, Y),
        limit=58,
        name="local_back",
    )


def last_body(
    gains_ref, gu_near_h, gu_met_h, gh_near_h, gh_far_h, d0_h, d2_h, h0_near_h, h2_near_h, h0_far_h, h2_far_h,
    h_first_h, h2_first_h,
    gain_out_ref, gu_keep_h, gu_last_h, gh_keep_h, gh_last_h, d_keep_h, d_last_h, h_keep_h, h_send_h,
    gain_v, gain_met, held_v, met_v, extra_v, z_met, sems, send, recv,
):
    half = D // 2
    quarter = half // 2
    owned = quarter // 2
    flying, filed = [], []

    def fly(hop, source, target):
        at = len(flying)
        copy = to_partner(hop, source, target, send.at[at], recv.at[at])
        copy.start()
        flying.append(copy)
        return copy

    def file(source, target):
        copy = pltpu.make_async_copy(source, target, sems.at[len(filed)])
        copy.start()
        filed.append(copy)
        return copy

    def summed(*terms):
        total = terms[0].astype(jnp.float32)
        for term in terms[1:]:
            total = total + term.astype(jnp.float32)
        return total.astype(jnp.bfloat16)

    greet((CORE, X, Y, Z1, Z2))
    upper, lower = pl.ds(0, quarter), pl.ds(quarter, quarter)
    gain_core = fly(CORE, gains_ref, gain_met.at[0])
    gh_low = fly(Y, gh_far_h.at[lower], met_v.at[1, lower])
    d_low = fly(X, d2_h.at[lower], met_v.at[2, lower])
    gu_in = [file(gu_near_h, held_v.at[0]), file(gu_met_h, met_v.at[0])]
    far_in = [file(h0_far_h.at[lower], extra_v.at[0, lower]), file(h2_far_h, extra_v.at[1, lower])]
    rest_in = [file(gh_near_h, held_v.at[1]), file(d0_h, held_v.at[2]), file(h0_near_h, held_v.at[3])]
    rest_in += [file(h2_first_h, met_v.at[3, upper]), file(h_first_h, extra_v.at[2, upper])]
    gain_core.wait_recv()
    gain_v[0] = gains_ref[...] + gain_met[0]
    gain_1 = fly(Z1, gain_v.at[0], gain_met.at[1])
    for one in gu_in:
        one.wait()
    held_v[0] = summed(held_v[0], met_v[0])
    gu_1 = fly(Z1, held_v.at[0, lower], z_met.at[0])
    gain_1.wait_recv()
    gain_v[1] = gain_v[0] + gain_met[1]
    gain_2 = fly(Z2, gain_v.at[1], gain_met.at[2])
    gh_up = fly(Y, gh_far_h.at[upper], met_v.at[1, upper])
    gain_2.wait_recv()
    gain_v[2] = gain_v[1] + gain_met[2]
    gain_x = fly(X, gain_v.at[2], gain_met.at[3])
    d_up = fly(X, d2_h.at[upper], met_v.at[2, upper])
    h_x = fly(X, h2_near_h.at[lower], met_v.at[3, lower])
    for one in far_in:
        one.wait()
    extra_v[0, quarter:, :] = summed(extra_v[0, quarter:, :], extra_v[1, quarter:, :])
    for one in rest_in:
        one.wait()
    done = []

    def add(at, first):
        rows = slice(0, quarter) if first else slice(quarter, half)
        held_v[at, rows, :] = summed(held_v[at, rows, :], met_v[at, rows, :])

    def second(at, first, last_h, keep_h):
        first.wait_recv()
        held_v[at, :quarter, :] = summed(held_v[at, :quarter, :], z_met[at])
        done.append(file(held_v.at[at, pl.ds(0, owned)], keep_h))
        return fly(Z2, held_v.at[at, pl.ds(owned, owned)], last_h)

    gh_low.wait_recv()
    add(1, False)
    gh_1 = fly(Z1, held_v.at[1, lower], z_met.at[1])
    d_low.wait_recv()
    add(2, False)
    gain_x.wait_recv()
    gain_v[3] = gain_v[2] + gain_met[3]
    gain_y = fly(Y, gain_v.at[3], gain_met.at[4])
    h_y = fly(Y, extra_v.at[0, lower], extra_v.at[2, lower])
    gu_2 = second(0, gu_1, gu_last_h, gu_keep_h)
    gh_up.wait_recv()
    add(1, True)
    gh_2 = second(1, gh_1, gh_last_h, gh_keep_h)
    d_1 = fly(Z1, held_v.at[2, lower], z_met.at[2])
    d_up.wait_recv()
    add(2, True)
    gain_y.wait_recv()
    gain_out_ref[...] = gain_v[3] + gain_met[4]
    h_x.wait_recv()
    h_y.wait_recv()
    held_v[3] = summed(held_v[3], met_v[3], extra_v[2])
    done.append(file(held_v.at[3, upper], h_keep_h))
    done.append(file(held_v.at[3, lower], h_send_h))
    d_1.wait_recv()
    held_v[2, :quarter, :] = summed(held_v[2, :quarter, :], z_met[2])
    done.append(file(held_v.at[2, pl.ds(0, owned)], d_keep_h))
    done.append(file(held_v.at[2, pl.ds(owned, owned)], d_last_h))
    for one in (gu_2, gh_2):
        one.wait_recv()
    for one in done:
        one.wait()
    for one in flying:
        one.wait_send()


def last_transfers(line, gains, parts):
    half, columns = parts[0].shape
    owned = half // 4
    low = jnp.bfloat16
    return line.run(
        last_body,
        (gains, *parts),
        in_specs=[VMEM_WHOLE] + [IN_HBM] * 12,
        out_specs=[VMEM_WHOLE] + [IN_HBM] * 8,
        out_shape=[shaped(gains.shape, jnp.float32)]
        + [shaped((owned, columns), low)] * 6
        + [shaped((2 * owned, columns), low)] * 2,
        scratch_shapes=[
            pltpu.VMEM((4,) + gains.shape, jnp.float32),
            pltpu.VMEM((5,) + gains.shape, jnp.float32),
            pltpu.VMEM((4, half, columns), low),
            pltpu.VMEM((4, half, columns), low),
            pltpu.VMEM((3, half, columns), low),
            pltpu.VMEM((3, half // 2, columns), low),
            pltpu.SemaphoreType.DMA((16,)),
            pltpu.SemaphoreType.DMA((16,)),
            pltpu.SemaphoreType.DMA((16,)),
        ],
        hops=(CORE, X, Y, Z1, Z2),
        limit=60,
        name="last_transfers",
    )


def add_body(*refs):
    total = refs[0][...].astype(jnp.float32)
    for ref in refs[1:-1]:
        total = total + ref[...].astype(jnp.float32)
    refs[-1][...] = total.astype(jnp.bfloat16)


def add_rows(line, terms, part=0, parts=1):
    rows = min(term.shape[0] for term in terms) if parts == 1 else terms[0].shape[0] // parts
    columns = terms[0].shape[1]

    def spec(term):
        return pl.BlockSpec(
            (rows, columns), (lambda step: (part, 0)) if term.shape[0] > rows else (lambda step: (0, 0))
        )

    return line.run(
        add_body,
        tuple(terms),
        grid=(1,),
        in_specs=[spec(term) for term in terms],
        out_specs=[pl.BlockSpec((rows, columns), lambda step: (0, 0))],
        out_shape=[shaped((rows, columns), jnp.bfloat16)],
        limit=24,
        name="add_terms",
    )[0]


def sum_pieces(line, terms, split=()):
    rows, columns = terms[0].shape[0] // 2, terms[0].shape[1]
    whole = len(terms)
    flat = list(terms) + [one for pair in split for one in pair]

    def body(*refs):
        for at, out_ref in enumerate(refs[-2:]):
            here = slice(at * rows, (at + 1) * rows)
            total = refs[0][here, :].astype(jnp.float32)
            for ref in refs[1:whole]:
                total = total + ref[here, :].astype(jnp.float32)
            for ref in refs[whole + at : -2 : 2]:
                total = total + ref[...].astype(jnp.float32)
            out_ref[...] = total.astype(jnp.bfloat16)

    return line.run(
        body,
        tuple(flat),
        in_specs=[VMEM_WHOLE] * len(flat),
        out_specs=[VMEM_WHOLE] * 2,
        out_shape=[shaped((rows, columns), jnp.bfloat16)] * 2,
        limit=24,
        name="sum_pieces",
    )


def pass_body(*refs):
    pass


def in_turn(line, *values):
    return line.run(
        pass_body,
        tuple(values),
        in_specs=[IN_HBM] * len(values),
        out_specs=[IN_HBM] * len(values),
        out_shape=[shaped(one.shape, one.dtype) for one in values],
        aliases={at: at for at in range(len(values))},
        name="in_turn",
    )


def split_dot(left, right):
    left_high = left.astype(jnp.bfloat16)
    left_low = (left - left_high.astype(jnp.float32)).astype(jnp.bfloat16)
    right_high = right.astype(jnp.bfloat16)
    right_low = (right - right_high.astype(jnp.float32)).astype(jnp.bfloat16)
    return (
        dot_rows(left_high, right_high) + dot_rows(left_high, right_low) + dot_rows(left_low, right_high)
    )


def adam_body(chained, one_ref, two_ref, left_ref, right_ref, master_ref, first_ref, second_ref, ema_ref, *refs):
    grads_ref, new_master_ref, new_first_ref, new_second_ref, new_ema_ref = refs[5:] if chained else refs
    left = left_ref[0]
    left_t = jnp.transpose(left)
    grads = one_ref[...].astype(jnp.float32) + two_ref[...].astype(jnp.float32)
    grads_ref[0] = grads
    turned_left = split_dot(left_t, grads)
    back = []
    for at in range(right_ref.shape[1]):
        tile = slice(at * 128, (at + 1) * 128)
        right = right_ref[0, at]
        rotated = split_dot(turned_left[:, tile], right)
        new_first = beta_first * first_ref[0, :, tile] + (1.0 - beta_first) * rotated
        new_second = beta_second * second_ref[0, :, tile] + (1.0 - beta_second) * rotated * rotated
        new_first_ref[0, :, tile] = new_first
        new_second_ref[0, :, tile] = new_second
        turned = new_first / (jnp.sqrt(new_second) + adam_eps)
        back.append(split_dot(turned, jnp.transpose(right)))
    back_full = split_dot(left, jnp.concatenate(back, axis=1))
    new_master = master_ref[0] - step_rate * back_full
    new_master_ref[0] = new_master
    new_ema_ref[0] = ema_decay * ema_ref[0] + (1.0 - ema_decay) * new_master


def adam(line, layer, third, pieces, left, right, master, first, second, ema, before, tile=1024):
    owned, columns = pieces[0].shape
    steps = columns // tile
    first_step = third * steps

    def state(step):
        return (layer, 0, first_step + step)

    state_spec = pl.BlockSpec((1, owned, tile), state)
    chained = before is not None
    return line.run(
        lambda *refs: adam_body(chained, *refs),
        (*pieces, left, right, master, first, second, ema, *(before or ()),),
        grid=(steps,),
        in_specs=[by_cols((owned, tile))] * 2
        + [
            pl.BlockSpec((1,) + left.shape[1:], lambda step: (layer, 0, 0)),
            pl.BlockSpec(
                (1, tile // 128) + right.shape[2:], lambda step: (layer, first_step + step, 0, 0)
            ),
        ]
        + [state_spec] * 4
        + ([IN_HBM] * 5 if chained else []),
        out_specs=[state_spec] * 5,
        out_shape=[shaped(master.shape, jnp.float32)] * 5,
        aliases={8 + at: at for at in range(5)} if chained else {},
        limit=32,
        name="adam_update",
    )


def hop_x(values):
    return lax.ppermute(values, TENSOR, [(at, at ^ 2) for at in range(4)])


def hop_core(values):
    return lax.ppermute(values, TENSOR, [(at, at ^ 1) for at in range(4)])


def hop_y(values):
    return lax.ppermute(values, DP, [(at, at ^ 1) for at in range(8)])


def hop_z(values, step):
    return lax.ppermute(values, DP, [(at, at ^ (2 * step)) for at in range(8)])


def shards_grid(
    frames_in,
    code_emb,
    cotangent,
    lengths,
    owner_list,
    master,
    first_moment,
    second_moment,
    ema,
    left_basis,
    right_basis,
    gains,
    gain_first,
    gain_second,
):
    share = frames_in.shape[0]
    owned = master.shape[1]
    groups = D // owned
    heads_w = D // lax.axis_size(TENSOR)
    ff_w = FF // lax.axis_size(TENSOR)
    my_dp = lax.axis_index(DP)
    my_group = lax.axis_index(TENSOR).astype(jnp.int32)

    rel = jnp.array([2 * z + y for y in range(2) for z in (0, 2, 1, 3)], jnp.int32)
    owner_at = my_dp ^ rel
    slots = jnp.arange(groups, dtype=jnp.int32)
    source = jnp.sum(
        jnp.where(owner_list[None, :] == owner_at[:, None], slots[None, :], 0), axis=1
    ).astype(jnp.int32)
    info = jnp.stack([my_group, lengths[0]])
    count = (lengths - my_group * share).astype(jnp.int32)

    line = Line()
    codes = jnp.transpose(code_emb, (1, 0, 2))

    (rows_in, gains_here, normed), shards = prep(line, source, frames_in, gains, master)
    grad, grad_t, codes_here = seed(line, source, count, jnp.transpose(cotangent, (1, 0, 2)), codes)
    (
        g_heads, g_up, g_down, l_heads, l_up, l_down, qkv, mixed, lse, middle, global_out, normed_a, normed_b,
        active, slope,
    ) = forward_global(line, info, rows_in, normed, gains_here, shards)

    l_qkv, l_mixed, l_middle, l_normed_b, l_a_t = local_heads(
        line, global_out, codes_here, gains_here, l_heads
    )
    l_active, l_slope, local_out, l_b_t = local_ff(line, source, l_normed_b, l_middle, l_up, l_down)
    local_out = jnp.transpose(local_out, (1, 0, 2))

    (
        grad_global, small, gain_c, gain_d, u_near, u_far, d2, d0, h2_near, h2_far, h0_near, h0_far,
    ) = local_back(
        line, grad, grad_t, l_b_t, l_a_t, l_active, l_slope, l_qkv, l_mixed, l_middle, global_out, codes_here,
        gains_here, l_heads, l_up, l_down,
    )
    def update(layer, third, pieces, before):
        return adam(
            line, layer, third, pieces, left_basis, right_basis, master, first_moment, second_moment, ema, before
        )

    def depth_second(keep, met):
        keep, send = sum_pieces(line, [keep, met])
        return keep, hop_z(send, 2)

    (
        grad_middle, grad_sum, gain_b, gu_near, gu_met, gh_near, gh_far, lu_keep, lu_met, gd_keep, gd_met, h2_met,
        h_first, h2_first,
    ) = backward_global(
        line, info, small, grad_global, middle, gains_here, lse, (g_up, g_down, g_heads), active, slope, normed_b,
        normed_a, qkv, mixed, (u_near, u_far, h2_far, h0_far, h2_near),
    )
    input_grad, gain_grads = finish(
        line, source, rows_in, grad_sum, grad_middle, gains_here, (gain_b, gain_c, gain_d)
    )
    (
        gain_grads, gu_keep, gu_met, gh_keep, gh_met, ld_keep, ld_send, lh_keep, lh_send,
    ) = last_transfers(
        line,
        gain_grads,
        (gu_near, gu_met, gh_near, gh_far, d0, d2, h0_near, h2_near, h0_far, h2_met, h_first, h2_first),
    )
    lh_met = hop_z(lh_send, 1)
    ld_met = hop_z(ld_send, 2)
    found = update(1, 1, (lu_keep, lu_met), None)
    found = update(0, 2, (gd_keep, gd_met), found)
    found = update(0, 1, (gu_keep, gu_met), found)
    lh = depth_second(lh_keep, lh_met)
    found = update(0, 0, (gh_keep, gh_met), found)
    found = update(1, 2, (ld_keep, ld_met), found)
    found = update(1, 0, lh, found)
    weight_grads, new_master, new_first, new_second, new_ema = found
    new_gain_first = beta_first * gain_first + (1.0 - beta_first) * gain_grads
    new_gain_second = beta_second * gain_second + (1.0 - beta_second) * gain_grads * gain_grads
    new_gains = gains - gain_rate * new_gain_first / (jnp.sqrt(new_gain_second) + adam_eps)
    return (
        local_out,
        input_grad,
        weight_grads,
        gain_grads,
        new_master,
        new_first,
        new_second,
        new_ema,
        new_gains,
        new_gain_first,
        new_gain_second,
    )


def solution(mesh):
    fits = mesh.shape[DP] == 8 and mesh.shape[TENSOR] == 4
    return jax.shard_map(
        shards_grid if fits else shards_any,
        mesh=mesh,
        in_specs=(
            P((DP, TENSOR), None),
            P((DP, TENSOR), None, None),
            P((DP, TENSOR), None, None),
            P(DP),
            P(),
            P(None, DP, TENSOR),
            P(None, DP, TENSOR),
            P(None, DP, TENSOR),
            P(None, DP, TENSOR),
            P(None, DP, TENSOR),
            P(None, DP, None, TENSOR),
            P(),
            P(),
            P(),
        ),
        out_specs=(
            P((DP, TENSOR), None, None),
            P((DP, TENSOR), None),
            P(None, DP, TENSOR),
            P(),
            P(None, DP, TENSOR),
            P(None, DP, TENSOR),
            P(None, DP, TENSOR),
            P(None, DP, TENSOR),
            P(),
            P(),
            P(),
        ),
        check_vma=False,
    )
```
